32 devices in a mesh: grp: 2 (over y), ctx: 4 (over z), head: 4 (over x, core).
Axes of the slice: x: 2, y: 2, z: 4, core: 2. Of those that a mesh axis runs over, the one named last changes fastest.
Arguments:
- key_rows: bfloat16 [8192, 8, 128], P(('grp', 'ctx'), 'head'), parts along dimension 0, may hold values from -6 to 6
- value_rows: bfloat16 [8192, 8, 128], P(('grp', 'ctx'), 'head'), parts along dimension 0, may hold values from -6 to 6
- cluster_labels: int32 [8, 8192], P('head', ('grp', 'ctx')), parts along dimension 1, may hold values from 0 to 4095, as said below
- owner_bounds: int32 [16, 5], P(('grp', 'head')), parts along dimension 0, may hold values from 0 to 4096, as said below
- init_centroids: float32 [16, 4096, 128], P(('grp', 'head')), parts along dimension 0, may hold values from -6 to 6
Outputs:
- centroids: float32 [16, 4096, 128], P(('grp', 'head'), 'ctx'), parts along dimension 0
- regrouped_keys: bfloat16 [16384, 8, 128], P(('grp', 'ctx'), 'head'), parts along dimension 0
- regrouped_values: bfloat16 [16384, 8, 128], P(('grp', 'ctx'), 'head'), parts along dimension 0
The draws below stay inside these ranges and needn't reach their ends.
There are 2 independent parts, one for each index of `grp`. The reference program is written for one: setup_inputs(seed, part) draws one part's arguments, and reference() takes and returns one part's arrays. A program takes and returns all parts, laid end to end along the dimension named above; each array names one. Nothing has to cross between parts.
Inputs may be any that keep to these rules, and one draw needn't show every extreme that they name: `cluster_labels`: for each head, each device's 1024 tokens hold at most 512 labels in the cluster range of any one owner; in every draw one owner of each head gets exactly 512 from every device, 2048 in all. `owner_bounds`: each row starts at 0, ends at 4096 and rises strictly.
All inputs are finite; a program needn't handle non-finite values.
Results may differ from the reference program's by a relative error of at most 0.011.
Values may be sent and summed in bfloat16 or wider, within the bound.
No kernel may reach another device: no remote copies, remote signals or barrier semaphores. Data moves between devices by JAX's collectives and lax.ppermute only.
A program may use at most 128 MiB of HBM per device.

```python
import jax
import jax.numpy as jnp
from jax import lax

H = 8
HEAD_DIM = 128
C = 4096
ITERS = 2
TOK_DEV = 1024
TOKENS = 4096
CAP = 2048
N_CTX = 4


def cluster_plan(key):
    bound_key, heavy_key, shift_key, shuffle_key, label_key = jax.random.split(key, 5)

    def one_bounds(head_key):
        cut_points = jnp.sort(jax.random.permutation(head_key, C - 1)[:N_CTX - 1] + 1).astype(jnp.int32)
        return jnp.concatenate([jnp.zeros((1,), jnp.int32), cut_points, jnp.full((1,), C, jnp.int32)])
    bounds = jax.vmap(one_bounds)(jax.random.split(bound_key, H))
    slot_size = 2 * TOK_DEV // N_CTX
    others = N_CTX - 1
    rest_rows = TOK_DEV - slot_size
    low_load = rest_rows // others
    extra_rows = rest_rows % others
    pair_count = others // 2 + 1
    heavy_owner = jax.random.randint(heavy_key, (H,), 0, N_CTX).astype(jnp.int32)
    shift_sizes = jax.random.randint(shift_key, (H, N_CTX, pair_count), 0, low_load // 2 + 1).astype(jnp.int32)
    other_slot = jnp.arange(others, dtype=jnp.int32)
    base_load = low_load + (other_slot < extra_rows).astype(jnp.int32)
    pair_shift = shift_sizes[:, :, other_slot // 2]
    gives_rows = (other_slot % 2 == 0) & (other_slot + 1 < others)
    takes_rows = other_slot % 2 == 1
    other_load = base_load - jnp.where(gives_rows, pair_shift, 0) + jnp.where(takes_rows, pair_shift, 0)
    owner_ids = jnp.arange(N_CTX, dtype=jnp.int32)
    after_heavy = (owner_ids[None, :] > heavy_owner[:, None]).astype(jnp.int32)
    other_index = jnp.clip(owner_ids[None, :] - after_heavy, 0, others - 1)
    head_index = jnp.arange(H, dtype=jnp.int32)[:, None, None]
    source_index = jnp.arange(N_CTX, dtype=jnp.int32)[None, :, None]
    gathered_load = other_load[head_index, source_index, other_index[:, None, :]]
    is_heavy = owner_ids[None, None, :] == heavy_owner[:, None, None]
    owner_load = jnp.where(is_heavy, slot_size, gathered_load).astype(jnp.int32)
    load_ends = jnp.cumsum(owner_load, axis=2)
    positions = jnp.arange(TOK_DEV, dtype=jnp.int32)
    ordered_owner = jnp.sum((positions[None, None, :, None] >= load_ends[:, :, None, :]).astype(jnp.int32), axis=3)
    shuffle_keys = jax.random.split(shuffle_key, H * N_CTX)
    token_owner = jax.vmap(jax.random.permutation)(shuffle_keys, ordered_owner.reshape(H * N_CTX, TOK_DEV))
    token_owner = token_owner.reshape(H, N_CTX, TOK_DEV)
    range_start = bounds[head_index, token_owner]
    range_size = bounds[head_index, token_owner + 1] - range_start
    raw_bits = jax.random.randint(label_key, (H, N_CTX, TOK_DEV), 0, 1 << 30).astype(jnp.int32)
    labels = range_start + raw_bits % range_size
    return (bounds, labels.reshape(H, TOKENS).astype(jnp.int32))


def draw_cluster_labels(key, part):
    return cluster_plan(key)[1]


def draw_owner_bounds(key, part):
    return cluster_plan(key)[0]


def steps_of(stream_key, dims, cuts, low, largest):
    gain = 1.0
    for position, parts in cuts:
        heights = jax.random.uniform(jax.random.fold_in(jax.random.fold_in(stream_key, 6), position), (parts,), jnp.float32, low / len(cuts), largest / len(cuts))
        gain = gain * jnp.repeat(jnp.exp(heights), dims[position] // parts).reshape((-1,) + (1,) * (len(dims) - 1 - position))
    return gain


def scatter_about(stream_key, dims, scale, limit, cuts=(), kind=jnp.bfloat16):
    factor_of = steps_of(stream_key, dims, cuts, -0.22, 0.18) if cuts else 1.0
    values = jax.random.normal(stream_key, dims, jnp.float32) * scale * factor_of
    return jnp.minimum(jnp.maximum(values, -limit), limit).astype(kind)


def setup_inputs(seed: int = 0, part: int = 0) -> dict:
    key_list = jax.random.split(jax.random.key(seed), 6)
    part_keys = jax.random.split(jax.random.fold_in(key_list[5], part), 6)
    key_rows = scatter_about(part_keys[0], (TOKENS, H, HEAD_DIM), 1.0, 6.0, ((0, 4), (1, 4)))
    value_rows = scatter_about(part_keys[1], (TOKENS, H, HEAD_DIM), 1.0, 6.0, ((0, 4), (1, 4)))
    cluster_labels = draw_cluster_labels(jax.random.fold_in(jax.random.fold_in(key_list[5], part), 71), part)
    owner_bounds = draw_owner_bounds(jax.random.fold_in(jax.random.fold_in(key_list[5], part), 71), part)
    init_centroids = scatter_about(part_keys[4], (H, C, HEAD_DIM), 1.0, 6.0, ((0, 4),), jnp.float32)
    return dict(key_rows=key_rows, value_rows=value_rows, cluster_labels=cluster_labels, owner_bounds=owner_bounds, init_centroids=init_centroids)


INV_TEMP = 20.0

def unit_rows(matrix):
    matrix = matrix.astype(jnp.float32)
    return matrix * lax.rsqrt(lax.optimization_barrier(jnp.sum(matrix * matrix, axis=-1, keepdims=True)) + 1e-06)

def soft_sums(unit_keys, centroid_bf):
    block_size = min(512, unit_keys.shape[0])
    blocks = unit_keys.reshape(-1, block_size, unit_keys.shape[1])

    def add_block(running, block_rows):
        scores = jnp.dot(block_rows, centroid_bf.T, preferred_element_type=jnp.float32)
        raw_weight = jnp.exp((scores - 1.0) * INV_TEMP)
        weights = (raw_weight / lax.optimization_barrier(jnp.sum(raw_weight, axis=1, keepdims=True))).astype(jnp.bfloat16)
        return (running + jnp.dot(weights.T, block_rows, preferred_element_type=jnp.float32), None)
    start = jnp.zeros((centroid_bf.shape[0], unit_keys.shape[1]), jnp.float32)
    summed, _ = lax.scan(add_block, start, blocks)
    return summed

def cluster_head(head_keys, head_start):
    unit_keys = unit_rows(head_keys).astype(jnp.bfloat16)
    centroid = unit_rows(head_start)
    for iteration in range(ITERS):
        centroid = unit_rows(soft_sums(unit_keys, centroid.astype(jnp.bfloat16)))
    return centroid

def regroup_head(head_keys, head_values, head_labels, bounds):
    sorted_order = jnp.argsort(head_labels, stable=True).astype(jnp.int32)
    sorted_labels = head_labels[sorted_order]
    starts = jnp.searchsorted(sorted_labels, bounds).astype(jnp.int32)
    counts = starts[1:] - starts[:-1]
    slot_lane = jnp.arange(CAP, dtype=jnp.int32)
    slot_index = starts[:-1, None] + slot_lane[None, :]
    row_mask = (slot_lane[None, :] < counts[:, None]).reshape(-1, 1)
    pick_rows = sorted_order[jnp.clip(slot_index, 0, TOKENS - 1).reshape(-1)]
    zero_value = jnp.zeros((), head_keys.dtype)
    return (jnp.where(row_mask, head_keys[pick_rows], zero_value), jnp.where(row_mask, head_values[pick_rows], zero_value))

def reference(key_rows, value_rows, cluster_labels, owner_bounds, init_centroids):
    by_head_keys = key_rows.transpose(1, 0, 2)
    by_head_values = value_rows.transpose(1, 0, 2)
    centroids = lax.map(lambda pair: cluster_head(pair[0], pair[1]), (by_head_keys, init_centroids))
    placed_keys, placed_values = lax.map(lambda quad: regroup_head(quad[0], quad[1], quad[2], quad[3]), (by_head_keys, by_head_values, cluster_labels, owner_bounds))
    return (centroids, placed_keys.transpose(1, 0, 2), placed_values.transpose(1, 0, 2))
```

```python
import functools
import math

import jax
import jax.numpy as jnp
from jax import lax
from jax.experimental import pallas as pl
from jax.experimental.pallas import tpu as pltpu
from jax.sharding import PartitionSpec as P

LANES = 128
EXP2_SCALE = 20.0 * math.log2(math.e)
VMEM_LIMIT = 56 * 1024 * 1024
F32 = jnp.float32
BF16 = jnp.bfloat16
NT = (((1,), (1,)), ((), ()))
NN = (((1,), (0,)), ((), ()))


def dot_nt(a, b):
    return lax.dot_general(a, b, NT, preferred_element_type=F32)


def dot_nn(a, b):
    return lax.dot_general(a, b, NN, preferred_element_type=F32)


def unit_rows(x):
    return x * lax.rsqrt(jnp.sum(x * x, axis=-1, keepdims=True) + 1e-06)


def params(**kwargs):
    return pltpu.CompilerParams(vmem_limit_bytes=VMEM_LIMIT, **kwargs)


def whole(shape):
    return pl.BlockSpec(shape, lambda *_: (0,) * len(shape))


def row_to_lanes(row):
    return jnp.transpose(jnp.broadcast_to(row, (LANES, LANES)))


def split_heads(flat_ref, wide_ref):
    wide_ref[...] = flat_ref[...].astype(F32)


def head_rows(wide_ref, head, heads):
    if heads == 1:
        return wide_ref[...]
    return wide_ref[pl.Slice(head, wide_ref.shape[0] // heads, heads), :]


def totals_kernel(keys_ref, cent_ref, tot_ref, wide_ref, unit_ref, sum_ref):
    head, step = pl.program_id(0), pl.program_id(1)
    heads, tokens, _ = unit_ref.shape

    @pl.when((head == 0) & (step == 0))
    def _():
        split_heads(keys_ref, wide_ref)
        for h in range(heads):
            unit_ref[h] = unit_rows(head_rows(wide_ref, h, heads)).astype(BF16)

    @pl.when(step == 0)
    def _():
        sum_ref[...] = jnp.zeros_like(sum_ref)

    rows = cent_ref.shape[1]
    cent = unit_rows(cent_ref[0]).astype(BF16)
    part = 256
    for t in range(0, tokens, part):
        total = sum_ref[:, t : t + part]
        unit = unit_ref[head, t : t + part, :]
        for c in range(0, rows, part):
            raw = jnp.exp2(dot_nt(cent[c : c + part], unit) * EXP2_SCALE)
            total += jnp.sum(raw.reshape(-1, 8, part), axis=0)
        sum_ref[:, t : t + part] = total

    @pl.when(step == pl.num_programs(1) - 1)
    def _():
        tot_ref[0] = jnp.sum(sum_ref[...], axis=0, keepdims=True)


def own_totals(keys, cents):
    heads, count, width = cents.shape
    tokens = keys.shape[0] // heads
    rows = min(1024, count)
    return pl.pallas_call(
        totals_kernel,
        grid=(heads, count // rows),
        in_specs=[
            whole(keys.shape),
            pl.BlockSpec((1, rows, width), lambda h, c: (h, c, 0)),
        ],
        out_specs=pl.BlockSpec((1, 1, tokens), lambda h, c: (h, 0, 0)),
        out_shape=jax.ShapeDtypeStruct((heads, 1, tokens), F32),
        scratch_shapes=[
            pltpu.VMEM(keys.shape, F32),
            pltpu.VMEM((heads, tokens, width), BF16),
            pltpu.VMEM((8, tokens), F32),
        ],
        compiler_params=params(),
        cost_estimate=pl.CostEstimate(
            flops=2 * heads * tokens * count * width * 2,
            bytes_accessed=cents.size * 4,
            transcendentals=heads * tokens * count,
        ),
        name="own_totals",
    )(keys, cents)


def rank_kernel(own_ref, all_ref, rank_ref):
    count = all_ref.shape[2]
    tokens = own_ref.shape[2]
    mine = jnp.broadcast_to(own_ref[0], (8, tokens))

    def step(i, total):
        row = all_ref[0, :, pl.ds(pl.multiple_of(i * LANES, LANES), LANES)]
        column = row_to_lanes(row)
        for r in range(0, LANES, 8):
            other = jnp.tile(column[r : r + 8], (1, tokens // LANES))
            total += (other < mine).astype(jnp.int32)
        return total

    total = lax.fori_loop(
        0, count // LANES, step, jnp.zeros((8, tokens), jnp.int32)
    )
    rank_ref[0] = jnp.sum(total, axis=0, keepdims=True)


def own_ranks(own, everyone):
    heads, tokens = own.shape
    count = everyone.shape[1]
    return pl.pallas_call(
        rank_kernel,
        grid=(heads,),
        in_specs=[
            pl.BlockSpec((1, 1, tokens), lambda h: (h, 0, 0)),
            pl.BlockSpec((1, 1, count), lambda h: (h, 0, 0)),
        ],
        out_specs=pl.BlockSpec((1, 1, tokens), lambda h: (h, 0, 0)),
        out_shape=jax.ShapeDtypeStruct((heads, 1, tokens), jnp.int32),
        compiler_params=params(),
        cost_estimate=pl.CostEstimate(
            flops=3 * heads * tokens * count, bytes_accessed=65536, transcendentals=0
        ),
        name="own_ranks",
    )(own[:, None, :], everyone[:, None, :])[:, 0, :]


def first_kernel(fresh, keys_ref, tot_ref, cent_ref, *refs):
    if fresh:
        sums_ref, unit_ref, wide_ref, scaled_ref = refs
    else:
        before_ref, _, sums_ref, unit_ref, wide_ref, scaled_ref = refs
    head = pl.program_id(0)
    tokens = unit_ref.shape[1]

    @pl.when(head == 0)
    def _():
        split_heads(keys_ref, wide_ref)

    inverse = 1.0 / tot_ref[0]
    heads = keys_ref.shape[0] // tokens
    unit_ref[0] = unit_rows(head_rows(wide_ref, head, heads)).astype(BF16)
    for t in range(0, tokens, LANES):
        scaled_ref[t : t + LANES] = (
            unit_ref[0, t : t + LANES, :].astype(F32)
            * row_to_lanes(inverse[:, t : t + LANES])
        ).astype(BF16)

    rows = cent_ref.shape[1]
    part = 256
    for c in range(0, rows, part):
        cent = cent_ref[0, c : c + part]
        if fresh:
            total = jnp.zeros((part, cent.shape[1]), F32)
        else:
            total = before_ref[0, c : c + part]
        for t in range(0, tokens, part):
            raw = jnp.exp2(dot_nt(cent, unit_ref[0, t : t + part, :]) * EXP2_SCALE)
            total += dot_nn(raw.astype(BF16), scaled_ref[t : t + part])
        sums_ref[0, c : c + part] = total


def first_block(keys, totals, cents, block, blocks, before):
    heads, rows, width = cents.shape
    tokens = keys.shape[0] // heads
    sums = jax.ShapeDtypeStruct(cents.shape, F32)
    units = jax.ShapeDtypeStruct((heads, blocks * tokens, width), BF16)
    share = pl.BlockSpec((1, rows, width), lambda h: (h, 0, 0))
    in_specs = [
        whole(keys.shape),
        pl.BlockSpec((1, 1, tokens), lambda h: (h, 0, 0)),
        share,
    ]
    args = [keys, totals, cents]
    aliases = {}
    if before is not None:
        in_specs += [share, pl.BlockSpec(memory_space=pl.ANY)]
        args += list(before)
        aliases = {3: 0, 4: 1}
    return pl.pallas_call(
        functools.partial(first_kernel, before is None),
        grid=(heads,),
        in_specs=in_specs,
        out_specs=(
            share,
            pl.BlockSpec((1, tokens, width), lambda h: (h, block, 0)),
        ),
        out_shape=(sums, units),
        input_output_aliases=aliases,
        scratch_shapes=[
            pltpu.VMEM(keys.shape, F32),
            pltpu.VMEM((tokens, width), BF16),
        ],
        compiler_params=params(),
        cost_estimate=pl.CostEstimate(
            flops=8 * heads * tokens * rows * width,
            bytes_accessed=4 * cents.size * 4,
            transcendentals=heads * tokens * rows,
        ),
        name="first_block",
    )(*args)


def raw_kernel(sums_ref, unit_ref, raw_ref, part_ref, cent_ref):
    @pl.when(pl.program_id(0) == 0)
    def _():
        cent_ref[...] = unit_rows(sums_ref[0]).astype(BF16)

    rows, tokens = raw_ref.shape
    part = 256
    for t in range(0, tokens, part):
        unit = unit_ref[0, t : t + part, :]
        total = jnp.zeros((8, part), F32)
        for c in range(0, rows, part):
            raw = jnp.exp2(dot_nt(cent_ref[c : c + part], unit) * EXP2_SCALE)
            raw_ref[c : c + part, t : t + part] = raw.astype(BF16)
            total += jnp.sum(raw.reshape(-1, 8, part), axis=0)
        part_ref[:, t : t + part] = jnp.sum(total, axis=0, keepdims=True)


def raw_weights(sums, units, head, tokens):
    _, rows, width = sums.shape
    count = units.shape[1]
    return pl.pallas_call(
        raw_kernel,
        grid=(count // tokens,),
        in_specs=[
            pl.BlockSpec((1, rows, width), lambda j: (head, 0, 0)),
            pl.BlockSpec((1, tokens, width), lambda j: (head, j, 0)),
        ],
        out_specs=(
            pl.BlockSpec((rows, tokens), lambda j: (0, j)),
            pl.BlockSpec((1, tokens), lambda j: (0, j)),
        ),
        out_shape=(
            jax.ShapeDtypeStruct((rows, count), BF16),
            jax.ShapeDtypeStruct((1, count), F32),
        ),
        scratch_shapes=[pltpu.VMEM((rows, width), BF16)],
        compiler_params=params(),
        cost_estimate=pl.CostEstimate(
            flops=4 * rows * count * width,
            bytes_accessed=2 * rows * count,
            transcendentals=rows * count,
        ),
        name="raw_weights",
    )(sums, units)


def sums_kernel(n_parts, has_before, raw_ref, unit_ref, *refs):
    parts = refs[:n_parts]
    out_ref, scaled_ref, total_ref = refs[n_parts + has_before :]
    step = pl.program_id(0)
    rows, tokens = raw_ref.shape

    @pl.when(step == 0)
    def _():
        total_ref[...] = jnp.zeros_like(total_ref)

    row_total = parts[0][...]
    for part_ref in parts[1:]:
        row_total += part_ref[...]
    inverse = 1.0 / row_total
    for t in range(0, tokens, LANES):
        scaled_ref[t : t + LANES] = (
            unit_ref[0, t : t + LANES, :].astype(F32)
            * row_to_lanes(inverse[:, t : t + LANES])
        ).astype(BF16)
    part = 256
    for c in range(0, rows, part):
        total_ref[c : c + part] += dot_nn(raw_ref[c : c + part, :], scaled_ref[...])

    @pl.when(step == pl.num_programs(0) - 1)
    def _():
        out_ref[0] = unit_rows(total_ref[...])


def weighted_sums(raw, units, parts, head, tokens, before):
    rows, count = raw.shape
    heads, _, width = units.shape
    blocks = count // tokens

    def rolled(shift):
        return pl.BlockSpec((1, tokens), lambda j: (0, lax.rem(j + blocks - shift, blocks)))

    in_specs = [
        pl.BlockSpec((rows, tokens), lambda j: (0, j)),
        pl.BlockSpec((1, tokens, width), lambda j: (head, j, 0)),
    ] + [rolled(shift) for shift in range(len(parts))]
    args = [raw, units, *parts]
    aliases = {}
    if before is not None:
        aliases = {len(args): 0}
        in_specs.append(pl.BlockSpec(memory_space=pl.ANY))
        args.append(before)
    return pl.pallas_call(
        functools.partial(sums_kernel, len(parts), int(before is not None)),
        grid=(blocks,),
        in_specs=in_specs,
        out_specs=pl.BlockSpec((1, rows, width), lambda j: (head, 0, 0)),
        out_shape=jax.ShapeDtypeStruct((heads, rows, width), F32),
        input_output_aliases=aliases,
        scratch_shapes=[
            pltpu.VMEM((tokens, width), BF16),
            pltpu.VMEM((rows, width), F32),
        ],
        compiler_params=params(),
        cost_estimate=pl.CostEstimate(
            flops=4 * rows * count * width,
            bytes_accessed=2 * rows * count,
            transcendentals=0,
        ),
        name="weighted_sums",
    )(*args)


def place_kernel(blocks, tokens, spot_ref, *refs):
    keys, values = refs[:blocks], refs[blocks : 2 * blocks]
    out_keys, out_values, wide_ref, rows_ref, mixed_ref = refs[2 * blocks :]
    step = pl.program_id(0)
    heads = rows_ref.shape[0]
    width = LANES

    @pl.when(step == 0)
    def _():
        for j in range(blocks):
            for side, source in enumerate((keys[j], values[j])):
                split_heads(source, wide_ref)
                for h in range(heads):
                    rows_ref[
                        h,
                        j * tokens : (j + 1) * tokens,
                        side * width : (side + 1) * width,
                    ] = head_rows(wide_ref, h, heads).astype(BF16)

    rows = out_keys.shape[0] // heads
    first = step * rows
    slots = lax.broadcasted_iota(jnp.int32, (rows, 512), 0) + first
    for h in range(heads):
        total = jnp.zeros((rows, 2 * width), F32)
        for t in range(0, blocks * tokens, 512):
            pick = slots == spot_ref[h : h + 1, t : t + 512]
            total += dot_nn(
                jnp.where(pick, 1.0, 0.0).astype(BF16), rows_ref[h, t : t + 512, :]
            )
        mixed_ref[0, pl.Slice(h, rows, heads), :] = total[:, :width]
        mixed_ref[1, pl.Slice(h, rows, heads), :] = total[:, width:]
    out_keys[...] = mixed_ref[0].astype(BF16)
    out_values[...] = mixed_ref[1].astype(BF16)


def place(spots, keys, values, cap):
    blocks = len(keys)
    flat, width = keys[0].shape
    heads = spots.shape[0]
    tokens = flat // heads
    rows = 256
    out = jax.ShapeDtypeStruct((heads * cap, width), BF16)
    return pl.pallas_call(
        functools.partial(place_kernel, blocks, tokens),
        grid=(cap // rows,),
        in_specs=[whole(spots.shape)] + [whole((flat, width))] * (2 * blocks),
        out_specs=(pl.BlockSpec((heads * rows, width), lambda r: (r, 0)),) * 2,
        out_shape=(out, out),
        scratch_shapes=[
            pltpu.VMEM((flat, width), F32),
            pltpu.VMEM((heads, blocks * tokens, 2 * width), BF16),
            pltpu.VMEM((2, heads * rows, width), F32),
        ],
        compiler_params=params(),
        cost_estimate=pl.CostEstimate(
            flops=8 * cap * blocks * tokens * width,
            bytes_accessed=8 * blocks * flat * width,
            transcendentals=0,
        ),
        name="place",
    )(spots, *keys, *values)


def body(key_rows, value_rows, cluster_labels, owner_bounds, init_centroids):
    n = lax.axis_size("ctx")
    me = lax.axis_index("ctx")
    tokens, heads, width = key_rows.shape
    share = init_centroids.shape[1] // n
    cap = 2 * tokens

    def shifted(x, by=1):
        return lax.ppermute(x, "ctx", [(i, (i + by) % n) for i in range(n)])

    def ring(x):
        blocks = [x]
        for _ in range(n - 1):
            blocks.append(shifted(blocks[-1]))
        return blocks

    def spread(x):
        return [x] + [shifted(x, by) for by in range(1, n)]

    keys = ring(key_rows.reshape(heads * tokens, width))
    value_flat, _ = lax.optimization_barrier((value_rows.reshape(heads * tokens, width), keys[-1]))
    values = ring(value_flat)

    labels = spread(cluster_labels)
    token = jnp.arange(tokens, dtype=jnp.int32)
    order = [
        labels[j] * (n * tokens) + lax.rem(me + n - j, n) * tokens + token
        for j in range(n)
    ]
    ranks = spread(own_ranks(order[0], jnp.concatenate(order, axis=1)))
    label_all = jnp.concatenate(labels, axis=1)
    rank_all = jnp.concatenate(ranks, axis=1)
    low = lax.dynamic_slice_in_dim(owner_bounds, me, 1, 1)
    high = lax.dynamic_slice_in_dim(owner_bounds, me + 1, 1, 1)
    start = jnp.sum((label_all < low).astype(jnp.int32), axis=1, keepdims=True)
    spots = jnp.where((label_all >= low) & (label_all < high), rank_all - start, -1)

    totals = spread(own_totals(keys[0], init_centroids))
    own_cents = lax.dynamic_slice_in_dim(init_centroids, me * share, share, 1)
    cents = unit_rows(own_cents).astype(BF16)
    state = None
    for j in range(n):
        state = first_block(keys[j], totals[j], cents, j, n, state)
    sums, units = state

    raws = [raw_weights(sums, units, h, tokens) for h in range(heads)]
    out = None
    for h in range(heads):
        raw, part = raws[h]
        out = weighted_sums(raw, units, spread(part), h, tokens, out)

    placed_keys, placed_values = place(spots, keys, values, cap)
    shape = (cap, heads, width)
    return out, placed_keys.reshape(shape), placed_values.reshape(shape)


def solution(mesh):
    placed = (
        P(("grp", "ctx"), "head", None),
        P(("grp", "ctx"), "head", None),
        P("head", ("grp", "ctx")),
        P(("grp", "head"), None),
        P(("grp", "head"), None, None),
    )
    return jax.shard_map(
        body,
        mesh=mesh,
        in_specs=placed,
        out_specs=(
            P(("grp", "head"), "ctx", None),
            P(("grp", "ctx"), "head", None),
            P(("grp", "ctx"), "head", None),
        ),
        check_vma=False,
    )
```

```python
import functools
import math

import jax
import jax.numpy as jnp
from jax import lax
from jax.experimental import pallas as pl
from jax.experimental.pallas import tpu as pltpu
from jax.sharding import PartitionSpec as P

LANES = 128
EXP2_SCALE = 20.0 * math.log2(math.e)
VMEM_LIMIT = 28 * 1024 * 1024
PARTS = 2
F32 = jnp.float32
BF16 = jnp.bfloat16
NT = (((1,), (1,)), ((), ()))
NN = (((1,), (0,)), ((), ()))


def dot_nt(a, b):
    return lax.dot_general(a, b, NT, preferred_element_type=F32)


def dot_nn(a, b):
    return lax.dot_general(a, b, NN, preferred_element_type=F32)


def unit_rows(x):
    return x * lax.rsqrt(jnp.sum(x * x, axis=-1, keepdims=True) + 1e-06)


def params(**kwargs):
    return pltpu.CompilerParams(vmem_limit_bytes=VMEM_LIMIT, **kwargs)


def whole(shape):
    return pl.BlockSpec(shape, lambda *_: (0,) * len(shape))


def in_vmem():
    return pl.BlockSpec(memory_space=pltpu.VMEM)


def row_to_lanes(row):
    return jnp.transpose(jnp.broadcast_to(row, (LANES, LANES)))


def split_heads(flat_ref, wide_ref):
    wide_ref[...] = flat_ref[...].astype(F32)


def head_rows(wide_ref, head, heads):
    if heads == 1:
        return wide_ref[...]
    return wide_ref[pl.Slice(head, wide_ref.shape[0] // heads, heads), :]


def totals_kernel(keys_ref, cent_ref, tot_ref, wide_ref, unit_ref, sum_ref):
    head, step = pl.program_id(0), pl.program_id(1)
    heads, tokens, _ = unit_ref.shape

    @pl.when((head == 0) & (step == 0))
    def _():
        split_heads(keys_ref, wide_ref)
        for h in range(heads):
            unit_ref[h] = unit_rows(head_rows(wide_ref, h, heads)).astype(BF16)

    @pl.when(step == 0)
    def _():
        sum_ref[...] = jnp.zeros_like(sum_ref)

    cent = unit_rows(cent_ref[0]).astype(BF16)
    part = 256
    for t in range(0, tokens, part):
        raw = jnp.exp2(dot_nt(cent, unit_ref[head, t : t + part, :]) * EXP2_SCALE)
        sum_ref[:, t : t + part] += jnp.sum(raw.reshape(-1, 8, part), axis=0)

    @pl.when(step == pl.num_programs(1) - 1)
    def _():
        tot_ref[0] = jnp.sum(sum_ref[...], axis=0, keepdims=True)


def own_totals(keys, cents):
    heads, count, width = cents.shape
    tokens = keys.shape[0] // heads
    rows = min(1024, count)
    return pl.pallas_call(
        totals_kernel,
        grid=(heads, count // rows),
        in_specs=[
            whole(keys.shape),
            pl.BlockSpec((1, rows, width), lambda h, c: (h, c, 0)),
        ],
        out_specs=pl.BlockSpec((1, 1, tokens), lambda h, c: (h, 0, 0)),
        out_shape=jax.ShapeDtypeStruct((heads, 1, tokens), F32),
        scratch_shapes=[
            pltpu.VMEM(keys.shape, F32),
            pltpu.VMEM((heads, tokens, width), BF16),
            pltpu.VMEM((8, tokens), F32),
        ],
        compiler_params=params(),
        cost_estimate=pl.CostEstimate(
            flops=4 * heads * tokens * count * width,
            bytes_accessed=cents.size * 4,
            transcendentals=heads * tokens * count,
        ),
        name="own_totals",
    )(keys, cents)


def rank_kernel(own_ref, all_ref, rank_ref):
    count = all_ref.shape[2]
    tokens = own_ref.shape[2]
    mine = jnp.broadcast_to(own_ref[0], (8, tokens))
    wide = 4 * LANES

    def step(i, total):
        row = all_ref[0, :, pl.ds(pl.multiple_of(i * wide, wide), wide)]
        for s in range(0, wide, LANES):
            column = row_to_lanes(row[:, s : s + LANES])
            for r in range(0, LANES, 8):
                other = jnp.tile(column[r : r + 8], (1, tokens // LANES))
                total += (other < mine).astype(jnp.int32)
        return total

    total = lax.fori_loop(0, count // wide, step, jnp.zeros((8, tokens), jnp.int32))
    rank_ref[0] = jnp.sum(total, axis=0, keepdims=True)


def own_ranks(own, everyone):
    heads, tokens = own.shape
    count = everyone.shape[1]
    return pl.pallas_call(
        rank_kernel,
        grid=(heads,),
        in_specs=[
            pl.BlockSpec((1, 1, tokens), lambda h: (h, 0, 0)),
            pl.BlockSpec((1, 1, count), lambda h: (h, 0, 0)),
        ],
        out_specs=pl.BlockSpec((1, 1, tokens), lambda h: (h, 0, 0)),
        out_shape=jax.ShapeDtypeStruct((heads, 1, tokens), jnp.int32),
        compiler_params=params(),
        cost_estimate=pl.CostEstimate(
            flops=3 * heads * tokens * count, bytes_accessed=65536, transcendentals=0
        ),
        name="own_ranks",
    )(own[:, None, :], everyone[:, None, :])[:, 0, :]


def first_kernel(fresh, _, keys_ref, tot_ref, init_ref, *refs):
    if fresh:
        sums_ref, unit_ref, wide_ref, scaled_ref, cent_ref = refs
    else:
        before_ref, sums_ref, unit_ref, wide_ref, scaled_ref, cent_ref = refs
    head = pl.program_id(0)
    tokens = unit_ref.shape[1]
    heads = keys_ref.shape[1] // tokens

    @pl.when(pl.program_id(1) == 0)
    def _():
        cent_ref[...] = unit_rows(init_ref[0]).astype(BF16)
        if fresh:
            sums_ref[...] = jnp.zeros_like(sums_ref)
        else:
            sums_ref[...] = before_ref[...]

    split_heads(keys_ref.at[0], wide_ref)
    unit_ref[0] = unit_rows(head_rows(wide_ref, head, heads)).astype(BF16)
    inverse = 1.0 / tot_ref[0, 0]
    scale_rows(unit_ref, inverse, scaled_ref)
    part = 256
    for t in range(0, tokens, part):
        raw = jnp.exp2(dot_nt(cent_ref[...], unit_ref[0, t : t + part, :]) * EXP2_SCALE)
        sums_ref[0] += dot_nn(raw.astype(BF16), scaled_ref[t : t + part])


def scale_rows(unit_ref, inverse, scaled_ref):
    for t in range(0, scaled_ref.shape[0], LANES):
        scaled_ref[t : t + LANES] = (
            unit_ref[0, t : t + LANES, :].astype(F32)
            * row_to_lanes(inverse[:, t : t + LANES])
        ).astype(BF16)


def first_part(me, keys, totals, init, part, before):
    n, flat, width = keys.shape
    heads = init.shape[0]
    tokens = flat // heads
    rows = init.shape[1] // n
    share = pl.BlockSpec((1, rows, width), lambda h, j, me: (h, 0, 0))
    in_specs = [
        pl.BlockSpec((1, flat, width), lambda h, j, me: (j, 0, 0)),
        pl.BlockSpec((1, 1, 1, tokens), lambda h, j, me: (j, h, 0, part)),
        pl.BlockSpec((1, rows, width), lambda h, j, me: (h, me[0], 0)),
    ]
    args = [me, keys, totals, init]
    aliases = {}
    if before is not None:
        in_specs.append(share)
        args.append(before)
        aliases = {4: 0}
    return pl.pallas_call(
        functools.partial(first_kernel, before is None),
        grid_spec=pltpu.PrefetchScalarGridSpec(
            num_scalar_prefetch=1,
            grid=(heads, n),
            in_specs=in_specs,
            out_specs=(
                share,
                pl.BlockSpec((1, tokens, width), lambda h, j, me: (h, j, 0)),
            ),
            scratch_shapes=[
                pltpu.VMEM((flat, width), F32),
                pltpu.VMEM((tokens, width), BF16),
                pltpu.VMEM((rows, width), BF16),
            ],
        ),
        out_shape=(
            jax.ShapeDtypeStruct((heads, rows, width), F32),
            jax.ShapeDtypeStruct((heads, n * tokens, width), BF16),
        ),
        input_output_aliases=aliases,
        compiler_params=params(),
        cost_estimate=pl.CostEstimate(
            flops=8 * heads * n * tokens * rows * width,
            bytes_accessed=4 * heads * rows * width * 4,
            transcendentals=heads * n * tokens * rows,
        ),
        name="first_part",
    )(*args)


def raw_kernel(parts, sums_ref, *refs):
    units = refs[:parts]
    raw_ref, total_ref, cent_ref = refs[parts:]
    cent_ref[...] = unit_rows(sums_ref[0]).astype(BF16)
    part = 256
    step = 1024

    for p in range(parts):
        unit_ref = units[p]
        size = unit_ref.shape[1]

        def chunk(i, _, unit_ref=unit_ref, p=p, size=size):
            for s in range(0, step, part):
                near = pl.ds(pl.multiple_of(i * step + s, part), part)
                far = pl.ds(pl.multiple_of(p * size + i * step + s, part), part)
                raw = jnp.exp2(dot_nt(cent_ref[...], unit_ref[0, near, :]) * EXP2_SCALE)
                raw_ref[:, far] = raw.astype(BF16)
                total = jnp.sum(raw.reshape(-1, 8, part), axis=0)
                total_ref[:, far] = jnp.sum(total, axis=0, keepdims=True)
            return 0

        lax.fori_loop(0, size // step, chunk, 0)


def raw_weights(sums, units, head):
    _, rows, width = sums.shape
    count = sum(unit.shape[1] for unit in units)
    return pl.pallas_call(
        functools.partial(raw_kernel, len(units)),
        grid=(1,),
        in_specs=[pl.BlockSpec((1, rows, width), lambda _: (head, 0, 0))]
        + [
            pl.BlockSpec((1, unit.shape[1], width), lambda _: (head, 0, 0))
            for unit in units
        ],
        out_specs=(in_vmem(), whole((1, count))),
        out_shape=(
            pltpu.VMEM((rows, count), BF16),
            jax.ShapeDtypeStruct((1, count), F32),
        ),
        scratch_shapes=[pltpu.VMEM((rows, width), BF16)],
        compiler_params=params(),
        cost_estimate=pl.CostEstimate(
            flops=4 * rows * count * width,
            bytes_accessed=2 * count * width,
            transcendentals=rows * count,
        ),
        name="raw_weights",
    )(sums, *units)


def sums_kernel(parts, has_before, raw_ref, tot_ref, *refs):
    units = refs[:parts]
    out_ref, scaled_ref, sum_ref = refs[parts + has_before :]
    inverse = 1.0 / jnp.sum(tot_ref[...], axis=0, keepdims=True)
    start = 0
    for unit_ref in units:
        size = unit_ref.shape[1]
        scale_rows(unit_ref, inverse[:, start : start + size], scaled_ref.at[start : start + size])
        start += size
    step = 1024
    for t in range(0, start, step):
        more = dot_nn(raw_ref[:, t : t + step], scaled_ref[t : t + step])
        if t == 0:
            sum_ref[...] = more
        else:
            sum_ref[...] += more
    out_ref[0] = unit_rows(sum_ref[...])


def weighted_sums(raw, units, totals, head, before):
    rows, count = raw.shape
    heads, _, width = units[0].shape
    raw = pltpu.with_memory_space_constraint(raw, pltpu.VMEM)
    in_specs = [in_vmem(), whole(totals.shape)] + [
        pl.BlockSpec((1, unit.shape[1], width), lambda _: (head, 0, 0)) for unit in units
    ]
    args = [raw, totals, *units]
    aliases = {}
    if before is not None:
        aliases = {len(args): 0}
        in_specs.append(pl.BlockSpec(memory_space=pl.ANY))
        args.append(before)
    return pl.pallas_call(
        functools.partial(sums_kernel, len(units), int(before is not None)),
        grid=(1,),
        in_specs=in_specs,
        out_specs=pl.BlockSpec((1, rows, width), lambda _: (head, 0, 0)),
        out_shape=jax.ShapeDtypeStruct((heads, rows, width), F32),
        input_output_aliases=aliases,
        scratch_shapes=[
            pltpu.VMEM((count, width), BF16),
            pltpu.VMEM((rows, width), F32),
        ],
        compiler_params=params(),
        cost_estimate=pl.CostEstimate(
            flops=4 * rows * count * width,
            bytes_accessed=2 * count * width,
            transcendentals=0,
        ),
        name="weighted_sums",
    )(*args)


def place_kernel(fresh, spot_ref, keys_ref, values_ref, *refs):
    before = refs[: 0 if fresh else 2]
    out_refs, (wide_ref, rows_ref, mixed_ref) = refs[-5:-3], refs[-3:]
    step = pl.program_id(0)
    n, flat, width = keys_ref.shape
    heads = rows_ref.shape[0]
    tokens = flat // heads

    @pl.when(step == 0)
    def _():
        for j in range(n):
            for side, source in enumerate((keys_ref, values_ref)):
                split_heads(source.at[j], wide_ref)
                for h in range(heads):
                    rows_ref[
                        h,
                        j * tokens : (j + 1) * tokens,
                        side * width : (side + 1) * width,
                    ] = head_rows(wide_ref, h, heads).astype(BF16)

    rows = out_refs[0].shape[0] // heads
    part = 1024
    slots = lax.broadcasted_iota(jnp.int16, (rows, part), 0)
    for h in range(heads):
        for t in range(0, n * tokens, part):
            spot = (spot_ref[h : h + 1, t : t + part] - step * rows).astype(jnp.int16)
            pick = jnp.where(slots == spot, jnp.ones((), BF16), jnp.zeros((), BF16))
            more = dot_nn(pick, rows_ref[h, t : t + part, :])
            total = more if t == 0 else total + more
        for side in range(2):
            mixed_ref[side, pl.Slice(h, rows, heads), :] = total[
                :, side * width : (side + 1) * width
            ]
    for side in range(2):
        mixed = mixed_ref[side]
        if not fresh:
            mixed += before[side][...].astype(F32)
        out_refs[side][...] = mixed.astype(BF16)


def place(spots, keys, values, cap, before):
    n, flat, width = keys.shape
    heads = spots.shape[0]
    rows = 512
    out = jax.ShapeDtypeStruct((heads * cap, width), BF16)
    block = pl.BlockSpec((heads * rows, width), lambda r: (r, 0))
    fresh = before is None
    return pl.pallas_call(
        functools.partial(place_kernel, fresh),
        grid=(cap // rows,),
        in_specs=[whole(spots.shape), whole(keys.shape), whole(values.shape)]
        + [block] * (0 if fresh else 2),
        out_specs=(block, block),
        out_shape=(out, out),
        input_output_aliases={} if fresh else {3: 0, 4: 1},
        scratch_shapes=[
            pltpu.VMEM((flat, width), F32),
            pltpu.VMEM((heads, n * flat // heads, 2 * width), BF16),
            pltpu.VMEM((2, heads * rows, width), F32),
        ],
        compiler_params=params(),
        cost_estimate=pl.CostEstimate(
            flops=4 * cap * n * flat * width,
            bytes_accessed=8 * n * flat * width,
            transcendentals=0,
        ),
        name="place",
    )(spots, keys, values, *(() if fresh else before))


def body(key_rows, value_rows, cluster_labels, owner_bounds, init_centroids):
    n = lax.axis_size("ctx")
    me = lax.axis_index("ctx")
    tokens, heads, width = key_rows.shape
    everyone = n * tokens
    cap = 2 * tokens

    def gather(x):
        return lax.all_gather(x, "ctx")

    def gather_parts(flat):
        size = flat.shape[0] // PARTS
        return [gather(flat[p * size : (p + 1) * size]) for p in range(PARTS)]

    key_flat = key_rows.reshape(heads * tokens, width)
    keys = gather_parts(key_flat)
    value_flat, _ = lax.optimization_barrier(
        (value_rows.reshape(heads * tokens, width), keys[-1])
    )
    values = gather_parts(value_flat)

    labels = jnp.swapaxes(gather(cluster_labels), 0, 1).reshape(heads, everyone)
    token = jnp.arange(everyone, dtype=jnp.int32)
    own_order = cluster_labels * everyone + me * tokens + token[:tokens]
    ranks = gather(own_ranks(own_order, labels * everyone + token))
    ranks = jnp.swapaxes(ranks, 0, 1).reshape(heads, everyone)
    low = lax.dynamic_slice_in_dim(owner_bounds, me, 1, 1)
    high = lax.dynamic_slice_in_dim(owner_bounds, me + 1, 1, 1)
    start = jnp.sum((labels < low).astype(jnp.int32), axis=1, keepdims=True)
    spots = jnp.where((labels >= low) & (labels < high), ranks - start, -1)
    spots = spots.reshape(heads, n, PARTS, tokens // PARTS)

    totals = gather(own_totals(key_flat, init_centroids))
    me_array = me.astype(jnp.int32).reshape(1)
    sums, units = None, []
    for p in range(PARTS):
        sums, unit = first_part(me_array, keys[p], totals, init_centroids, p, sums)
        units.append(unit)

    raws = [raw_weights(sums, units, h) for h in range(heads)]
    out = None
    for h in range(heads):
        raw, part = raws[h]
        out = weighted_sums(raw, units, gather(part).reshape(n, everyone), h, out)

    placed = None
    for p in range(PARTS):
        placed = place(
            spots[:, :, p].reshape(heads, everyone // PARTS), keys[p], values[p], cap, placed
        )
    shape = (cap, heads, width)
    return out, placed[0].reshape(shape), placed[1].reshape(shape)


def solution(mesh):
    placed = (
        P(("grp", "ctx"), "head", None),
        P(("grp", "ctx"), "head", None),
        P("head", ("grp", "ctx")),
        P(("grp", "head"), None),
        P(("grp", "head"), None, None),
    )
    return jax.shard_map(
        body,
        mesh=mesh,
        in_specs=placed,
        out_specs=(
            P(("grp", "head"), "ctx", None),
            P(("grp", "ctx"), "head", None),
            P(("grp", "ctx"), "head", None),
        ),
        check_vma=False,
    )
```

```python
import functools
import math

import jax
import jax.numpy as jnp
from jax import lax
from jax.experimental import pallas as pl
from jax.experimental.pallas import tpu as pltpu
from jax.sharding import PartitionSpec as P

LANES = 128
EXP2_SCALE = 20.0 * math.log2(math.e)
VMEM_LIMIT = 28 * 1024 * 1024
F32 = jnp.float32
BF16 = jnp.bfloat16
NT = (((1,), (1,)), ((), ()))
NN = (((1,), (0,)), ((), ()))


def dot_nt(a, b):
    return lax.dot_general(a, b, NT, preferred_element_type=F32)


def dot_nn(a, b):
    return lax.dot_general(a, b, NN, preferred_element_type=F32)


def unit_rows(x):
    return x * lax.rsqrt(jnp.sum(x * x, axis=-1, keepdims=True) + 1e-06)


def params(**kwargs):
    return pltpu.CompilerParams(vmem_limit_bytes=VMEM_LIMIT, **kwargs)


def whole(shape):
    return pl.BlockSpec(shape, lambda *_: (0,) * len(shape))


def in_vmem():
    return pl.BlockSpec(memory_space=pltpu.VMEM)


def row_to_lanes(row):
    return jnp.transpose(jnp.broadcast_to(row, (LANES, LANES)))


def split_heads(flat_ref, wide_ref):
    wide_ref[...] = flat_ref[...].astype(F32)


def head_rows(wide_ref, head, heads):
    if heads == 1:
        return wide_ref[...]
    return wide_ref[pl.Slice(head, wide_ref.shape[0] // heads, heads), :]


def count_below(all_ref, own_row, count):
    tokens = own_row.shape[1]
    mine = jnp.broadcast_to(own_row, (8, tokens))
    wide = 4 * LANES

    def step(i, total):
        row = all_ref[0, :, pl.ds(pl.multiple_of(i * wide, wide), wide)]
        for s in range(0, wide, LANES):
            column = row_to_lanes(row[:, s : s + LANES])
            for r in range(0, LANES, 8):
                other = jnp.tile(column[r : r + 8], (1, tokens // LANES))
                total += (other < mine).astype(jnp.int32)
        return total

    total = lax.fori_loop(0, count // wide, step, jnp.zeros((8, tokens), jnp.int32))
    return jnp.sum(total, axis=0, keepdims=True)


def one_hot_rows(size, spot):
    slots = lax.broadcasted_iota(jnp.int16, (size, spot.shape[1]), 0)
    return jnp.where(
        slots == spot.astype(jnp.int16), jnp.ones((), BF16), jnp.zeros((), BF16)
    )


def sort_kernel(label_ref, keys_ref, values_ref, *refs):
    out_keys, out_values, out_labels, wide_ref, both_ref, order_ref = refs
    head = pl.program_id(0)
    heads = pl.num_programs(0)
    _, tokens, width = out_keys.shape
    flat = wide_ref.shape[1]

    @pl.when(head == 0)
    def _():
        split_heads(keys_ref, wide_ref.at[0])
        split_heads(values_ref, wide_ref.at[1])

    for side in range(2):
        both_ref[:, side * width : (side + 1) * width] = head_rows(
            wide_ref.at[side], head, flat // tokens
        ).astype(BF16)
    label = label_ref[0]
    order = label * tokens + lax.broadcasted_iota(jnp.int32, label.shape, 1)
    order_ref[0] = order
    spot = count_below(order_ref, order, tokens)
    digits = jnp.concatenate(
        [
            jnp.broadcast_to(label >> 6, (8, tokens)),
            jnp.broadcast_to(label & 63, (8, tokens)),
        ],
        axis=0,
    )
    digits = digits.astype(F32).astype(BF16)
    rows = 512
    for r in range(0, tokens, rows):
        pick = one_hot_rows(rows, spot - r)
        moved = dot_nn(pick, both_ref[...]).astype(BF16)
        out_keys[0, r : r + rows] = moved[:, :width]
        out_values[0, r : r + rows] = moved[:, width:]
        digit = dot_nt(digits, pick)
        out_labels[0, :, r : r + rows] = (
            digit[0:1] * 64.0 + digit[8:9]
        ).astype(jnp.int32)


def sort_tokens(labels, keys, values):
    heads, tokens = labels.shape
    flat, width = keys.shape
    rows = jax.ShapeDtypeStruct((heads, tokens, width), BF16)
    row_block = pl.BlockSpec((1, tokens, width), lambda h: (h, 0, 0))
    label_block = pl.BlockSpec((1, 1, tokens), lambda h: (h, 0, 0))
    return pl.pallas_call(
        sort_kernel,
        grid=(heads,),
        in_specs=[label_block, whole(keys.shape), whole(values.shape)],
        out_specs=(row_block, row_block, label_block),
        out_shape=(rows, rows, jax.ShapeDtypeStruct((heads, 1, tokens), jnp.int32)),
        scratch_shapes=[
            pltpu.VMEM((2, flat, width), F32),
            pltpu.VMEM((tokens, 2 * width), BF16),
            pltpu.VMEM((1, 1, tokens), jnp.int32),
        ],
        compiler_params=params(),
        cost_estimate=pl.CostEstimate(
            flops=4 * heads * tokens * tokens * width,
            bytes_accessed=8 * flat * width,
            transcendentals=0,
        ),
        name="sort_tokens",
    )(labels[:, None, :], keys, values)


def windows_kernel(start_ref, values_ref, *out_refs):
    heads = values_ref.shape[0]
    for m, out_ref in enumerate(out_refs):
        size = out_ref.shape[1]
        for h in range(heads):
            start = pl.multiple_of(start_ref[h, m], 16)
            out_ref[h] = values_ref[h, pl.ds(start, size), :]


def windows(starts, values, size):
    heads, tokens, width = values.shape
    n = starts.shape[1]
    out = jax.ShapeDtypeStruct((heads, size, width), BF16)
    return pl.pallas_call(
        windows_kernel,
        in_specs=[pl.BlockSpec(memory_space=pltpu.SMEM), in_vmem()],
        out_specs=(in_vmem(),) * n,
        out_shape=(out,) * n,
        compiler_params=params(),
        cost_estimate=pl.CostEstimate(
            flops=0, bytes_accessed=4 * n * heads * size * width, transcendentals=0
        ),
        name="windows",
    )(starts, values)


def rank_kernel(own_ref, all_ref, rank_ref):
    rank_ref[0] = count_below(all_ref, own_ref[0], all_ref.shape[2])


def own_ranks(own, everyone):
    heads, _, tokens = own.shape
    count = everyone.shape[2]
    own_block = pl.BlockSpec((1, 1, tokens), lambda h: (h, 0, 0))
    return pl.pallas_call(
        rank_kernel,
        grid=(heads,),
        in_specs=[own_block, pl.BlockSpec((1, 1, count), lambda h: (h, 0, 0))],
        out_specs=own_block,
        out_shape=jax.ShapeDtypeStruct((heads, 1, tokens), jnp.int32),
        compiler_params=params(),
        cost_estimate=pl.CostEstimate(
            flops=3 * heads * tokens * count, bytes_accessed=65536, transcendentals=0
        ),
        name="own_ranks",
    )(own, everyone)


def totals_kernel(keys_ref, cent_ref, tot_ref, unit_ref, sum_ref):
    step = pl.program_id(1)
    tokens = unit_ref.shape[0]

    @pl.when(step == 0)
    def _():
        unit_ref[...] = unit_rows(keys_ref[0].astype(F32)).astype(BF16)
        sum_ref[...] = jnp.zeros_like(sum_ref)

    cent = unit_rows(cent_ref[0]).astype(BF16)
    part = 256
    for t in range(0, tokens, part):
        raw = jnp.exp2(dot_nt(cent, unit_ref[t : t + part, :]) * EXP2_SCALE)
        sum_ref[:, t : t + part] += jnp.sum(raw.reshape(-1, 8, part), axis=0)

    @pl.when(step == pl.num_programs(1) - 1)
    def _():
        tot_ref[0] = jnp.sum(sum_ref[...], axis=0, keepdims=True)


def own_totals(keys, cents):
    heads, count, width = cents.shape
    tokens = keys.shape[1]
    rows = min(1024, count)
    return pl.pallas_call(
        totals_kernel,
        grid=(heads, count // rows),
        in_specs=[
            pl.BlockSpec((1, tokens, width), lambda h, c: (h, 0, 0)),
            pl.BlockSpec((1, rows, width), lambda h, c: (h, c, 0)),
        ],
        out_specs=pl.BlockSpec((1, 1, tokens), lambda h, c: (h, 0, 0)),
        out_shape=jax.ShapeDtypeStruct((heads, 1, tokens), F32),
        scratch_shapes=[
            pltpu.VMEM((tokens, width), BF16),
            pltpu.VMEM((8, tokens), F32),
        ],
        compiler_params=params(),
        cost_estimate=pl.CostEstimate(
            flops=4 * heads * tokens * count * width,
            bytes_accessed=cents.size * 4,
            transcendentals=heads * tokens * count,
        ),
        name="own_totals",
    )(keys, cents)


def scale_rows(unit, inverse, scaled_ref):
    for t in range(0, unit.shape[0], LANES):
        scaled_ref[t : t + LANES] = (
            unit[t : t + LANES, :].astype(F32) * row_to_lanes(inverse[:, t : t + LANES])
        ).astype(BF16)


def first_kernel(fresh, _, keys_ref, tot_ref, init_ref, *refs):
    if fresh:
        sums_ref, unit_ref, scaled_ref, cent_ref = refs
    else:
        before_ref, sums_ref, unit_ref, scaled_ref, cent_ref = refs
    tokens = unit_ref.shape[1]
    cent_ref[...] = unit_rows(init_ref[0]).astype(BF16)
    if fresh:
        sums_ref[...] = jnp.zeros_like(sums_ref)
    else:
        sums_ref[...] = before_ref[...]
    unit_ref[0] = unit_rows(keys_ref[0].astype(F32)).astype(BF16)
    scale_rows(unit_ref[0], 1.0 / tot_ref[0], scaled_ref)
    part = 256
    for t in range(0, tokens, part):
        raw = jnp.exp2(dot_nt(cent_ref[...], unit_ref[0, t : t + part, :]) * EXP2_SCALE)
        sums_ref[0] += dot_nn(raw.astype(BF16), scaled_ref[t : t + part])


def first_block(me, keys, totals, init, n, before):
    heads, tokens, width = keys.shape
    rows = init.shape[1] // n
    share = pl.BlockSpec((1, rows, width), lambda h, me: (h, 0, 0))
    key_block = pl.BlockSpec((1, tokens, width), lambda h, me: (h, 0, 0))
    in_specs = [
        key_block,
        pl.BlockSpec((1, 1, tokens), lambda h, me: (h, 0, 0)),
        pl.BlockSpec((1, rows, width), lambda h, me: (h, me[0], 0)),
    ]
    args = [me, keys, totals, init]
    aliases = {}
    if before is not None:
        in_specs.append(share)
        args.append(before)
        aliases = {4: 0}
    return pl.pallas_call(
        functools.partial(first_kernel, before is None),
        grid_spec=pltpu.PrefetchScalarGridSpec(
            num_scalar_prefetch=1,
            grid=(heads,),
            in_specs=in_specs,
            out_specs=(share, key_block),
            scratch_shapes=[
                pltpu.VMEM((tokens, width), BF16),
                pltpu.VMEM((rows, width), BF16),
            ],
        ),
        out_shape=(
            jax.ShapeDtypeStruct((heads, rows, width), F32),
            jax.ShapeDtypeStruct((heads, tokens, width), BF16),
        ),
        input_output_aliases=aliases,
        compiler_params=params(),
        cost_estimate=pl.CostEstimate(
            flops=8 * heads * tokens * rows * width,
            bytes_accessed=4 * heads * rows * width * 4,
            transcendentals=heads * tokens * rows,
        ),
        name="first_block",
    )(*args)


def raw_kernel(blocks, sums_ref, *refs):
    units = refs[:blocks]
    raw_ref, total_ref, cent_ref = refs[blocks:]
    head = pl.program_id(0)
    cent_ref[...] = unit_rows(sums_ref[0]).astype(BF16)
    part = 256
    start = 0
    for unit_ref in units:
        for t in range(0, unit_ref.shape[1], part):
            here = slice(start + t, start + t + part)
            raw = jnp.exp2(dot_nt(cent_ref[...], unit_ref[0, t : t + part, :]) * EXP2_SCALE)
            raw_ref[head, :, here] = raw.astype(BF16)
            total = jnp.sum(raw.reshape(-1, 8, part), axis=0)
            total_ref[0, :, here] = jnp.sum(total, axis=0, keepdims=True)
        start += unit_ref.shape[1]


def raw_weights(sums, units):
    heads, rows, width = sums.shape
    tokens = units[0].shape[1]
    count = tokens * len(units)
    return pl.pallas_call(
        functools.partial(raw_kernel, len(units)),
        grid=(heads,),
        in_specs=[pl.BlockSpec((1, rows, width), lambda h: (h, 0, 0))]
        + [pl.BlockSpec((1, tokens, width), lambda h: (h, 0, 0))] * len(units),
        out_specs=(in_vmem(), pl.BlockSpec((1, 1, count), lambda h: (h, 0, 0))),
        out_shape=(
            pltpu.VMEM((heads, rows, count), BF16),
            jax.ShapeDtypeStruct((heads, 1, count), F32),
        ),
        scratch_shapes=[pltpu.VMEM((rows, width), BF16)],
        compiler_params=params(),
        cost_estimate=pl.CostEstimate(
            flops=4 * heads * rows * count * width,
            bytes_accessed=2 * heads * count * width,
            transcendentals=heads * rows * count,
        ),
        name="raw_weights",
    )(sums, *units)


def sums_kernel(blocks, raw_ref, *refs):
    totals, units = refs[:blocks], refs[blocks : 2 * blocks]
    out_ref, scaled_ref, sum_ref = refs[2 * blocks :]
    head = pl.program_id(0)
    tokens = units[0].shape[1]
    for m, unit_ref in enumerate(units):
        row_total = totals[0][0, :, m * tokens : (m + 1) * tokens]
        for d in range(1, blocks):
            peer = m ^ d
            row_total += totals[d][0, :, peer * tokens : (peer + 1) * tokens]
        scale_rows(unit_ref[0], 1.0 / row_total, scaled_ref)
        more = dot_nn(raw_ref[head, :, m * tokens : (m + 1) * tokens], scaled_ref[...])
        if m == 0:
            sum_ref[...] = more
        else:
            sum_ref[...] += more
    out_ref[0] = unit_rows(sum_ref[...])


def weighted_sums(raw, units, totals):
    heads, rows, count = raw.shape
    _, tokens, width = units[0].shape
    blocks = len(units)
    raw = pltpu.with_memory_space_constraint(raw, pltpu.VMEM)
    return pl.pallas_call(
        functools.partial(sums_kernel, blocks),
        grid=(heads,),
        in_specs=[in_vmem()]
        + [pl.BlockSpec((1, 1, count), lambda h: (h, 0, 0))] * blocks
        + [pl.BlockSpec((1, tokens, width), lambda h: (h, 0, 0))] * blocks,
        out_specs=pl.BlockSpec((1, rows, width), lambda h: (h, 0, 0)),
        out_shape=jax.ShapeDtypeStruct((heads, rows, width), F32),
        scratch_shapes=[
            pltpu.VMEM((tokens, width), BF16),
            pltpu.VMEM((rows, width), F32),
        ],
        compiler_params=params(),
        cost_estimate=pl.CostEstimate(
            flops=4 * heads * rows * count * width,
            bytes_accessed=2 * heads * count * width,
            transcendentals=0,
        ),
        name="weighted_sums",
    )(raw, *totals, *units)


def place_kernel(blocks, size, start_ref, gap_ref, spot_ref, *refs):
    keys, values = refs[:blocks], refs[blocks : 2 * blocks]
    out_refs, (rows_ref, near_ref, mixed_ref) = refs[-5:-3], refs[-3:]
    step = pl.program_id(0)
    heads, tokens, width = keys[0].shape

    @pl.when(step == 0)
    def _():
        rows_ref[:, :, width:] = jnp.zeros((heads, blocks * size, width), BF16)
        for h in range(heads):
            for m in range(blocks):
                start = pl.multiple_of(start_ref[h, m], 16)
                gap = pl.multiple_of(gap_ref[h, m], 16)
                rows_ref[h, m * size : (m + 1) * size, :width] = keys[m][
                    h, pl.ds(start, size), :
                ]
                rows_ref[h, pl.ds(m * size + gap, values[m].shape[1]), width:] = values[m][h]
                spot = pltpu.roll(spot_ref[h, m : m + 1, :], lax.rem(tokens - start, tokens), 1)
                near_ref[h, :, m * size : (m + 1) * size] = spot[:, :size]

    rows = out_refs[0].shape[0] // heads
    total_size = blocks * size
    part = total_size // 2
    for h in range(heads):
        for t in range(0, total_size, part):
            pick = one_hot_rows(rows, near_ref[h, :, t : t + part] - step * rows)
            more = dot_nn(pick, rows_ref[h, t : t + part, :])
            total = more if t == 0 else total + more
        for side in range(2):
            mixed_ref[side, pl.Slice(h, rows, heads), :] = total[
                :, side * width : (side + 1) * width
            ]
    for side in range(2):
        out_refs[side][...] = mixed_ref[side].astype(BF16)


def place(starts, gaps, spots, keys, values, size, cap):
    blocks = len(keys)
    heads, _, width = keys[0].shape
    rows = 512
    out = jax.ShapeDtypeStruct((heads * cap, width), BF16)
    block = pl.BlockSpec((heads * rows, width), lambda r: (r, 0))
    scalars = pl.BlockSpec(memory_space=pltpu.SMEM)
    return pl.pallas_call(
        functools.partial(place_kernel, blocks, size),
        grid=(cap // rows,),
        in_specs=[scalars, scalars]
        + [whole(x.shape) for x in (spots, *keys, *values)],
        out_specs=(block, block),
        out_shape=(out, out),
        scratch_shapes=[
            pltpu.VMEM((heads, blocks * size, 2 * width), BF16),
            pltpu.VMEM((heads, 1, blocks * size), jnp.int32),
            pltpu.VMEM((2, heads * rows, width), F32),
        ],
        compiler_params=params(),
        cost_estimate=pl.CostEstimate(
            flops=4 * heads * cap * blocks * size * width,
            bytes_accessed=12 * heads * cap * width,
            transcendentals=0,
        ),
        name="place",
    )(starts, gaps, spots, *keys, *values)


def body(key_rows, value_rows, cluster_labels, owner_bounds, init_centroids):
    n = lax.axis_size("ctx")
    me = lax.axis_index("ctx").astype(jnp.int32)
    tokens, heads, width = key_rows.shape
    everyone = n * tokens
    cap = 2 * tokens
    slot = cap // n
    send_size = slot + 16
    key_size = min(tokens, -(-send_size // LANES) * LANES)

    def swap(x, d):
        return lax.ppermute(x, "ctx", [(i, i ^ d) for i in range(n)])

    def cube(x):
        blocks = [x]
        for m in range(1, n):
            low = m & -m
            blocks.append(swap(blocks[m ^ low], low))
        return blocks

    def spread(x):
        return [x] + [swap(x, d) for d in range(1, n)]

    def aligned(start, size):
        return jnp.minimum(start // 16 * 16, tokens - size)

    own_keys, own_values, own_labels = sort_tokens(
        cluster_labels,
        key_rows.reshape(heads * tokens, width),
        value_rows.reshape(heads * tokens, width),
    )
    keys = cube(own_keys)
    labels = spread(own_labels)

    place_ids = jnp.arange(tokens, dtype=jnp.int32)
    orders = [
        labels[m] * everyone + (me ^ m) * tokens + place_ids for m in range(n)
    ]
    own_rank = own_ranks(orders[0], jnp.concatenate(orders, axis=2))
    own_total = own_totals(own_keys, init_centroids)
    shared = spread(jnp.concatenate([own_total, own_rank.astype(F32)], axis=1))
    totals = [x[:, 0:1] for x in shared]
    ranks = jnp.stack([x[:, 1] for x in shared], axis=1).astype(jnp.int32)
    block_labels = jnp.concatenate(labels, axis=1)
    low = lax.dynamic_slice_in_dim(owner_bounds, me, 1, 1)[:, :, None]
    high = lax.dynamic_slice_in_dim(owner_bounds, me + 1, 1, 1)[:, :, None]
    below = jnp.sum((block_labels < low).astype(jnp.int32), axis=2)
    first = jnp.sum(below, axis=1)[:, None, None]
    mine = (block_labels >= low) & (block_labels < high)
    spots = jnp.where(mine, ranks - first, -1)
    key_starts = aligned(below, key_size)
    gaps = aligned(below, send_size) - key_starts

    peers = jnp.stack([me ^ m for m in range(n)])
    peer_low = jnp.take(owner_bounds, peers, axis=1)
    own_below = jnp.sum((own_labels < peer_low[:, :, None]).astype(jnp.int32), axis=2)
    own_windows = windows(aligned(own_below, send_size), own_values, send_size)
    *own_windows, _ = lax.optimization_barrier((*own_windows, keys[-1]))
    values = [own_windows[0]] + [swap(own_windows[d], d) for d in range(1, n)]

    sums, units = None, []
    for m in range(n):
        sums, unit = first_block(me.reshape(1), keys[m], totals[m], init_centroids, n, sums)
        units.append(unit)
    raw, part = raw_weights(sums, units)
    out = weighted_sums(raw, units, spread(part))

    placed = place(key_starts, gaps, spots, keys, values, key_size, cap)
    shape = (cap, heads, width)
    return out, placed[0].reshape(shape), placed[1].reshape(shape)


def solution(mesh):
    placed = (
        P(("grp", "ctx"), "head", None),
        P(("grp", "ctx"), "head", None),
        P("head", ("grp", "ctx")),
        P(("grp", "head"), None),
        P(("grp", "head"), None, None),
    )
    return jax.shard_map(
        body,
        mesh=mesh,
        in_specs=placed,
        out_specs=(
            P(("grp", "head"), "ctx", None),
            P(("grp", "ctx"), "head", None),
            P(("grp", "ctx"), "head", None),
        ),
        check_vma=False,
    )
```

```python
import functools
import math

import jax
import jax.numpy as jnp
from jax import lax
from jax.experimental import pallas as pl
from jax.experimental.pallas import tpu as pltpu
from jax.sharding import PartitionSpec as P

LANES = 128
EXP2_SCALE = 20.0 * math.log2(math.e)
VMEM_LIMIT = 28 * 1024 * 1024
F32 = jnp.float32
BF16 = jnp.bfloat16
NT = (((1,), (1,)), ((), ()))
NN = (((1,), (0,)), ((), ()))


def dot_nt(a, b):
    return lax.dot_general(a, b, NT, preferred_element_type=F32)


def dot_nn(a, b):
    return lax.dot_general(a, b, NN, preferred_element_type=F32)


def unit_rows(x):
    return x * lax.rsqrt(jnp.sum(x * x, axis=-1, keepdims=True) + 1e-06)


def params(**kwargs):
    return pltpu.CompilerParams(vmem_limit_bytes=VMEM_LIMIT, **kwargs)


def whole(shape):
    return pl.BlockSpec(shape, lambda *_: (0,) * len(shape))


def in_vmem():
    return pl.BlockSpec(memory_space=pltpu.VMEM)


def anywhere():
    return pl.BlockSpec(memory_space=pl.ANY)


def keep_hbm(x):
    return pltpu.with_memory_space_constraint(x, pltpu.HBM)


def keep_vmem(x):
    return pltpu.with_memory_space_constraint(x, pltpu.VMEM)


def row_to_lanes(row):
    return jnp.transpose(jnp.broadcast_to(row, (LANES, LANES)))


def split_heads(flat_ref, wide_ref):
    wide_ref[...] = flat_ref[...].astype(F32)


def head_rows(wide_ref, head, heads):
    if heads == 1:
        return wide_ref[...]
    return wide_ref[pl.Slice(head, wide_ref.shape[0] // heads, heads), :]


def count_below(all_ref, own_row, count):
    tokens = own_row.shape[1]
    mine = jnp.broadcast_to(own_row, (8, tokens))
    wide = 4 * LANES

    def step(i, total):
        row = all_ref[0, :, pl.ds(pl.multiple_of(i * wide, wide), wide)]
        for s in range(0, wide, LANES):
            column = row_to_lanes(row[:, s : s + LANES])
            for r in range(0, LANES, 8):
                other = jnp.tile(column[r : r + 8], (1, tokens // LANES))
                total += (other < mine).astype(jnp.int32)
        return total

    total = lax.fori_loop(0, count // wide, step, jnp.zeros((8, tokens), jnp.int32))
    return jnp.sum(total, axis=0, keepdims=True)


def one_hot_rows(size, spot):
    slots = lax.broadcasted_iota(jnp.int16, (size, spot.shape[1]), 0)
    return jnp.where(
        slots == spot.astype(jnp.int16), jnp.ones((), BF16), jnp.zeros((), BF16)
    )


def sort_kernel(label_ref, keys_hbm, values_hbm, *refs):
    out_keys, out_values, out_labels, flat_ref, wide_ref, both_ref, order_ref, sems = refs
    head = pl.program_id(0)
    heads = pl.num_programs(0)
    _, tokens, width = out_keys.shape
    copies = [
        pltpu.make_async_copy(source, flat_ref.at[side], sems.at[side])
        for side, source in enumerate((keys_hbm, values_hbm))
    ]

    @pl.when(head == 0)
    def _():
        for copy in copies:
            copy.start()

    label = label_ref[pl.ds(head, 1), :]
    order = label * tokens + lax.broadcasted_iota(jnp.int32, label.shape, 1)
    order_ref[0] = order
    spot = count_below(order_ref, order, tokens)

    @pl.when(head == 0)
    def _():
        for side, copy in enumerate(copies):
            copy.wait()
            split_heads(flat_ref.at[side], wide_ref.at[side])

    for side in range(2):
        both_ref[:, side * width : (side + 1) * width] = head_rows(
            wide_ref.at[side], head, wide_ref.shape[1] // tokens
        ).astype(BF16)
    digits = jnp.concatenate(
        [
            jnp.broadcast_to(label >> 6, (8, tokens)),
            jnp.broadcast_to(label & 63, (8, tokens)),
        ],
        axis=0,
    )
    digits = digits.astype(F32).astype(BF16)
    rows = 512
    for r in range(0, tokens, rows):
        pick = one_hot_rows(rows, spot - r)
        moved = dot_nn(pick, both_ref[...]).astype(BF16)
        out_keys[0, r : r + rows] = moved[:, :width]
        out_values[0, r : r + rows] = moved[:, width:]
        digit = dot_nt(digits, pick)
        out_labels[0, :, r : r + rows] = digit[0:1] * 64.0 + digit[8:9]


def sort_tokens(labels, keys, values):
    heads, tokens = labels.shape
    flat, width = keys.shape
    rows = jax.ShapeDtypeStruct((heads, tokens, width), BF16)
    row_block = pl.BlockSpec((1, tokens, width), lambda h: (h, 0, 0))
    label_block = pl.BlockSpec((1, 1, tokens), lambda h: (h, 0, 0))
    return pl.pallas_call(
        sort_kernel,
        grid=(heads,),
        in_specs=[whole(labels.shape), anywhere(), anywhere()],
        out_specs=(row_block, row_block, label_block),
        out_shape=(rows, rows, jax.ShapeDtypeStruct((heads, 1, tokens), F32)),
        scratch_shapes=[
            pltpu.VMEM((2, flat, width), BF16),
            pltpu.VMEM((2, flat, width), F32),
            pltpu.VMEM((tokens, 2 * width), BF16),
            pltpu.VMEM((1, 1, tokens), jnp.int32),
            pltpu.SemaphoreType.DMA((2,)),
        ],
        compiler_params=params(),
        cost_estimate=pl.CostEstimate(
            flops=4 * heads * tokens * tokens * width,
            bytes_accessed=8 * flat * width,
            transcendentals=0,
        ),
        name="sort_tokens",
    )(labels, keep_hbm(keys), keep_hbm(values))


def windows_kernel(size, start_ref, rank_ref, values_ref, *out_refs):
    heads, tokens, _ = values_ref.shape
    for h in range(heads):
        rank = rank_ref[h]
        digits = [
            digit[:, t : t + LANES]
            for digit in (rank >> 7, rank & 127)
            for t in range(0, tokens, LANES)
        ]
        digits = jnp.concatenate(digits, axis=0).astype(F32).astype(BF16)
        for m, out_ref in enumerate(out_refs):
            start = pl.multiple_of(start_ref[h, m], 16)
            out_ref[h, :size] = values_ref[h, pl.ds(start, size), :]
            out_ref[h, size:] = digits


def windows(starts, ranks, values, size):
    heads, tokens, width = values.shape
    n = starts.shape[1]
    out = jax.ShapeDtypeStruct((heads, size + 2 * tokens // LANES, width), BF16)
    return pl.pallas_call(
        functools.partial(windows_kernel, size),
        in_specs=[pl.BlockSpec(memory_space=pltpu.SMEM), in_vmem(), in_vmem()],
        out_specs=(in_vmem(),) * n,
        out_shape=(out,) * n,
        compiler_params=params(),
        cost_estimate=pl.CostEstimate(
            flops=0, bytes_accessed=4 * n * heads * size * width, transcendentals=0
        ),
        name="windows",
    )(starts, ranks, keep_hbm(values))


def rank_kernel(own_ref, all_ref, rank_ref):
    rank_ref[0] = count_below(all_ref, own_ref[0], all_ref.shape[2])


def own_ranks(own, everyone):
    heads, _, tokens = own.shape
    count = everyone.shape[2]
    own_block = pl.BlockSpec((1, 1, tokens), lambda h: (h, 0, 0))
    return pl.pallas_call(
        rank_kernel,
        grid=(heads,),
        in_specs=[own_block, pl.BlockSpec((1, 1, count), lambda h: (h, 0, 0))],
        out_specs=own_block,
        out_shape=jax.ShapeDtypeStruct((heads, 1, tokens), jnp.int32),
        compiler_params=params(),
        cost_estimate=pl.CostEstimate(
            flops=3 * heads * tokens * count, bytes_accessed=65536, transcendentals=0
        ),
        name="own_ranks",
    )(own, everyone)


def totals_kernel(keys_ref, cent_ref, tot_ref, unit_ref, sum_ref):
    step = pl.program_id(1)
    tokens = unit_ref.shape[0]

    @pl.when(step == 0)
    def _():
        unit_ref[...] = unit_rows(keys_ref[0].astype(F32)).astype(BF16)
        sum_ref[...] = jnp.zeros_like(sum_ref)

    part = 256
    rows = min(1024, cent_ref.shape[1])
    for c in range(0, cent_ref.shape[1], rows):
        cent = unit_rows(cent_ref[0, c : c + rows]).astype(BF16)
        for t in range(0, tokens, part):
            raw = jnp.exp2(dot_nt(cent, unit_ref[t : t + part, :]) * EXP2_SCALE)
            sum_ref[:, t : t + part] += jnp.sum(raw.reshape(-1, 8, part), axis=0)

    @pl.when(step == pl.num_programs(1) - 1)
    def _():
        tot_ref[0] = jnp.sum(sum_ref[...], axis=0, keepdims=True)


def own_totals(keys, cents):
    heads, count, width = cents.shape
    tokens = keys.shape[1]
    rows = min(2048, count)
    return pl.pallas_call(
        totals_kernel,
        grid=(heads, count // rows),
        in_specs=[
            pl.BlockSpec((1, tokens, width), lambda h, c: (h, 0, 0)),
            pl.BlockSpec((1, rows, width), lambda h, c: (h, c, 0)),
        ],
        out_specs=pl.BlockSpec((1, 1, tokens), lambda h, c: (h, 0, 0)),
        out_shape=jax.ShapeDtypeStruct((heads, 1, tokens), F32),
        scratch_shapes=[
            pltpu.VMEM((tokens, width), BF16),
            pltpu.VMEM((8, tokens), F32),
        ],
        compiler_params=params(),
        cost_estimate=pl.CostEstimate(
            flops=4 * heads * tokens * count * width,
            bytes_accessed=cents.size * 4,
            transcendentals=heads * tokens * count,
        ),
        name="own_totals",
    )(keep_hbm(keys), keep_hbm(cents))


def scale_rows(unit, inverse, scaled_ref):
    for t in range(0, unit.shape[0], LANES):
        scaled_ref[t : t + LANES] = (
            unit[t : t + LANES, :].astype(F32) * row_to_lanes(inverse[:, t : t + LANES])
        ).astype(BF16)


def first_kernel(fresh, _, keys_ref, tot_ref, cent_in, *refs):
    head = pl.program_id(0)
    if fresh:
        sums_ref, unit_ref, cent_ref, scaled_ref = refs
        cent = unit_rows(cent_in[0]).astype(BF16)
        cent_ref[head] = cent
    else:
        _, sums_ref, unit_ref, scaled_ref = refs
        cent = cent_in[head]
    unit = unit_rows(keys_ref[0].astype(F32)).astype(BF16)
    unit_ref[head] = unit
    scale_rows(unit, 1.0 / tot_ref[0], scaled_ref)
    part = 256
    for t in range(0, unit.shape[0], part):
        raw = jnp.exp2(dot_nt(cent, unit[t : t + part, :]) * EXP2_SCALE)
        more = dot_nn(raw.astype(BF16), scaled_ref[t : t + part])
        if fresh and t == 0:
            sums_ref[head] = more
        else:
            sums_ref[head] += more


def first_block(me, keys, totals, cents, n, before):
    heads, tokens, width = keys.shape
    fresh = before is None
    rows = cents.shape[1] // n if fresh else cents.shape[1]
    in_specs = [
        pl.BlockSpec((1, tokens, width), lambda h, me: (h, 0, 0)),
        pl.BlockSpec((1, 1, tokens), lambda h, me: (h, 0, 0)),
    ]
    args = [me, keep_hbm(keys), totals]
    out_shape = [
        pltpu.VMEM((heads, rows, width), F32),
        pltpu.VMEM((heads, tokens, width), BF16),
    ]
    aliases = {}
    if fresh:
        in_specs.append(pl.BlockSpec((1, rows, width), lambda h, me: (h, me[0], 0)))
        args.append(keep_hbm(cents))
        out_shape.append(pltpu.VMEM((heads, rows, width), BF16))
    else:
        in_specs += [in_vmem(), in_vmem()]
        args += [keep_vmem(cents), keep_vmem(before)]
        aliases = {4: 0}
    return pl.pallas_call(
        functools.partial(first_kernel, fresh),
        grid_spec=pltpu.PrefetchScalarGridSpec(
            num_scalar_prefetch=1,
            grid=(heads,),
            in_specs=in_specs,
            out_specs=(in_vmem(),) * len(out_shape),
            scratch_shapes=[pltpu.VMEM((tokens, width), BF16)],
        ),
        out_shape=tuple(out_shape),
        input_output_aliases=aliases,
        compiler_params=params(),
        cost_estimate=pl.CostEstimate(
            flops=8 * heads * tokens * rows * width,
            bytes_accessed=4 * heads * rows * width * 4,
            transcendentals=heads * tokens * rows,
        ),
        name="first_block",
    )(*args)


def raw_kernel(blocks, sums_ref, *refs):
    units = refs[:blocks]
    raw_ref, total_ref, cent_ref = refs[blocks:]
    head = pl.program_id(0)
    cent_ref[...] = unit_rows(sums_ref[head]).astype(BF16)
    part = 256
    start = 0
    for unit_ref in units:
        for t in range(0, unit_ref.shape[1], part):
            here = slice(start + t, start + t + part)
            raw = jnp.exp2(dot_nt(cent_ref[...], unit_ref[head, t : t + part, :]) * EXP2_SCALE)
            raw_ref[head, :, here] = raw.astype(BF16)
            total = jnp.sum(raw.reshape(-1, 8, part), axis=0)
            total_ref[0, :, here] = jnp.sum(total, axis=0, keepdims=True)
        start += unit_ref.shape[1]


def raw_weights(sums, units):
    heads, rows, width = sums.shape
    tokens = units[0].shape[1]
    count = tokens * len(units)
    return pl.pallas_call(
        functools.partial(raw_kernel, len(units)),
        grid=(heads,),
        in_specs=[in_vmem()] * (1 + len(units)),
        out_specs=(in_vmem(), pl.BlockSpec((1, 1, count), lambda h: (h, 0, 0))),
        out_shape=(
            pltpu.VMEM((heads, rows, count), BF16),
            jax.ShapeDtypeStruct((heads, 1, count), F32),
        ),
        scratch_shapes=[pltpu.VMEM((rows, width), BF16)],
        compiler_params=params(),
        cost_estimate=pl.CostEstimate(
            flops=4 * heads * rows * count * width,
            bytes_accessed=2 * heads * count * width,
            transcendentals=heads * rows * count,
        ),
        name="raw_weights",
    )(keep_vmem(sums), *map(keep_vmem, units))


def sums_kernel(blocks, raw_ref, *refs):
    totals, units = refs[:blocks], refs[blocks : 2 * blocks]
    out_ref, scaled_ref, sum_ref = refs[2 * blocks :]
    head = pl.program_id(0)
    tokens = units[0].shape[1]
    for m, unit_ref in enumerate(units):
        row_total = totals[0][0, :, m * tokens : (m + 1) * tokens]
        for d in range(1, blocks):
            peer = m ^ d
            row_total += totals[d][0, :, peer * tokens : (peer + 1) * tokens]
        scale_rows(unit_ref[head], 1.0 / row_total, scaled_ref)
        more = dot_nn(raw_ref[head, :, m * tokens : (m + 1) * tokens], scaled_ref[...])
        if m == 0:
            sum_ref[...] = more
        else:
            sum_ref[...] += more
    out_ref[0] = unit_rows(sum_ref[...])


def weighted_sums(raw, units, totals):
    heads, rows, count = raw.shape
    _, tokens, width = units[0].shape
    blocks = len(units)
    return pl.pallas_call(
        functools.partial(sums_kernel, blocks),
        grid=(heads,),
        in_specs=[in_vmem()]
        + [pl.BlockSpec((1, 1, count), lambda h: (h, 0, 0))] * blocks
        + [in_vmem()] * blocks,
        out_specs=pl.BlockSpec((1, rows, width), lambda h: (h, 0, 0)),
        out_shape=jax.ShapeDtypeStruct((heads, rows, width), F32),
        scratch_shapes=[
            pltpu.VMEM((tokens, width), BF16),
            pltpu.VMEM((rows, width), F32),
        ],
        compiler_params=params(),
        cost_estimate=pl.CostEstimate(
            flops=4 * heads * rows * count * width,
            bytes_accessed=2 * heads * count * width,
            transcendentals=0,
        ),
        name="weighted_sums",
    )(keep_vmem(raw), *totals, *map(keep_vmem, units))


def place_kernel(blocks, size, scalar_ref, *refs):
    labels, keys, values = (refs[i * blocks : (i + 1) * blocks] for i in range(3))
    out_refs, (rows_ref, tail_ref, near_ref, mixed_ref, sems) = refs[-7:-5], refs[-5:]
    step = pl.program_id(0)
    heads, tokens, width = keys[0].shape
    digit_rows = tokens // LANES
    sent = values[0].shape[1] - 2 * digit_rows

    @pl.when(step == 0)
    def _():
        rows_ref[:, :, width:] = jnp.zeros((heads, blocks * size, width), BF16)
        copies = []
        for h in range(heads):
            for m in range(blocks):
                start = pl.multiple_of(scalar_ref[0, h, m], 16)
                gap = pl.multiple_of(scalar_ref[1, h, m], 16)
                first = m * size
                copies += [
                    pltpu.make_async_copy(source, target, sems.at[len(copies) + i])
                    for i, (source, target) in enumerate(
                        (
                            (
                                keys[m].at[h, pl.ds(start, size), :],
                                rows_ref.at[h, first : first + size, :width],
                            ),
                            (
                                values[m].at[h, :sent, :],
                                rows_ref.at[h, pl.ds(first + gap, sent), width:],
                            ),
                            (values[m].at[h, sent:, :], tail_ref.at[h, m]),
                        )
                    )
                ]
        for copy in copies:
            copy.start()
        for copy in copies:
            copy.wait()
        for h in range(heads):
            for m in range(blocks):
                start = scalar_ref[0, h, m]
                digits = tail_ref[h, m].astype(F32)
                rank = digits[:digit_rows] * 128.0 + digits[digit_rows:]
                rank = jnp.concatenate([rank[r : r + 1] for r in range(digit_rows)], axis=1)
                label = labels[m][h]
                low, high, before = (
                    scalar_ref[i, h, 0].astype(F32) for i in range(2, 5)
                )
                mine = (label >= low) & (label < high)
                spot = jnp.where(mine, rank - before, -1.0).astype(jnp.int32)
                spot = pltpu.roll(spot, lax.rem(tokens - start, tokens), 1)
                near_ref[h, :, m * size : (m + 1) * size] = spot[:, :size]

    rows = out_refs[0].shape[0] // heads
    total_size = blocks * size
    part = total_size // 2
    for h in range(heads):
        for t in range(0, total_size, part):
            pick = one_hot_rows(rows, near_ref[h, :, t : t + part] - step * rows)
            more = dot_nn(pick, rows_ref[h, t : t + part, :])
            total = more if t == 0 else total + more
        for side in range(2):
            mixed_ref[side, pl.Slice(h, rows, heads), :] = total[
                :, side * width : (side + 1) * width
            ]
    for side in range(2):
        out_refs[side][...] = mixed_ref[side].astype(BF16)


def place(scalars, labels, keys, values, size, cap):
    blocks = len(keys)
    heads, tokens, width = keys[0].shape
    rows = 512
    out = jax.ShapeDtypeStruct((heads * cap, width), BF16)
    block = pl.BlockSpec((heads * rows, width), lambda r: (r, 0))
    return pl.pallas_call(
        functools.partial(place_kernel, blocks, size),
        grid=(cap // rows,),
        in_specs=[pl.BlockSpec(memory_space=pltpu.SMEM)]
        + [whole(labels[0].shape)] * blocks
        + [anywhere()] * (2 * blocks),
        out_specs=(block, block),
        out_shape=(out, out),
        scratch_shapes=[
            pltpu.VMEM((heads, blocks * size, 2 * width), BF16),
            pltpu.VMEM((heads, blocks, 2 * tokens // LANES, width), BF16),
            pltpu.VMEM((heads, 1, blocks * size), jnp.int32),
            pltpu.VMEM((2, heads * rows, width), F32),
            pltpu.SemaphoreType.DMA((3 * heads * blocks,)),
        ],
        compiler_params=params(),
        cost_estimate=pl.CostEstimate(
            flops=4 * heads * cap * blocks * size * width,
            bytes_accessed=12 * heads * cap * width,
            transcendentals=0,
        ),
        name="place",
    )(scalars, *labels, *map(keep_hbm, keys), *map(keep_hbm, values))


def body(key_rows, value_rows, cluster_labels, owner_bounds, init_centroids):
    n = lax.axis_size("ctx")
    me = lax.axis_index("ctx").astype(jnp.int32)
    tokens, heads, width = key_rows.shape
    everyone = n * tokens
    cap = 2 * tokens
    slot = cap // n
    send_size = slot + 16
    key_size = min(tokens, -(-send_size // LANES) * LANES)

    def swap(x, d):
        return lax.ppermute(x, "ctx", [(i, i ^ d) for i in range(n)])

    def cube(x):
        blocks = [x]
        for m in range(1, n):
            low = m & -m
            blocks.append(swap(blocks[m ^ low], low))
        return blocks

    def spread(x):
        return [x] + [swap(x, d) for d in range(1, n)]

    def aligned(start, size):
        return jnp.minimum(start // 16 * 16, tokens - size)

    own_keys, own_values, own_labels = sort_tokens(
        cluster_labels,
        key_rows.reshape(heads * tokens, width),
        value_rows.reshape(heads * tokens, width),
    )
    keys = cube(own_keys)
    own_total = own_totals(own_keys, init_centroids)
    shared = spread(jnp.concatenate([own_total, own_labels], axis=1))
    totals = [own_total] + [x[:, 0:1] for x in shared[1:]]
    labels = [own_labels] + [x[:, 1:2] for x in shared[1:]]

    place_ids = jnp.arange(tokens, dtype=jnp.int32)
    orders = [
        labels[m].astype(jnp.int32) * everyone + (me ^ m) * tokens + place_ids
        for m in range(n)
    ]
    ranks = own_ranks(orders[0], jnp.concatenate(orders, axis=2))
    low = lax.dynamic_slice_in_dim(owner_bounds, me, 1, 1)
    high = lax.dynamic_slice_in_dim(owner_bounds, me + 1, 1, 1)
    block_labels = jnp.concatenate(labels, axis=1).astype(jnp.int32)
    below = jnp.sum((block_labels < low[:, :, None]).astype(jnp.int32), axis=2)
    first = jnp.sum(below, axis=1, keepdims=True)
    key_starts = aligned(below, key_size)
    gaps = aligned(below, send_size) - key_starts
    one = jnp.ones((1, n), jnp.int32)
    scalars = jnp.stack([key_starts, gaps, low * one, high * one, first * one])

    sums, unit, cents = first_block(
        me.reshape(1), keys[0], totals[0], init_centroids, n, None
    )
    units = [unit]
    for m in range(1, n):
        sums, unit = first_block(me.reshape(1), keys[m], totals[m], cents, n, sums)
        units.append(unit)
        if m == 1:
            peers = jnp.stack([me ^ m for m in range(n)])
            peer_low = jnp.take(owner_bounds, peers, axis=1)
            own_below = jnp.sum(
                (own_labels.astype(jnp.int32) < peer_low[:, :, None]).astype(jnp.int32), axis=2
            )
            own_windows = windows(
                aligned(own_below, send_size), ranks, own_values, send_size
            )
            *own_windows, sums = lax.optimization_barrier((*own_windows, sums))
            values = [own_windows[0]] + [swap(own_windows[d], d) for d in range(1, n)]

    raw, part = raw_weights(sums, units)
    out = weighted_sums(raw, units, spread(part))

    placed = place(scalars, labels, keys, values, key_size, cap)
    shape = (cap, heads, width)
    return out, placed[0].reshape(shape), placed[1].reshape(shape)


def solution(mesh):
    placed = (
        P(("grp", "ctx"), "head", None),
        P(("grp", "ctx"), "head", None),
        P("head", ("grp", "ctx")),
        P(("grp", "head"), None),
        P(("grp", "head"), None, None),
    )
    return jax.shard_map(
        body,
        mesh=mesh,
        in_specs=placed,
        out_specs=(
            P(("grp", "head"), "ctx", None),
            P(("grp", "ctx"), "head", None),
            P(("grp", "ctx"), "head", None),
        ),
        check_vma=False,
    )
```

```python
import functools
import math

import jax
import jax.numpy as jnp
from jax import lax
from jax.experimental import pallas as pl
from jax.experimental.pallas import tpu as pltpu
from jax.sharding import PartitionSpec as P

LANES = 128
EXP2_SCALE = 20.0 * math.log2(math.e)
VMEM_LIMIT = 24 * 1024 * 1024
F32 = jnp.float32
BF16 = jnp.bfloat16
NT = (((1,), (1,)), ((), ()))
NN = (((1,), (0,)), ((), ()))


def dot_nt(a, b):
    return lax.dot_general(a, b, NT, preferred_element_type=F32)


def dot_nn(a, b):
    return lax.dot_general(a, b, NN, preferred_element_type=F32)


def unit_rows(x):
    return x * lax.rsqrt(jnp.sum(x * x, axis=-1, keepdims=True) + 1e-06)


def params(**kwargs):
    return pltpu.CompilerParams(vmem_limit_bytes=VMEM_LIMIT, **kwargs)


def whole(shape):
    return pl.BlockSpec(shape, lambda *_: (0,) * len(shape))


def in_vmem():
    return pl.BlockSpec(memory_space=pltpu.VMEM)


def anywhere():
    return pl.BlockSpec(memory_space=pl.ANY)


def keep_hbm(x):
    return pltpu.with_memory_space_constraint(x, pltpu.HBM)


def keep_vmem(x):
    return pltpu.with_memory_space_constraint(x, pltpu.VMEM)


def row_to_lanes(row):
    return jnp.transpose(jnp.broadcast_to(row, (LANES, LANES)))


def split_heads(flat_ref, wide_ref):
    wide_ref[...] = flat_ref[...].astype(F32)


def head_rows(wide_ref, head, heads):
    if heads == 1:
        return wide_ref[...]
    return wide_ref[pl.Slice(head, wide_ref.shape[0] // heads, heads), :]


def count_below(all_ref, own_row, count):
    tokens = own_row.shape[1]
    mine = jnp.broadcast_to(own_row, (8, tokens))
    wide = 4 * LANES

    def step(i, total):
        row = all_ref[0, :, pl.ds(pl.multiple_of(i * wide, wide), wide)]
        for s in range(0, wide, LANES):
            column = row_to_lanes(row[:, s : s + LANES])
            for r in range(0, LANES, 8):
                other = jnp.tile(column[r : r + 8], (1, tokens // LANES))
                total += (other < mine).astype(jnp.int32)
        return total

    total = lax.fori_loop(0, count // wide, step, jnp.zeros((8, tokens), jnp.int32))
    return jnp.sum(total, axis=0, keepdims=True)


def one_hot_rows(size, spot):
    slots = lax.broadcasted_iota(jnp.int16, (size, spot.shape[1]), 0)
    return jnp.where(
        slots == spot.astype(jnp.int16), jnp.ones((), BF16), jnp.zeros((), BF16)
    )


def sort_kernel(label_hbm, keys_hbm, values_hbm, *refs):
    out_keys, out_values, out_labels, flat_ref, wide_ref, both_ref, order_ref, label_ref, sems = refs
    head = pl.program_id(0)
    _, tokens, width = out_keys.shape
    copies = [
        pltpu.make_async_copy(source, flat_ref.at[side], sems.at[side])
        for side, source in enumerate((keys_hbm, values_hbm))
    ]

    @pl.when(head == 0)
    def _():
        label_copy = pltpu.make_async_copy(label_hbm, label_ref, sems.at[2])
        label_copy.start()
        for copy in copies:
            copy.start()
        label_copy.wait()

    label = label_ref[pl.ds(head, 1), :]
    order = label * tokens + lax.broadcasted_iota(jnp.int32, label.shape, 1)
    order_ref[0] = order
    spot = count_below(order_ref, order, tokens)

    @pl.when(head == 0)
    def _():
        for side, copy in enumerate(copies):
            copy.wait()
            split_heads(flat_ref.at[side], wide_ref.at[side])

    for side in range(2):
        both_ref[:, side * width : (side + 1) * width] = head_rows(
            wide_ref.at[side], head, wide_ref.shape[1] // tokens
        ).astype(BF16)
    digits = jnp.concatenate(
        [
            jnp.broadcast_to(label >> 6, (8, tokens)),
            jnp.broadcast_to(label & 63, (8, tokens)),
        ],
        axis=0,
    )
    digits = digits.astype(F32).astype(BF16)
    rows = 512
    for r in range(0, tokens, rows):
        pick = one_hot_rows(rows, spot - r)
        moved = dot_nn(pick, both_ref[...]).astype(BF16)
        out_keys[head, r : r + rows] = moved[:, :width]
        out_values[head, r : r + rows] = moved[:, width:]
        digit = dot_nt(digits, pick)
        out_labels[head, :, r : r + rows] = digit[0:1] * 64.0 + digit[8:9]


def sort_tokens(labels, keys, values):
    heads, tokens = labels.shape
    flat, width = keys.shape
    rows = pltpu.VMEM((heads, tokens, width), BF16)
    return pl.pallas_call(
        sort_kernel,
        grid=(heads,),
        in_specs=[anywhere()] * 3,
        out_specs=(in_vmem(),) * 3,
        out_shape=(rows, rows, pltpu.VMEM((heads, 1, tokens), F32)),
        scratch_shapes=[
            pltpu.VMEM((2, flat, width), BF16),
            pltpu.VMEM((2, flat, width), F32),
            pltpu.VMEM((tokens, 2 * width), BF16),
            pltpu.VMEM((1, 1, tokens), jnp.int32),
            pltpu.VMEM(labels.shape, jnp.int32),
            pltpu.SemaphoreType.DMA((3,)),
        ],
        compiler_params=params(),
        cost_estimate=pl.CostEstimate(
            flops=4 * heads * tokens * tokens * width,
            bytes_accessed=8 * flat * width,
            transcendentals=0,
        ),
        name="sort_tokens",
    )(keep_hbm(labels), keep_hbm(keys), keep_hbm(values))


def windows_kernel(size, start_ref, rank_ref, values_ref, *out_refs):
    heads, tokens, _ = values_ref.shape
    for h in range(heads):
        rank = rank_ref[h]
        digits = [
            digit[:, t : t + LANES]
            for digit in (rank >> 7, rank & 127)
            for t in range(0, tokens, LANES)
        ]
        digits = jnp.concatenate(digits, axis=0).astype(F32).astype(BF16)
        for m, out_ref in enumerate(out_refs):
            start = pl.multiple_of(start_ref[h, m], 16)
            out_ref[h, :size] = values_ref[h, pl.ds(start, size), :]
            out_ref[h, size:] = digits


def windows(starts, ranks, values, size):
    heads, tokens, width = values.shape
    n = starts.shape[1]
    out = pltpu.VMEM((heads, size + 2 * tokens // LANES, width), BF16)
    return pl.pallas_call(
        functools.partial(windows_kernel, size),
        in_specs=[pl.BlockSpec(memory_space=pltpu.SMEM), in_vmem(), in_vmem()],
        out_specs=(in_vmem(),) * n,
        out_shape=(out,) * n,
        compiler_params=params(),
        cost_estimate=pl.CostEstimate(
            flops=0, bytes_accessed=4 * n * heads * size * width, transcendentals=0
        ),
        name="windows",
    )(starts, ranks, keep_vmem(values))


def rank_kernel(own_ref, all_ref, rank_ref):
    rank_ref[0] = count_below(all_ref, own_ref[0], all_ref.shape[2])


def own_ranks(own, everyone):
    heads, _, tokens = own.shape
    count = everyone.shape[2]
    own_block = pl.BlockSpec((1, 1, tokens), lambda h: (h, 0, 0))
    return pl.pallas_call(
        rank_kernel,
        grid=(heads,),
        in_specs=[own_block, pl.BlockSpec((1, 1, count), lambda h: (h, 0, 0))],
        out_specs=own_block,
        out_shape=jax.ShapeDtypeStruct((heads, 1, tokens), jnp.int32),
        compiler_params=params(),
        cost_estimate=pl.CostEstimate(
            flops=3 * heads * tokens * count, bytes_accessed=65536, transcendentals=0
        ),
        name="own_ranks",
    )(own, everyone)


def totals_kernel(keys_ref, cent_ref, tot_ref, unit_ref, sum_ref):
    step = pl.program_id(1)
    tokens = unit_ref.shape[0]

    @pl.when(step == 0)
    def _():
        unit_ref[...] = unit_rows(keys_ref[pl.program_id(0)].astype(F32)).astype(BF16)
        sum_ref[...] = jnp.zeros_like(sum_ref)

    part = 256
    rows = min(1024, cent_ref.shape[1])
    for c in range(0, cent_ref.shape[1], rows):
        cent = unit_rows(cent_ref[0, c : c + rows]).astype(BF16)
        for t in range(0, tokens, part):
            raw = jnp.exp2(dot_nt(cent, unit_ref[t : t + part, :]) * EXP2_SCALE)
            sum_ref[:, t : t + part] += jnp.sum(raw.reshape(-1, 8, part), axis=0)

    @pl.when(step == pl.num_programs(1) - 1)
    def _():
        tot_ref[0] = jnp.sum(sum_ref[...], axis=0, keepdims=True)


def own_totals(keys, cents):
    heads, count, width = cents.shape
    tokens = keys.shape[1]
    rows = min(2048, count)
    return pl.pallas_call(
        totals_kernel,
        grid=(heads, count // rows),
        in_specs=[
            in_vmem(),
            pl.BlockSpec((1, rows, width), lambda h, c: (h, c, 0)),
        ],
        out_specs=pl.BlockSpec((1, 1, tokens), lambda h, c: (h, 0, 0)),
        out_shape=jax.ShapeDtypeStruct((heads, 1, tokens), F32),
        scratch_shapes=[
            pltpu.VMEM((tokens, width), BF16),
            pltpu.VMEM((8, tokens), F32),
        ],
        compiler_params=params(),
        cost_estimate=pl.CostEstimate(
            flops=4 * heads * tokens * count * width,
            bytes_accessed=cents.size * 4,
            transcendentals=heads * tokens * count,
        ),
        name="own_totals",
    )(keep_vmem(keys), keep_hbm(cents))


def scale_rows(unit, inverse, scaled_ref):
    for t in range(0, unit.shape[0], LANES):
        scaled_ref[t : t + LANES] = (
            unit[t : t + LANES, :].astype(F32) * row_to_lanes(inverse[:, t : t + LANES])
        ).astype(BF16)


def first_kernel(fresh, _, keys_ref, tot_ref, cent_in, *refs):
    head = pl.program_id(0)
    if fresh:
        sums_ref, unit_ref, cent_ref, scaled_ref = refs
        cent = unit_rows(cent_in[0]).astype(BF16)
        cent_ref[head] = cent
    else:
        _, sums_ref, unit_ref, scaled_ref = refs
        cent = cent_in[head]
    unit = unit_rows(keys_ref[head].astype(F32)).astype(BF16)
    unit_ref[head] = unit
    scale_rows(unit, 1.0 / tot_ref[0], scaled_ref)
    part = 256
    for t in range(0, unit.shape[0], part):
        raw = jnp.exp2(dot_nt(cent, unit[t : t + part, :]) * EXP2_SCALE)
        more = dot_nn(raw.astype(BF16), scaled_ref[t : t + part])
        if fresh and t == 0:
            sums_ref[head] = more
        else:
            sums_ref[head] += more


def first_block(me, keys, totals, cents, n, before):
    heads, tokens, width = keys.shape
    fresh = before is None
    rows = cents.shape[1] // n if fresh else cents.shape[1]
    in_specs = [
        in_vmem(),
        pl.BlockSpec((1, 1, tokens), lambda h, me: (h, 0, 0)),
    ]
    args = [me, keep_vmem(keys), totals]
    out_shape = [
        pltpu.VMEM((heads, rows, width), F32),
        pltpu.VMEM((heads, tokens, width), BF16),
    ]
    aliases = {}
    if fresh:
        in_specs.append(pl.BlockSpec((1, rows, width), lambda h, me: (h, me[0], 0)))
        args.append(keep_hbm(cents))
        out_shape.append(pltpu.VMEM((heads, rows, width), BF16))
    else:
        in_specs += [in_vmem(), in_vmem()]
        args += [keep_vmem(cents), keep_vmem(before)]
        aliases = {4: 0}
    return pl.pallas_call(
        functools.partial(first_kernel, fresh),
        grid_spec=pltpu.PrefetchScalarGridSpec(
            num_scalar_prefetch=1,
            grid=(heads,),
            in_specs=in_specs,
            out_specs=(in_vmem(),) * len(out_shape),
            scratch_shapes=[pltpu.VMEM((tokens, width), BF16)],
        ),
        out_shape=tuple(out_shape),
        input_output_aliases=aliases,
        compiler_params=params(),
        cost_estimate=pl.CostEstimate(flops=1, bytes_accessed=1, transcendentals=0),
        name="first_block",
    )(*args)


def raw_kernel(blocks, sums_ref, *refs):
    units = refs[:blocks]
    raw_ref, total_ref, cent_ref = refs[blocks:]
    head = pl.program_id(0)
    cent_ref[...] = unit_rows(sums_ref[head]).astype(BF16)
    part = 256
    start = 0
    for unit_ref in units:
        for t in range(0, unit_ref.shape[1], part):
            here = slice(start + t, start + t + part)
            raw = jnp.exp2(dot_nt(cent_ref[...], unit_ref[head, t : t + part, :]) * EXP2_SCALE)
            raw_ref[head, :, here] = raw.astype(BF16)
            total = jnp.sum(raw.reshape(-1, 8, part), axis=0)
            total_ref[0, :, here] = jnp.sum(total, axis=0, keepdims=True)
        start += unit_ref.shape[1]


def raw_weights(sums, units):
    heads, rows, width = sums.shape
    tokens = units[0].shape[1]
    count = tokens * len(units)
    return pl.pallas_call(
        functools.partial(raw_kernel, len(units)),
        grid=(heads,),
        in_specs=[in_vmem()] * (1 + len(units)),
        out_specs=(in_vmem(), pl.BlockSpec((1, 1, count), lambda h: (h, 0, 0))),
        out_shape=(
            pltpu.VMEM((heads, rows, count), BF16),
            jax.ShapeDtypeStruct((heads, 1, count), F32),
        ),
        scratch_shapes=[pltpu.VMEM((rows, width), BF16)],
        compiler_params=params(),
        cost_estimate=pl.CostEstimate(flops=1, bytes_accessed=1, transcendentals=0),
        name="raw_weights",
    )(keep_vmem(sums), *map(keep_vmem, units))


def sums_kernel(blocks, raw_ref, *refs):
    totals, units = refs[:blocks], refs[blocks : 2 * blocks]
    out_ref, scaled_ref, sum_ref = refs[2 * blocks :]
    head = pl.program_id(0)
    tokens = units[0].shape[1]
    for m, unit_ref in enumerate(units):
        row_total = totals[0][0, :, m * tokens : (m + 1) * tokens]
        for d in range(1, blocks):
            peer = m ^ d
            row_total += totals[d][0, :, peer * tokens : (peer + 1) * tokens]
        scale_rows(unit_ref[head], 1.0 / row_total, scaled_ref)
        more = dot_nn(raw_ref[head, :, m * tokens : (m + 1) * tokens], scaled_ref[...])
        if m == 0:
            sum_ref[...] = more
        else:
            sum_ref[...] += more
    out_ref[0] = unit_rows(sum_ref[...])


def weighted_sums(raw, units, totals):
    heads, rows, count = raw.shape
    _, tokens, width = units[0].shape
    blocks = len(units)
    return pl.pallas_call(
        functools.partial(sums_kernel, blocks),
        grid=(heads,),
        in_specs=[in_vmem()]
        + [pl.BlockSpec((1, 1, count), lambda h: (h, 0, 0))] * blocks
        + [in_vmem()] * blocks,
        out_specs=pl.BlockSpec((1, rows, width), lambda h: (h, 0, 0)),
        out_shape=jax.ShapeDtypeStruct((heads, rows, width), F32),
        scratch_shapes=[
            pltpu.VMEM((tokens, width), BF16),
            pltpu.VMEM((rows, width), F32),
        ],
        compiler_params=params(),
        cost_estimate=pl.CostEstimate(flops=1, bytes_accessed=1, transcendentals=0),
        name="weighted_sums",
    )(keep_vmem(raw), *totals, *map(keep_vmem, units))


def place_kernel(blocks, size, scalar_ref, label_ref, *refs):
    keys, values = refs[:blocks], refs[blocks : 2 * blocks]
    out_refs, (rows_ref, near_ref, mixed_ref) = refs[-5:-3], refs[-3:]
    step = pl.program_id(0)
    heads, tokens, width = keys[0].shape
    digit_rows = tokens // LANES
    sent = values[0].shape[1] - 2 * digit_rows

    @pl.when(step == 0)
    def _():
        rows_ref[:, :, width:] = jnp.zeros((heads, blocks * size, width), BF16)
        for h in range(heads):
            for m in range(blocks):
                start = pl.multiple_of(scalar_ref[0, h, m], 16)
                gap = pl.multiple_of(scalar_ref[1, h, m], 16)
                first = m * size
                rows_ref[h, first : first + size, :width] = keys[m][h, pl.ds(start, size), :]
                rows_ref[h, pl.ds(first + gap, sent), width:] = values[m][h, :sent, :]
                digits = values[m][h, sent:, :].astype(F32)
                rank = digits[:digit_rows] * 128.0 + digits[digit_rows:]
                rank = jnp.concatenate([rank[r : r + 1] for r in range(digit_rows)], axis=1)
                label = label_ref[h, m : m + 1, :]
                low, high, before = (
                    scalar_ref[i, h, 0].astype(F32) for i in range(2, 5)
                )
                mine = (label >= low) & (label < high)
                spot = jnp.where(mine, rank - before, -1.0).astype(jnp.int32)
                spot = pltpu.roll(spot, lax.rem(tokens - start, tokens), 1)
                near_ref[h, :, m * size : (m + 1) * size] = spot[:, :size]

    rows = out_refs[0].shape[0] // heads
    total_size = blocks * size
    part = total_size // 2
    for h in range(heads):
        for t in range(0, total_size, part):
            pick = one_hot_rows(rows, near_ref[h, :, t : t + part] - step * rows)
            more = dot_nn(pick, rows_ref[h, t : t + part, :])
            total = more if t == 0 else total + more
        for side in range(2):
            mixed_ref[side, pl.Slice(h, rows, heads), :] = total[
                :, side * width : (side + 1) * width
            ]
    for side in range(2):
        out_refs[side][...] = mixed_ref[side].astype(BF16)


def place(scalars, labels, keys, values, size, cap):
    blocks = len(keys)
    heads, tokens, width = keys[0].shape
    rows = 512
    out = jax.ShapeDtypeStruct((heads * cap, width), BF16)
    block = pl.BlockSpec((heads * rows, width), lambda r: (r, 0))
    return pl.pallas_call(
        functools.partial(place_kernel, blocks, size),
        grid=(cap // rows,),
        in_specs=[pl.BlockSpec(memory_space=pltpu.SMEM)]
        + [whole(labels.shape)]
        + [in_vmem()] * (2 * blocks),
        out_specs=(block, block),
        out_shape=(out, out),
        scratch_shapes=[
            pltpu.VMEM((heads, blocks * size, 2 * width), BF16),
            pltpu.VMEM((heads, 1, blocks * size), jnp.int32),
            pltpu.VMEM((2, heads * rows, width), F32),
        ],
        compiler_params=params(),
        cost_estimate=pl.CostEstimate(flops=1, bytes_accessed=1, transcendentals=0),
        name="place",
    )(scalars, labels, *map(keep_vmem, keys), *map(keep_vmem, values))


def body(key_rows, value_rows, cluster_labels, owner_bounds, init_centroids):
    n = lax.axis_size("ctx")
    me = lax.axis_index("ctx").astype(jnp.int32)
    tokens, heads, width = key_rows.shape
    everyone = n * tokens
    cap = 2 * tokens
    slot = cap // n
    send_size = slot + 16
    key_size = min(tokens, -(-send_size // LANES) * LANES)

    def swap(x, d):
        return lax.ppermute(x, "ctx", [(i, i ^ d) for i in range(n)])

    def spread(x):
        return [x] + [swap(x, d) for d in range(1, n)]

    def widen(x, d):
        return jnp.concatenate([x, swap(x, d)], axis=1)

    def aligned(start, size):
        return jnp.minimum(start // 16 * 16, tokens - size)

    own_keys, own_values, own_labels = sort_tokens(
        cluster_labels,
        key_rows.reshape(heads * tokens, width),
        value_rows.reshape(heads * tokens, width),
    )
    keys = {0: own_keys}
    d = 1
    while d < n:
        keys[d] = swap(own_keys, d)
        d *= 2
    labels = widen(own_labels, 1)
    total_keys, labels = lax.optimization_barrier((own_keys, labels))
    own_total = own_totals(total_keys, init_centroids)
    totals = own_total
    d = 1
    while d < n:
        labels = widen(labels, d) if d > 1 else labels
        totals = widen(totals, d)
        d *= 2

    place_ids = jnp.arange(tokens, dtype=jnp.int32)
    peers = me ^ jnp.arange(n, dtype=jnp.int32)
    block_labels = labels.astype(jnp.int32)
    orders = block_labels * everyone + (peers[:, None] * tokens + place_ids)
    ranks = own_ranks(orders[:, 0:1], orders.reshape(heads, 1, everyone))
    low = lax.dynamic_slice_in_dim(owner_bounds, me, 1, 1)
    high = lax.dynamic_slice_in_dim(owner_bounds, me + 1, 1, 1)
    below = jnp.sum((block_labels < low[:, :, None]).astype(jnp.int32), axis=2)
    first = jnp.sum(below, axis=1, keepdims=True)
    key_starts = aligned(below, key_size)
    gaps = aligned(below, send_size) - key_starts
    one = jnp.ones((1, n), jnp.int32)
    scalars = jnp.stack([key_starts, gaps, low * one, high * one, first * one])

    *came, ranks = lax.optimization_barrier((*keys.values(), ranks))
    keys = dict(zip(keys, came))
    for m in range(1, n):
        if m not in keys:
            keys[m] = swap(keys[m & (m - 1)], m & -m)
    keys = [keys[m] for m in range(n)]

    sums, unit, cents = first_block(
        me.reshape(1), own_keys, own_total, init_centroids, n, None
    )
    units = [unit]
    for m in range(1, n):
        sums, unit = first_block(
            me.reshape(1), keys[m], totals[:, m : m + 1], cents, n, sums
        )
        units.append(unit)
        if m == min(2, n - 1):
            peer_low = jnp.take(owner_bounds, peers, axis=1)
            own_below = jnp.sum(
                (own_labels.astype(jnp.int32) < peer_low[:, :, None]).astype(jnp.int32), axis=2
            )
            own_windows = windows(
                aligned(own_below, send_size), ranks, own_values, send_size
            )
            *own_windows, sums = lax.optimization_barrier((*own_windows, sums))
            values = [own_windows[0]] + [swap(own_windows[d], d) for d in range(1, n)]

    raw, part = raw_weights(sums, units)
    out = weighted_sums(raw, units, spread(part))

    scalars, out = lax.optimization_barrier((scalars, out))
    placed = place(scalars, labels, keys, values, key_size, cap)
    shape = (cap, heads, width)
    return out, placed[0].reshape(shape), placed[1].reshape(shape)


def solution(mesh):
    placed = (
        P(("grp", "ctx"), "head", None),
        P(("grp", "ctx"), "head", None),
        P("head", ("grp", "ctx")),
        P(("grp", "head"), None),
        P(("grp", "head"), None, None),
    )
    return jax.shard_map(
        body,
        mesh=mesh,
        in_specs=placed,
        out_specs=(
            P(("grp", "head"), "ctx", None),
            P(("grp", "ctx"), "head", None),
            P(("grp", "ctx"), "head", None),
        ),
        check_vma=False,
    )
```

```python
import functools
import math

import jax
import jax.numpy as jnp
from jax import lax
from jax.experimental import pallas as pl
from jax.experimental.pallas import tpu as pltpu
from jax.sharding import PartitionSpec as P

LANES = 128
EXP2_SCALE = 20.0 * math.log2(math.e)
VMEM_LIMIT = 24 * 1024 * 1024
F32 = jnp.float32
BF16 = jnp.bfloat16
NT = (((1,), (1,)), ((), ()))
NN = (((1,), (0,)), ((), ()))


def dot_nt(a, b):
    return lax.dot_general(a, b, NT, preferred_element_type=F32)


def dot_nn(a, b):
    return lax.dot_general(a, b, NN, preferred_element_type=F32)


def unit_rows(x):
    return x * lax.rsqrt(jnp.sum(x * x, axis=-1, keepdims=True) + 1e-06)


def params(**kwargs):
    return pltpu.CompilerParams(vmem_limit_bytes=VMEM_LIMIT, **kwargs)


def whole(shape):
    return pl.BlockSpec(shape, lambda *_: (0,) * len(shape))


def in_vmem():
    return pl.BlockSpec(memory_space=pltpu.VMEM)


def anywhere():
    return pl.BlockSpec(memory_space=pl.ANY)


def keep_hbm(x):
    return pltpu.with_memory_space_constraint(x, pltpu.HBM)


def keep_vmem(x):
    return pltpu.with_memory_space_constraint(x, pltpu.VMEM)


def row_to_lanes(row):
    return jnp.transpose(jnp.broadcast_to(row, (LANES, LANES)))


def split_heads(flat_ref, wide_ref):
    wide_ref[...] = flat_ref[...].astype(F32)


def head_rows(wide_ref, head, heads):
    if heads == 1:
        return wide_ref[...]
    return wide_ref[pl.Slice(head, wide_ref.shape[0] // heads, heads), :]


def count_below(all_ref, own_row, count):
    tokens = own_row.shape[1]
    mine = jnp.broadcast_to(own_row, (8, tokens))
    wide = 4 * LANES

    def step(i, total):
        row = all_ref[0, :, pl.ds(pl.multiple_of(i * wide, wide), wide)]
        for s in range(0, wide, LANES):
            column = row_to_lanes(row[:, s : s + LANES])
            for r in range(0, LANES, 8):
                other = jnp.tile(column[r : r + 8], (1, tokens // LANES))
                total += (other < mine).astype(jnp.int32)
        return total

    total = lax.fori_loop(0, count // wide, step, jnp.zeros((8, tokens), jnp.int32))
    return jnp.sum(total, axis=0, keepdims=True)


def one_hot_rows(size, spot):
    slots = lax.broadcasted_iota(jnp.int16, (size, spot.shape[1]), 0)
    return jnp.where(
        slots == spot.astype(jnp.int16), jnp.ones((), BF16), jnp.zeros((), BF16)
    )


def sort_kernel(label_hbm, keys_hbm, *refs):
    out_keys, out_labels, out_spots, flat_ref, wide_ref, rows_ref, order_ref, label_ref, sems = refs
    head = pl.program_id(0)
    _, tokens, width = out_keys.shape
    copy = pltpu.make_async_copy(keys_hbm, flat_ref, sems.at[0])

    @pl.when(head == 0)
    def _():
        label_copy = pltpu.make_async_copy(label_hbm, label_ref, sems.at[1])
        label_copy.start()
        copy.start()
        label_copy.wait()

    label = label_ref[pl.ds(head, 1), :]
    order = label * tokens + lax.broadcasted_iota(jnp.int32, label.shape, 1)
    order_ref[0] = order
    spot = count_below(order_ref, order, tokens)
    out_spots[head] = spot

    @pl.when(head == 0)
    def _():
        copy.wait()
        split_heads(flat_ref, wide_ref)

    rows_ref[...] = head_rows(wide_ref, head, wide_ref.shape[0] // tokens).astype(BF16)
    digits = jnp.concatenate(
        [
            jnp.broadcast_to(label >> 6, (8, tokens)),
            jnp.broadcast_to(label & 63, (8, tokens)),
        ],
        axis=0,
    )
    digits = digits.astype(F32).astype(BF16)
    rows = 512
    for r in range(0, tokens, rows):
        pick = one_hot_rows(rows, spot - r)
        out_keys[head, r : r + rows] = dot_nn(pick, rows_ref[...]).astype(BF16)
        digit = dot_nt(digits, pick)
        out_labels[head, :, r : r + rows] = digit[0:1] * 64.0 + digit[8:9]


def sort_keys(labels, keys):
    heads, tokens = labels.shape
    flat, width = keys.shape
    return pl.pallas_call(
        sort_kernel,
        grid=(heads,),
        in_specs=[anywhere()] * 2,
        out_specs=(in_vmem(),) * 3,
        out_shape=(
            pltpu.VMEM((heads, tokens, width), BF16),
            pltpu.VMEM((heads, 1, tokens), F32),
            pltpu.VMEM((heads, 1, tokens), jnp.int32),
        ),
        scratch_shapes=[
            pltpu.VMEM((flat, width), BF16),
            pltpu.VMEM((flat, width), F32),
            pltpu.VMEM((tokens, width), BF16),
            pltpu.VMEM((1, 1, tokens), jnp.int32),
            pltpu.VMEM(labels.shape, jnp.int32),
            pltpu.SemaphoreType.DMA((2,)),
        ],
        compiler_params=params(),
        name="sort_keys",
    )(keep_hbm(labels), keep_hbm(keys))


def windows_kernel(size, start_ref, spot_ref, values_hbm, *refs):
    out_refs, (flat_ref, wide_ref, rows_ref, sem) = refs[:-4], refs[-4:]
    heads, _, tokens = spot_ref.shape
    copy = pltpu.make_async_copy(values_hbm, flat_ref, sem)
    copy.start()
    copy.wait()
    split_heads(flat_ref, wide_ref)
    rows = 512
    for h in range(heads):
        values = head_rows(wide_ref, h, heads).astype(BF16)
        for r in range(0, tokens, rows):
            pick = one_hot_rows(rows, spot_ref[h] - r)
            rows_ref[h, r : r + rows] = dot_nn(pick, values).astype(BF16)
        for m, out_ref in enumerate(out_refs):
            start = pl.multiple_of(start_ref[h, m], 16)
            out_ref[h] = rows_ref[h, pl.ds(start, size), :]


def windows(starts, spots, values, size):
    heads, _, tokens = spots.shape
    flat, width = values.shape
    n = starts.shape[1]
    out = pltpu.VMEM((heads, size, width), BF16)
    return pl.pallas_call(
        functools.partial(windows_kernel, size),
        in_specs=[pl.BlockSpec(memory_space=pltpu.SMEM), in_vmem(), anywhere()],
        out_specs=(in_vmem(),) * n,
        out_shape=(out,) * n,
        scratch_shapes=[
            pltpu.VMEM((flat, width), BF16),
            pltpu.VMEM((flat, width), F32),
            pltpu.VMEM((heads, tokens, width), BF16),
            pltpu.SemaphoreType.DMA,
        ],
        compiler_params=params(),
        name="windows",
    )(starts, keep_vmem(spots), keep_hbm(values))


def rank_kernel(me_ref, label_ref, rank_ref):
    n, tokens = label_ref.shape[1:]
    me = me_ref[0]
    own = label_ref[0, 0:1, :].astype(jnp.int32)
    rank = lax.broadcasted_iota(jnp.int32, own.shape, 1)
    for m in range(1, n):
        bar = own + ((me ^ m) < me).astype(jnp.int32)
        bar = jnp.broadcast_to(bar, (16, tokens)).astype(jnp.int16)
        count = jnp.zeros((16, tokens), BF16)
        for s in range(0, tokens, LANES):
            column = row_to_lanes(label_ref[0, m : m + 1, s : s + LANES])
            column = column.astype(jnp.int32).astype(jnp.int16)
            for r in range(0, LANES, 16):
                other = jnp.tile(column[r : r + 16], (1, tokens // LANES))
                count += jnp.where(other < bar, jnp.ones((), BF16), jnp.zeros((), BF16))
        rank += jnp.sum(count.astype(F32), axis=0, keepdims=True).astype(jnp.int32)
    rank_ref[0] = rank.astype(F32)


def own_ranks(me, labels):
    heads, n, tokens = labels.shape
    return pl.pallas_call(
        rank_kernel,
        grid=(heads,),
        in_specs=[
            pl.BlockSpec(memory_space=pltpu.SMEM),
            pl.BlockSpec((1, n, tokens), lambda h: (h, 0, 0)),
        ],
        out_specs=pl.BlockSpec((1, 1, tokens), lambda h: (h, 0, 0)),
        out_shape=jax.ShapeDtypeStruct((heads, 1, tokens), F32),
        compiler_params=params(),
        name="own_ranks",
    )(me, labels)


def totals_kernel(keys_ref, cent_ref, tot_ref, unit_ref, sum_ref):
    step = pl.program_id(1)
    tokens = unit_ref.shape[0]

    @pl.when(step == 0)
    def _():
        unit_ref[...] = unit_rows(keys_ref[pl.program_id(0)].astype(F32)).astype(BF16)
        sum_ref[...] = jnp.zeros_like(sum_ref)

    part = 256
    rows = min(1024, cent_ref.shape[1])
    for c in range(0, cent_ref.shape[1], rows):
        cent = unit_rows(cent_ref[0, c : c + rows]).astype(BF16)
        for t in range(0, tokens, part):
            raw = jnp.exp2(dot_nt(cent, unit_ref[t : t + part, :]) * EXP2_SCALE)
            sum_ref[:, t : t + part] += jnp.sum(raw.reshape(-1, 8, part), axis=0)

    @pl.when(step == pl.num_programs(1) - 1)
    def _():
        tot_ref[0] = jnp.sum(sum_ref[...], axis=0, keepdims=True)


def own_totals(keys, cents):
    heads, count, width = cents.shape
    tokens = keys.shape[1]
    rows = min(2048, count)
    return pl.pallas_call(
        totals_kernel,
        grid=(heads, count // rows),
        in_specs=[
            in_vmem(),
            pl.BlockSpec((1, rows, width), lambda h, c: (h, c, 0)),
        ],
        out_specs=pl.BlockSpec((1, 1, tokens), lambda h, c: (h, 0, 0)),
        out_shape=jax.ShapeDtypeStruct((heads, 1, tokens), F32),
        scratch_shapes=[
            pltpu.VMEM((tokens, width), BF16),
            pltpu.VMEM((8, tokens), F32),
        ],
        compiler_params=params(),
        name="own_totals",
    )(keep_vmem(keys), keep_hbm(cents))


def scale_rows(unit, inverse, scaled_ref):
    for t in range(0, unit.shape[0], LANES):
        scaled_ref[t : t + LANES] = (
            unit[t : t + LANES, :].astype(F32) * row_to_lanes(inverse[:, t : t + LANES])
        ).astype(BF16)


def first_kernel(fresh, _, keys_ref, tot_ref, cent_in, *refs):
    head = pl.program_id(0)
    if fresh:
        sums_ref, unit_ref, cent_ref, scaled_ref = refs
        cent = unit_rows(cent_in[0]).astype(BF16)
        cent_ref[head] = cent
    else:
        _, sums_ref, unit_ref, scaled_ref = refs
        cent = cent_in[head]
    unit = unit_rows(keys_ref[head].astype(F32)).astype(BF16)
    unit_ref[head] = unit
    scale_rows(unit, 1.0 / tot_ref[0], scaled_ref)
    part = 256
    for t in range(0, unit.shape[0], part):
        raw = jnp.exp2(dot_nt(cent, unit[t : t + part, :]) * EXP2_SCALE)
        more = dot_nn(raw.astype(BF16), scaled_ref[t : t + part])
        if fresh and t == 0:
            sums_ref[head] = more
        else:
            sums_ref[head] += more


def first_block(me, keys, totals, cents, n, before):
    heads, tokens, width = keys.shape
    fresh = before is None
    rows = cents.shape[1] // n if fresh else cents.shape[1]
    in_specs = [
        in_vmem(),
        pl.BlockSpec((1, 1, tokens), lambda h, me: (h, 0, 0)),
    ]
    args = [me, keep_vmem(keys), totals]
    out_shape = [
        pltpu.VMEM((heads, rows, width), F32),
        pltpu.VMEM((heads, tokens, width), BF16),
    ]
    aliases = {}
    if fresh:
        in_specs.append(pl.BlockSpec((1, rows, width), lambda h, me: (h, me[0], 0)))
        args.append(keep_hbm(cents))
        out_shape.append(pltpu.VMEM((heads, rows, width), BF16))
    else:
        in_specs += [in_vmem(), in_vmem()]
        args += [keep_vmem(cents), keep_vmem(before)]
        aliases = {4: 0}
    return pl.pallas_call(
        functools.partial(first_kernel, fresh),
        grid_spec=pltpu.PrefetchScalarGridSpec(
            num_scalar_prefetch=1,
            grid=(heads,),
            in_specs=in_specs,
            out_specs=(in_vmem(),) * len(out_shape),
            scratch_shapes=[pltpu.VMEM((tokens, width), BF16)],
        ),
        out_shape=tuple(out_shape),
        input_output_aliases=aliases,
        compiler_params=params(),
        name="first_block",
    )(*args)


def raw_kernel(blocks, sums_ref, *refs):
    units = refs[:blocks]
    raw_ref, total_ref, cent_ref = refs[blocks:]
    head = pl.program_id(0)
    cent_ref[...] = unit_rows(sums_ref[head]).astype(BF16)
    part = 256
    start = 0
    for unit_ref in units:
        for t in range(0, unit_ref.shape[1], part):
            here = slice(start + t, start + t + part)
            raw = jnp.exp2(dot_nt(cent_ref[...], unit_ref[head, t : t + part, :]) * EXP2_SCALE)
            raw_ref[head, :, here] = raw.astype(BF16)
            total = jnp.sum(raw.reshape(-1, 8, part), axis=0)
            total_ref[0, :, here] = jnp.sum(total, axis=0, keepdims=True)
        start += unit_ref.shape[1]


def raw_weights(sums, units):
    heads, rows, width = sums.shape
    tokens = units[0].shape[1]
    count = tokens * len(units)
    return pl.pallas_call(
        functools.partial(raw_kernel, len(units)),
        grid=(heads,),
        in_specs=[in_vmem()] * (1 + len(units)),
        out_specs=(in_vmem(), pl.BlockSpec((1, 1, count), lambda h: (h, 0, 0))),
        out_shape=(
            pltpu.VMEM((heads, rows, count), BF16),
            jax.ShapeDtypeStruct((heads, 1, count), F32),
        ),
        scratch_shapes=[pltpu.VMEM((rows, width), BF16)],
        compiler_params=params(),
        name="raw_weights",
    )(keep_vmem(sums), *map(keep_vmem, units))


def sums_kernel(blocks, raw_ref, *refs):
    totals, units = refs[:blocks], refs[blocks : 2 * blocks]
    out_ref, scaled_ref = refs[2 * blocks :]
    head = pl.program_id(0)
    tokens = units[0].shape[1]
    for m, unit_ref in enumerate(units):
        row_total = totals[0][head, :, m * tokens : (m + 1) * tokens]
        for d in range(1, blocks):
            peer = m ^ d
            row_total += totals[d][head, :, peer * tokens : (peer + 1) * tokens]
        scale_rows(
            unit_ref[head], 1.0 / row_total, scaled_ref.at[m * tokens : (m + 1) * tokens]
        )
    out_ref[0] = unit_rows(dot_nn(raw_ref[head], scaled_ref[...]))


def weighted_sums(raw, units, totals):
    heads, rows, count = raw.shape
    _, tokens, width = units[0].shape
    blocks = len(units)
    return pl.pallas_call(
        functools.partial(sums_kernel, blocks),
        grid=(heads,),
        in_specs=[in_vmem()]
        + [in_vmem()] * (2 * blocks),
        out_specs=pl.BlockSpec((1, rows, width), lambda h: (h, 0, 0)),
        out_shape=jax.ShapeDtypeStruct((heads, rows, width), F32),
        scratch_shapes=[
            pltpu.VMEM((count, width), BF16),
        ],
        compiler_params=params(),
        name="weighted_sums",
    )(keep_vmem(raw), *map(keep_vmem, totals), *map(keep_vmem, units))


def place_kernel(blocks, size, scalar_ref, label_ref, *refs):
    keys, values, ranks = (refs[i * blocks : (i + 1) * blocks] for i in range(3))
    out_refs, (rows_ref, near_ref, mixed_ref) = refs[-5:-3], refs[-3:]
    step = pl.program_id(0)
    heads, tokens, width = keys[0].shape
    sent = values[0].shape[1]

    @pl.when(step == 0)
    def _():
        rows_ref[:, :, width:] = jnp.zeros((heads, blocks * size, width), BF16)
        for h in range(heads):
            for m in range(blocks):
                start = pl.multiple_of(scalar_ref[0, h, m], 16)
                gap = pl.multiple_of(scalar_ref[1, h, m], 16)
                first = m * size
                rows_ref[h, first : first + size, :width] = keys[m][h, pl.ds(start, size), :]
                rows_ref[h, pl.ds(first + gap, sent), width:] = values[m][h]
                rank = ranks[m][h, :, -tokens:]
                label = label_ref[h, m : m + 1, :]
                low, high, before = (
                    scalar_ref[i, h, 0].astype(F32) for i in range(2, 5)
                )
                mine = (label >= low) & (label < high)
                spot = jnp.where(mine, rank - before, -1.0).astype(jnp.int32)
                spot = pltpu.roll(spot, lax.rem(tokens - start, tokens), 1)
                near_ref[h, :, m * size : (m + 1) * size] = spot[:, :size]

    rows = out_refs[0].shape[0] // heads
    for h in range(heads):
        pick = one_hot_rows(rows, near_ref[h] - step * rows)
        total = dot_nn(pick, rows_ref[h])
        for side in range(2):
            mixed_ref[side, pl.Slice(h, rows, heads), :] = total[
                :, side * width : (side + 1) * width
            ]
    for side in range(2):
        out_refs[side][...] = mixed_ref[side].astype(BF16)


def place(scalars, labels, keys, values, ranks, size, cap):
    blocks = len(keys)
    heads, tokens, width = keys[0].shape
    rows = 512
    out = jax.ShapeDtypeStruct((heads * cap, width), BF16)
    block = pl.BlockSpec((heads * rows, width), lambda r: (r, 0))
    return pl.pallas_call(
        functools.partial(place_kernel, blocks, size),
        grid=(cap // rows,),
        in_specs=[pl.BlockSpec(memory_space=pltpu.SMEM)]
        + [whole(labels.shape)]
        + [in_vmem()] * (3 * blocks),
        out_specs=(block, block),
        out_shape=(out, out),
        scratch_shapes=[
            pltpu.VMEM((heads, blocks * size, 2 * width), BF16),
            pltpu.VMEM((heads, 1, blocks * size), jnp.int32),
            pltpu.VMEM((2, heads * rows, width), F32),
        ],
        compiler_params=params(),
        name="place",
    )(scalars, labels, *(keep_vmem(x) for x in (*keys, *values, *ranks)))


def body(key_rows, value_rows, cluster_labels, owner_bounds, init_centroids):
    n = lax.axis_size("ctx")
    me = lax.axis_index("ctx").astype(jnp.int32)
    tokens, heads, width = key_rows.shape
    cap = 2 * tokens
    slot = cap // n
    send_size = slot + 16
    key_size = min(tokens, -(-send_size // LANES) * LANES)

    def swap(x, d):
        return lax.ppermute(x, "ctx", [(i, i ^ d) for i in range(n)])

    def spread(x):
        return [x] + [swap(x, d) for d in range(1, n)]

    def aligned(start, size):
        return jnp.minimum(start // 16 * 16, tokens - size)

    me_array = me.reshape(1)
    own_keys, own_labels, own_spots = sort_keys(
        cluster_labels, key_rows.reshape(heads * tokens, width)
    )
    keys = {0: own_keys}
    d = 1
    while d < n:
        keys[d] = swap(own_keys, d)
        d *= 2
    own_total = own_totals(own_keys, init_centroids)
    shared = spread(jnp.concatenate([own_total, own_labels], axis=1))
    totals = [own_total] + [x[:, 0:1] for x in shared[1:]]

    sums, unit, cents = first_block(me_array, own_keys, own_total, init_centroids, n, None)
    units = [unit]
    *came, sums = lax.optimization_barrier((*keys.values(), sums))
    keys = dict(zip(keys, came))
    for m in range(1, n):
        if m not in keys:
            keys[m] = swap(keys[m & (m - 1)], m & -m)
    keys = [keys[m] for m in range(n)]
    peer_low = jnp.take(owner_bounds, me ^ jnp.arange(n, dtype=jnp.int32), axis=1)
    own_below = jnp.sum((own_labels < peer_low[:, :, None]).astype(jnp.int32), axis=2)
    own_windows = windows(
        aligned(own_below, send_size),
        own_spots,
        value_rows.reshape(heads * tokens, width),
        send_size,
    )
    for m in range(1, n):
        sums, unit = first_block(me_array, keys[m], totals[m], cents, n, sums)
        units.append(unit)
        if m == min(2, n - 1):
            *own_windows, sums = lax.optimization_barrier((*own_windows, sums))
            values = [own_windows[0]] + [swap(own_windows[d], d) for d in range(1, n)]
            labels, sums = lax.optimization_barrier(
                (jnp.concatenate([x[:, -1:] for x in shared], axis=1), sums)
            )
            ranks = own_ranks(me_array, labels)

    raw, part = raw_weights(sums, units)
    parts = spread(jnp.concatenate([part, ranks], axis=2))
    out = weighted_sums(raw, units, parts)

    low = lax.dynamic_slice_in_dim(owner_bounds, me, 1, 1)
    high = lax.dynamic_slice_in_dim(owner_bounds, me + 1, 1, 1)
    below = jnp.sum((labels < low[:, :, None]).astype(jnp.int32), axis=2)
    first = jnp.sum(below, axis=1, keepdims=True)
    key_starts = aligned(below, key_size)
    gaps = aligned(below, send_size) - key_starts
    one = jnp.ones((1, n), jnp.int32)
    scalars = jnp.stack([key_starts, gaps, low * one, high * one, first * one])
    scalars, out = lax.optimization_barrier((scalars, out))
    placed = place(scalars, labels, keys, values, parts, key_size, cap)
    shape = (cap, heads, width)
    return out, placed[0].reshape(shape), placed[1].reshape(shape)


def solution(mesh):
    placed = (
        P(("grp", "ctx"), "head", None),
        P(("grp", "ctx"), "head", None),
        P("head", ("grp", "ctx")),
        P(("grp", "head"), None),
        P(("grp", "head"), None, None),
    )
    return jax.shard_map(
        body,
        mesh=mesh,
        in_specs=placed,
        out_specs=(
            P(("grp", "head"), "ctx", None),
            P(("grp", "ctx"), "head", None),
            P(("grp", "ctx"), "head", None),
        ),
        check_vma=False,
    )
```

```python
import functools
import math

import jax
import jax.numpy as jnp
from jax import lax
from jax.experimental import pallas as pl
from jax.experimental.pallas import tpu as pltpu
from jax.sharding import PartitionSpec as P

LANES = 128
EXP2_SCALE = 20.0 * math.log2(math.e)
VMEM_LIMIT = 16 * 1024 * 1024
F32 = jnp.float32
BF16 = jnp.bfloat16
NT = (((1,), (1,)), ((), ()))
NN = (((1,), (0,)), ((), ()))


def dot_nt(a, b):
    return lax.dot_general(a, b, NT, preferred_element_type=F32)


def dot_nn(a, b):
    return lax.dot_general(a, b, NN, preferred_element_type=F32)


def unit_rows(x):
    return x * lax.rsqrt(jnp.sum(x * x, axis=-1, keepdims=True) + 1e-06)


def params(**kwargs):
    return pltpu.CompilerParams(vmem_limit_bytes=VMEM_LIMIT, **kwargs)


def whole(shape):
    return pl.BlockSpec(shape, lambda *_: (0,) * len(shape))


def in_vmem():
    return pl.BlockSpec(memory_space=pltpu.VMEM)


def anywhere():
    return pl.BlockSpec(memory_space=pl.ANY)


def keep_hbm(x):
    return pltpu.with_memory_space_constraint(x, pltpu.HBM)


def keep_vmem(x):
    return pltpu.with_memory_space_constraint(x, pltpu.VMEM)


def row_to_lanes(row):
    return jnp.transpose(jnp.broadcast_to(row, (LANES, LANES)))


def split_heads(flat_ref, wide_ref):
    wide_ref[...] = flat_ref[...].astype(F32)


def head_rows(wide_ref, head, heads):
    if heads == 1:
        return wide_ref[...]
    return wide_ref[pl.Slice(head, wide_ref.shape[0] // heads, heads), :]


def count_below(all_ref, own_row, count):
    tokens = own_row.shape[1]
    mine = jnp.broadcast_to(own_row, (8, tokens))
    wide = 4 * LANES

    def step(i, total):
        row = all_ref[0, :, pl.ds(pl.multiple_of(i * wide, wide), wide)]
        for s in range(0, wide, LANES):
            column = row_to_lanes(row[:, s : s + LANES])
            for r in range(0, LANES, 8):
                other = jnp.tile(column[r : r + 8], (1, tokens // LANES))
                total += (other < mine).astype(jnp.int32)
        return total

    total = lax.fori_loop(0, count // wide, step, jnp.zeros((8, tokens), jnp.int32))
    return jnp.sum(total, axis=0, keepdims=True)


def one_hot_rows(size, spot):
    slots = lax.broadcasted_iota(jnp.int16, (size, spot.shape[1]), 0)
    return jnp.where(
        slots == spot.astype(jnp.int16), jnp.ones((), BF16), jnp.zeros((), BF16)
    )


def sort_kernel(label_hbm, keys_hbm, *refs):
    out_keys, out_labels, out_spots, flat_ref, wide_ref, rows_ref, order_ref, label_ref, sems = refs
    head = pl.program_id(0)
    _, tokens, width = out_keys.shape
    copy = pltpu.make_async_copy(keys_hbm, flat_ref, sems.at[0])

    @pl.when(head == 0)
    def _():
        label_copy = pltpu.make_async_copy(label_hbm, label_ref, sems.at[1])
        label_copy.start()
        copy.start()
        label_copy.wait()

    label = label_ref[pl.ds(head, 1), :]
    order = label * tokens + lax.broadcasted_iota(jnp.int32, label.shape, 1)
    order_ref[0] = order
    spot = count_below(order_ref, order, tokens)
    out_spots[head] = spot

    @pl.when(head == 0)
    def _():
        copy.wait()
        split_heads(flat_ref, wide_ref)

    rows_ref[...] = head_rows(wide_ref, head, wide_ref.shape[0] // tokens).astype(BF16)
    digits = jnp.concatenate(
        [
            jnp.broadcast_to(label >> 6, (8, tokens)),
            jnp.broadcast_to(label & 63, (8, tokens)),
        ],
        axis=0,
    )
    digits = digits.astype(F32).astype(BF16)
    rows = 512
    for r in range(0, tokens, rows):
        pick = one_hot_rows(rows, spot - r)
        out_keys[head, r : r + rows] = dot_nn(pick, rows_ref[...]).astype(BF16)
        digit = dot_nt(digits, pick)
        out_labels[head, :, r : r + rows] = digit[0:1] * 64.0 + digit[8:9]


def sort_keys(labels, keys):
    heads, tokens = labels.shape
    flat, width = keys.shape
    return pl.pallas_call(
        sort_kernel,
        grid=(heads,),
        in_specs=[anywhere()] * 2,
        out_specs=(in_vmem(),) * 3,
        out_shape=(
            pltpu.VMEM((heads, tokens, width), BF16),
            pltpu.VMEM((heads, 1, tokens), F32),
            pltpu.VMEM((heads, 1, tokens), jnp.int32),
        ),
        scratch_shapes=[
            pltpu.VMEM((flat, width), BF16),
            pltpu.VMEM((flat, width), F32),
            pltpu.VMEM((tokens, width), BF16),
            pltpu.VMEM((1, 1, tokens), jnp.int32),
            pltpu.VMEM(labels.shape, jnp.int32),
            pltpu.SemaphoreType.DMA((2,)),
        ],
        compiler_params=params(),
        name="sort_keys",
    )(keep_hbm(labels), keep_hbm(keys))


def values_kernel(spot_ref, values_hbm, out_ref, flat_ref, wide_ref, sem):
    heads, _, tokens = spot_ref.shape
    copy = pltpu.make_async_copy(values_hbm, flat_ref, sem)
    copy.start()
    copy.wait()
    split_heads(flat_ref, wide_ref)
    rows = 512
    for h in range(heads):
        values = head_rows(wide_ref, h, heads).astype(BF16)
        for r in range(0, tokens, rows):
            pick = one_hot_rows(rows, spot_ref[h] - r)
            out_ref[h, r : r + rows] = dot_nn(pick, values).astype(BF16)


def sort_values(spots, values):
    heads, _, tokens = spots.shape
    flat, width = values.shape
    return pl.pallas_call(
        values_kernel,
        in_specs=[in_vmem(), anywhere()],
        out_specs=in_vmem(),
        out_shape=pltpu.VMEM((heads, tokens, width), BF16),
        scratch_shapes=[
            pltpu.VMEM((flat, width), BF16),
            pltpu.VMEM((flat, width), F32),
            pltpu.SemaphoreType.DMA,
        ],
        compiler_params=params(),
        name="sort_values",
    )(keep_vmem(spots), keep_hbm(values))


def windows_kernel(size, start_ref, rank_ref, values_ref, _, *out_refs):
    heads, tokens, _ = values_ref.shape
    for h in range(heads):
        rank = rank_ref[h].astype(jnp.int32)
        digits = [
            digit[:, t : t + LANES]
            for digit in (rank >> 7, rank & 127)
            for t in range(0, tokens, LANES)
        ]
        digits = jnp.concatenate(digits, axis=0).astype(F32).astype(BF16)
        for m, out_ref in enumerate(out_refs):
            start = pl.multiple_of(start_ref[h, m], 16)
            out_ref[h, :size] = values_ref[h, pl.ds(start, size), :]
            out_ref[h, size:] = digits


def windows(starts, ranks, values, size, after):
    heads, tokens, width = values.shape
    n = starts.shape[1]
    out = pltpu.VMEM((heads, size + 2 * tokens // LANES, width), BF16)
    return pl.pallas_call(
        functools.partial(windows_kernel, size),
        in_specs=[pl.BlockSpec(memory_space=pltpu.SMEM), in_vmem(), in_vmem(), in_vmem()],
        out_specs=(in_vmem(),) * n,
        out_shape=(out,) * n,
        compiler_params=params(),
        name="windows",
    )(starts, ranks, keep_vmem(values), keep_vmem(after))


def rank_kernel(me_ref, label_ref, rank_ref):
    n, tokens = label_ref.shape[1:]
    me = me_ref[0]
    own = label_ref[0, 0:1, :].astype(jnp.int32)
    rank = lax.broadcasted_iota(jnp.int32, own.shape, 1)
    for m in range(1, n):
        bar = own + ((me ^ m) < me).astype(jnp.int32)
        bar = jnp.broadcast_to(bar, (16, tokens)).astype(jnp.int16)
        count = jnp.zeros((16, tokens), BF16)
        for s in range(0, tokens, LANES):
            column = row_to_lanes(label_ref[0, m : m + 1, s : s + LANES])
            column = column.astype(jnp.int32).astype(jnp.int16)
            for r in range(0, LANES, 16):
                other = jnp.tile(column[r : r + 16], (1, tokens // LANES))
                count += jnp.where(other < bar, jnp.ones((), BF16), jnp.zeros((), BF16))
        rank += jnp.sum(count.astype(F32), axis=0, keepdims=True).astype(jnp.int32)
    rank_ref[0] = rank.astype(F32)


def own_ranks(me, labels):
    heads, n, tokens = labels.shape
    return pl.pallas_call(
        rank_kernel,
        grid=(heads,),
        in_specs=[
            pl.BlockSpec(memory_space=pltpu.SMEM),
            pl.BlockSpec((1, n, tokens), lambda h: (h, 0, 0)),
        ],
        out_specs=pl.BlockSpec((1, 1, tokens), lambda h: (h, 0, 0)),
        out_shape=jax.ShapeDtypeStruct((heads, 1, tokens), F32),
        compiler_params=params(),
        name="own_ranks",
    )(me, labels)


def totals_kernel(keys_ref, cent_ref, _, tot_ref, unit_ref, sum_ref):
    step = pl.program_id(1)
    tokens = unit_ref.shape[0]

    @pl.when(step == 0)
    def _():
        unit_ref[...] = unit_rows(keys_ref[pl.program_id(0)].astype(F32)).astype(BF16)
        sum_ref[...] = jnp.zeros_like(sum_ref)

    part = 256
    rows = min(1024, cent_ref.shape[1])
    for c in range(0, cent_ref.shape[1], rows):
        cent = unit_rows(cent_ref[0, c : c + rows]).astype(BF16)
        for t in range(0, tokens, part):
            raw = jnp.exp2(dot_nt(cent, unit_ref[t : t + part, :]) * EXP2_SCALE)
            sum_ref[:, t : t + part] += jnp.sum(raw.reshape(-1, 8, part), axis=0)

    @pl.when(step == pl.num_programs(1) - 1)
    def _():
        tot_ref[0] = jnp.sum(sum_ref[...], axis=0, keepdims=True)


def own_totals(keys, cents, after):
    heads, count, width = cents.shape
    tokens = keys.shape[1]
    rows = min(2048, count)
    return pl.pallas_call(
        totals_kernel,
        grid=(heads, count // rows),
        in_specs=[
            in_vmem(),
            pl.BlockSpec((1, rows, width), lambda h, c: (h, c, 0)),
            in_vmem(),
        ],
        out_specs=pl.BlockSpec((1, 1, tokens), lambda h, c: (h, 0, 0)),
        out_shape=jax.ShapeDtypeStruct((heads, 1, tokens), F32),
        scratch_shapes=[
            pltpu.VMEM((tokens, width), BF16),
            pltpu.VMEM((8, tokens), F32),
        ],
        compiler_params=params(),
        name="own_totals",
    )(keep_vmem(keys), keep_hbm(cents), after)


def scale_rows(unit, inverse, scaled_ref):
    for t in range(0, unit.shape[0], LANES):
        scaled_ref[t : t + LANES] = (
            unit[t : t + LANES, :].astype(F32) * row_to_lanes(inverse[:, t : t + LANES])
        ).astype(BF16)


def first_kernel(fresh, _, keys_ref, tot_ref, cent_in, *refs):
    head = pl.program_id(0)
    if fresh:
        sums_ref, unit_ref, cent_ref, scaled_ref = refs
        cent = unit_rows(cent_in[0]).astype(BF16)
        cent_ref[head] = cent
    else:
        _, sums_ref, unit_ref, scaled_ref = refs
        cent = cent_in[head]
    unit = unit_rows(keys_ref[head].astype(F32)).astype(BF16)
    unit_ref[head] = unit
    scale_rows(unit, 1.0 / tot_ref[0], scaled_ref)
    part = 256
    for t in range(0, unit.shape[0], part):
        raw = jnp.exp2(dot_nt(cent, unit[t : t + part, :]) * EXP2_SCALE)
        more = dot_nn(raw.astype(BF16), scaled_ref[t : t + part])
        if fresh and t == 0:
            sums_ref[head] = more
        else:
            sums_ref[head] += more


def first_block(me, keys, totals, cents, n, before):
    heads, tokens, width = keys.shape
    fresh = before is None
    rows = cents.shape[1] // n if fresh else cents.shape[1]
    in_specs = [
        in_vmem(),
        pl.BlockSpec((1, 1, tokens), lambda h, me: (h, 0, 0)),
    ]
    args = [me, keep_vmem(keys), totals]
    out_shape = [
        pltpu.VMEM((heads, rows, width), F32),
        pltpu.VMEM((heads, tokens, width), BF16),
    ]
    aliases = {}
    if fresh:
        in_specs.append(pl.BlockSpec((1, rows, width), lambda h, me: (h, me[0], 0)))
        args.append(keep_hbm(cents))
        out_shape.append(pltpu.VMEM((heads, rows, width), BF16))
    else:
        in_specs += [in_vmem(), in_vmem()]
        args += [keep_vmem(cents), keep_vmem(before)]
        aliases = {4: 0}
    return pl.pallas_call(
        functools.partial(first_kernel, fresh),
        grid_spec=pltpu.PrefetchScalarGridSpec(
            num_scalar_prefetch=1,
            grid=(heads,),
            in_specs=in_specs,
            out_specs=(in_vmem(),) * len(out_shape),
            scratch_shapes=[pltpu.VMEM((tokens, width), BF16)],
        ),
        out_shape=tuple(out_shape),
        input_output_aliases=aliases,
        compiler_params=params(),
        name="first_block",
    )(*args)


def raw_kernel(blocks, sums_ref, *refs):
    units = refs[:blocks]
    raw_ref, total_ref, cent_ref = refs[blocks:]
    head = pl.program_id(0)
    cent_ref[...] = unit_rows(sums_ref[head]).astype(BF16)
    part = 256
    start = 0
    for unit_ref in units:
        for t in range(0, unit_ref.shape[1], part):
            here = slice(start + t, start + t + part)
            raw = jnp.exp2(dot_nt(cent_ref[...], unit_ref[head, t : t + part, :]) * EXP2_SCALE)
            raw_ref[head, :, here] = raw.astype(BF16)
            total = jnp.sum(raw.reshape(-1, 8, part), axis=0)
            total_ref[0, :, here] = jnp.sum(total, axis=0, keepdims=True)
        start += unit_ref.shape[1]


def raw_weights(sums, units):
    heads, rows, width = sums.shape
    tokens = units[0].shape[1]
    count = tokens * len(units)
    return pl.pallas_call(
        functools.partial(raw_kernel, len(units)),
        grid=(heads,),
        in_specs=[in_vmem()] * (1 + len(units)),
        out_specs=(in_vmem(), pl.BlockSpec((1, 1, count), lambda h: (h, 0, 0))),
        out_shape=(
            pltpu.VMEM((heads, rows, count), BF16),
            jax.ShapeDtypeStruct((heads, 1, count), F32),
        ),
        scratch_shapes=[pltpu.VMEM((rows, width), BF16)],
        compiler_params=params(),
        name="raw_weights",
    )(keep_vmem(sums), *map(keep_vmem, units))


def sums_kernel(blocks, raw_ref, *refs):
    totals, units = refs[:blocks], refs[blocks : 2 * blocks]
    out_ref, scaled_ref = refs[2 * blocks :]
    head = pl.program_id(0)
    tokens = units[0].shape[1]
    for m, unit_ref in enumerate(units):
        row_total = totals[0][head, :, m * tokens : (m + 1) * tokens]
        for d in range(1, blocks):
            peer = m ^ d
            row_total += totals[d][head, :, peer * tokens : (peer + 1) * tokens]
        scale_rows(
            unit_ref[head], 1.0 / row_total, scaled_ref.at[m * tokens : (m + 1) * tokens]
        )
    out_ref[0] = unit_rows(dot_nn(raw_ref[head], scaled_ref[...]))


def weighted_sums(raw, units, totals):
    heads, rows, count = raw.shape
    _, tokens, width = units[0].shape
    blocks = len(units)
    return pl.pallas_call(
        functools.partial(sums_kernel, blocks),
        grid=(heads,),
        in_specs=[in_vmem()]
        + [in_vmem()] * (2 * blocks),
        out_specs=pl.BlockSpec((1, rows, width), lambda h: (h, 0, 0)),
        out_shape=jax.ShapeDtypeStruct((heads, rows, width), F32),
        scratch_shapes=[
            pltpu.VMEM((count, width), BF16),
        ],
        compiler_params=params(),
        name="weighted_sums",
    )(keep_vmem(raw), *map(keep_vmem, totals), *map(keep_vmem, units))


def place_kernel(blocks, size, fresh, scalar_ref, label_ref, *refs):
    count = len(blocks)
    keys, values, refs = refs[:count], refs[count : 2 * count], refs[2 * count :]
    before, (*out_refs, rows_ref, near_ref, mixed_ref) = refs[: 0 if fresh else 2], refs[0 if fresh else 2 :]
    step = pl.program_id(0)
    heads, tokens, width = keys[0].shape
    digit_rows = tokens // LANES
    sent = values[0].shape[1] - 2 * digit_rows
    rows = mixed_ref.shape[1] // heads

    @pl.when(step == 0)
    def _():
        rows_ref[:, :, width:] = jnp.zeros((heads, count * size, width), BF16)
        for h in range(heads):
            low, high, first = (scalar_ref[i, h, 0].astype(F32) for i in range(2, 5))
            for i, m in enumerate(blocks):
                start = pl.multiple_of(scalar_ref[0, h, m], 16)
                gap = pl.multiple_of(scalar_ref[1, h, m], 16)
                here = i * size
                rows_ref[h, here : here + size, :width] = keys[i][h, pl.ds(start, size), :]
                rows_ref[h, pl.ds(here + gap, sent), width:] = values[i][h, :sent, :]
                digits = values[i][h, sent:, :].astype(F32)
                rank = digits[:digit_rows] * 128.0 + digits[digit_rows:]
                rank = jnp.concatenate([rank[r : r + 1] for r in range(digit_rows)], axis=1)
                label = label_ref[h, m : m + 1, :]
                mine = (label >= low) & (label < high)
                spot = jnp.where(mine, rank - first, -1.0).astype(jnp.int32)
                spot = pltpu.roll(spot, lax.rem(tokens - start, tokens), 1)
                near_ref[h, :, here : here + size] = spot[:, :size]

    for h in range(heads):
        pick = one_hot_rows(rows, near_ref[h] - step * rows)
        total = dot_nn(pick, rows_ref[h])
        for side in range(2):
            mixed_ref[side, pl.Slice(h, rows, heads), :] = total[
                :, side * width : (side + 1) * width
            ]
    for side in range(2):
        if fresh:
            here = pl.ds(pl.multiple_of(step * rows * heads, rows * heads), rows * heads)
            out_refs[side][here] = mixed_ref[side].astype(BF16)
        else:
            here = pl.ds(pl.multiple_of(step * rows * heads, rows * heads), rows * heads)
            more = mixed_ref[side] + before[side][here].astype(F32)
            out_refs[side][...] = more.astype(BF16)


def place(scalars, labels, keys, values, blocks, size, cap, before):
    heads, _, width = keys[0].shape
    rows = 512
    fresh = before is None
    if fresh:
        out = pltpu.VMEM((heads * cap, width), BF16)
        block = in_vmem()
    else:
        out = jax.ShapeDtypeStruct((heads * cap, width), BF16)
        block = pl.BlockSpec((heads * rows, width), lambda r: (r, 0))
    moved = [x[m] for x in (keys, values) for m in blocks] + list(before or ())
    return pl.pallas_call(
        functools.partial(place_kernel, blocks, size, fresh),
        grid=(cap // rows,),
        in_specs=[pl.BlockSpec(memory_space=pltpu.SMEM)]
        + [whole(labels.shape)]
        + [in_vmem()] * len(moved),
        out_specs=(block, block),
        out_shape=(out, out),
        scratch_shapes=[
            pltpu.VMEM((heads, len(blocks) * size, 2 * width), BF16),
            pltpu.VMEM((heads, 1, len(blocks) * size), jnp.int32),
            pltpu.VMEM((2, heads * rows, width), F32),
        ],
        compiler_params=params(),
        name="place",
    )(scalars, labels, *map(keep_vmem, moved))


def body(key_rows, value_rows, cluster_labels, owner_bounds, init_centroids):
    n = lax.axis_size("ctx")
    me = lax.axis_index("ctx").astype(jnp.int32)
    tokens, heads, width = key_rows.shape
    cap = 2 * tokens
    slot = cap // n
    send_size = slot + 16
    key_size = min(tokens, -(-send_size // LANES) * LANES)

    def swap(x, d):
        return lax.ppermute(x, "ctx", [(i, i ^ d) for i in range(n)])

    def spread(x):
        return [x] + [swap(x, d) for d in range(1, n)]

    def aligned(start, size):
        return jnp.minimum(start // 16 * 16, tokens - size)

    me_array = me.reshape(1)
    own_keys, own_labels, own_spots = sort_keys(
        cluster_labels, key_rows.reshape(heads * tokens, width)
    )
    keys = {0: own_keys}
    d = 1
    while d < n:
        keys[d] = swap(own_keys, d)
        d *= 2
    pairs = [(i, i ^ 1) for i in range(lax.axis_size("head"))]
    word = lax.ppermute(own_labels[:, :, :LANES], "head", pairs)
    own_total = own_totals(own_keys, init_centroids, word)
    shared = spread(jnp.concatenate([own_total, own_labels], axis=1))
    totals = [own_total] + [x[:, 0:1] for x in shared[1:]]

    sums, unit, cents = first_block(me_array, own_keys, own_total, init_centroids, n, None)
    units = [unit]
    *came, sums = lax.optimization_barrier((*keys.values(), sums))
    keys = dict(zip(keys, came))
    for m in range(1, n):
        if m not in keys:
            keys[m] = swap(keys[m & (m - 1)], m & -m)
    keys = [keys[m] for m in range(n)]
    peer_low = jnp.take(owner_bounds, me ^ jnp.arange(n, dtype=jnp.int32), axis=1)
    own_below = jnp.sum((own_labels < peer_low[:, :, None]).astype(jnp.int32), axis=2)
    own_values = sort_values(own_spots, value_rows.reshape(heads * tokens, width))

    labels = jnp.concatenate([x[:, -1:] for x in shared], axis=1)
    ranks = own_ranks(me_array, labels)
    value_starts = aligned(own_below, send_size)
    low = lax.dynamic_slice_in_dim(owner_bounds, me, 1, 1)
    high = lax.dynamic_slice_in_dim(owner_bounds, me + 1, 1, 1)
    below = jnp.sum((labels < low[:, :, None]).astype(jnp.int32), axis=2)
    first = jnp.sum(below, axis=1, keepdims=True)
    key_starts = aligned(below, key_size)
    gaps = aligned(below, send_size) - key_starts
    one = jnp.ones((1, n), jnp.int32)
    scalars = jnp.stack([key_starts, gaps, low * one, high * one, first * one])

    late = [2]
    early = [d for d in range(1, n) if d not in late]
    values = {}
    for m in range(1, n):
        sums, unit = first_block(me_array, keys[m], totals[m], cents, n, sums)
        units.append(unit)
        going = {1: early, 2: [0, *late]}.get(m, [])
        if going:
            starts = jnp.stack([value_starts[:, d] for d in going], axis=1)
            for d, window in zip(going, windows(starts, ranks, own_values, send_size, unit)):
                values[d] = swap(window, d) if d else window

    raw, part = raw_weights(sums, units)
    parts = spread(part)
    placed = place(scalars, labels, keys, values, [0, *early], key_size, cap, None)
    out = weighted_sums(raw, units, parts)
    placed = place(scalars, labels, keys, values, late, key_size, cap, placed)
    shape = (cap, heads, width)
    return out, placed[0].reshape(shape), placed[1].reshape(shape)


def solution(mesh):
    placed = (
        P(("grp", "ctx"), "head", None),
        P(("grp", "ctx"), "head", None),
        P("head", ("grp", "ctx")),
        P(("grp", "head"), None),
        P(("grp", "head"), None, None),
    )
    return jax.shard_map(
        body,
        mesh=mesh,
        in_specs=placed,
        out_specs=(
            P(("grp", "head"), "ctx", None),
            P(("grp", "ctx"), "head", None),
            P(("grp", "ctx"), "head", None),
        ),
        check_vma=False,
    )
```

```python
import functools
import math

import jax
import jax.numpy as jnp
from jax import lax
from jax.experimental import pallas as pl
from jax.experimental.pallas import tpu as pltpu
from jax.sharding import PartitionSpec as P

LANES = 128
EXP2_SCALE = 20.0 * math.log2(math.e)
VMEM_LIMIT = 16 * 1024 * 1024
F32 = jnp.float32
BF16 = jnp.bfloat16
NT = (((1,), (1,)), ((), ()))
NN = (((1,), (0,)), ((), ()))


def dot_nt(a, b):
    return lax.dot_general(a, b, NT, preferred_element_type=F32)


def dot_nn(a, b):
    return lax.dot_general(a, b, NN, preferred_element_type=F32)


def unit_rows(x):
    return x * lax.rsqrt(jnp.sum(x * x, axis=-1, keepdims=True) + 1e-06)


def params(**kwargs):
    return pltpu.CompilerParams(vmem_limit_bytes=VMEM_LIMIT, **kwargs)


def whole(shape):
    return pl.BlockSpec(shape, lambda *_: (0,) * len(shape))


def in_vmem():
    return pl.BlockSpec(memory_space=pltpu.VMEM)


def anywhere():
    return pl.BlockSpec(memory_space=pl.ANY)


def keep_hbm(x):
    return pltpu.with_memory_space_constraint(x, pltpu.HBM)


def keep_vmem(x):
    return pltpu.with_memory_space_constraint(x, pltpu.VMEM)


def row_to_lanes(row):
    return jnp.transpose(jnp.broadcast_to(row, (LANES, LANES)))


def split_heads(flat_ref, wide_ref):
    wide_ref[...] = flat_ref[...].astype(F32)


def head_rows(wide_ref, head, heads):
    if heads == 1:
        return wide_ref[...]
    return wide_ref[pl.Slice(head, wide_ref.shape[0] // heads, heads), :]


def count_below(all_ref, own_row, count):
    tokens = own_row.shape[1]
    mine = jnp.broadcast_to(own_row, (8, tokens))
    wide = 4 * LANES

    def step(i, total):
        row = all_ref[0, :, pl.ds(pl.multiple_of(i * wide, wide), wide)]
        for s in range(0, wide, LANES):
            column = row_to_lanes(row[:, s : s + LANES])
            for r in range(0, LANES, 8):
                other = jnp.tile(column[r : r + 8], (1, tokens // LANES))
                total += (other < mine).astype(jnp.int32)
        return total

    total = lax.fori_loop(0, count // wide, step, jnp.zeros((8, tokens), jnp.int32))
    return jnp.sum(total, axis=0, keepdims=True)


def one_hot_rows(size, spot):
    slots = lax.broadcasted_iota(jnp.int16, (size, spot.shape[1]), 0)
    return jnp.where(
        slots == spot.astype(jnp.int16), jnp.ones((), BF16), jnp.zeros((), BF16)
    )


def sort_kernel(label_hbm, keys_hbm, *refs):
    out_keys, out_labels, out_spots, flat_ref, wide_ref, rows_ref, order_ref, label_ref, sems = refs
    head = pl.program_id(0)
    _, tokens, width = out_keys.shape
    copy = pltpu.make_async_copy(keys_hbm, flat_ref, sems.at[0])

    @pl.when(head == 0)
    def _():
        label_copy = pltpu.make_async_copy(label_hbm, label_ref, sems.at[1])
        label_copy.start()
        copy.start()
        label_copy.wait()

    label = label_ref[pl.ds(head, 1), :]
    order = label * tokens + lax.broadcasted_iota(jnp.int32, label.shape, 1)
    order_ref[0] = order
    spot = count_below(order_ref, order, tokens)
    out_spots[head] = spot

    @pl.when(head == 0)
    def _():
        copy.wait()
        split_heads(flat_ref, wide_ref)

    rows_ref[...] = head_rows(wide_ref, head, wide_ref.shape[0] // tokens).astype(BF16)
    digits = jnp.concatenate(
        [
            jnp.broadcast_to(label >> 6, (8, tokens)),
            jnp.broadcast_to(label & 63, (8, tokens)),
        ],
        axis=0,
    )
    digits = digits.astype(F32).astype(BF16)
    rows = 512
    for r in range(0, tokens, rows):
        pick = one_hot_rows(rows, spot - r)
        out_keys[head, r : r + rows] = dot_nn(pick, rows_ref[...]).astype(BF16)
        digit = dot_nt(digits, pick)
        out_labels[head, :, r : r + rows] = digit[0:1] * 64.0 + digit[8:9]


def sort_keys(labels, keys):
    heads, tokens = labels.shape
    flat, width = keys.shape
    return pl.pallas_call(
        sort_kernel,
        grid=(heads,),
        in_specs=[anywhere()] * 2,
        out_specs=(in_vmem(),) * 3,
        out_shape=(
            pltpu.VMEM((heads, tokens, width), BF16),
            pltpu.VMEM((heads, 1, tokens), F32),
            pltpu.VMEM((heads, 1, tokens), jnp.int32),
        ),
        scratch_shapes=[
            pltpu.VMEM((flat, width), BF16),
            pltpu.VMEM((flat, width), F32),
            pltpu.VMEM((tokens, width), BF16),
            pltpu.VMEM((1, 1, tokens), jnp.int32),
            pltpu.VMEM(labels.shape, jnp.int32),
            pltpu.SemaphoreType.DMA((2,)),
        ],
        compiler_params=params(),
        name="sort_keys",
    )(keep_hbm(labels), keep_hbm(keys))


def values_kernel(spot_ref, values_hbm, out_ref, flat_ref, wide_ref, sem):
    heads, _, tokens = spot_ref.shape
    copy = pltpu.make_async_copy(values_hbm, flat_ref, sem)
    copy.start()
    copy.wait()
    split_heads(flat_ref, wide_ref)
    rows = 512
    for h in range(heads):
        values = head_rows(wide_ref, h, heads).astype(BF16)
        for r in range(0, tokens, rows):
            pick = one_hot_rows(rows, spot_ref[h] - r)
            out_ref[h, r : r + rows] = dot_nn(pick, values).astype(BF16)


def sort_values(spots, values):
    heads, _, tokens = spots.shape
    flat, width = values.shape
    return pl.pallas_call(
        values_kernel,
        in_specs=[in_vmem(), anywhere()],
        out_specs=in_vmem(),
        out_shape=pltpu.VMEM((heads, tokens, width), BF16),
        scratch_shapes=[
            pltpu.VMEM((flat, width), BF16),
            pltpu.VMEM((flat, width), F32),
            pltpu.SemaphoreType.DMA,
        ],
        compiler_params=params(),
        name="sort_values",
    )(keep_vmem(spots), keep_hbm(values))


def windows_kernel(size, start_ref, rank_ref, values_ref, _, *out_refs):
    heads, tokens, _ = values_ref.shape
    for h in range(heads):
        rank = rank_ref[h].astype(jnp.int32)
        digits = [
            digit[:, t : t + LANES]
            for digit in (rank >> 7, rank & 127)
            for t in range(0, tokens, LANES)
        ]
        digits = jnp.concatenate(digits, axis=0).astype(F32).astype(BF16)
        for m, out_ref in enumerate(out_refs):
            start = pl.multiple_of(start_ref[h, m], 16)
            out_ref[h, :size] = values_ref[h, pl.ds(start, size), :]
            out_ref[h, size:] = digits


def windows(starts, ranks, values, size, after):
    heads, tokens, width = values.shape
    n = starts.shape[1]
    out = pltpu.VMEM((heads, size + 2 * tokens // LANES, width), BF16)
    return pl.pallas_call(
        functools.partial(windows_kernel, size),
        in_specs=[pl.BlockSpec(memory_space=pltpu.SMEM), in_vmem(), in_vmem(), in_vmem()],
        out_specs=(in_vmem(),) * n,
        out_shape=(out,) * n,
        compiler_params=params(),
        name="windows",
    )(starts, ranks, keep_vmem(values), keep_vmem(after))


def rank_kernel(me_ref, label_ref, rank_ref):
    n, tokens = label_ref.shape[1:]
    me = me_ref[0]
    own = label_ref[0, 0:1, :].astype(jnp.int32)
    rank = lax.broadcasted_iota(jnp.int32, own.shape, 1)
    for m in range(1, n):
        bar = own + ((me ^ m) < me).astype(jnp.int32)
        bar = jnp.broadcast_to(bar, (16, tokens)).astype(jnp.int16)
        count = jnp.zeros((16, tokens), BF16)
        for s in range(0, tokens, LANES):
            column = row_to_lanes(label_ref[0, m : m + 1, s : s + LANES])
            column = column.astype(jnp.int32).astype(jnp.int16)
            for r in range(0, LANES, 16):
                other = jnp.tile(column[r : r + 16], (1, tokens // LANES))
                count += jnp.where(other < bar, jnp.ones((), BF16), jnp.zeros((), BF16))
        rank += jnp.sum(count.astype(F32), axis=0, keepdims=True).astype(jnp.int32)
    rank_ref[0] = rank.astype(F32)


def own_ranks(me, labels):
    heads, n, tokens = labels.shape
    return pl.pallas_call(
        rank_kernel,
        grid=(heads,),
        in_specs=[
            pl.BlockSpec(memory_space=pltpu.SMEM),
            pl.BlockSpec((1, n, tokens), lambda h: (h, 0, 0)),
        ],
        out_specs=pl.BlockSpec((1, 1, tokens), lambda h: (h, 0, 0)),
        out_shape=jax.ShapeDtypeStruct((heads, 1, tokens), F32),
        compiler_params=params(),
        name="own_ranks",
    )(me, labels)


def totals_kernel(keys_ref, cent_ref, _, tot_ref, unit_ref, sum_ref):
    step = pl.program_id(1)
    tokens = unit_ref.shape[0]

    @pl.when(step == 0)
    def _():
        unit_ref[...] = unit_rows(keys_ref[pl.program_id(0)].astype(F32)).astype(BF16)
        sum_ref[...] = jnp.zeros_like(sum_ref)

    part = 256
    rows = min(1024, cent_ref.shape[1])
    for c in range(0, cent_ref.shape[1], rows):
        cent = unit_rows(cent_ref[0, c : c + rows]).astype(BF16)
        for t in range(0, tokens, part):
            raw = jnp.exp2(dot_nt(cent, unit_ref[t : t + part, :]) * EXP2_SCALE)
            sum_ref[:, t : t + part] += jnp.sum(raw.reshape(-1, 8, part), axis=0)

    @pl.when(step == pl.num_programs(1) - 1)
    def _():
        tot_ref[0] = jnp.sum(sum_ref[...], axis=0, keepdims=True)


def own_totals(keys, cents, after):
    heads, count, width = cents.shape
    tokens = keys.shape[1]
    rows = min(2048, count)
    return pl.pallas_call(
        totals_kernel,
        grid=(heads, count // rows),
        in_specs=[
            in_vmem(),
            pl.BlockSpec((1, rows, width), lambda h, c: (h, c, 0)),
            in_vmem(),
        ],
        out_specs=pl.BlockSpec((1, 1, tokens), lambda h, c: (h, 0, 0)),
        out_shape=jax.ShapeDtypeStruct((heads, 1, tokens), F32),
        scratch_shapes=[
            pltpu.VMEM((tokens, width), BF16),
            pltpu.VMEM((8, tokens), F32),
        ],
        compiler_params=params(),
        name="own_totals",
    )(keep_vmem(keys), keep_hbm(cents), after)


def scale_rows(unit, inverse, scaled_ref):
    for t in range(0, unit.shape[0], LANES):
        scaled_ref[t : t + LANES] = (
            unit[t : t + LANES, :].astype(F32) * row_to_lanes(inverse[:, t : t + LANES])
        ).astype(BF16)


def first_kernel(fresh, _, keys_ref, tot_ref, cent_in, *refs):
    head = pl.program_id(0)
    if fresh:
        sums_ref, unit_ref, cent_ref, scaled_ref = refs
        cent = unit_rows(cent_in[0]).astype(BF16)
        cent_ref[head] = cent
    else:
        _, sums_ref, unit_ref, scaled_ref = refs
        cent = cent_in[head]
    unit = unit_rows(keys_ref[head].astype(F32)).astype(BF16)
    unit_ref[head] = unit
    scale_rows(unit, 1.0 / tot_ref[0], scaled_ref)
    part = 256
    for t in range(0, unit.shape[0], part):
        raw = jnp.exp2(dot_nt(cent, unit[t : t + part, :]) * EXP2_SCALE)
        more = dot_nn(raw.astype(BF16), scaled_ref[t : t + part])
        if fresh and t == 0:
            sums_ref[head] = more
        else:
            sums_ref[head] += more


def first_block(me, keys, totals, cents, n, before):
    heads, tokens, width = keys.shape
    fresh = before is None
    rows = cents.shape[1] // n if fresh else cents.shape[1]
    in_specs = [
        in_vmem(),
        pl.BlockSpec((1, 1, tokens), lambda h, me: (h, 0, 0)),
    ]
    args = [me, keep_vmem(keys), totals]
    out_shape = [
        pltpu.VMEM((heads, rows, width), F32),
        pltpu.VMEM((heads, tokens, width), BF16),
    ]
    aliases = {}
    if fresh:
        in_specs.append(pl.BlockSpec((1, rows, width), lambda h, me: (h, me[0], 0)))
        args.append(keep_hbm(cents))
        out_shape.append(pltpu.VMEM((heads, rows, width), BF16))
    else:
        in_specs += [in_vmem(), in_vmem()]
        args += [keep_vmem(cents), keep_vmem(before)]
        aliases = {4: 0}
    return pl.pallas_call(
        functools.partial(first_kernel, fresh),
        grid_spec=pltpu.PrefetchScalarGridSpec(
            num_scalar_prefetch=1,
            grid=(heads,),
            in_specs=in_specs,
            out_specs=(in_vmem(),) * len(out_shape),
            scratch_shapes=[pltpu.VMEM((tokens, width), BF16)],
        ),
        out_shape=tuple(out_shape),
        input_output_aliases=aliases,
        compiler_params=params(),
        name="first_block",
    )(*args)


def raw_kernel(blocks, sums_ref, *refs):
    units = refs[:blocks]
    raw_ref, total_ref, cent_ref = refs[blocks:]
    head = pl.program_id(0)
    cent_ref[...] = unit_rows(sums_ref[head]).astype(BF16)
    part = 256
    start = 0
    for unit_ref in units:
        for t in range(0, unit_ref.shape[1], part):
            here = slice(start + t, start + t + part)
            raw = jnp.exp2(dot_nt(cent_ref[...], unit_ref[head, t : t + part, :]) * EXP2_SCALE)
            raw_ref[head, :, here] = raw.astype(BF16)
            total = jnp.sum(raw.reshape(-1, 8, part), axis=0)
            total_ref[0, :, here] = jnp.sum(total, axis=0, keepdims=True)
        start += unit_ref.shape[1]


def raw_weights(sums, units):
    heads, rows, width = sums.shape
    tokens = units[0].shape[1]
    count = tokens * len(units)
    return pl.pallas_call(
        functools.partial(raw_kernel, len(units)),
        grid=(heads,),
        in_specs=[in_vmem()] * (1 + len(units)),
        out_specs=(in_vmem(), pl.BlockSpec((1, 1, count), lambda h: (h, 0, 0))),
        out_shape=(
            pltpu.VMEM((heads, rows, count), BF16),
            jax.ShapeDtypeStruct((heads, 1, count), F32),
        ),
        scratch_shapes=[pltpu.VMEM((rows, width), BF16)],
        compiler_params=params(),
        name="raw_weights",
    )(keep_vmem(sums), *map(keep_vmem, units))


def sums_kernel(blocks, raw_ref, *refs):
    totals, units = refs[:blocks], refs[blocks : 2 * blocks]
    out_hbm, scaled_ref, result_ref, sems = refs[2 * blocks :]
    heads, tokens, _ = units[0].shape
    copies = []
    for h in range(heads):
        for m, unit_ref in enumerate(units):
            row_total = totals[0][h, :, m * tokens : (m + 1) * tokens]
            for d in range(1, blocks):
                peer = m ^ d
                row_total += totals[d][h, :, peer * tokens : (peer + 1) * tokens]
            here = slice(m * tokens, (m + 1) * tokens)
            scale_rows(unit_ref[h], 1.0 / row_total, scaled_ref.at[h, here])
        result_ref[h] = unit_rows(dot_nn(raw_ref[h], scaled_ref[h]))
        copies.append(pltpu.make_async_copy(result_ref.at[h], out_hbm.at[h], sems.at[h]))
        copies[-1].start()
    for copy in copies:
        copy.wait()


def weighted_sums(raw, units, totals):
    heads, rows, count = raw.shape
    width = units[0].shape[2]
    return pl.pallas_call(
        functools.partial(sums_kernel, len(units)),
        in_specs=[in_vmem()] * (1 + 2 * len(units)),
        out_specs=anywhere(),
        out_shape=jax.ShapeDtypeStruct((heads, rows, width), F32),
        scratch_shapes=[
            pltpu.VMEM((heads, count, width), BF16),
            pltpu.VMEM((heads, rows, width), F32),
            pltpu.SemaphoreType.DMA((heads,)),
        ],
        compiler_params=params(),
        name="weighted_sums",
    )(keep_vmem(raw), *map(keep_vmem, totals), *map(keep_vmem, units))


def place_kernel(blocks, size, scalar_ref, label_ref, _, *refs):
    keys, values, refs = refs[:blocks], refs[blocks : 2 * blocks], refs[2 * blocks :]
    *out_hbm, rows_ref, near_ref, mixed_ref, done_ref, sems = refs
    heads, tokens, width = keys[0].shape
    digit_rows = tokens // LANES
    sent = values[0].shape[1] - 2 * digit_rows
    rows_ref[:, :, width:] = jnp.zeros((heads, blocks * size, width), BF16)
    for h in range(heads):
        low, high, first = (scalar_ref[i, h, 0].astype(F32) for i in range(2, 5))
        for m in range(blocks):
            start = pl.multiple_of(scalar_ref[0, h, m], 16)
            gap = pl.multiple_of(scalar_ref[1, h, m], 16)
            here = m * size
            rows_ref[h, here : here + size, :width] = keys[m][h, pl.ds(start, size), :]
            rows_ref[h, pl.ds(here + gap, sent), width:] = values[m][h, :sent, :]
            digits = values[m][h, sent:, :].astype(F32)
            rank = digits[:digit_rows] * 128.0 + digits[digit_rows:]
            rank = jnp.concatenate([rank[r : r + 1] for r in range(digit_rows)], axis=1)
            label = label_ref[h, m : m + 1, :]
            mine = (label >= low) & (label < high)
            spot = jnp.where(mine, rank - first, -1.0).astype(jnp.int32)
            spot = pltpu.roll(spot, lax.rem(tokens - start, tokens), 1)
            near_ref[h, :, here : here + size] = spot[:, :size]

    rows = mixed_ref.shape[1] // heads
    copies = []
    for step in range(out_hbm[0].shape[0] // (rows * heads)):
        for h in range(heads):
            pick = one_hot_rows(rows, near_ref[h] - step * rows)
            total = dot_nn(pick, rows_ref[h])
            for side in range(2):
                mixed_ref[side, pl.Slice(h, rows, heads), :] = total[
                    :, side * width : (side + 1) * width
                ]
        here = slice(step * rows * heads, (step + 1) * rows * heads)
        for side in range(2):
            done_ref[side, here] = mixed_ref[side].astype(BF16)
            copies.append(
                pltpu.make_async_copy(
                    done_ref.at[side, here], out_hbm[side].at[here], sems.at[len(copies)]
                )
            )
            copies[-1].start()
    for copy in copies:
        copy.wait()


def place(scalars, labels, keys, values, size, cap, after):
    blocks = len(keys)
    heads, _, width = keys[0].shape
    rows = 512
    out = jax.ShapeDtypeStruct((heads * cap, width), BF16)
    return pl.pallas_call(
        functools.partial(place_kernel, blocks, size),
        in_specs=[pl.BlockSpec(memory_space=pltpu.SMEM), in_vmem(), anywhere()]
        + [in_vmem()] * (2 * blocks),
        out_specs=(anywhere(), anywhere()),
        out_shape=(out, out),
        scratch_shapes=[
            pltpu.VMEM((heads, blocks * size, 2 * width), BF16),
            pltpu.VMEM((heads, 1, blocks * size), jnp.int32),
            pltpu.VMEM((2, heads * rows, width), F32),
            pltpu.VMEM((2, heads * cap, width), BF16),
            pltpu.SemaphoreType.DMA((2 * cap // rows,)),
        ],
        compiler_params=params(),
        name="place",
    )(scalars, labels, keep_hbm(after), *(keep_vmem(x) for x in (*keys, *values)))


def body(key_rows, value_rows, cluster_labels, owner_bounds, init_centroids):
    n = lax.axis_size("ctx")
    me = lax.axis_index("ctx").astype(jnp.int32)
    tokens, heads, width = key_rows.shape
    cap = 2 * tokens
    slot = cap // n
    send_size = slot + 16
    key_size = min(tokens, -(-send_size // LANES) * LANES)

    def swap(x, d):
        return lax.ppermute(x, "ctx", [(i, i ^ d) for i in range(n)])

    def spread(x):
        return [x] + [swap(x, d) for d in range(1, n)]

    def aligned(start, size):
        return jnp.minimum(start // 16 * 16, tokens - size)

    me_array = me.reshape(1)
    own_keys, own_labels, own_spots = sort_keys(
        cluster_labels, key_rows.reshape(heads * tokens, width)
    )
    keys = {0: own_keys}
    d = 1
    while d < n:
        keys[d] = swap(own_keys, d)
        d *= 2
    pairs = [(i, i ^ 1) for i in range(lax.axis_size("head"))]
    word = lax.ppermute(own_labels[:, :, :LANES], "head", pairs)
    own_total = own_totals(own_keys, init_centroids, word)
    shared = spread(jnp.concatenate([own_total, own_labels], axis=1))
    totals = [own_total] + [x[:, 0:1] for x in shared[1:]]

    sums, unit, cents = first_block(me_array, own_keys, own_total, init_centroids, n, None)
    units = [unit]
    *came, sums = lax.optimization_barrier((*keys.values(), sums))
    keys = dict(zip(keys, came))
    for m in range(1, n):
        if m not in keys:
            keys[m] = swap(keys[m & (m - 1)], m & -m)
    keys = [keys[m] for m in range(n)]
    peer_low = jnp.take(owner_bounds, me ^ jnp.arange(n, dtype=jnp.int32), axis=1)
    own_below = jnp.sum((own_labels < peer_low[:, :, None]).astype(jnp.int32), axis=2)
    own_values = sort_values(own_spots, value_rows.reshape(heads * tokens, width))

    labels = jnp.concatenate([x[:, -1:] for x in shared], axis=1)
    ranks = own_ranks(me_array, labels)
    low = lax.dynamic_slice_in_dim(owner_bounds, me, 1, 1)
    high = lax.dynamic_slice_in_dim(owner_bounds, me + 1, 1, 1)
    below = jnp.sum((labels < low[:, :, None]).astype(jnp.int32), axis=2)
    first = jnp.sum(below, axis=1, keepdims=True)
    key_starts = aligned(below, key_size)
    gaps = aligned(below, send_size) - key_starts
    one = jnp.ones((1, n), jnp.int32)
    scalars = jnp.stack([key_starts, gaps, low * one, high * one, first * one])

    starts = aligned(own_below, send_size)
    own_windows = windows(starts, ranks, own_values, send_size, own_labels)
    middle = [2]
    far = [d for d in range(1, n) if d & (d - 1)]
    near = [1] + [d for d in range(3, n) if not d & (d - 1)]
    values = {0: own_windows[0]}
    for m in range(1, n):
        group = {1: far, 2: near, 3: middle}.get(m)
        if group:
            *leaving, sums = lax.optimization_barrier((*(own_windows[d] for d in group), sums))
            for d, window in zip(group, leaving):
                values[d] = swap(window, d)
        sums, unit = first_block(me_array, keys[m], totals[m], cents, n, sums)
        units.append(unit)

    raw, part = raw_weights(sums, units)
    parts = spread(part)
    out = weighted_sums(raw, units, parts)
    values = [values[m] for m in range(n)]
    placed = place(scalars, labels, keys, values, key_size, cap, out)
    shape = (cap, heads, width)
    return out, placed[0].reshape(shape), placed[1].reshape(shape)


def solution(mesh):
    placed = (
        P(("grp", "ctx"), "head", None),
        P(("grp", "ctx"), "head", None),
        P("head", ("grp", "ctx")),
        P(("grp", "head"), None),
        P(("grp", "head"), None, None),
    )
    return jax.shard_map(
        body,
        mesh=mesh,
        in_specs=placed,
        out_specs=(
            P(("grp", "head"), "ctx", None),
            P(("grp", "ctx"), "head", None),
            P(("grp", "ctx"), "head", None),
        ),
        check_vma=False,
    )
```

```python
import functools
import math

import jax
import jax.numpy as jnp
from jax import lax
from jax.experimental import pallas as pl
from jax.experimental.pallas import tpu as pltpu
from jax.sharding import PartitionSpec as P

LANES = 128
EXP2_SCALE = 20.0 * math.log2(math.e)
VMEM_LIMIT = 16 * 1024 * 1024
F32 = jnp.float32
BF16 = jnp.bfloat16
NT = (((1,), (1,)), ((), ()))
NN = (((1,), (0,)), ((), ()))


def dot_nt(a, b):
    return lax.dot_general(a, b, NT, preferred_element_type=F32)


def dot_nn(a, b):
    return lax.dot_general(a, b, NN, preferred_element_type=F32)


def unit_rows(x):
    return x * lax.rsqrt(jnp.sum(x * x, axis=-1, keepdims=True) + 1e-06)


def params(**kwargs):
    return pltpu.CompilerParams(vmem_limit_bytes=VMEM_LIMIT, **kwargs)


def whole(shape):
    return pl.BlockSpec(shape, lambda *_: (0,) * len(shape))


def in_vmem():
    return pl.BlockSpec(memory_space=pltpu.VMEM)


def anywhere():
    return pl.BlockSpec(memory_space=pl.ANY)


def keep_hbm(x):
    return pltpu.with_memory_space_constraint(x, pltpu.HBM)


def keep_vmem(x):
    return pltpu.with_memory_space_constraint(x, pltpu.VMEM)


def row_to_lanes(row):
    return jnp.transpose(jnp.broadcast_to(row, (LANES, LANES)))


def split_heads(flat_ref, wide_ref):
    wide_ref[...] = flat_ref[...].astype(F32)


def head_rows(wide_ref, head, heads):
    if heads == 1:
        return wide_ref[...]
    return wide_ref[pl.Slice(head, wide_ref.shape[0] // heads, heads), :]


def count_below(all_ref, own_row, count):
    tokens = own_row.shape[1]
    mine = jnp.broadcast_to(own_row, (8, tokens))
    wide = 4 * LANES

    def step(i, total):
        row = all_ref[0, :, pl.ds(pl.multiple_of(i * wide, wide), wide)]
        for s in range(0, wide, LANES):
            column = row_to_lanes(row[:, s : s + LANES])
            for r in range(0, LANES, 8):
                other = jnp.tile(column[r : r + 8], (1, tokens // LANES))
                total += (other < mine).astype(jnp.int32)
        return total

    total = lax.fori_loop(0, count // wide, step, jnp.zeros((8, tokens), jnp.int32))
    return jnp.sum(total, axis=0, keepdims=True)


def one_hot_rows(size, spot):
    slots = lax.broadcasted_iota(jnp.int16, (size, spot.shape[1]), 0)
    return jnp.where(
        slots == spot.astype(jnp.int16), jnp.ones((), BF16), jnp.zeros((), BF16)
    )


def sort_kernel(label_hbm, keys_hbm, *refs):
    out_keys, out_labels, out_spots, flat_ref, wide_ref, rows_ref, order_ref, label_ref, sems = refs
    head = pl.program_id(0)
    _, tokens, width = out_keys.shape
    copy = pltpu.make_async_copy(keys_hbm, flat_ref, sems.at[0])

    @pl.when(head == 0)
    def _():
        label_copy = pltpu.make_async_copy(label_hbm, label_ref, sems.at[1])
        label_copy.start()
        copy.start()
        label_copy.wait()

    label = label_ref[pl.ds(head, 1), :]
    order = label * tokens + lax.broadcasted_iota(jnp.int32, label.shape, 1)
    order_ref[0] = order
    spot = count_below(order_ref, order, tokens)
    out_spots[head] = spot

    @pl.when(head == 0)
    def _():
        copy.wait()
        split_heads(flat_ref, wide_ref)

    rows_ref[...] = head_rows(wide_ref, head, wide_ref.shape[0] // tokens).astype(BF16)
    digits = jnp.concatenate(
        [
            jnp.broadcast_to(label >> 6, (8, tokens)),
            jnp.broadcast_to(label & 63, (8, tokens)),
        ],
        axis=0,
    )
    digits = digits.astype(F32).astype(BF16)
    rows = 512
    for r in range(0, tokens, rows):
        pick = one_hot_rows(rows, spot - r)
        out_keys[head, r : r + rows] = dot_nn(pick, rows_ref[...]).astype(BF16)
        digit = dot_nt(digits, pick)
        out_labels[head, :, r : r + rows] = digit[0:1] * 64.0 + digit[8:9]


def sort_keys(labels, keys):
    heads, tokens = labels.shape
    flat, width = keys.shape
    return pl.pallas_call(
        sort_kernel,
        grid=(heads,),
        in_specs=[anywhere()] * 2,
        out_specs=(in_vmem(),) * 3,
        out_shape=(
            pltpu.VMEM((heads, tokens, width), BF16),
            pltpu.VMEM((heads, 1, tokens), F32),
            pltpu.VMEM((heads, 1, tokens), jnp.int32),
        ),
        scratch_shapes=[
            pltpu.VMEM((flat, width), BF16),
            pltpu.VMEM((flat, width), F32),
            pltpu.VMEM((tokens, width), BF16),
            pltpu.VMEM((1, 1, tokens), jnp.int32),
            pltpu.VMEM(labels.shape, jnp.int32),
            pltpu.SemaphoreType.DMA((2,)),
        ],
        compiler_params=params(),
        name="sort_keys",
    )(keep_hbm(labels), keep_hbm(keys))


def values_kernel(spot_ref, values_hbm, out_ref, flat_ref, wide_ref, sem):
    heads, _, tokens = spot_ref.shape
    copy = pltpu.make_async_copy(values_hbm, flat_ref, sem)
    copy.start()
    copy.wait()
    split_heads(flat_ref, wide_ref)
    rows = 512
    for h in range(heads):
        values = head_rows(wide_ref, h, heads).astype(BF16)
        for r in range(0, tokens, rows):
            pick = one_hot_rows(rows, spot_ref[h] - r)
            out_ref[h, r : r + rows] = dot_nn(pick, values).astype(BF16)


def sort_values(spots, values):
    heads, _, tokens = spots.shape
    flat, width = values.shape
    return pl.pallas_call(
        values_kernel,
        in_specs=[in_vmem(), anywhere()],
        out_specs=in_vmem(),
        out_shape=pltpu.VMEM((heads, tokens, width), BF16),
        scratch_shapes=[
            pltpu.VMEM((flat, width), BF16),
            pltpu.VMEM((flat, width), F32),
            pltpu.SemaphoreType.DMA,
        ],
        compiler_params=params(),
        name="sort_values",
    )(keep_vmem(spots), keep_hbm(values))


def windows_kernel(size, start_ref, rank_ref, values_ref, _, *out_refs):
    heads, tokens, _ = values_ref.shape
    for h in range(heads):
        rank = rank_ref[h].astype(jnp.int32)
        digits = [
            digit[:, t : t + LANES]
            for digit in (rank >> 7, rank & 127)
            for t in range(0, tokens, LANES)
        ]
        digits = jnp.concatenate(digits, axis=0).astype(F32).astype(BF16)
        for m, out_ref in enumerate(out_refs):
            start = pl.multiple_of(start_ref[h, m], 16)
            out_ref[h, :size] = values_ref[h, pl.ds(start, size), :]
            out_ref[h, size:] = digits


def windows(starts, ranks, values, size, after):
    heads, tokens, width = values.shape
    n = starts.shape[1]
    out = pltpu.VMEM((heads, size + 2 * tokens // LANES, width), BF16)
    return pl.pallas_call(
        functools.partial(windows_kernel, size),
        in_specs=[pl.BlockSpec(memory_space=pltpu.SMEM), in_vmem(), in_vmem(), in_vmem()],
        out_specs=(in_vmem(),) * n,
        out_shape=(out,) * n,
        compiler_params=params(),
        name="windows",
    )(starts, ranks, keep_vmem(values), keep_vmem(after))


def rank_kernel(me_ref, label_ref, rank_ref):
    n, tokens = label_ref.shape[1:]
    me = me_ref[0]
    own = label_ref[0, 0:1, :].astype(jnp.int32)
    rank = lax.broadcasted_iota(jnp.int32, own.shape, 1)
    for m in range(1, n):
        bar = own + ((me ^ m) < me).astype(jnp.int32)
        bar = jnp.broadcast_to(bar, (16, tokens)).astype(jnp.int16)
        count = jnp.zeros((16, tokens), BF16)
        for s in range(0, tokens, LANES):
            column = row_to_lanes(label_ref[0, m : m + 1, s : s + LANES])
            column = column.astype(jnp.int32).astype(jnp.int16)
            for r in range(0, LANES, 16):
                other = jnp.tile(column[r : r + 16], (1, tokens // LANES))
                count += jnp.where(other < bar, jnp.ones((), BF16), jnp.zeros((), BF16))
        rank += jnp.sum(count.astype(F32), axis=0, keepdims=True).astype(jnp.int32)
    rank_ref[0] = rank.astype(F32)


def own_ranks(me, labels):
    heads, n, tokens = labels.shape
    return pl.pallas_call(
        rank_kernel,
        grid=(heads,),
        in_specs=[
            pl.BlockSpec(memory_space=pltpu.SMEM),
            pl.BlockSpec((1, n, tokens), lambda h: (h, 0, 0)),
        ],
        out_specs=pl.BlockSpec((1, 1, tokens), lambda h: (h, 0, 0)),
        out_shape=jax.ShapeDtypeStruct((heads, 1, tokens), F32),
        compiler_params=params(),
        name="own_ranks",
    )(me, labels)


def totals_kernel(keys_ref, cent_ref, _, tot_ref, unit_ref, sum_ref):
    step = pl.program_id(1)
    tokens = unit_ref.shape[0]

    @pl.when(step == 0)
    def _():
        unit_ref[...] = unit_rows(keys_ref[pl.program_id(0)].astype(F32)).astype(BF16)
        sum_ref[...] = jnp.zeros_like(sum_ref)

    part = 256
    rows = min(1024, cent_ref.shape[1])
    for c in range(0, cent_ref.shape[1], rows):
        cent = unit_rows(cent_ref[0, c : c + rows]).astype(BF16)
        for t in range(0, tokens, part):
            raw = jnp.exp2(dot_nt(cent, unit_ref[t : t + part, :]) * EXP2_SCALE)
            sum_ref[:, t : t + part] += jnp.sum(raw.reshape(-1, 8, part), axis=0)

    @pl.when(step == pl.num_programs(1) - 1)
    def _():
        tot_ref[0] = jnp.sum(sum_ref[...], axis=0, keepdims=True)


def own_totals(keys, cents, after):
    heads, count, width = cents.shape
    tokens = keys.shape[1]
    rows = min(2048, count)
    return pl.pallas_call(
        totals_kernel,
        grid=(heads, count // rows),
        in_specs=[
            in_vmem(),
            pl.BlockSpec((1, rows, width), lambda h, c: (h, c, 0)),
            in_vmem(),
        ],
        out_specs=pl.BlockSpec((1, 1, tokens), lambda h, c: (h, 0, 0)),
        out_shape=jax.ShapeDtypeStruct((heads, 1, tokens), F32),
        scratch_shapes=[
            pltpu.VMEM((tokens, width), BF16),
            pltpu.VMEM((8, tokens), F32),
        ],
        compiler_params=params(),
        name="own_totals",
    )(keep_vmem(keys), keep_hbm(cents), after)


def scale_rows(unit, inverse, scaled_ref):
    for t in range(0, unit.shape[0], LANES):
        scaled_ref[t : t + LANES] = (
            unit[t : t + LANES, :].astype(F32) * row_to_lanes(inverse[:, t : t + LANES])
        ).astype(BF16)


def first_kernel(fresh, _, keys_ref, tot_ref, cent_in, *refs):
    head = pl.program_id(0)
    if fresh:
        sums_ref, unit_ref, cent_ref, scaled_ref = refs
        cent = unit_rows(cent_in[0]).astype(BF16)
        cent_ref[head] = cent
    else:
        _, sums_ref, unit_ref, scaled_ref = refs
        cent = cent_in[head]
    unit = unit_rows(keys_ref[head].astype(F32)).astype(BF16)
    unit_ref[head] = unit
    scale_rows(unit, 1.0 / tot_ref[0], scaled_ref)
    part = 256
    for t in range(0, unit.shape[0], part):
        raw = jnp.exp2(dot_nt(cent, unit[t : t + part, :]) * EXP2_SCALE)
        more = dot_nn(raw.astype(BF16), scaled_ref[t : t + part])
        if fresh and t == 0:
            sums_ref[head] = more
        else:
            sums_ref[head] += more


def first_block(me, keys, totals, cents, n, before):
    heads, tokens, width = keys.shape
    fresh = before is None
    rows = cents.shape[1] // n if fresh else cents.shape[1]
    in_specs = [
        in_vmem(),
        pl.BlockSpec((1, 1, tokens), lambda h, me: (h, 0, 0)),
    ]
    args = [me, keep_vmem(keys), totals]
    out_shape = [
        pltpu.VMEM((heads, rows, width), F32),
        pltpu.VMEM((heads, tokens, width), BF16),
    ]
    aliases = {}
    if fresh:
        in_specs.append(pl.BlockSpec((1, rows, width), lambda h, me: (h, me[0], 0)))
        args.append(keep_hbm(cents))
        out_shape.append(pltpu.VMEM((heads, rows, width), BF16))
    else:
        in_specs += [in_vmem(), in_vmem()]
        args += [keep_vmem(cents), keep_vmem(before)]
        aliases = {4: 0}
    return pl.pallas_call(
        functools.partial(first_kernel, fresh),
        grid_spec=pltpu.PrefetchScalarGridSpec(
            num_scalar_prefetch=1,
            grid=(heads,),
            in_specs=in_specs,
            out_specs=(in_vmem(),) * len(out_shape),
            scratch_shapes=[pltpu.VMEM((tokens, width), BF16)],
        ),
        out_shape=tuple(out_shape),
        input_output_aliases=aliases,
        compiler_params=params(),
        name="first_block",
    )(*args)


def raw_kernel(blocks, sums_ref, *refs):
    units = refs[:blocks]
    raw_ref, total_ref, cent_ref = refs[blocks:]
    head = pl.program_id(0)
    cent_ref[...] = unit_rows(sums_ref[head]).astype(BF16)
    part = 256
    start = 0
    for unit_ref in units:
        for t in range(0, unit_ref.shape[1], part):
            here = slice(start + t, start + t + part)
            raw = jnp.exp2(dot_nt(cent_ref[...], unit_ref[head, t : t + part, :]) * EXP2_SCALE)
            raw_ref[head, :, here] = raw.astype(BF16)
            total = jnp.sum(raw.reshape(-1, 8, part), axis=0)
            total_ref[0, :, here] = jnp.sum(total, axis=0, keepdims=True)
        start += unit_ref.shape[1]


def raw_weights(sums, units):
    heads, rows, width = sums.shape
    tokens = units[0].shape[1]
    count = tokens * len(units)
    return pl.pallas_call(
        functools.partial(raw_kernel, len(units)),
        grid=(heads,),
        in_specs=[in_vmem()] * (1 + len(units)),
        out_specs=(in_vmem(), pl.BlockSpec((1, 1, count), lambda h: (h, 0, 0))),
        out_shape=(
            pltpu.VMEM((heads, rows, count), BF16),
            jax.ShapeDtypeStruct((heads, 1, count), F32),
        ),
        scratch_shapes=[pltpu.VMEM((rows, width), BF16)],
        compiler_params=params(),
        name="raw_weights",
    )(keep_vmem(sums), *map(keep_vmem, units))


def sums_kernel(blocks, raw_ref, *refs):
    totals, units = refs[:blocks], refs[blocks : 2 * blocks]
    out_hbm, scaled_ref, result_ref, sems = refs[2 * blocks :]
    heads, tokens, _ = units[0].shape
    copies = []
    for h in range(heads):
        for m, unit_ref in enumerate(units):
            row_total = totals[0][h, :, m * tokens : (m + 1) * tokens]
            for d in range(1, blocks):
                peer = m ^ d
                row_total += totals[d][h, :, peer * tokens : (peer + 1) * tokens]
            here = slice(m * tokens, (m + 1) * tokens)
            scale_rows(unit_ref[h], 1.0 / row_total, scaled_ref.at[h, here])
        result_ref[h] = unit_rows(dot_nn(raw_ref[h], scaled_ref[h]))
        copies.append(pltpu.make_async_copy(result_ref.at[h], out_hbm.at[h], sems.at[h]))
        copies[-1].start()
    for copy in copies:
        copy.wait()


def weighted_sums(raw, units, totals):
    heads, rows, count = raw.shape
    width = units[0].shape[2]
    return pl.pallas_call(
        functools.partial(sums_kernel, len(units)),
        in_specs=[in_vmem()] * (1 + 2 * len(units)),
        out_specs=anywhere(),
        out_shape=jax.ShapeDtypeStruct((heads, rows, width), F32),
        scratch_shapes=[
            pltpu.VMEM((heads, count, width), BF16),
            pltpu.VMEM((heads, rows, width), F32),
            pltpu.SemaphoreType.DMA((heads,)),
        ],
        compiler_params=params(),
        name="weighted_sums",
    )(keep_vmem(raw), *map(keep_vmem, totals), *map(keep_vmem, units))


def fill_windows(ids, size, scalar_ref, label_ref, keys, values, rows_ref, near_ref):
    heads, tokens, width = keys[0].shape
    digit_rows = tokens // LANES
    sent = values[0].shape[1] - 2 * digit_rows
    rows_ref[:, :, width:] = jnp.zeros((heads, len(ids) * size, width), BF16)
    for h in range(heads):
        low, high, first = (scalar_ref[i, h, 0].astype(F32) for i in range(2, 5))
        for i, m in enumerate(ids):
            start = pl.multiple_of(scalar_ref[0, h, m], 16)
            gap = pl.multiple_of(scalar_ref[1, h, m], 16)
            here = i * size
            rows_ref[h, here : here + size, :width] = keys[i][h, pl.ds(start, size), :]
            rows_ref[h, pl.ds(here + gap, sent), width:] = values[i][h, :sent, :]
            digits = values[i][h, sent:, :].astype(F32)
            rank = digits[:digit_rows] * 128.0 + digits[digit_rows:]
            rank = jnp.concatenate([rank[r : r + 1] for r in range(digit_rows)], axis=1)
            label = label_ref[h, m : m + 1, :]
            mine = (label >= low) & (label < high)
            spot = jnp.where(mine, rank - first, -1.0).astype(jnp.int32)
            spot = pltpu.roll(spot, lax.rem(tokens - start, tokens), 1)
            near_ref[h, :, here : here + size] = spot[:, :size]


def collect_kernel(ids, size, scalar_ref, label_ref, *refs):
    count = len(ids)
    keys, values, (rows_ref, near_ref) = refs[:count], refs[count : 2 * count], refs[2 * count :]
    fill_windows(ids, size, scalar_ref, label_ref, keys, values, rows_ref, near_ref)


def collect(scalars, labels, keys, values, ids, size):
    heads, _, width = keys[0].shape
    moved = [x[m] for x in (keys, values) for m in ids]
    return pl.pallas_call(
        functools.partial(collect_kernel, ids, size),
        in_specs=[pl.BlockSpec(memory_space=pltpu.SMEM)] + [in_vmem()] * (1 + len(moved)),
        out_specs=(in_vmem(), in_vmem()),
        out_shape=(
            pltpu.VMEM((heads, len(ids) * size, 2 * width), BF16),
            pltpu.VMEM((heads, 1, len(ids) * size), jnp.int32),
        ),
        compiler_params=params(),
        name="collect",
    )(scalars, labels, *map(keep_vmem, moved))


def place_kernel(ids, size, scalar_ref, label_ref, most_ref, most_near_ref, _, *refs):
    count = len(ids)
    keys, values, refs = refs[:count], refs[count : 2 * count], refs[2 * count :]
    *out_hbm, rows_ref, near_ref, mixed_ref, done_ref, sems = refs
    fill_windows(ids, size, scalar_ref, label_ref, keys, values, rows_ref, near_ref)
    heads, _, width = keys[0].shape
    rows = mixed_ref.shape[1] // heads
    copies = []
    for step in range(out_hbm[0].shape[0] // (rows * heads)):
        for h in range(heads):
            pick = one_hot_rows(rows, most_near_ref[h] - step * rows)
            total = dot_nn(pick, most_ref[h])
            pick = one_hot_rows(rows, near_ref[h] - step * rows)
            total += dot_nn(pick, rows_ref[h])
            for side in range(2):
                mixed_ref[side, pl.Slice(h, rows, heads), :] = total[
                    :, side * width : (side + 1) * width
                ]
        here = slice(step * rows * heads, (step + 1) * rows * heads)
        for side in range(2):
            done_ref[side, here] = mixed_ref[side].astype(BF16)
            copies.append(
                pltpu.make_async_copy(
                    done_ref.at[side, here], out_hbm[side].at[here], sems.at[len(copies)]
                )
            )
            copies[-1].start()
    for copy in copies:
        copy.wait()


def place(scalars, labels, most, keys, values, ids, size, cap, after):
    heads, _, width = keys[0].shape
    rows = 512
    out = jax.ShapeDtypeStruct((heads * cap, width), BF16)
    moved = [x[m] for x in (keys, values) for m in ids]
    return pl.pallas_call(
        functools.partial(place_kernel, ids, size),
        in_specs=[pl.BlockSpec(memory_space=pltpu.SMEM)]
        + [in_vmem()] * 3
        + [anywhere()]
        + [in_vmem()] * len(moved),
        out_specs=(anywhere(), anywhere()),
        out_shape=(out, out),
        scratch_shapes=[
            pltpu.VMEM((heads, len(ids) * size, 2 * width), BF16),
            pltpu.VMEM((heads, 1, len(ids) * size), jnp.int32),
            pltpu.VMEM((2, heads * rows, width), F32),
            pltpu.VMEM((2, heads * cap, width), BF16),
            pltpu.SemaphoreType.DMA((2 * cap // rows,)),
        ],
        compiler_params=params(),
        name="place",
    )(scalars, labels, *map(keep_vmem, most), keep_hbm(after), *map(keep_vmem, moved))


def body(key_rows, value_rows, cluster_labels, owner_bounds, init_centroids):
    n = lax.axis_size("ctx")
    me = lax.axis_index("ctx").astype(jnp.int32)
    tokens, heads, width = key_rows.shape
    cap = 2 * tokens
    slot = cap // n
    send_size = slot + 16
    key_size = min(tokens, -(-send_size // LANES) * LANES)

    def swap(x, d):
        return lax.ppermute(x, "ctx", [(i, i ^ d) for i in range(n)])

    def spread(x):
        return [x] + [swap(x, d) for d in range(1, n)]

    def aligned(start, size):
        return jnp.minimum(start // 16 * 16, tokens - size)

    me_array = me.reshape(1)
    own_keys, own_labels, own_spots = sort_keys(
        cluster_labels, key_rows.reshape(heads * tokens, width)
    )
    keys = {0: own_keys}
    d = 1
    while d < n:
        keys[d] = swap(own_keys, d)
        d *= 2
    pairs = [(i, i ^ 1) for i in range(lax.axis_size("head"))]
    word = lax.ppermute(own_labels[:, :, :LANES], "head", pairs)
    own_total = own_totals(own_keys, init_centroids, word)
    shared = spread(jnp.concatenate([own_total, own_labels], axis=1))
    totals = [own_total] + [x[:, 0:1] for x in shared[1:]]

    sums, unit, cents = first_block(me_array, own_keys, own_total, init_centroids, n, None)
    units = [unit]
    *came, sums = lax.optimization_barrier((*keys.values(), sums))
    keys = dict(zip(keys, came))
    for m in range(1, n):
        if m not in keys:
            keys[m] = swap(keys[m & (m - 1)], m & -m)
    keys = [keys[m] for m in range(n)]
    peer_low = jnp.take(owner_bounds, me ^ jnp.arange(n, dtype=jnp.int32), axis=1)
    own_below = jnp.sum((own_labels < peer_low[:, :, None]).astype(jnp.int32), axis=2)
    own_values = sort_values(own_spots, value_rows.reshape(heads * tokens, width))

    labels = jnp.concatenate([x[:, -1:] for x in shared], axis=1)
    ranks = own_ranks(me_array, labels)
    low = lax.dynamic_slice_in_dim(owner_bounds, me, 1, 1)
    high = lax.dynamic_slice_in_dim(owner_bounds, me + 1, 1, 1)
    below = jnp.sum((labels < low[:, :, None]).astype(jnp.int32), axis=2)
    first = jnp.sum(below, axis=1, keepdims=True)
    key_starts = aligned(below, key_size)
    gaps = aligned(below, send_size) - key_starts
    one = jnp.ones((1, n), jnp.int32)
    scalars = jnp.stack([key_starts, gaps, low * one, high * one, first * one])

    starts = aligned(own_below, send_size)
    near, middle = [1], [2]
    far = [d for d in range(1, n) if d not in near + middle]

    def cut(group, after):
        some = jnp.stack([starts[:, d] for d in group], axis=1)
        return windows(some, ranks, own_values, send_size, after)

    values = {}
    for m in range(1, n):
        sums, unit = first_block(me_array, keys[m], totals[m], cents, n, sums)
        units.append(unit)
        group = {1: far, 2: [0, *middle]}.get(m)
        if group:
            *leaving, sums = lax.optimization_barrier((*cut(group, unit), sums))
            for d, window in zip(group, leaving):
                values[d] = swap(window, d) if d else window

    raw, part = raw_weights(sums, units)
    scalars, part = lax.optimization_barrier((scalars, part))
    parts = spread(part)
    most = [*collect(scalars, labels, keys, values, [0, *far, *middle], key_size)]
    own_values, *parts = lax.optimization_barrier((own_values, *parts))
    for d, window in zip(near, cut(near, most[1])):
        values[d] = swap(window, d)
    most[0], *parts = lax.optimization_barrier((most[0], *parts))
    out = weighted_sums(raw, units, parts)
    placed = place(scalars, labels, most, keys, values, near, key_size, cap, out)
    shape = (cap, heads, width)
    return out, placed[0].reshape(shape), placed[1].reshape(shape)


def solution(mesh):
    placed = (
        P(("grp", "ctx"), "head", None),
        P(("grp", "ctx"), "head", None),
        P("head", ("grp", "ctx")),
        P(("grp", "head"), None),
        P(("grp", "head"), None, None),
    )
    return jax.shard_map(
        body,
        mesh=mesh,
        in_specs=placed,
        out_specs=(
            P(("grp", "head"), "ctx", None),
            P(("grp", "ctx"), "head", None),
            P(("grp", "ctx"), "head", None),
        ),
        check_vma=False,
    )
```

```python
import functools
import math

import jax
import jax.numpy as jnp
from jax import lax
from jax.experimental import pallas as pl
from jax.experimental.pallas import tpu as pltpu
from jax.sharding import PartitionSpec as P

LANES = 128
EXP2_SCALE = 20.0 * math.log2(math.e)
VMEM_LIMIT = 16 * 1024 * 1024
F32 = jnp.float32
BF16 = jnp.bfloat16
NT = (((1,), (1,)), ((), ()))
NN = (((1,), (0,)), ((), ()))


def dot_nt(a, b):
    return lax.dot_general(a, b, NT, preferred_element_type=F32)


def dot_nn(a, b):
    return lax.dot_general(a, b, NN, preferred_element_type=F32)


def unit_rows(x):
    return x * lax.rsqrt(jnp.sum(x * x, axis=-1, keepdims=True) + 1e-06)


def params(**kwargs):
    return pltpu.CompilerParams(vmem_limit_bytes=VMEM_LIMIT, **kwargs)


def whole(shape):
    return pl.BlockSpec(shape, lambda *_: (0,) * len(shape))


def in_vmem():
    return pl.BlockSpec(memory_space=pltpu.VMEM)


def anywhere():
    return pl.BlockSpec(memory_space=pl.ANY)


def keep_hbm(x):
    return pltpu.with_memory_space_constraint(x, pltpu.HBM)


def keep_vmem(x):
    return pltpu.with_memory_space_constraint(x, pltpu.VMEM)


def row_to_lanes(row):
    return jnp.transpose(jnp.broadcast_to(row, (LANES, LANES)))


def split_heads(flat_ref, wide_ref):
    wide_ref[...] = flat_ref[...].astype(F32)


def head_rows(wide_ref, head, heads):
    if heads == 1:
        return wide_ref[...]
    return wide_ref[pl.Slice(head, wide_ref.shape[0] // heads, heads), :]


def count_below(all_ref, own_row, count):
    tokens = own_row.shape[1]
    mine = jnp.broadcast_to(own_row, (8, tokens))
    wide = 4 * LANES

    def step(i, total):
        row = all_ref[0, :, pl.ds(pl.multiple_of(i * wide, wide), wide)]
        for s in range(0, wide, LANES):
            column = row_to_lanes(row[:, s : s + LANES])
            for r in range(0, LANES, 8):
                other = jnp.tile(column[r : r + 8], (1, tokens // LANES))
                total += (other < mine).astype(jnp.int32)
        return total

    total = lax.fori_loop(
        0, count // wide, step, jnp.zeros((8, tokens), jnp.int32), unroll=True
    )
    return jnp.sum(total, axis=0, keepdims=True)


def one_hot_rows(size, spot):
    slots = lax.broadcasted_iota(jnp.int16, (size, spot.shape[1]), 0)
    return jnp.where(
        slots == spot.astype(jnp.int16), jnp.ones((), BF16), jnp.zeros((), BF16)
    )


def sort_kernel(label_hbm, keys_hbm, *refs):
    out_keys, out_labels, out_spots, flat_ref, wide_ref, order_ref, label_ref, sems = refs
    heads, tokens, _ = out_keys.shape
    label_copy = pltpu.make_async_copy(label_hbm, label_ref, sems.at[1])
    label_copy.start()
    copy = pltpu.make_async_copy(keys_hbm, flat_ref, sems.at[0])
    copy.start()
    label_copy.wait()
    labels = [label_ref[h : h + 1, :] for h in range(heads)]
    spots = []
    for h, label in enumerate(labels):
        order = label * tokens + lax.broadcasted_iota(jnp.int32, label.shape, 1)
        order_ref[0] = order
        spots.append(count_below(order_ref, order, tokens))
        out_spots[h] = spots[h]
    copy.wait()
    split_heads(flat_ref, wide_ref)
    rows = 512
    for h, label in enumerate(labels):
        keys = head_rows(wide_ref, h, heads).astype(BF16)
        digits = jnp.concatenate(
            [
                jnp.broadcast_to(label >> 6, (8, tokens)),
                jnp.broadcast_to(label & 63, (8, tokens)),
            ],
            axis=0,
        )
        digits = digits.astype(F32).astype(BF16)
        for r in range(0, tokens, rows):
            pick = one_hot_rows(rows, spots[h] - r)
            out_keys[h, r : r + rows] = dot_nn(pick, keys).astype(BF16)
            digit = dot_nt(digits, pick)
            out_labels[h, :, r : r + rows] = digit[0:1] * 64.0 + digit[8:9]


def sort_keys(labels, keys):
    heads, tokens = labels.shape
    flat, width = keys.shape
    return pl.pallas_call(
        sort_kernel,
        in_specs=[anywhere()] * 2,
        out_specs=(in_vmem(),) * 3,
        out_shape=(
            pltpu.VMEM((heads, tokens, width), BF16),
            pltpu.VMEM((heads, 1, tokens), F32),
            pltpu.VMEM((heads, 1, tokens), jnp.int32),
        ),
        scratch_shapes=[
            pltpu.VMEM((flat, width), BF16),
            pltpu.VMEM((flat, width), F32),
            pltpu.VMEM((1, 1, tokens), jnp.int32),
            pltpu.VMEM(labels.shape, jnp.int32),
            pltpu.SemaphoreType.DMA((2,)),
        ],
        compiler_params=params(),
        name="sort_keys",
    )(keep_hbm(labels), keep_hbm(keys))


def values_kernel(spot_ref, values_hbm, out_ref, flat_ref, wide_ref, sem):
    heads, _, tokens = spot_ref.shape
    copy = pltpu.make_async_copy(values_hbm, flat_ref, sem)
    copy.start()
    copy.wait()
    split_heads(flat_ref, wide_ref)
    rows = 512
    for h in range(heads):
        values = head_rows(wide_ref, h, heads).astype(BF16)
        for r in range(0, tokens, rows):
            pick = one_hot_rows(rows, spot_ref[h] - r)
            out_ref[h, r : r + rows] = dot_nn(pick, values).astype(BF16)


def sort_values(spots, values):
    heads, _, tokens = spots.shape
    flat, width = values.shape
    return pl.pallas_call(
        values_kernel,
        in_specs=[in_vmem(), anywhere()],
        out_specs=in_vmem(),
        out_shape=pltpu.VMEM((heads, tokens, width), BF16),
        scratch_shapes=[
            pltpu.VMEM((flat, width), BF16),
            pltpu.VMEM((flat, width), F32),
            pltpu.SemaphoreType.DMA,
        ],
        compiler_params=params(),
        name="sort_values",
    )(keep_vmem(spots), keep_hbm(values))


def windows_kernel(size, start_ref, rank_ref, values_ref, _, *out_refs):
    heads, tokens, _ = values_ref.shape
    for h in range(heads):
        rank = rank_ref[h].astype(jnp.int32)
        digits = [
            digit[:, t : t + LANES]
            for digit in (rank >> 7, rank & 127)
            for t in range(0, tokens, LANES)
        ]
        digits = jnp.concatenate(digits, axis=0).astype(F32).astype(BF16)
        for m, out_ref in enumerate(out_refs):
            start = pl.multiple_of(start_ref[h, m], 16)
            out_ref[h, :size] = values_ref[h, pl.ds(start, size), :]
            out_ref[h, size:] = digits


def windows(starts, ranks, values, size, after):
    heads, tokens, width = values.shape
    n = starts.shape[1]
    out = pltpu.VMEM((heads, size + 2 * tokens // LANES, width), BF16)
    return pl.pallas_call(
        functools.partial(windows_kernel, size),
        in_specs=[pl.BlockSpec(memory_space=pltpu.SMEM), in_vmem(), in_vmem(), in_vmem()],
        out_specs=(in_vmem(),) * n,
        out_shape=(out,) * n,
        compiler_params=params(),
        name="windows",
    )(starts, ranks, keep_vmem(values), keep_vmem(after))


def rank_kernel(me_ref, label_ref, rank_ref):
    n, tokens = label_ref.shape[1:]
    me = me_ref[0]
    own = label_ref[0, 0:1, :].astype(jnp.int32)
    rank = lax.broadcasted_iota(jnp.int32, own.shape, 1)
    for m in range(1, n):
        bar = own + ((me ^ m) < me).astype(jnp.int32)
        bar = jnp.broadcast_to(bar, (16, tokens)).astype(jnp.int16)
        count = jnp.zeros((16, tokens), BF16)
        for s in range(0, tokens, LANES):
            column = row_to_lanes(label_ref[0, m : m + 1, s : s + LANES])
            column = column.astype(jnp.int32).astype(jnp.int16)
            for r in range(0, LANES, 16):
                other = jnp.tile(column[r : r + 16], (1, tokens // LANES))
                count += jnp.where(other < bar, jnp.ones((), BF16), jnp.zeros((), BF16))
        rank += jnp.sum(count.astype(F32), axis=0, keepdims=True).astype(jnp.int32)
    rank_ref[0] = rank.astype(F32)


def own_ranks(me, labels):
    heads, n, tokens = labels.shape
    return pl.pallas_call(
        rank_kernel,
        grid=(heads,),
        in_specs=[
            pl.BlockSpec(memory_space=pltpu.SMEM),
            pl.BlockSpec((1, n, tokens), lambda h: (h, 0, 0)),
        ],
        out_specs=pl.BlockSpec((1, 1, tokens), lambda h: (h, 0, 0)),
        out_shape=jax.ShapeDtypeStruct((heads, 1, tokens), F32),
        compiler_params=params(),
        name="own_ranks",
    )(me, labels)


def totals_kernel(keys_ref, cent_ref, _, tot_ref, unit_ref, sum_ref):
    step = pl.program_id(1)
    tokens = unit_ref.shape[0]

    @pl.when(step == 0)
    def _():
        unit_ref[...] = unit_rows(keys_ref[pl.program_id(0)].astype(F32)).astype(BF16)
        sum_ref[...] = jnp.zeros_like(sum_ref)

    part = 256
    rows = min(1024, cent_ref.shape[1])
    for c in range(0, cent_ref.shape[1], rows):
        cent = unit_rows(cent_ref[0, c : c + rows]).astype(BF16)
        for t in range(0, tokens, part):
            raw = jnp.exp2(dot_nt(cent, unit_ref[t : t + part, :]) * EXP2_SCALE)
            sum_ref[:, t : t + part] += jnp.sum(raw.reshape(-1, 8, part), axis=0)

    @pl.when(step == pl.num_programs(1) - 1)
    def _():
        tot_ref[0] = jnp.sum(sum_ref[...], axis=0, keepdims=True)


def own_totals(keys, cents, after):
    heads, count, width = cents.shape
    tokens = keys.shape[1]
    rows = min(2048, count)
    return pl.pallas_call(
        totals_kernel,
        grid=(heads, count // rows),
        in_specs=[
            in_vmem(),
            pl.BlockSpec((1, rows, width), lambda h, c: (h, c, 0)),
            in_vmem(),
        ],
        out_specs=pl.BlockSpec((1, 1, tokens), lambda h, c: (h, 0, 0)),
        out_shape=jax.ShapeDtypeStruct((heads, 1, tokens), F32),
        scratch_shapes=[
            pltpu.VMEM((tokens, width), BF16),
            pltpu.VMEM((8, tokens), F32),
        ],
        compiler_params=params(),
        name="own_totals",
    )(keep_vmem(keys), keep_hbm(cents), after)


def scale_rows(unit, inverse, scaled_ref):
    for t in range(0, unit.shape[0], LANES):
        scaled_ref[t : t + LANES] = (
            unit[t : t + LANES, :].astype(F32) * row_to_lanes(inverse[:, t : t + LANES])
        ).astype(BF16)


def first_kernel(fresh, _, keys_ref, tot_ref, cent_in, *refs):
    head = pl.program_id(0)
    if fresh:
        sums_ref, unit_ref, cent_ref, scaled_ref = refs
        cent = unit_rows(cent_in[0]).astype(BF16)
        cent_ref[head] = cent
    else:
        _, sums_ref, unit_ref, scaled_ref = refs
        cent = cent_in[head]
    unit = unit_rows(keys_ref[head].astype(F32)).astype(BF16)
    unit_ref[head] = unit
    scale_rows(unit, 1.0 / tot_ref[0], scaled_ref)
    part = 256
    for t in range(0, unit.shape[0], part):
        raw = jnp.exp2(dot_nt(cent, unit[t : t + part, :]) * EXP2_SCALE)
        more = dot_nn(raw.astype(BF16), scaled_ref[t : t + part])
        if fresh and t == 0:
            sums_ref[head] = more
        else:
            sums_ref[head] += more


def first_block(me, keys, totals, cents, n, before):
    heads, tokens, width = keys.shape
    fresh = before is None
    rows = cents.shape[1] // n if fresh else cents.shape[1]
    in_specs = [
        in_vmem(),
        pl.BlockSpec((1, 1, tokens), lambda h, me: (h, 0, 0)),
    ]
    args = [me, keep_vmem(keys), totals]
    out_shape = [
        pltpu.VMEM((heads, rows, width), F32),
        pltpu.VMEM((heads, tokens, width), BF16),
    ]
    aliases = {}
    if fresh:
        in_specs.append(pl.BlockSpec((1, rows, width), lambda h, me: (h, me[0], 0)))
        args.append(keep_hbm(cents))
        out_shape.append(pltpu.VMEM((heads, rows, width), BF16))
    else:
        in_specs += [in_vmem(), in_vmem()]
        args += [keep_vmem(cents), keep_vmem(before)]
        aliases = {4: 0}
    return pl.pallas_call(
        functools.partial(first_kernel, fresh),
        grid_spec=pltpu.PrefetchScalarGridSpec(
            num_scalar_prefetch=1,
            grid=(heads,),
            in_specs=in_specs,
            out_specs=(in_vmem(),) * len(out_shape),
            scratch_shapes=[pltpu.VMEM((tokens, width), BF16)],
        ),
        out_shape=tuple(out_shape),
        input_output_aliases=aliases,
        compiler_params=params(),
        name="first_block",
    )(*args)


def raw_kernel(blocks, sums_ref, *refs):
    units = refs[:blocks]
    raw_ref, total_ref, cent_ref = refs[blocks:]
    head = pl.program_id(0)
    cent_ref[...] = unit_rows(sums_ref[head]).astype(BF16)
    part = 256
    start = 0
    for unit_ref in units:
        for t in range(0, unit_ref.shape[1], part):
            here = slice(start + t, start + t + part)
            raw = jnp.exp2(dot_nt(cent_ref[...], unit_ref[head, t : t + part, :]) * EXP2_SCALE)
            raw_ref[head, :, here] = raw.astype(BF16)
            total = jnp.sum(raw.reshape(-1, 8, part), axis=0)
            total_ref[0, :, here] = jnp.sum(total, axis=0, keepdims=True)
        start += unit_ref.shape[1]


def raw_weights(sums, units):
    heads, rows, width = sums.shape
    tokens = units[0].shape[1]
    count = tokens * len(units)
    return pl.pallas_call(
        functools.partial(raw_kernel, len(units)),
        grid=(heads,),
        in_specs=[in_vmem()] * (1 + len(units)),
        out_specs=(in_vmem(), pl.BlockSpec((1, 1, count), lambda h: (h, 0, 0))),
        out_shape=(
            pltpu.VMEM((heads, rows, count), BF16),
            jax.ShapeDtypeStruct((heads, 1, count), F32),
        ),
        scratch_shapes=[pltpu.VMEM((rows, width), BF16)],
        compiler_params=params(),
        name="raw_weights",
    )(keep_vmem(sums), *map(keep_vmem, units))


def sums_kernel(blocks, raw_ref, *refs):
    totals, units = refs[:blocks], refs[blocks : 2 * blocks]
    out_hbm, scaled_ref, result_ref, sems = refs[2 * blocks :]
    heads, tokens, _ = units[0].shape
    copies = []
    for h in range(heads):
        for m, unit_ref in enumerate(units):
            row_total = totals[0][h, :, m * tokens : (m + 1) * tokens]
            for d in range(1, blocks):
                peer = m ^ d
                row_total += totals[d][h, :, peer * tokens : (peer + 1) * tokens]
            here = slice(m * tokens, (m + 1) * tokens)
            scale_rows(unit_ref[h], 1.0 / row_total, scaled_ref.at[h, here])
        result_ref[h] = unit_rows(dot_nn(raw_ref[h], scaled_ref[h]))
        copies.append(pltpu.make_async_copy(result_ref.at[h], out_hbm.at[h], sems.at[h]))
        copies[-1].start()
    for copy in copies:
        copy.wait()


def weighted_sums(raw, units, totals):
    heads, rows, count = raw.shape
    width = units[0].shape[2]
    return pl.pallas_call(
        functools.partial(sums_kernel, len(units)),
        in_specs=[in_vmem()] * (1 + 2 * len(units)),
        out_specs=anywhere(),
        out_shape=jax.ShapeDtypeStruct((heads, rows, width), F32),
        scratch_shapes=[
            pltpu.VMEM((heads, count, width), BF16),
            pltpu.VMEM((heads, rows, width), F32),
            pltpu.SemaphoreType.DMA((heads,)),
        ],
        compiler_params=params(),
        name="weighted_sums",
    )(keep_vmem(raw), *map(keep_vmem, totals), *map(keep_vmem, units))


def fill_windows(ids, size, scalar_ref, label_ref, keys, values, rows_ref, near_ref):
    heads, tokens, width = keys[0].shape
    digit_rows = tokens // LANES
    sent = values[0][0].shape[1] - 2 * digit_rows
    rows_ref[:, :, width:] = jnp.zeros((heads, len(ids) * size, width), BF16)
    for h in range(heads):
        low, high, first = (scalar_ref[i, h, 0].astype(F32) for i in range(2, 5))
        for i, m in enumerate(ids):
            start = pl.multiple_of(scalar_ref[0, h, m], 16)
            gap = pl.multiple_of(scalar_ref[1, h, m], 16)
            here = i * size
            rows_ref[h, here : here + size, :width] = keys[i][h, pl.ds(start, size), :]
            value = values[i][0][h]
            if len(values[i]) == 2:
                value = jnp.where(scalar_ref[5, 0, 0] > 0, value, values[i][1][h])
            rows_ref[h, pl.ds(here + gap, sent), width:] = value[:sent]
            digits = value[sent:].astype(F32)
            rank = digits[:digit_rows] * 128.0 + digits[digit_rows:]
            rank = jnp.concatenate([rank[r : r + 1] for r in range(digit_rows)], axis=1)
            label = label_ref[h, m : m + 1, :]
            mine = (label >= low) & (label < high)
            spot = jnp.where(mine, rank - first, -1.0).astype(jnp.int32)
            spot = pltpu.roll(spot, lax.rem(tokens - start, tokens), 1)
            near_ref[h, :, here : here + size] = spot[:, :size]


def grouped(refs, counts):
    refs = iter(refs)
    return [[next(refs) for _ in range(count)] for count in counts]


def place_kernel(ids, counts, size, fresh, scalar_ref, label_ref, *refs):
    keys, refs = refs[: len(ids)], refs[len(ids) :]
    values, refs = grouped(refs, counts), refs[sum(counts) :]
    if fresh:
        so_far_ref, rows_ref, near_ref = refs
    else:
        so_far_ref, *out_hbm, rows_ref, near_ref, mixed_ref, done_ref, sems = refs
    fill_windows(ids, size, scalar_ref, label_ref, keys, values, rows_ref, near_ref)
    heads, cap, both = so_far_ref.shape
    width = both // 2
    rows = 512
    copies = []
    for r in range(0, cap, rows):
        for h in range(heads):
            total = dot_nn(one_hot_rows(rows, near_ref[h] - r), rows_ref[h])
            if fresh:
                so_far_ref[h, r : r + rows] = total.astype(BF16)
                continue
            total += so_far_ref[h, r : r + rows].astype(F32)
            for side in range(2):
                mixed_ref[side, pl.Slice(h, rows, heads), :] = total[
                    :, side * width : (side + 1) * width
                ]
        if fresh:
            continue
        here = slice(r * heads, (r + rows) * heads)
        for side in range(2):
            done_ref[side, here] = mixed_ref[side].astype(BF16)
            copies.append(
                pltpu.make_async_copy(
                    done_ref.at[side, here], out_hbm[side].at[here], sems.at[len(copies)]
                )
            )
            copies[-1].start()
    for copy in copies:
        copy.wait()


def place(scalars, labels, keys, values, ids, size, cap, so_far):
    heads, _, width = keys[0].shape
    fresh = so_far is None
    counts = [len(values[m]) for m in ids]
    moved = [keys[m] for m in ids] + [x for m in ids for x in values[m]]
    scratch = [
        pltpu.VMEM((heads, len(ids) * size, 2 * width), BF16),
        pltpu.VMEM((heads, 1, len(ids) * size), jnp.int32),
    ]
    if fresh:
        out_shape = pltpu.VMEM((heads, cap, 2 * width), BF16)
        out_specs = in_vmem()
    else:
        moved.append(so_far)
        out_shape = (jax.ShapeDtypeStruct((heads * cap, width), BF16),) * 2
        out_specs = (anywhere(), anywhere())
        scratch += [
            pltpu.VMEM((2, heads * 512, width), F32),
            pltpu.VMEM((2, heads * cap, width), BF16),
            pltpu.SemaphoreType.DMA((2 * cap // 512,)),
        ]
    return pl.pallas_call(
        functools.partial(place_kernel, ids, counts, size, fresh),
        in_specs=[pl.BlockSpec(memory_space=pltpu.SMEM)] + [in_vmem()] * (1 + len(moved)),
        out_specs=out_specs,
        out_shape=out_shape,
        scratch_shapes=scratch,
        compiler_params=params(),
        name="place",
    )(scalars, labels, *map(keep_vmem, moved))


def body(key_rows, value_rows, cluster_labels, owner_bounds, init_centroids):
    n = lax.axis_size("ctx")
    me = lax.axis_index("ctx").astype(jnp.int32)
    tokens, heads, width = key_rows.shape
    cap = 2 * tokens
    slot = cap // n
    send_size = slot + 16
    key_size = min(tokens, -(-send_size // LANES) * LANES)

    def swap(x, d):
        return lax.ppermute(x, "ctx", [(i, i ^ d) for i in range(n)])

    def spread(x):
        return [x] + [swap(x, d) for d in range(1, n)]

    def aligned(start, size):
        return jnp.minimum(start // 16 * 16, tokens - size)

    me_array = me.reshape(1)
    own_keys, own_labels, own_spots = sort_keys(
        cluster_labels, key_rows.reshape(heads * tokens, width)
    )
    keys = {0: own_keys}
    d = 1
    while d < n:
        keys[d] = swap(own_keys, d)
        d *= 2
    pairs = [(i, i ^ 1) for i in range(lax.axis_size("head"))]
    word = lax.ppermute(own_labels[:, :, :LANES], "head", pairs)
    own_total = own_totals(own_keys, init_centroids, word)
    shared = spread(jnp.concatenate([own_total, own_labels], axis=1))
    totals = [own_total] + [x[:, 0:1] for x in shared[1:]]

    sums, unit, cents = first_block(me_array, own_keys, own_total, init_centroids, n, None)
    units = [unit]
    *came, sums = lax.optimization_barrier((*keys.values(), sums))
    keys = dict(zip(keys, came))
    for m in range(1, n):
        if m not in keys:
            keys[m] = swap(keys[m & (m - 1)], m & -m)
    keys = [keys[m] for m in range(n)]
    peer_low = jnp.take(owner_bounds, me ^ jnp.arange(n, dtype=jnp.int32), axis=1)
    own_below = jnp.sum((own_labels < peer_low[:, :, None]).astype(jnp.int32), axis=2)
    own_values = sort_values(own_spots, value_rows.reshape(heads * tokens, width))

    labels = jnp.concatenate([x[:, -1:] for x in shared], axis=1)
    ranks = own_ranks(me_array, labels)
    low = lax.dynamic_slice_in_dim(owner_bounds, me, 1, 1)
    high = lax.dynamic_slice_in_dim(owner_bounds, me + 1, 1, 1)
    below = jnp.sum((labels < low[:, :, None]).astype(jnp.int32), axis=2)
    first = jnp.sum(below, axis=1, keepdims=True)
    key_starts = aligned(below, key_size)
    gaps = aligned(below, send_size) - key_starts
    one = jnp.ones((1, n), jnp.int32)
    inner = ((me & 3) == 1) | ((me & 3) == 2)
    scalars = jnp.stack(
        [key_starts, gaps, low * one, high * one, first * one, inner * jnp.ones_like(below)]
    )

    starts = aligned(own_below, send_size)
    own_windows = windows(starts, ranks, own_values, send_size, own_labels)
    values = {0: [own_windows[0]]}

    def inner_swap(x, wanted):
        pairs = [(i, i ^ 3 if (i & 3 in (1, 2)) == wanted else i) for i in range(n)]
        return lax.ppermute(x, "ctx", pairs)

    def leave(m, x):
        if m == 1 and n > 2:
            own_windows[3], x = lax.optimization_barrier((own_windows[3], x))
            values[3] = [inner_swap(own_windows[3], True)]
        if m == min(2, n - 1):
            own_windows[1], x = lax.optimization_barrier((own_windows[1], x))
            values[1] = [swap(own_windows[1], 1)]
        if m == n - 1:
            *own_windows[2:], x = lax.optimization_barrier((*own_windows[2:], x))
            for d in range(2, n):
                if d == 3:
                    values[3].append(inner_swap(own_windows[3], False))
                else:
                    values[d] = [swap(own_windows[d], d)]
        return x

    own_windows = list(own_windows)
    for m in range(1, n):
        sums = leave(m, sums)
        sums, unit = first_block(me_array, keys[m], totals[m], cents, n, sums)
        units.append(unit)

    raw, part = raw_weights(sums, units)
    values[1][0], values[3][0], scalars, part = lax.optimization_barrier(
        (values[1][0], values[3][0], scalars, part)
    )
    parts = spread(part)
    so_far = place(scalars, labels, keys, values, [0, 1], key_size, cap, None)
    out = weighted_sums(raw, units, parts)
    placed = place(scalars, labels, keys, values, list(range(2, n)), key_size, cap, so_far)
    shape = (cap, heads, width)
    return out, placed[0].reshape(shape), placed[1].reshape(shape)


def solution(mesh):
    placed = (
        P(("grp", "ctx"), "head", None),
        P(("grp", "ctx"), "head", None),
        P("head", ("grp", "ctx")),
        P(("grp", "head"), None),
        P(("grp", "head"), None, None),
    )
    return jax.shard_map(
        body,
        mesh=mesh,
        in_specs=placed,
        out_specs=(
            P(("grp", "head"), "ctx", None),
            P(("grp", "ctx"), "head", None),
            P(("grp", "ctx"), "head", None),
        ),
        check_vma=False,
    )
```

```python
import functools
import math

import jax
import jax.numpy as jnp
from jax import lax
from jax.experimental import pallas as pl
from jax.experimental.pallas import tpu as pltpu
from jax.sharding import PartitionSpec as P

LANES = 128
EXP2_SCALE = 20.0 * math.log2(math.e)
VMEM_LIMIT = 16 * 1024 * 1024
F32 = jnp.float32
BF16 = jnp.bfloat16
NT = (((1,), (1,)), ((), ()))
NN = (((1,), (0,)), ((), ()))


def dot_nt(a, b):
    return lax.dot_general(a, b, NT, preferred_element_type=F32)


def dot_nn(a, b):
    return lax.dot_general(a, b, NN, preferred_element_type=F32)


def unit_rows(x):
    return x * lax.rsqrt(jnp.sum(x * x, axis=-1, keepdims=True) + 1e-06)


def params(**kwargs):
    return pltpu.CompilerParams(vmem_limit_bytes=VMEM_LIMIT, **kwargs)


def whole(shape):
    return pl.BlockSpec(shape, lambda *_: (0,) * len(shape))


def in_vmem():
    return pl.BlockSpec(memory_space=pltpu.VMEM)


def anywhere():
    return pl.BlockSpec(memory_space=pl.ANY)


def keep_hbm(x):
    return pltpu.with_memory_space_constraint(x, pltpu.HBM)


def keep_vmem(x):
    return pltpu.with_memory_space_constraint(x, pltpu.VMEM)


def row_to_lanes(row):
    return jnp.transpose(jnp.broadcast_to(row, (LANES, LANES)))


def split_heads(flat_ref, wide_ref):
    wide_ref[...] = flat_ref[...].astype(F32)


def head_rows(wide_ref, head, heads):
    if heads == 1:
        return wide_ref[...]
    return wide_ref[pl.Slice(head, wide_ref.shape[0] // heads, heads), :]


def count_below(all_ref, own_row, count):
    tokens = own_row.shape[1]
    mine = jnp.broadcast_to(own_row, (8, tokens))
    wide = 4 * LANES

    def step(i, total):
        row = all_ref[0, :, pl.ds(pl.multiple_of(i * wide, wide), wide)]
        for s in range(0, wide, LANES):
            column = row_to_lanes(row[:, s : s + LANES])
            for r in range(0, LANES, 8):
                other = jnp.tile(column[r : r + 8], (1, tokens // LANES))
                total += (other < mine).astype(jnp.int32)
        return total

    total = lax.fori_loop(
        0, count // wide, step, jnp.zeros((8, tokens), jnp.int32), unroll=True
    )
    return jnp.sum(total, axis=0, keepdims=True)


def one_hot_rows(size, spot):
    slots = lax.broadcasted_iota(jnp.int16, (size, spot.shape[1]), 0)
    return jnp.where(
        slots == spot.astype(jnp.int16), jnp.ones((), BF16), jnp.zeros((), BF16)
    )


def sort_kernel(label_hbm, keys_hbm, *refs):
    out_keys, out_labels, out_spots, flat_ref, wide_ref, order_ref, label_ref, sems = refs
    heads, tokens, _ = out_keys.shape
    label_copy = pltpu.make_async_copy(label_hbm, label_ref, sems.at[1])
    label_copy.start()
    copy = pltpu.make_async_copy(keys_hbm, flat_ref, sems.at[0])
    copy.start()
    label_copy.wait()
    labels = [label_ref[h : h + 1, :] for h in range(heads)]
    spots = []
    for h, label in enumerate(labels):
        order = label * tokens + lax.broadcasted_iota(jnp.int32, label.shape, 1)
        order_ref[0] = order
        spots.append(count_below(order_ref, order, tokens))
        out_spots[h] = spots[h]
    copy.wait()
    split_heads(flat_ref, wide_ref)
    rows = 512
    for h, label in enumerate(labels):
        keys = head_rows(wide_ref, h, heads).astype(BF16)
        digits = jnp.concatenate(
            [
                jnp.broadcast_to(label >> 6, (8, tokens)),
                jnp.broadcast_to(label & 63, (8, tokens)),
            ],
            axis=0,
        )
        digits = digits.astype(F32).astype(BF16)
        for r in range(0, tokens, rows):
            pick = one_hot_rows(rows, spots[h] - r)
            out_keys[h, r : r + rows] = dot_nn(pick, keys).astype(BF16)
            digit = dot_nt(digits, pick)
            out_labels[h, :, r : r + rows] = digit[0:1] * 64.0 + digit[8:9]


def sort_keys(labels, keys):
    heads, tokens = labels.shape
    flat, width = keys.shape
    return pl.pallas_call(
        sort_kernel,
        in_specs=[anywhere()] * 2,
        out_specs=(in_vmem(),) * 3,
        out_shape=(
            pltpu.VMEM((heads, tokens, width), BF16),
            pltpu.VMEM((heads, 1, tokens), F32),
            pltpu.VMEM((heads, 1, tokens), jnp.int32),
        ),
        scratch_shapes=[
            pltpu.VMEM((flat, width), BF16),
            pltpu.VMEM((flat, width), F32),
            pltpu.VMEM((1, 1, tokens), jnp.int32),
            pltpu.VMEM(labels.shape, jnp.int32),
            pltpu.SemaphoreType.DMA((2,)),
        ],
        compiler_params=params(),
        name="sort_keys",
    )(keep_hbm(labels), keep_hbm(keys))


def values_kernel(spot_ref, values_hbm, out_ref, flat_ref, wide_ref, sem):
    heads, _, tokens = spot_ref.shape
    copy = pltpu.make_async_copy(values_hbm, flat_ref, sem)
    copy.start()
    copy.wait()
    split_heads(flat_ref, wide_ref)
    rows = 512
    for h in range(heads):
        values = head_rows(wide_ref, h, heads).astype(BF16)
        for r in range(0, tokens, rows):
            pick = one_hot_rows(rows, spot_ref[h] - r)
            out_ref[h, r : r + rows] = dot_nn(pick, values).astype(BF16)


def sort_values(spots, values):
    heads, _, tokens = spots.shape
    flat, width = values.shape
    return pl.pallas_call(
        values_kernel,
        in_specs=[in_vmem(), anywhere()],
        out_specs=in_vmem(),
        out_shape=pltpu.VMEM((heads, tokens, width), BF16),
        scratch_shapes=[
            pltpu.VMEM((flat, width), BF16),
            pltpu.VMEM((flat, width), F32),
            pltpu.SemaphoreType.DMA,
        ],
        compiler_params=params(),
        name="sort_values",
    )(keep_vmem(spots), keep_hbm(values))


def windows_kernel(size, start_ref, rank_ref, values_ref, _, *out_refs):
    heads, tokens, _ = values_ref.shape
    for h in range(heads):
        rank = rank_ref[h].astype(jnp.int32)
        digits = [
            digit[:, t : t + LANES]
            for digit in (rank >> 7, rank & 127)
            for t in range(0, tokens, LANES)
        ]
        digits = jnp.concatenate(digits, axis=0).astype(F32).astype(BF16)
        for m, out_ref in enumerate(out_refs):
            start = pl.multiple_of(start_ref[h, m], 16)
            out_ref[h, :size] = values_ref[h, pl.ds(start, size), :]
            out_ref[h, size:] = digits


def windows(starts, ranks, values, size, after):
    heads, tokens, width = values.shape
    n = starts.shape[1]
    out = pltpu.VMEM((heads, size + 2 * tokens // LANES, width), BF16)
    return pl.pallas_call(
        functools.partial(windows_kernel, size),
        in_specs=[pl.BlockSpec(memory_space=pltpu.SMEM), in_vmem(), in_vmem(), in_vmem()],
        out_specs=(in_vmem(),) * n,
        out_shape=(out,) * n,
        compiler_params=params(),
        name="windows",
    )(starts, ranks, keep_vmem(values), keep_vmem(after))


def rank_kernel(me_ref, label_ref, rank_ref):
    n, tokens = label_ref.shape[1:]
    me = me_ref[0]
    own = label_ref[0, 0:1, :].astype(jnp.int32)
    rank = lax.broadcasted_iota(jnp.int32, own.shape, 1)
    for m in range(1, n):
        bar = own + ((me ^ m) < me).astype(jnp.int32)
        bar = jnp.broadcast_to(bar, (16, tokens)).astype(jnp.int16)
        count = jnp.zeros((16, tokens), BF16)
        for s in range(0, tokens, LANES):
            column = row_to_lanes(label_ref[0, m : m + 1, s : s + LANES])
            column = column.astype(jnp.int32).astype(jnp.int16)
            for r in range(0, LANES, 16):
                other = jnp.tile(column[r : r + 16], (1, tokens // LANES))
                count += jnp.where(other < bar, jnp.ones((), BF16), jnp.zeros((), BF16))
        rank += jnp.sum(count.astype(F32), axis=0, keepdims=True).astype(jnp.int32)
    rank_ref[0] = rank.astype(F32)


def own_ranks(me, labels):
    heads, n, tokens = labels.shape
    return pl.pallas_call(
        rank_kernel,
        grid=(heads,),
        in_specs=[
            pl.BlockSpec(memory_space=pltpu.SMEM),
            pl.BlockSpec((1, n, tokens), lambda h: (h, 0, 0)),
        ],
        out_specs=pl.BlockSpec((1, 1, tokens), lambda h: (h, 0, 0)),
        out_shape=jax.ShapeDtypeStruct((heads, 1, tokens), F32),
        compiler_params=params(),
        name="own_ranks",
    )(me, labels)


def totals_kernel(keys_ref, cent_ref, _, tot_ref, unit_ref, sum_ref):
    step = pl.program_id(1)
    tokens = unit_ref.shape[0]

    @pl.when(step == 0)
    def _():
        unit_ref[...] = unit_rows(keys_ref[pl.program_id(0)].astype(F32)).astype(BF16)
        sum_ref[...] = jnp.zeros_like(sum_ref)

    part = 256
    rows = min(1024, cent_ref.shape[1])
    for c in range(0, cent_ref.shape[1], rows):
        cent = unit_rows(cent_ref[0, c : c + rows]).astype(BF16)
        for t in range(0, tokens, part):
            raw = jnp.exp2(dot_nt(cent, unit_ref[t : t + part, :]) * EXP2_SCALE)
            sum_ref[:, t : t + part] += jnp.sum(raw.reshape(-1, 8, part), axis=0)

    @pl.when(step == pl.num_programs(1) - 1)
    def _():
        tot_ref[0] = jnp.sum(sum_ref[...], axis=0, keepdims=True)


def own_totals(keys, cents, after):
    heads, count, width = cents.shape
    tokens = keys.shape[1]
    rows = min(2048, count)
    return pl.pallas_call(
        totals_kernel,
        grid=(heads, count // rows),
        in_specs=[
            in_vmem(),
            pl.BlockSpec((1, rows, width), lambda h, c: (h, c, 0)),
            in_vmem(),
        ],
        out_specs=pl.BlockSpec((1, 1, tokens), lambda h, c: (h, 0, 0)),
        out_shape=jax.ShapeDtypeStruct((heads, 1, tokens), F32),
        scratch_shapes=[
            pltpu.VMEM((tokens, width), BF16),
            pltpu.VMEM((8, tokens), F32),
        ],
        compiler_params=params(),
        name="own_totals",
    )(keep_vmem(keys), keep_hbm(cents), after)


def scale_rows(unit, inverse, scaled_ref):
    for t in range(0, unit.shape[0], LANES):
        scaled_ref[t : t + LANES] = (
            unit[t : t + LANES, :].astype(F32) * row_to_lanes(inverse[:, t : t + LANES])
        ).astype(BF16)


def first_kernel(fresh, _, keys_ref, tot_ref, cent_in, *refs):
    head = pl.program_id(0)
    if fresh:
        sums_ref, unit_ref, cent_ref, scaled_ref = refs
        cent = unit_rows(cent_in[0]).astype(BF16)
        cent_ref[head] = cent
    else:
        _, sums_ref, unit_ref, scaled_ref = refs
        cent = cent_in[head]
    unit = unit_rows(keys_ref[head].astype(F32)).astype(BF16)
    unit_ref[head] = unit
    scale_rows(unit, 1.0 / tot_ref[0], scaled_ref)
    part = 256
    for t in range(0, unit.shape[0], part):
        raw = jnp.exp2(dot_nt(cent, unit[t : t + part, :]) * EXP2_SCALE)
        more = dot_nn(raw.astype(BF16), scaled_ref[t : t + part])
        if fresh and t == 0:
            sums_ref[head] = more
        else:
            sums_ref[head] += more


def first_block(me, keys, totals, cents, n, before):
    heads, tokens, width = keys.shape
    fresh = before is None
    rows = cents.shape[1] // n if fresh else cents.shape[1]
    in_specs = [
        in_vmem(),
        pl.BlockSpec((1, 1, tokens), lambda h, me: (h, 0, 0)),
    ]
    args = [me, keep_vmem(keys), totals]
    out_shape = [
        pltpu.VMEM((heads, rows, width), F32),
        pltpu.VMEM((heads, tokens, width), BF16),
    ]
    aliases = {}
    if fresh:
        in_specs.append(pl.BlockSpec((1, rows, width), lambda h, me: (h, me[0], 0)))
        args.append(keep_hbm(cents))
        out_shape.append(pltpu.VMEM((heads, rows, width), BF16))
    else:
        in_specs += [in_vmem(), in_vmem()]
        args += [keep_vmem(cents), keep_vmem(before)]
        aliases = {4: 0}
    return pl.pallas_call(
        functools.partial(first_kernel, fresh),
        grid_spec=pltpu.PrefetchScalarGridSpec(
            num_scalar_prefetch=1,
            grid=(heads,),
            in_specs=in_specs,
            out_specs=(in_vmem(),) * len(out_shape),
            scratch_shapes=[pltpu.VMEM((tokens, width), BF16)],
        ),
        out_shape=tuple(out_shape),
        input_output_aliases=aliases,
        compiler_params=params(),
        name="first_block",
    )(*args)


def raw_kernel(blocks, sums_ref, *refs):
    units = refs[:blocks]
    raw_ref, total_ref, cent_ref = refs[blocks:]
    head = pl.program_id(0)
    cent_ref[...] = unit_rows(sums_ref[head]).astype(BF16)
    part = 256
    start = 0
    for unit_ref in units:
        for t in range(0, unit_ref.shape[1], part):
            here = slice(start + t, start + t + part)
            raw = jnp.exp2(dot_nt(cent_ref[...], unit_ref[head, t : t + part, :]) * EXP2_SCALE)
            raw_ref[head, :, here] = raw.astype(BF16)
            total = jnp.sum(raw.reshape(-1, 8, part), axis=0)
            total_ref[0, :, here] = jnp.sum(total, axis=0, keepdims=True)
        start += unit_ref.shape[1]


def raw_weights(sums, units):
    heads, rows, width = sums.shape
    tokens = units[0].shape[1]
    count = tokens * len(units)
    return pl.pallas_call(
        functools.partial(raw_kernel, len(units)),
        grid=(heads,),
        in_specs=[in_vmem()] * (1 + len(units)),
        out_specs=(in_vmem(), pl.BlockSpec((1, 1, count), lambda h: (h, 0, 0))),
        out_shape=(
            pltpu.VMEM((heads, rows, count), BF16),
            jax.ShapeDtypeStruct((heads, 1, count), F32),
        ),
        scratch_shapes=[pltpu.VMEM((rows, width), BF16)],
        compiler_params=params(),
        name="raw_weights",
    )(keep_vmem(sums), *map(keep_vmem, units))


def sums_kernel(blocks, raw_ref, *refs):
    totals, units = refs[:blocks], refs[blocks : 2 * blocks]
    out_hbm, scaled_ref, result_ref, sems = refs[2 * blocks :]
    heads, tokens, _ = units[0].shape
    copies = []
    for h in range(heads):
        for m, unit_ref in enumerate(units):
            row_total = totals[0][h, :, m * tokens : (m + 1) * tokens]
            for d in range(1, blocks):
                peer = m ^ d
                row_total += totals[d][h, :, peer * tokens : (peer + 1) * tokens]
            here = slice(m * tokens, (m + 1) * tokens)
            scale_rows(unit_ref[h], 1.0 / row_total, scaled_ref.at[h, here])
        result_ref[h] = unit_rows(dot_nn(raw_ref[h], scaled_ref[h]))
        copies.append(pltpu.make_async_copy(result_ref.at[h], out_hbm.at[h], sems.at[h]))
        copies[-1].start()
    for copy in copies:
        copy.wait()


def weighted_sums(raw, units, totals):
    heads, rows, count = raw.shape
    width = units[0].shape[2]
    return pl.pallas_call(
        functools.partial(sums_kernel, len(units)),
        in_specs=[in_vmem()] * (1 + 2 * len(units)),
        out_specs=anywhere(),
        out_shape=jax.ShapeDtypeStruct((heads, rows, width), F32),
        scratch_shapes=[
            pltpu.VMEM((heads, count, width), BF16),
            pltpu.VMEM((heads, rows, width), F32),
            pltpu.SemaphoreType.DMA((heads,)),
        ],
        compiler_params=params(),
        name="weighted_sums",
    )(keep_vmem(raw), *map(keep_vmem, totals), *map(keep_vmem, units))


def fill_windows(ids, size, scalar_ref, label_ref, keys, values, rows_ref, near_ref):
    heads, tokens, width = keys[0].shape
    digit_rows = tokens // LANES
    sent = values[0].shape[1] - 2 * digit_rows
    rows_ref[:, :, width:] = jnp.zeros((heads, len(ids) * size, width), BF16)
    for h in range(heads):
        low, high, first = (scalar_ref[i, h, 0].astype(F32) for i in range(2, 5))
        for i, m in enumerate(ids):
            start = pl.multiple_of(scalar_ref[0, h, m], 16)
            gap = pl.multiple_of(scalar_ref[1, h, m], 16)
            here = i * size
            rows_ref[h, here : here + size, :width] = keys[i][h, pl.ds(start, size), :]
            rows_ref[h, pl.ds(here + gap, sent), width:] = values[i][h, :sent, :]
            digits = values[i][h, sent:, :].astype(F32)
            rank = digits[:digit_rows] * 128.0 + digits[digit_rows:]
            rank = jnp.concatenate([rank[r : r + 1] for r in range(digit_rows)], axis=1)
            label = label_ref[h, m : m + 1, :]
            mine = (label >= low) & (label < high)
            spot = jnp.where(mine, rank - first, -1.0).astype(jnp.int32)
            spot = pltpu.roll(spot, lax.rem(tokens - start, tokens), 1)
            near_ref[h, :, here : here + size] = spot[:, :size]


def place_kernel(ids, size, fresh, scalar_ref, label_ref, *refs):
    count = len(ids)
    keys, values, refs = refs[:count], refs[count : 2 * count], refs[2 * count :]
    if fresh:
        so_far_ref, rows_ref, near_ref = refs
    else:
        so_far_ref, *out_hbm, rows_ref, near_ref, mixed_ref, done_ref, sems = refs
    fill_windows(ids, size, scalar_ref, label_ref, keys, values, rows_ref, near_ref)
    heads, cap, both = so_far_ref.shape
    width = both // 2
    rows = 512
    copies = []
    for r in range(0, cap, rows):
        for h in range(heads):
            total = dot_nn(one_hot_rows(rows, near_ref[h] - r), rows_ref[h])
            if fresh:
                so_far_ref[h, r : r + rows] = total.astype(BF16)
                continue
            total += so_far_ref[h, r : r + rows].astype(F32)
            for side in range(2):
                mixed_ref[side, pl.Slice(h, rows, heads), :] = total[
                    :, side * width : (side + 1) * width
                ]
        if fresh:
            continue
        here = slice(r * heads, (r + rows) * heads)
        for side in range(2):
            done_ref[side, here] = mixed_ref[side].astype(BF16)
            copies.append(
                pltpu.make_async_copy(
                    done_ref.at[side, here], out_hbm[side].at[here], sems.at[len(copies)]
                )
            )
            copies[-1].start()
    for copy in copies:
        copy.wait()


def place(scalars, labels, keys, values, ids, size, cap, so_far):
    heads, _, width = keys[0].shape
    fresh = so_far is None
    moved = [x[m] for x in (keys, values) for m in ids]
    scratch = [
        pltpu.VMEM((heads, len(ids) * size, 2 * width), BF16),
        pltpu.VMEM((heads, 1, len(ids) * size), jnp.int32),
    ]
    if fresh:
        out_shape = pltpu.VMEM((heads, cap, 2 * width), BF16)
        out_specs = in_vmem()
    else:
        moved.append(so_far)
        out_shape = (jax.ShapeDtypeStruct((heads * cap, width), BF16),) * 2
        out_specs = (anywhere(), anywhere())
        scratch += [
            pltpu.VMEM((2, heads * 512, width), F32),
            pltpu.VMEM((2, heads * cap, width), BF16),
            pltpu.SemaphoreType.DMA((2 * cap // 512,)),
        ]
    return pl.pallas_call(
        functools.partial(place_kernel, ids, size, fresh),
        in_specs=[pl.BlockSpec(memory_space=pltpu.SMEM)] + [in_vmem()] * (1 + len(moved)),
        out_specs=out_specs,
        out_shape=out_shape,
        scratch_shapes=scratch,
        compiler_params=params(),
        name="place",
    )(scalars, labels, *map(keep_vmem, moved))


def body(key_rows, value_rows, cluster_labels, owner_bounds, init_centroids):
    n = lax.axis_size("ctx")
    me = lax.axis_index("ctx").astype(jnp.int32)
    tokens, heads, width = key_rows.shape
    cap = 2 * tokens
    slot = cap // n
    send_size = slot + 16
    key_size = min(tokens, -(-send_size // LANES) * LANES)

    def swap(x, d):
        return lax.ppermute(x, "ctx", [(i, i ^ d) for i in range(n)])

    def spread(x):
        return [x] + [swap(x, d) for d in range(1, n)]

    def aligned(start, size):
        return jnp.minimum(start // 16 * 16, tokens - size)

    me_array = me.reshape(1)
    own_keys, own_labels, own_spots = sort_keys(
        cluster_labels, key_rows.reshape(heads * tokens, width)
    )
    keys = {0: own_keys}
    d = 1
    while d < n:
        keys[d] = swap(own_keys, d)
        d *= 2
    pairs = [(i, i ^ 1) for i in range(lax.axis_size("head"))]
    word = lax.ppermute(own_labels[:, :, :LANES], "head", pairs)
    own_total = own_totals(own_keys, init_centroids, word)
    shared = spread(jnp.concatenate([own_total, own_labels], axis=1))
    totals = [own_total] + [x[:, 0:1] for x in shared[1:]]

    sums, unit, cents = first_block(me_array, own_keys, own_total, init_centroids, n, None)
    units = [unit]
    *came, sums = lax.optimization_barrier((*keys.values(), sums))
    keys = dict(zip(keys, came))
    for m in range(1, n):
        if m not in keys:
            keys[m] = swap(keys[m & (m - 1)], m & -m)
    keys = [keys[m] for m in range(n)]
    peer_low = jnp.take(owner_bounds, me ^ jnp.arange(n, dtype=jnp.int32), axis=1)
    own_below = jnp.sum((own_labels < peer_low[:, :, None]).astype(jnp.int32), axis=2)
    own_values = sort_values(own_spots, value_rows.reshape(heads * tokens, width))

    labels, sums = lax.optimization_barrier(
        (jnp.concatenate([x[:, -1:] for x in shared], axis=1), sums)
    )
    ranks = own_ranks(me_array, labels)
    low = lax.dynamic_slice_in_dim(owner_bounds, me, 1, 1)
    high = lax.dynamic_slice_in_dim(owner_bounds, me + 1, 1, 1)
    below = jnp.sum((labels < low[:, :, None]).astype(jnp.int32), axis=2)
    first = jnp.sum(below, axis=1, keepdims=True)
    key_starts = aligned(below, key_size)
    gaps = aligned(below, send_size) - key_starts
    one = jnp.ones((1, n), jnp.int32)
    scalars = jnp.stack([key_starts, gaps, low * one, high * one, first * one])

    own_windows = list(
        windows(aligned(own_below, send_size), ranks, own_values, send_size, own_labels)
    )
    values = {0: own_windows[0]}
    for m in range(1, n):
        group = {min(2, n - 1): [1], n - 1: list(range(2, n))}.get(m)
        if group:
            *leaving, sums = lax.optimization_barrier((*(own_windows[d] for d in group), sums))
            for d, window in zip(group, leaving):
                values[d] = swap(window, d)
        sums, unit = first_block(me_array, keys[m], totals[m], cents, n, sums)
        units.append(unit)

    raw, part = raw_weights(sums, units)
    values[1], scalars, part = lax.optimization_barrier((values[1], scalars, part))
    parts = spread(part)
    so_far = place(scalars, labels, keys, values, [0, 1], key_size, cap, None)
    out = weighted_sums(raw, units, parts)
    placed = place(scalars, labels, keys, values, list(range(2, n)), key_size, cap, so_far)
    shape = (cap, heads, width)
    return out, placed[0].reshape(shape), placed[1].reshape(shape)


def solution(mesh):
    placed = (
        P(("grp", "ctx"), "head", None),
        P(("grp", "ctx"), "head", None),
        P("head", ("grp", "ctx")),
        P(("grp", "head"), None),
        P(("grp", "head"), None, None),
    )
    return jax.shard_map(
        body,
        mesh=mesh,
        in_specs=placed,
        out_specs=(
            P(("grp", "head"), "ctx", None),
            P(("grp", "ctx"), "head", None),
            P(("grp", "ctx"), "head", None),
        ),
        check_vma=False,
    )
```

```python
import functools
import math

import jax
import jax.numpy as jnp
from jax import lax
from jax.experimental import pallas as pl
from jax.experimental.pallas import tpu as pltpu
from jax.sharding import PartitionSpec as P

LANES = 128
EXP2_SCALE = 20.0 * math.log2(math.e)
VMEM_LIMIT = 16 * 1024 * 1024
F32 = jnp.float32
BF16 = jnp.bfloat16
NT = (((1,), (1,)), ((), ()))
NN = (((1,), (0,)), ((), ()))


def dot_nt(a, b):
    return lax.dot_general(a, b, NT, preferred_element_type=F32)


def dot_nn(a, b):
    return lax.dot_general(a, b, NN, preferred_element_type=F32)


def unit_rows(x):
    return x * lax.rsqrt(jnp.sum(x * x, axis=-1, keepdims=True) + 1e-06)


def params(**kwargs):
    return pltpu.CompilerParams(vmem_limit_bytes=VMEM_LIMIT, **kwargs)


def whole(shape):
    return pl.BlockSpec(shape, lambda *_: (0,) * len(shape))


def in_vmem():
    return pl.BlockSpec(memory_space=pltpu.VMEM)


def anywhere():
    return pl.BlockSpec(memory_space=pl.ANY)


def keep_hbm(x):
    return pltpu.with_memory_space_constraint(x, pltpu.HBM)


def keep_vmem(x):
    return pltpu.with_memory_space_constraint(x, pltpu.VMEM)


def row_to_lanes(row):
    return jnp.transpose(jnp.broadcast_to(row, (LANES, LANES)))


def split_heads(flat_ref, wide_ref):
    wide_ref[...] = flat_ref[...].astype(F32)


def head_rows(wide_ref, head, heads):
    if heads == 1:
        return wide_ref[...]
    return wide_ref[pl.Slice(head, wide_ref.shape[0] // heads, heads), :]


def count_below(all_ref, own_row, count):
    tokens = own_row.shape[1]
    mine = jnp.broadcast_to(own_row, (8, tokens))
    wide = 4 * LANES

    def step(i, total):
        row = all_ref[0, :, pl.ds(pl.multiple_of(i * wide, wide), wide)]
        for s in range(0, wide, LANES):
            column = row_to_lanes(row[:, s : s + LANES])
            for r in range(0, LANES, 8):
                other = jnp.tile(column[r : r + 8], (1, tokens // LANES))
                total += (other < mine).astype(jnp.int32)
        return total

    total = lax.fori_loop(
        0, count // wide, step, jnp.zeros((8, tokens), jnp.int32), unroll=True
    )
    return jnp.sum(total, axis=0, keepdims=True)


def one_hot_rows(size, spot):
    slots = lax.broadcasted_iota(jnp.int16, (size, spot.shape[1]), 0)
    return jnp.where(
        slots == spot.astype(jnp.int16), jnp.ones((), BF16), jnp.zeros((), BF16)
    )


def sort_kernel(label_hbm, keys_hbm, *refs):
    out_keys, out_labels, out_spots, flat_ref, wide_ref, order_ref, label_ref, sems = refs
    heads, tokens, _ = out_keys.shape
    label_copy = pltpu.make_async_copy(label_hbm, label_ref, sems.at[1])
    label_copy.start()
    copy = pltpu.make_async_copy(keys_hbm, flat_ref, sems.at[0])
    copy.start()
    label_copy.wait()
    labels = [label_ref[h : h + 1, :] for h in range(heads)]
    spots = []
    for h, label in enumerate(labels):
        order = label * tokens + lax.broadcasted_iota(jnp.int32, label.shape, 1)
        order_ref[0] = order
        spots.append(count_below(order_ref, order, tokens))
        out_spots[h] = spots[h]
    copy.wait()
    split_heads(flat_ref, wide_ref)
    rows = 512
    for h, label in enumerate(labels):
        keys = head_rows(wide_ref, h, heads).astype(BF16)
        digits = jnp.concatenate(
            [
                jnp.broadcast_to(label >> 6, (8, tokens)),
                jnp.broadcast_to(label & 63, (8, tokens)),
            ],
            axis=0,
        )
        digits = digits.astype(F32).astype(BF16)
        for r in range(0, tokens, rows):
            pick = one_hot_rows(rows, spots[h] - r)
            out_keys[h, r : r + rows] = dot_nn(pick, keys).astype(BF16)
            digit = dot_nt(digits, pick)
            out_labels[h, :, r : r + rows] = digit[0:1] * 64.0 + digit[8:9]


def sort_keys(labels, keys):
    heads, tokens = labels.shape
    flat, width = keys.shape
    return pl.pallas_call(
        sort_kernel,
        in_specs=[anywhere()] * 2,
        out_specs=(in_vmem(),) * 3,
        out_shape=(
            pltpu.VMEM((heads, tokens, width), BF16),
            pltpu.VMEM((heads, 1, tokens), F32),
            pltpu.VMEM((heads, 1, tokens), jnp.int32),
        ),
        scratch_shapes=[
            pltpu.VMEM((flat, width), BF16),
            pltpu.VMEM((flat, width), F32),
            pltpu.VMEM((1, 1, tokens), jnp.int32),
            pltpu.VMEM(labels.shape, jnp.int32),
            pltpu.SemaphoreType.DMA((2,)),
        ],
        compiler_params=params(),
        name="sort_keys",
    )(keep_hbm(labels), keep_hbm(keys))


def values_kernel(spot_ref, values_hbm, out_ref, flat_ref, wide_ref, sem):
    heads, _, tokens = spot_ref.shape
    copy = pltpu.make_async_copy(values_hbm, flat_ref, sem)
    copy.start()
    copy.wait()
    split_heads(flat_ref, wide_ref)
    rows = 512
    for h in range(heads):
        values = head_rows(wide_ref, h, heads).astype(BF16)
        for r in range(0, tokens, rows):
            pick = one_hot_rows(rows, spot_ref[h] - r)
            out_ref[h, r : r + rows] = dot_nn(pick, values).astype(BF16)


def sort_values(spots, values):
    heads, _, tokens = spots.shape
    flat, width = values.shape
    return pl.pallas_call(
        values_kernel,
        in_specs=[in_vmem(), anywhere()],
        out_specs=in_vmem(),
        out_shape=pltpu.VMEM((heads, tokens, width), BF16),
        scratch_shapes=[
            pltpu.VMEM((flat, width), BF16),
            pltpu.VMEM((flat, width), F32),
            pltpu.SemaphoreType.DMA,
        ],
        compiler_params=params(),
        name="sort_values",
    )(keep_vmem(spots), keep_hbm(values))


def windows_kernel(size, start_ref, rank_ref, values_ref, _, *out_refs):
    heads, tokens, _ = values_ref.shape
    for h in range(heads):
        rank = rank_ref[h].astype(jnp.int32)
        digits = [
            digit[:, t : t + LANES]
            for digit in (rank >> 7, rank & 127)
            for t in range(0, tokens, LANES)
        ]
        digits = jnp.concatenate(digits, axis=0).astype(F32).astype(BF16)
        for m, out_ref in enumerate(out_refs):
            start = pl.multiple_of(start_ref[h, m], 16)
            out_ref[h, :size] = values_ref[h, pl.ds(start, size), :]
            out_ref[h, size:] = digits


def windows(starts, ranks, values, size, after):
    heads, tokens, width = values.shape
    n = starts.shape[1]
    out = pltpu.VMEM((heads, size + 2 * tokens // LANES, width), BF16)
    return pl.pallas_call(
        functools.partial(windows_kernel, size),
        in_specs=[pl.BlockSpec(memory_space=pltpu.SMEM), in_vmem(), in_vmem(), in_vmem()],
        out_specs=(in_vmem(),) * n,
        out_shape=(out,) * n,
        compiler_params=params(),
        name="windows",
    )(starts, ranks, keep_vmem(values), keep_vmem(after))


def rank_kernel(me_ref, label_ref, rank_ref):
    n, tokens = label_ref.shape[1:]
    me = me_ref[0]
    own = label_ref[0, 0:1, :].astype(jnp.int32)
    rank = lax.broadcasted_iota(jnp.int32, own.shape, 1)
    for m in range(1, n):
        bar = own + ((me ^ m) < me).astype(jnp.int32)
        bar = jnp.broadcast_to(bar, (16, tokens)).astype(jnp.int16)
        count = jnp.zeros((16, tokens), BF16)
        for s in range(0, tokens, LANES):
            column = row_to_lanes(label_ref[0, m : m + 1, s : s + LANES])
            column = column.astype(jnp.int32).astype(jnp.int16)
            for r in range(0, LANES, 16):
                other = jnp.tile(column[r : r + 16], (1, tokens // LANES))
                count += jnp.where(other < bar, jnp.ones((), BF16), jnp.zeros((), BF16))
        rank += jnp.sum(count.astype(F32), axis=0, keepdims=True).astype(jnp.int32)
    rank_ref[0] = rank.astype(F32)


def own_ranks(me, labels):
    heads, n, tokens = labels.shape
    return pl.pallas_call(
        rank_kernel,
        grid=(heads,),
        in_specs=[
            pl.BlockSpec(memory_space=pltpu.SMEM),
            pl.BlockSpec((1, n, tokens), lambda h: (h, 0, 0)),
        ],
        out_specs=pl.BlockSpec((1, 1, tokens), lambda h: (h, 0, 0)),
        out_shape=jax.ShapeDtypeStruct((heads, 1, tokens), F32),
        compiler_params=params(),
        name="own_ranks",
    )(me, labels)


def totals_kernel(keys_ref, cent_ref, _, tot_ref, unit_ref, sum_ref):
    step = pl.program_id(1)
    tokens = unit_ref.shape[0]

    @pl.when(step == 0)
    def _():
        unit_ref[...] = unit_rows(keys_ref[pl.program_id(0)].astype(F32)).astype(BF16)
        sum_ref[...] = jnp.zeros_like(sum_ref)

    part = 256
    rows = min(1024, cent_ref.shape[1])
    for c in range(0, cent_ref.shape[1], rows):
        cent = unit_rows(cent_ref[0, c : c + rows]).astype(BF16)
        for t in range(0, tokens, part):
            raw = jnp.exp2(dot_nt(cent, unit_ref[t : t + part, :]) * EXP2_SCALE)
            sum_ref[:, t : t + part] += jnp.sum(raw.reshape(-1, 8, part), axis=0)

    @pl.when(step == pl.num_programs(1) - 1)
    def _():
        tot_ref[0] = jnp.sum(sum_ref[...], axis=0, keepdims=True)


def own_totals(keys, cents, after):
    heads, count, width = cents.shape
    tokens = keys.shape[1]
    rows = min(2048, count)
    return pl.pallas_call(
        totals_kernel,
        grid=(heads, count // rows),
        in_specs=[
            in_vmem(),
            pl.BlockSpec((1, rows, width), lambda h, c: (h, c, 0)),
            in_vmem(),
        ],
        out_specs=pl.BlockSpec((1, 1, tokens), lambda h, c: (h, 0, 0)),
        out_shape=jax.ShapeDtypeStruct((heads, 1, tokens), F32),
        scratch_shapes=[
            pltpu.VMEM((tokens, width), BF16),
            pltpu.VMEM((8, tokens), F32),
        ],
        compiler_params=params(),
        name="own_totals",
    )(keep_vmem(keys), keep_hbm(cents), after)


def scale_rows(unit, inverse, scaled_ref):
    for t in range(0, unit.shape[0], LANES):
        scaled_ref[t : t + LANES] = (
            unit[t : t + LANES, :].astype(F32) * row_to_lanes(inverse[:, t : t + LANES])
        ).astype(BF16)


def first_kernel(fresh, _, keys_ref, tot_ref, cent_in, *refs):
    head = pl.program_id(0)
    if fresh:
        sums_ref, unit_ref, cent_ref, scaled_ref = refs
        cent = unit_rows(cent_in[0]).astype(BF16)
        cent_ref[head] = cent
    else:
        _, sums_ref, unit_ref, scaled_ref = refs
        cent = cent_in[head]
    unit = unit_rows(keys_ref[head].astype(F32)).astype(BF16)
    unit_ref[head] = unit
    scale_rows(unit, 1.0 / tot_ref[0], scaled_ref)
    part = 256
    for t in range(0, unit.shape[0], part):
        raw = jnp.exp2(dot_nt(cent, unit[t : t + part, :]) * EXP2_SCALE)
        more = dot_nn(raw.astype(BF16), scaled_ref[t : t + part])
        if fresh and t == 0:
            sums_ref[head] = more
        else:
            sums_ref[head] += more


def first_block(me, keys, totals, cents, n, before):
    heads, tokens, width = keys.shape
    fresh = before is None
    rows = cents.shape[1] // n if fresh else cents.shape[1]
    in_specs = [
        in_vmem(),
        pl.BlockSpec((1, 1, tokens), lambda h, me: (h, 0, 0)),
    ]
    args = [me, keep_vmem(keys), totals]
    out_shape = [
        pltpu.VMEM((heads, rows, width), F32),
        pltpu.VMEM((heads, tokens, width), BF16),
    ]
    aliases = {}
    if fresh:
        in_specs.append(pl.BlockSpec((1, rows, width), lambda h, me: (h, me[0], 0)))
        args.append(keep_hbm(cents))
        out_shape.append(pltpu.VMEM((heads, rows, width), BF16))
    else:
        in_specs += [in_vmem(), in_vmem()]
        args += [keep_vmem(cents), keep_vmem(before)]
        aliases = {4: 0}
    return pl.pallas_call(
        functools.partial(first_kernel, fresh),
        grid_spec=pltpu.PrefetchScalarGridSpec(
            num_scalar_prefetch=1,
            grid=(heads,),
            in_specs=in_specs,
            out_specs=(in_vmem(),) * len(out_shape),
            scratch_shapes=[pltpu.VMEM((tokens, width), BF16)],
        ),
        out_shape=tuple(out_shape),
        input_output_aliases=aliases,
        compiler_params=params(),
        name="first_block",
    )(*args)


def raw_kernel(blocks, sums_ref, *refs):
    units = refs[:blocks]
    raw_ref, total_ref, cent_ref = refs[blocks:]
    head = pl.program_id(0)
    cent_ref[...] = unit_rows(sums_ref[head]).astype(BF16)
    part = 256
    start = 0
    for unit_ref in units:
        for t in range(0, unit_ref.shape[1], part):
            here = slice(start + t, start + t + part)
            raw = jnp.exp2(dot_nt(cent_ref[...], unit_ref[head, t : t + part, :]) * EXP2_SCALE)
            raw_ref[head, :, here] = raw.astype(BF16)
            total = jnp.sum(raw.reshape(-1, 8, part), axis=0)
            total_ref[0, :, here] = jnp.sum(total, axis=0, keepdims=True)
        start += unit_ref.shape[1]


def raw_weights(sums, units):
    heads, rows, width = sums.shape
    tokens = units[0].shape[1]
    count = tokens * len(units)
    return pl.pallas_call(
        functools.partial(raw_kernel, len(units)),
        grid=(heads,),
        in_specs=[in_vmem()] * (1 + len(units)),
        out_specs=(in_vmem(), pl.BlockSpec((1, 1, count), lambda h: (h, 0, 0))),
        out_shape=(
            pltpu.VMEM((heads, rows, count), BF16),
            jax.ShapeDtypeStruct((heads, 1, count), F32),
        ),
        scratch_shapes=[pltpu.VMEM((rows, width), BF16)],
        compiler_params=params(),
        name="raw_weights",
    )(keep_vmem(sums), *map(keep_vmem, units))


def sums_kernel(blocks, raw_ref, *refs):
    totals, units = refs[:blocks], refs[blocks : 2 * blocks]
    out_hbm, scaled_ref, result_ref, sems = refs[2 * blocks :]
    heads, tokens, _ = units[0].shape
    copies = []
    for h in range(heads):
        for m, unit_ref in enumerate(units):
            row_total = totals[0][h, :, m * tokens : (m + 1) * tokens]
            for d in range(1, blocks):
                peer = m ^ d
                row_total += totals[d][h, :, peer * tokens : (peer + 1) * tokens]
            here = slice(m * tokens, (m + 1) * tokens)
            scale_rows(unit_ref[h], 1.0 / row_total, scaled_ref.at[h, here])
        result_ref[h] = unit_rows(dot_nn(raw_ref[h], scaled_ref[h]))
        copies.append(pltpu.make_async_copy(result_ref.at[h], out_hbm.at[h], sems.at[h]))
        copies[-1].start()
    for copy in copies:
        copy.wait()


def weighted_sums(raw, units, totals):
    heads, rows, count = raw.shape
    width = units[0].shape[2]
    return pl.pallas_call(
        functools.partial(sums_kernel, len(units)),
        in_specs=[in_vmem()] * (1 + 2 * len(units)),
        out_specs=anywhere(),
        out_shape=jax.ShapeDtypeStruct((heads, rows, width), F32),
        scratch_shapes=[
            pltpu.VMEM((heads, count, width), BF16),
            pltpu.VMEM((heads, rows, width), F32),
            pltpu.SemaphoreType.DMA((heads,)),
        ],
        compiler_params=params(),
        name="weighted_sums",
    )(keep_vmem(raw), *map(keep_vmem, totals), *map(keep_vmem, units))


def fill_windows(ids, size, scalar_ref, label_ref, keys, values, rows_ref, near_ref):
    heads, tokens, width = keys[0].shape
    digit_rows = tokens // LANES
    sent = values[0].shape[1] - 2 * digit_rows
    rows_ref[:, :, width:] = jnp.zeros((heads, len(ids) * size, width), BF16)
    for h in range(heads):
        low, high, first = (scalar_ref[i, h, 0].astype(F32) for i in range(2, 5))
        for i, m in enumerate(ids):
            start = pl.multiple_of(scalar_ref[0, h, m], 16)
            gap = pl.multiple_of(scalar_ref[1, h, m], 16)
            here = i * size
            rows_ref[h, here : here + size, :width] = keys[i][h, pl.ds(start, size), :]
            rows_ref[h, pl.ds(here + gap, sent), width:] = values[i][h, :sent, :]
            digits = values[i][h, sent:, :].astype(F32)
            rank = digits[:digit_rows] * 128.0 + digits[digit_rows:]
            rank = jnp.concatenate([rank[r : r + 1] for r in range(digit_rows)], axis=1)
            label = label_ref[h, m : m + 1, :]
            mine = (label >= low) & (label < high)
            spot = jnp.where(mine, rank - first, -1.0).astype(jnp.int32)
            spot = pltpu.roll(spot, lax.rem(tokens - start, tokens), 1)
            near_ref[h, :, here : here + size] = spot[:, :size]


def place_kernel(ids, size, fresh, scalar_ref, label_ref, *refs):
    count = len(ids)
    keys, values, refs = refs[:count], refs[count : 2 * count], refs[2 * count :]
    if fresh:
        so_far_ref, rows_ref, near_ref = refs
    else:
        so_far_ref, *out_hbm, rows_ref, near_ref, mixed_ref, done_ref, sems = refs
    fill_windows(ids, size, scalar_ref, label_ref, keys, values, rows_ref, near_ref)
    heads, cap, both = so_far_ref.shape
    width = both // 2
    rows = 512
    copies = []
    for r in range(0, cap, rows):
        for h in range(heads):
            total = dot_nn(one_hot_rows(rows, near_ref[h] - r), rows_ref[h])
            if fresh:
                so_far_ref[h, r : r + rows] = total.astype(BF16)
                continue
            total += so_far_ref[h, r : r + rows].astype(F32)
            for side in range(2):
                mixed_ref[side, pl.Slice(h, rows, heads), :] = total[
                    :, side * width : (side + 1) * width
                ]
        if fresh:
            continue
        here = slice(r * heads, (r + rows) * heads)
        for side in range(2):
            done_ref[side, here] = mixed_ref[side].astype(BF16)
            copies.append(
                pltpu.make_async_copy(
                    done_ref.at[side, here], out_hbm[side].at[here], sems.at[len(copies)]
                )
            )
            copies[-1].start()
    for copy in copies:
        copy.wait()


def place(scalars, labels, keys, values, ids, size, cap, so_far):
    heads, _, width = keys[0].shape
    fresh = so_far is None
    moved = [x[m] for x in (keys, values) for m in ids]
    scratch = [
        pltpu.VMEM((heads, len(ids) * size, 2 * width), BF16),
        pltpu.VMEM((heads, 1, len(ids) * size), jnp.int32),
    ]
    if fresh:
        out_shape = pltpu.VMEM((heads, cap, 2 * width), BF16)
        out_specs = in_vmem()
    else:
        moved.append(so_far)
        out_shape = (jax.ShapeDtypeStruct((heads * cap, width), BF16),) * 2
        out_specs = (anywhere(), anywhere())
        scratch += [
            pltpu.VMEM((2, heads * 512, width), F32),
            pltpu.VMEM((2, heads * cap, width), BF16),
            pltpu.SemaphoreType.DMA((2 * cap // 512,)),
        ]
    return pl.pallas_call(
        functools.partial(place_kernel, ids, size, fresh),
        in_specs=[pl.BlockSpec(memory_space=pltpu.SMEM)] + [in_vmem()] * (1 + len(moved)),
        out_specs=out_specs,
        out_shape=out_shape,
        scratch_shapes=scratch,
        compiler_params=params(),
        name="place",
    )(scalars, labels, *map(keep_vmem, moved))


def body(key_rows, value_rows, cluster_labels, owner_bounds, init_centroids):
    n = lax.axis_size("ctx")
    me = lax.axis_index("ctx").astype(jnp.int32)
    tokens, heads, width = key_rows.shape
    cap = 2 * tokens
    slot = cap // n
    send_size = slot + 16
    key_size = min(tokens, -(-send_size // LANES) * LANES)

    def swap(x, d):
        return lax.ppermute(x, "ctx", [(i, i ^ d) for i in range(n)])

    def spread(x):
        return [x] + [swap(x, d) for d in range(1, n)]

    def aligned(start, size):
        return jnp.minimum(start // 16 * 16, tokens - size)

    me_array = me.reshape(1)
    own_keys, own_labels, own_spots = sort_keys(
        cluster_labels, key_rows.reshape(heads * tokens, width)
    )
    keys = {0: own_keys}
    d = 1
    while d < n:
        keys[d] = swap(own_keys, d)
        d *= 2
    pairs = [(i, i ^ 1) for i in range(lax.axis_size("head"))]
    word = lax.ppermute(own_labels[:, :, :LANES], "head", pairs)
    own_total = own_totals(own_keys, init_centroids, word)
    shared = spread(jnp.concatenate([own_total, own_labels], axis=1))
    totals = [own_total] + [x[:, 0:1] for x in shared[1:]]

    sums, unit, cents = first_block(me_array, own_keys, own_total, init_centroids, n, None)
    units = [unit]
    *came, sums = lax.optimization_barrier((*keys.values(), sums))
    keys = dict(zip(keys, came))
    for m in range(1, n):
        if m not in keys:
            keys[m] = swap(keys[m & (m - 1)], m & -m)
    keys = [keys[m] for m in range(n)]
    peer_low = jnp.take(owner_bounds, me ^ jnp.arange(n, dtype=jnp.int32), axis=1)
    own_below = jnp.sum((own_labels < peer_low[:, :, None]).astype(jnp.int32), axis=2)
    own_values = sort_values(own_spots, value_rows.reshape(heads * tokens, width))

    labels, sums = lax.optimization_barrier(
        (jnp.concatenate([x[:, -1:] for x in shared], axis=1), sums)
    )
    ranks = own_ranks(me_array, labels)
    low = lax.dynamic_slice_in_dim(owner_bounds, me, 1, 1)
    high = lax.dynamic_slice_in_dim(owner_bounds, me + 1, 1, 1)
    below = jnp.sum((labels < low[:, :, None]).astype(jnp.int32), axis=2)
    first = jnp.sum(below, axis=1, keepdims=True)
    key_starts = aligned(below, key_size)
    gaps = aligned(below, send_size) - key_starts
    one = jnp.ones((1, n), jnp.int32)
    scalars = jnp.stack([key_starts, gaps, low * one, high * one, first * one])

    own_windows = list(
        windows(aligned(own_below, send_size), ranks, own_values, send_size, own_labels)
    )
    late = [2]
    early = [d for d in range(1, n) if d not in late]
    values = {0: own_windows[0]}

    def leave(group, x):
        *leaving, x = lax.optimization_barrier((*(own_windows[d] for d in group), x))
        for d, window in zip(group, leaving):
            values[d] = swap(window, d)
        return x

    for m in range(1, n):
        if m == min(2, n - 1):
            sums = leave(early, sums)
        sums, unit = first_block(me_array, keys[m], totals[m], cents, n, sums)
        units.append(unit)
    sums = leave(late, sums)

    raw, part = raw_weights(sums, units)
    scalars, part = lax.optimization_barrier((scalars, part))
    parts = spread(part)
    so_far = place(scalars, labels, keys, values, [0, *early], key_size, cap, None)
    out = weighted_sums(raw, units, parts)
    placed = place(scalars, labels, keys, values, late, key_size, cap, so_far)
    shape = (cap, heads, width)
    return out, placed[0].reshape(shape), placed[1].reshape(shape)


def solution(mesh):
    placed = (
        P(("grp", "ctx"), "head", None),
        P(("grp", "ctx"), "head", None),
        P("head", ("grp", "ctx")),
        P(("grp", "head"), None),
        P(("grp", "head"), None, None),
    )
    return jax.shard_map(
        body,
        mesh=mesh,
        in_specs=placed,
        out_specs=(
            P(("grp", "head"), "ctx", None),
            P(("grp", "ctx"), "head", None),
            P(("grp", "ctx"), "head", None),
        ),
        check_vma=False,
    )
```

```python
import functools
import math

import jax
import jax.numpy as jnp
from jax import lax
from jax.experimental import pallas as pl
from jax.experimental.pallas import tpu as pltpu
from jax.sharding import PartitionSpec as P

LANES = 128
EXP2_SCALE = 20.0 * math.log2(math.e)
VMEM_LIMIT = 16 * 1024 * 1024
F32 = jnp.float32
BF16 = jnp.bfloat16
NT = (((1,), (1,)), ((), ()))
NN = (((1,), (0,)), ((), ()))


def dot_nt(a, b):
    return lax.dot_general(a, b, NT, preferred_element_type=F32)


def dot_nn(a, b):
    return lax.dot_general(a, b, NN, preferred_element_type=F32)


def unit_rows(x):
    return x * lax.rsqrt(jnp.sum(x * x, axis=-1, keepdims=True) + 1e-06)


def params(**kwargs):
    return pltpu.CompilerParams(vmem_limit_bytes=VMEM_LIMIT, **kwargs)


def whole(shape):
    return pl.BlockSpec(shape, lambda *_: (0,) * len(shape))


def in_vmem():
    return pl.BlockSpec(memory_space=pltpu.VMEM)


def anywhere():
    return pl.BlockSpec(memory_space=pl.ANY)


def keep_hbm(x):
    return pltpu.with_memory_space_constraint(x, pltpu.HBM)


def keep_vmem(x):
    return pltpu.with_memory_space_constraint(x, pltpu.VMEM)


def row_to_lanes(row):
    return jnp.transpose(jnp.broadcast_to(row, (LANES, LANES)))


def split_heads(flat_ref, wide_ref):
    wide_ref[...] = flat_ref[...].astype(F32)


def head_rows(wide_ref, head, heads):
    if heads == 1:
        return wide_ref[...]
    return wide_ref[pl.Slice(head, wide_ref.shape[0] // heads, heads), :]


def count_below(all_ref, own_row, count):
    tokens = own_row.shape[1]
    mine = jnp.broadcast_to(own_row, (8, tokens))
    wide = 4 * LANES

    def step(i, total):
        row = all_ref[0, :, pl.ds(pl.multiple_of(i * wide, wide), wide)]
        for s in range(0, wide, LANES):
            column = row_to_lanes(row[:, s : s + LANES])
            for r in range(0, LANES, 8):
                other = jnp.tile(column[r : r + 8], (1, tokens // LANES))
                total += (other < mine).astype(jnp.int32)
        return total

    total = lax.fori_loop(
        0, count // wide, step, jnp.zeros((8, tokens), jnp.int32), unroll=True
    )
    return jnp.sum(total, axis=0, keepdims=True)


def one_hot_rows(size, spot):
    slots = lax.broadcasted_iota(jnp.int16, (size, spot.shape[1]), 0)
    return jnp.where(
        slots == spot.astype(jnp.int16), jnp.ones((), BF16), jnp.zeros((), BF16)
    )


def sort_kernel(label_hbm, keys_hbm, *refs):
    out_keys, out_labels, out_spots, flat_ref, wide_ref, order_ref, label_ref, sems = refs
    heads, tokens, _ = out_keys.shape
    label_copy = pltpu.make_async_copy(label_hbm, label_ref, sems.at[1])
    label_copy.start()
    copy = pltpu.make_async_copy(keys_hbm, flat_ref, sems.at[0])
    copy.start()
    label_copy.wait()
    labels = [label_ref[h : h + 1, :] for h in range(heads)]
    spots = []
    for h, label in enumerate(labels):
        order = label * tokens + lax.broadcasted_iota(jnp.int32, label.shape, 1)
        order_ref[0] = order
        spots.append(count_below(order_ref, order, tokens))
        out_spots[h] = spots[h]
    copy.wait()
    split_heads(flat_ref, wide_ref)
    rows = 512
    for h, label in enumerate(labels):
        keys = head_rows(wide_ref, h, heads).astype(BF16)
        digits = jnp.concatenate(
            [
                jnp.broadcast_to(label >> 6, (8, tokens)),
                jnp.broadcast_to(label & 63, (8, tokens)),
            ],
            axis=0,
        )
        digits = digits.astype(F32).astype(BF16)
        for r in range(0, tokens, rows):
            pick = one_hot_rows(rows, spots[h] - r)
            out_keys[h, r : r + rows] = dot_nn(pick, keys).astype(BF16)
            digit = dot_nt(digits, pick)
            out_labels[h, :, r : r + rows] = digit[0:1] * 64.0 + digit[8:9]


def sort_keys(labels, keys):
    heads, tokens = labels.shape
    flat, width = keys.shape
    return pl.pallas_call(
        sort_kernel,
        in_specs=[anywhere()] * 2,
        out_specs=(in_vmem(),) * 3,
        out_shape=(
            pltpu.VMEM((heads, tokens, width), BF16),
            pltpu.VMEM((heads, 1, tokens), F32),
            pltpu.VMEM((heads, 1, tokens), jnp.int32),
        ),
        scratch_shapes=[
            pltpu.VMEM((flat, width), BF16),
            pltpu.VMEM((flat, width), F32),
            pltpu.VMEM((1, 1, tokens), jnp.int32),
            pltpu.VMEM(labels.shape, jnp.int32),
            pltpu.SemaphoreType.DMA((2,)),
        ],
        compiler_params=params(),
        name="sort_keys",
    )(keep_hbm(labels), keep_hbm(keys))


def values_kernel(spot_ref, values_hbm, out_ref, flat_ref, wide_ref, sem):
    heads, _, tokens = spot_ref.shape
    copy = pltpu.make_async_copy(values_hbm, flat_ref, sem)
    copy.start()
    copy.wait()
    split_heads(flat_ref, wide_ref)
    rows = 512
    for h in range(heads):
        values = head_rows(wide_ref, h, heads).astype(BF16)
        for r in range(0, tokens, rows):
            pick = one_hot_rows(rows, spot_ref[h] - r)
            out_ref[h, r : r + rows] = dot_nn(pick, values).astype(BF16)


def sort_values(spots, values):
    heads, _, tokens = spots.shape
    flat, width = values.shape
    return pl.pallas_call(
        values_kernel,
        in_specs=[in_vmem(), anywhere()],
        out_specs=in_vmem(),
        out_shape=pltpu.VMEM((heads, tokens, width), BF16),
        scratch_shapes=[
            pltpu.VMEM((flat, width), BF16),
            pltpu.VMEM((flat, width), F32),
            pltpu.SemaphoreType.DMA,
        ],
        compiler_params=params(),
        name="sort_values",
    )(keep_vmem(spots), keep_hbm(values))


def windows_kernel(size, start_ref, rank_ref, values_ref, _, *out_refs):
    heads, tokens, _ = values_ref.shape
    for h in range(heads):
        rank = rank_ref[h].astype(jnp.int32)
        digits = [
            digit[:, t : t + LANES]
            for digit in (rank >> 7, rank & 127)
            for t in range(0, tokens, LANES)
        ]
        digits = jnp.concatenate(digits, axis=0).astype(F32).astype(BF16)
        for m, out_ref in enumerate(out_refs):
            start = pl.multiple_of(start_ref[h, m], 16)
            out_ref[h, :size] = values_ref[h, pl.ds(start, size), :]
            out_ref[h, size:] = digits


def windows(starts, ranks, values, size, after):
    heads, tokens, width = values.shape
    n = starts.shape[1]
    out = pltpu.VMEM((heads, size + 2 * tokens // LANES, width), BF16)
    return pl.pallas_call(
        functools.partial(windows_kernel, size),
        in_specs=[pl.BlockSpec(memory_space=pltpu.SMEM), in_vmem(), in_vmem(), in_vmem()],
        out_specs=(in_vmem(),) * n,
        out_shape=(out,) * n,
        compiler_params=params(),
        name="windows",
    )(starts, ranks, keep_vmem(values), keep_vmem(after))


def rank_kernel(me_ref, label_ref, rank_ref):
    n, tokens = label_ref.shape[1:]
    me = me_ref[0]
    own = label_ref[0, 0:1, :].astype(jnp.int32)
    rank = lax.broadcasted_iota(jnp.int32, own.shape, 1)
    for m in range(1, n):
        bar = own + ((me ^ m) < me).astype(jnp.int32)
        bar = jnp.broadcast_to(bar, (16, tokens)).astype(jnp.int16)
        count = jnp.zeros((16, tokens), BF16)
        for s in range(0, tokens, LANES):
            column = row_to_lanes(label_ref[0, m : m + 1, s : s + LANES])
            column = column.astype(jnp.int32).astype(jnp.int16)
            for r in range(0, LANES, 16):
                other = jnp.tile(column[r : r + 16], (1, tokens // LANES))
                count += jnp.where(other < bar, jnp.ones((), BF16), jnp.zeros((), BF16))
        rank += jnp.sum(count.astype(F32), axis=0, keepdims=True).astype(jnp.int32)
    rank_ref[0] = rank.astype(F32)


def own_ranks(me, labels):
    heads, n, tokens = labels.shape
    return pl.pallas_call(
        rank_kernel,
        grid=(heads,),
        in_specs=[
            pl.BlockSpec(memory_space=pltpu.SMEM),
            pl.BlockSpec((1, n, tokens), lambda h: (h, 0, 0)),
        ],
        out_specs=pl.BlockSpec((1, 1, tokens), lambda h: (h, 0, 0)),
        out_shape=jax.ShapeDtypeStruct((heads, 1, tokens), F32),
        compiler_params=params(),
        name="own_ranks",
    )(me, labels)


def totals_kernel(keys_ref, cent_ref, _, tot_ref, unit_ref, sum_ref):
    step = pl.program_id(1)
    tokens = unit_ref.shape[0]

    @pl.when(step == 0)
    def _():
        unit_ref[...] = unit_rows(keys_ref[pl.program_id(0)].astype(F32)).astype(BF16)
        sum_ref[...] = jnp.zeros_like(sum_ref)

    part = 256
    rows = min(1024, cent_ref.shape[1])
    for c in range(0, cent_ref.shape[1], rows):
        cent = unit_rows(cent_ref[0, c : c + rows]).astype(BF16)
        for t in range(0, tokens, part):
            raw = jnp.exp2(dot_nt(cent, unit_ref[t : t + part, :]) * EXP2_SCALE)
            sum_ref[:, t : t + part] += jnp.sum(raw.reshape(-1, 8, part), axis=0)

    @pl.when(step == pl.num_programs(1) - 1)
    def _():
        tot_ref[0] = jnp.sum(sum_ref[...], axis=0, keepdims=True)


def own_totals(keys, cents, after):
    heads, count, width = cents.shape
    tokens = keys.shape[1]
    rows = min(2048, count)
    return pl.pallas_call(
        totals_kernel,
        grid=(heads, count // rows),
        in_specs=[
            in_vmem(),
            pl.BlockSpec((1, rows, width), lambda h, c: (h, c, 0)),
            in_vmem(),
        ],
        out_specs=pl.BlockSpec((1, 1, tokens), lambda h, c: (h, 0, 0)),
        out_shape=jax.ShapeDtypeStruct((heads, 1, tokens), F32),
        scratch_shapes=[
            pltpu.VMEM((tokens, width), BF16),
            pltpu.VMEM((8, tokens), F32),
        ],
        compiler_params=params(),
        name="own_totals",
    )(keep_vmem(keys), keep_hbm(cents), after)


def scale_rows(unit, inverse, scaled_ref):
    for t in range(0, unit.shape[0], LANES):
        scaled_ref[t : t + LANES] = (
            unit[t : t + LANES, :].astype(F32) * row_to_lanes(inverse[:, t : t + LANES])
        ).astype(BF16)


def first_kernel(fresh, _, keys_ref, tot_ref, cent_in, *refs):
    head = pl.program_id(0)
    if fresh:
        sums_ref, unit_ref, cent_ref, scaled_ref = refs
        cent = unit_rows(cent_in[0]).astype(BF16)
        cent_ref[head] = cent
    else:
        _, sums_ref, unit_ref, scaled_ref = refs
        cent = cent_in[head]
    unit = unit_rows(keys_ref[head].astype(F32)).astype(BF16)
    unit_ref[head] = unit
    scale_rows(unit, 1.0 / tot_ref[0], scaled_ref)
    part = 256
    for t in range(0, unit.shape[0], part):
        raw = jnp.exp2(dot_nt(cent, unit[t : t + part, :]) * EXP2_SCALE)
        more = dot_nn(raw.astype(BF16), scaled_ref[t : t + part])
        if fresh and t == 0:
            sums_ref[head] = more
        else:
            sums_ref[head] += more


def first_block(me, keys, totals, cents, n, before):
    heads, tokens, width = keys.shape
    fresh = before is None
    rows = cents.shape[1] // n if fresh else cents.shape[1]
    in_specs = [
        in_vmem(),
        pl.BlockSpec((1, 1, tokens), lambda h, me: (h, 0, 0)),
    ]
    args = [me, keep_vmem(keys), totals]
    out_shape = [
        pltpu.VMEM((heads, rows, width), F32),
        pltpu.VMEM((heads, tokens, width), BF16),
    ]
    aliases = {}
    if fresh:
        in_specs.append(pl.BlockSpec((1, rows, width), lambda h, me: (h, me[0], 0)))
        args.append(keep_hbm(cents))
        out_shape.append(pltpu.VMEM((heads, rows, width), BF16))
    else:
        in_specs += [in_vmem(), in_vmem()]
        args += [keep_vmem(cents), keep_vmem(before)]
        aliases = {4: 0}
    return pl.pallas_call(
        functools.partial(first_kernel, fresh),
        grid_spec=pltpu.PrefetchScalarGridSpec(
            num_scalar_prefetch=1,
            grid=(heads,),
            in_specs=in_specs,
            out_specs=(in_vmem(),) * len(out_shape),
            scratch_shapes=[pltpu.VMEM((tokens, width), BF16)],
        ),
        out_shape=tuple(out_shape),
        input_output_aliases=aliases,
        compiler_params=params(),
        name="first_block",
    )(*args)


def raw_kernel(blocks, sums_ref, *refs):
    units = refs[:blocks]
    raw_ref, total_ref, cent_ref = refs[blocks:]
    head = pl.program_id(0)
    cent_ref[...] = unit_rows(sums_ref[head]).astype(BF16)
    part = 256
    start = 0
    for unit_ref in units:
        for t in range(0, unit_ref.shape[1], part):
            here = slice(start + t, start + t + part)
            raw = jnp.exp2(dot_nt(cent_ref[...], unit_ref[head, t : t + part, :]) * EXP2_SCALE)
            raw_ref[head, :, here] = raw.astype(BF16)
            total = jnp.sum(raw.reshape(-1, 8, part), axis=0)
            total_ref[0, :, here] = jnp.sum(total, axis=0, keepdims=True)
        start += unit_ref.shape[1]


def raw_weights(sums, units):
    heads, rows, width = sums.shape
    tokens = units[0].shape[1]
    count = tokens * len(units)
    return pl.pallas_call(
        functools.partial(raw_kernel, len(units)),
        grid=(heads,),
        in_specs=[in_vmem()] * (1 + len(units)),
        out_specs=(in_vmem(), pl.BlockSpec((1, 1, count), lambda h: (h, 0, 0))),
        out_shape=(
            pltpu.VMEM((heads, rows, count), BF16),
            jax.ShapeDtypeStruct((heads, 1, count), F32),
        ),
        scratch_shapes=[pltpu.VMEM((rows, width), BF16)],
        compiler_params=params(),
        name="raw_weights",
    )(keep_vmem(sums), *map(keep_vmem, units))


def sums_kernel(blocks, raw_ref, *refs):
    totals, units = refs[:blocks], refs[blocks : 2 * blocks]
    out_hbm, scaled_ref, result_ref, sems = refs[2 * blocks :]
    heads, tokens, _ = units[0].shape
    copies = []
    for h in range(heads):
        for m, unit_ref in enumerate(units):
            row_total = totals[0][h, :, m * tokens : (m + 1) * tokens]
            for d in range(1, blocks):
                peer = m ^ d
                row_total += totals[d][h, :, peer * tokens : (peer + 1) * tokens]
            here = slice(m * tokens, (m + 1) * tokens)
            scale_rows(unit_ref[h], 1.0 / row_total, scaled_ref.at[h, here])
        result_ref[h] = unit_rows(dot_nn(raw_ref[h], scaled_ref[h]))
        copies.append(pltpu.make_async_copy(result_ref.at[h], out_hbm.at[h], sems.at[h]))
        copies[-1].start()
    for copy in copies:
        copy.wait()


def weighted_sums(raw, units, totals):
    heads, rows, count = raw.shape
    width = units[0].shape[2]
    return pl.pallas_call(
        functools.partial(sums_kernel, len(units)),
        in_specs=[in_vmem()] * (1 + 2 * len(units)),
        out_specs=anywhere(),
        out_shape=jax.ShapeDtypeStruct((heads, rows, width), F32),
        scratch_shapes=[
            pltpu.VMEM((heads, count, width), BF16),
            pltpu.VMEM((heads, rows, width), F32),
            pltpu.SemaphoreType.DMA((heads,)),
        ],
        compiler_params=params(),
        name="weighted_sums",
    )(keep_vmem(raw), *map(keep_vmem, totals), *map(keep_vmem, units))


def fill_windows(ids, size, scalar_ref, label_ref, keys, values, rows_ref, near_ref):
    heads, tokens, width = keys[0].shape
    digit_rows = tokens // LANES
    one = values[0][0] if isinstance(values[0], list) else values[0]
    sent = one.shape[1] - 2 * digit_rows
    rows_ref[:, :, width:] = jnp.zeros((heads, len(ids) * size, width), BF16)
    for h in range(heads):
        low, high, first = (scalar_ref[i, h, 0].astype(F32) for i in range(2, 5))
        for i, m in enumerate(ids):
            start = pl.multiple_of(scalar_ref[0, h, m], 16)
            gap = pl.multiple_of(scalar_ref[1, h, m], 16)
            here = i * size
            rows_ref[h, here : here + size, :width] = keys[i][h, pl.ds(start, size), :]
            value = values[i][h][0] if isinstance(values[i], list) else values[i][h]
            rows_ref[h, pl.ds(here + gap, sent), width:] = value[:sent]
            digits = value[sent:].astype(F32)
            rank = digits[:digit_rows] * 128.0 + digits[digit_rows:]
            rank = jnp.concatenate([rank[r : r + 1] for r in range(digit_rows)], axis=1)
            label = label_ref[h, m : m + 1, :]
            mine = (label >= low) & (label < high)
            spot = jnp.where(mine, rank - first, -1.0).astype(jnp.int32)
            spot = pltpu.roll(spot, lax.rem(tokens - start, tokens), 1)
            near_ref[h, :, here : here + size] = spot[:, :size]


def place_kernel(ids, size, fresh, scalar_ref, label_ref, *refs):
    count = len(ids)
    keys, refs = refs[:count], refs[count:]
    if fresh:
        values, refs = refs[:count], refs[count:]
    else:
        heads = keys[0].shape[0]
        values, refs = [list(refs[:heads])], refs[heads:]
    if fresh:
        so_far_ref, rows_ref, near_ref = refs
    else:
        so_far_ref, *out_hbm, rows_ref, near_ref, mixed_ref, done_ref, sems = refs
    fill_windows(ids, size, scalar_ref, label_ref, keys, values, rows_ref, near_ref)
    heads, cap, both = so_far_ref.shape
    width = both // 2
    rows = 1024 if fresh else 512
    copies = []
    for r in range(0, cap, rows):
        for h in range(heads):
            total = dot_nn(one_hot_rows(rows, near_ref[h] - r), rows_ref[h])
            if fresh:
                so_far_ref[h, r : r + rows] = total.astype(BF16)
                continue
            total += so_far_ref[h, r : r + rows].astype(F32)
            for side in range(2):
                mixed_ref[side, pl.Slice(h, rows, heads), :] = total[
                    :, side * width : (side + 1) * width
                ]
        if fresh:
            continue
        here = slice(r * heads, (r + rows) * heads)
        for side in range(2):
            done_ref[side, here] = mixed_ref[side].astype(BF16)
            copies.append(
                pltpu.make_async_copy(
                    done_ref.at[side, here], out_hbm[side].at[here], sems.at[len(copies)]
                )
            )
            copies[-1].start()
    for copy in copies:
        copy.wait()


def place(scalars, labels, keys, values, ids, size, cap, so_far):
    heads, _, width = keys[0].shape
    fresh = so_far is None
    moved = [keys[m] for m in ids] + ([values[m] for m in ids] if fresh else values[ids[0]])
    scratch = [
        pltpu.VMEM((heads, len(ids) * size, 2 * width), BF16),
        pltpu.VMEM((heads, 1, len(ids) * size), jnp.int32),
    ]
    if fresh:
        out_shape = pltpu.VMEM((heads, cap, 2 * width), BF16)
        out_specs = in_vmem()
    else:
        moved.append(so_far)
        out_shape = (jax.ShapeDtypeStruct((heads * cap, width), BF16),) * 2
        out_specs = (anywhere(), anywhere())
        scratch += [
            pltpu.VMEM((2, heads * 512, width), F32),
            pltpu.VMEM((2, heads * cap, width), BF16),
            pltpu.SemaphoreType.DMA((2 * cap // 512,)),
        ]
    return pl.pallas_call(
        functools.partial(place_kernel, ids, size, fresh),
        in_specs=[pl.BlockSpec(memory_space=pltpu.SMEM)] + [in_vmem()] * (1 + len(moved)),
        out_specs=out_specs,
        out_shape=out_shape,
        scratch_shapes=scratch,
        compiler_params=params(),
        name="place",
    )(scalars, labels, *map(keep_vmem, moved))


def body(key_rows, value_rows, cluster_labels, owner_bounds, init_centroids):
    n = lax.axis_size("ctx")
    me = lax.axis_index("ctx").astype(jnp.int32)
    tokens, heads, width = key_rows.shape
    cap = 2 * tokens
    slot = cap // n
    send_size = slot + 16
    key_size = min(tokens, -(-send_size // LANES) * LANES)

    def swap(x, d):
        return lax.ppermute(x, "ctx", [(i, i ^ d) for i in range(n)])

    def spread(x):
        return [x] + [swap(x, d) for d in range(1, n)]

    def aligned(start, size):
        return jnp.minimum(start // 16 * 16, tokens - size)

    me_array = me.reshape(1)
    own_keys, own_labels, own_spots = sort_keys(
        cluster_labels, key_rows.reshape(heads * tokens, width)
    )
    keys = {0: own_keys}
    d = 1
    while d < n:
        keys[d] = swap(own_keys, d)
        d *= 2
    pairs = [(i, i ^ 1) for i in range(lax.axis_size("head"))]
    word = lax.ppermute(own_labels[:, :, :LANES], "head", pairs)
    own_total = own_totals(own_keys, init_centroids, word)
    shared = spread(jnp.concatenate([own_total, own_labels], axis=1))
    totals = [own_total] + [x[:, 0:1] for x in shared[1:]]

    sums, unit, cents = first_block(me_array, own_keys, own_total, init_centroids, n, None)
    units = [unit]
    *came, sums = lax.optimization_barrier((*keys.values(), sums))
    keys = dict(zip(keys, came))
    for m in range(1, n):
        if m not in keys:
            keys[m] = swap(keys[m & (m - 1)], m & -m)
    keys = [keys[m] for m in range(n)]
    peer_low = jnp.take(owner_bounds, me ^ jnp.arange(n, dtype=jnp.int32), axis=1)
    own_below = jnp.sum((own_labels < peer_low[:, :, None]).astype(jnp.int32), axis=2)
    own_values = sort_values(own_spots, value_rows.reshape(heads * tokens, width))

    labels, sums = lax.optimization_barrier(
        (jnp.concatenate([x[:, -1:] for x in shared], axis=1), sums)
    )
    ranks = own_ranks(me_array, labels)
    low = lax.dynamic_slice_in_dim(owner_bounds, me, 1, 1)
    high = lax.dynamic_slice_in_dim(owner_bounds, me + 1, 1, 1)
    below = jnp.sum((labels < low[:, :, None]).astype(jnp.int32), axis=2)
    first = jnp.sum(below, axis=1, keepdims=True)
    key_starts = aligned(below, key_size)
    gaps = aligned(below, send_size) - key_starts
    one = jnp.ones((1, n), jnp.int32)
    scalars = jnp.stack([key_starts, gaps, low * one, high * one, first * one])

    own_windows = list(
        windows(aligned(own_below, send_size), ranks, own_values, send_size, own_labels)
    )
    late = [2]
    early = [d for d in range(1, n) if d not in late]
    values = {0: own_windows[0]}

    def leave(group, x):
        *leaving, x = lax.optimization_barrier((*(own_windows[d] for d in group), x))
        for d, window in zip(group, leaving):
            values[d] = swap(window, d)
        return x

    for m in range(1, n):
        if m == min(2, n - 1):
            sums = leave(early, sums)
        sums, unit = first_block(me_array, keys[m], totals[m], cents, n, sums)
        units.append(unit)
    pieces = [own_windows[late[0]][h : h + 1] for h in range(heads)]
    pieces[0], sums = lax.optimization_barrier((pieces[0], sums))
    values[late[0]] = [swap(pieces[0], late[0])]

    raw, part = raw_weights(sums, units)
    scalars, part = lax.optimization_barrier((scalars, part))
    parts = spread(part)
    *parts, pieces[-1] = lax.optimization_barrier((*parts, pieces[-1]))
    values[late[0]] += [swap(piece, late[0]) for piece in pieces[1:]]
    so_far = place(scalars, labels, keys, values, [0, *early], key_size, cap, None)
    out = weighted_sums(raw, units, parts)
    placed = place(scalars, labels, keys, values, late, key_size, cap, so_far)
    shape = (cap, heads, width)
    return out, placed[0].reshape(shape), placed[1].reshape(shape)


def solution(mesh):
    placed = (
        P(("grp", "ctx"), "head", None),
        P(("grp", "ctx"), "head", None),
        P("head", ("grp", "ctx")),
        P(("grp", "head"), None),
        P(("grp", "head"), None, None),
    )
    return jax.shard_map(
        body,
        mesh=mesh,
        in_specs=placed,
        out_specs=(
            P(("grp", "head"), "ctx", None),
            P(("grp", "ctx"), "head", None),
            P(("grp", "ctx"), "head", None),
        ),
        check_vma=False,
    )
```

```python
import functools
import math

import jax
import jax.numpy as jnp
from jax import lax
from jax.experimental import pallas as pl
from jax.experimental.pallas import tpu as pltpu
from jax.sharding import PartitionSpec as P

LANES = 128
EXP2_SCALE = 20.0 * math.log2(math.e)
VMEM_LIMIT = 16 * 1024 * 1024
F32 = jnp.float32
BF16 = jnp.bfloat16
NT = (((1,), (1,)), ((), ()))
NN = (((1,), (0,)), ((), ()))


def dot_nt(a, b):
    return lax.dot_general(a, b, NT, preferred_element_type=F32)


def dot_nn(a, b):
    return lax.dot_general(a, b, NN, preferred_element_type=F32)


def unit_rows(x):
    return x * lax.rsqrt(jnp.sum(x * x, axis=-1, keepdims=True) + 1e-06)


def two_terms(cent):
    scaled = cent.astype(F32) * EXP2_SCALE
    high = scaled.astype(BF16)
    return jnp.concatenate([high, (scaled - high.astype(F32)).astype(BF16)], axis=1)


def params(**kwargs):
    return pltpu.CompilerParams(vmem_limit_bytes=VMEM_LIMIT, **kwargs)


def whole(shape):
    return pl.BlockSpec(shape, lambda *_: (0,) * len(shape))


def in_vmem():
    return pl.BlockSpec(memory_space=pltpu.VMEM)


def anywhere():
    return pl.BlockSpec(memory_space=pl.ANY)


def keep_hbm(x):
    return pltpu.with_memory_space_constraint(x, pltpu.HBM)


def keep_vmem(x):
    return pltpu.with_memory_space_constraint(x, pltpu.VMEM)


def row_to_lanes(row):
    return jnp.transpose(jnp.broadcast_to(row, (LANES, LANES)))


def split_heads(flat_ref, wide_ref):
    wide_ref[...] = flat_ref[...].astype(F32)


def head_rows(wide_ref, head, heads):
    if heads == 1:
        return wide_ref[...]
    return wide_ref[pl.Slice(head, wide_ref.shape[0] // heads, heads), :]


def count_below(all_ref, own_row, count):
    tokens = own_row.shape[1]
    mine = jnp.broadcast_to(own_row, (8, tokens))
    wide = 4 * LANES

    def step(i, total):
        row = all_ref[0, :, pl.ds(pl.multiple_of(i * wide, wide), wide)]
        for s in range(0, wide, LANES):
            column = row_to_lanes(row[:, s : s + LANES])
            for r in range(0, LANES, 8):
                other = jnp.tile(column[r : r + 8], (1, tokens // LANES))
                total += (other < mine).astype(jnp.int32)
        return total

    total = lax.fori_loop(
        0, count // wide, step, jnp.zeros((8, tokens), jnp.int32), unroll=True
    )
    return jnp.sum(total, axis=0, keepdims=True)


def one_hot_rows(size, spot):
    slots = lax.broadcasted_iota(jnp.int16, (size, spot.shape[1]), 0)
    return jnp.where(
        slots == spot.astype(jnp.int16), jnp.ones((), BF16), jnp.zeros((), BF16)
    )


def sort_kernel(label_hbm, keys_hbm, *refs):
    out_keys, out_labels, out_spots, flat_ref, wide_ref, order_ref, label_ref, sems = refs
    heads, tokens, _ = out_keys.shape
    label_copy = pltpu.make_async_copy(label_hbm, label_ref, sems.at[1])
    label_copy.start()
    copy = pltpu.make_async_copy(keys_hbm, flat_ref, sems.at[0])
    copy.start()
    label_copy.wait()
    labels = [label_ref[h : h + 1, :] for h in range(heads)]
    spots = []
    for h, label in enumerate(labels):
        order = label * tokens + lax.broadcasted_iota(jnp.int32, label.shape, 1)
        order_ref[0] = order
        spots.append(count_below(order_ref, order, tokens))
        out_spots[h] = spots[h]
    copy.wait()
    split_heads(flat_ref, wide_ref)
    rows = 512
    for h, label in enumerate(labels):
        keys = head_rows(wide_ref, h, heads).astype(BF16)
        digits = jnp.concatenate(
            [
                jnp.broadcast_to(label >> 6, (8, tokens)),
                jnp.broadcast_to(label & 63, (8, tokens)),
            ],
            axis=0,
        )
        digits = digits.astype(F32).astype(BF16)
        for r in range(0, tokens, rows):
            pick = one_hot_rows(rows, spots[h] - r)
            out_keys[h, r : r + rows] = dot_nn(pick, keys).astype(BF16)
            digit = dot_nt(digits, pick)
            out_labels[h, :, r : r + rows] = digit[0:1] * 64.0 + digit[8:9]


def sort_keys(labels, keys):
    heads, tokens = labels.shape
    flat, width = keys.shape
    return pl.pallas_call(
        sort_kernel,
        in_specs=[anywhere()] * 2,
        out_specs=(in_vmem(),) * 3,
        out_shape=(
            pltpu.VMEM((heads, tokens, width), BF16),
            pltpu.VMEM((heads, 1, tokens), F32),
            pltpu.VMEM((heads, 1, tokens), jnp.int32),
        ),
        scratch_shapes=[
            pltpu.VMEM((flat, width), BF16),
            pltpu.VMEM((flat, width), F32),
            pltpu.VMEM((1, 1, tokens), jnp.int32),
            pltpu.VMEM(labels.shape, jnp.int32),
            pltpu.SemaphoreType.DMA((2,)),
        ],
        compiler_params=params(),
        name="sort_keys",
    )(keep_hbm(labels), keep_hbm(keys))


def values_kernel(spot_ref, values_hbm, out_ref, flat_ref, wide_ref, sem):
    heads, _, tokens = spot_ref.shape
    copy = pltpu.make_async_copy(values_hbm, flat_ref, sem)
    copy.start()
    copy.wait()
    split_heads(flat_ref, wide_ref)
    rows = 512
    for h in range(heads):
        values = head_rows(wide_ref, h, heads).astype(BF16)
        for r in range(0, tokens, rows):
            pick = one_hot_rows(rows, spot_ref[h] - r)
            out_ref[h, r : r + rows] = dot_nn(pick, values).astype(BF16)


def sort_values(spots, values):
    heads, _, tokens = spots.shape
    flat, width = values.shape
    return pl.pallas_call(
        values_kernel,
        in_specs=[in_vmem(), anywhere()],
        out_specs=in_vmem(),
        out_shape=pltpu.VMEM((heads, tokens, width), BF16),
        scratch_shapes=[
            pltpu.VMEM((flat, width), BF16),
            pltpu.VMEM((flat, width), F32),
            pltpu.SemaphoreType.DMA,
        ],
        compiler_params=params(),
        name="sort_values",
    )(keep_vmem(spots), keep_hbm(values))


def windows_kernel(size, start_ref, rank_ref, values_ref, _, *out_refs):
    heads, tokens, _ = values_ref.shape
    for h in range(heads):
        rank = rank_ref[h].astype(jnp.int32)
        digits = [
            digit[:, t : t + LANES]
            for digit in (rank >> 7, rank & 127)
            for t in range(0, tokens, LANES)
        ]
        digits = jnp.concatenate(digits, axis=0).astype(F32).astype(BF16)
        for m, out_ref in enumerate(out_refs):
            start = pl.multiple_of(start_ref[h, m], 16)
            out_ref[h, :size] = values_ref[h, pl.ds(start, size), :]
            out_ref[h, size:] = digits


def windows(starts, ranks, values, size, after):
    heads, tokens, width = values.shape
    n = starts.shape[1]
    out = pltpu.VMEM((heads, size + 2 * tokens // LANES, width), BF16)
    return pl.pallas_call(
        functools.partial(windows_kernel, size),
        in_specs=[pl.BlockSpec(memory_space=pltpu.SMEM), in_vmem(), in_vmem(), in_vmem()],
        out_specs=(in_vmem(),) * n,
        out_shape=(out,) * n,
        compiler_params=params(),
        name="windows",
    )(starts, ranks, keep_vmem(values), keep_vmem(after))


def rank_kernel(me_ref, label_ref, rank_ref):
    n, tokens = label_ref.shape[1:]
    me = me_ref[0]
    own = label_ref[0, 0:1, :].astype(jnp.int32)
    rank = lax.broadcasted_iota(jnp.int32, own.shape, 1)
    for m in range(1, n):
        bar = own + ((me ^ m) < me).astype(jnp.int32)
        bar = jnp.broadcast_to(bar, (16, tokens)).astype(jnp.int16)
        count = jnp.zeros((16, tokens), BF16)
        for s in range(0, tokens, LANES):
            column = row_to_lanes(label_ref[0, m : m + 1, s : s + LANES])
            column = column.astype(jnp.int32).astype(jnp.int16)
            for r in range(0, LANES, 16):
                other = jnp.tile(column[r : r + 16], (1, tokens // LANES))
                count += jnp.where(other < bar, jnp.ones((), BF16), jnp.zeros((), BF16))
        rank += jnp.sum(count.astype(F32), axis=0, keepdims=True).astype(jnp.int32)
    rank_ref[0] = rank.astype(F32)


def own_ranks(me, labels):
    heads, n, tokens = labels.shape
    return pl.pallas_call(
        rank_kernel,
        grid=(heads,),
        in_specs=[
            pl.BlockSpec(memory_space=pltpu.SMEM),
            pl.BlockSpec((1, n, tokens), lambda h: (h, 0, 0)),
        ],
        out_specs=pl.BlockSpec((1, 1, tokens), lambda h: (h, 0, 0)),
        out_shape=jax.ShapeDtypeStruct((heads, 1, tokens), F32),
        compiler_params=params(),
        name="own_ranks",
    )(me, labels)


def totals_kernel(keys_ref, cent_ref, _, tot_ref, unit_ref, sum_ref):
    step = pl.program_id(1)
    tokens = unit_ref.shape[0]

    @pl.when(step == 0)
    def _():
        unit = unit_rows(keys_ref[pl.program_id(0)].astype(F32)).astype(BF16)
        unit_ref[...] = jnp.concatenate([unit, unit], axis=1)
        sum_ref[...] = jnp.zeros_like(sum_ref)

    part = 256
    rows = min(1024, cent_ref.shape[1])
    for c in range(0, cent_ref.shape[1], rows):
        cent = two_terms(unit_rows(cent_ref[0, c : c + rows]).astype(BF16))
        for t in range(0, tokens, part):
            raw = jnp.exp2(dot_nt(cent, unit_ref[t : t + part, :]))
            sum_ref[:, t : t + part] += jnp.sum(raw.reshape(-1, 8, part), axis=0)

    @pl.when(step == pl.num_programs(1) - 1)
    def _():
        tot_ref[0] = jnp.sum(sum_ref[...], axis=0, keepdims=True)


def own_totals(keys, cents, after):
    heads, count, width = cents.shape
    tokens = keys.shape[1]
    rows = min(2048, count)
    return pl.pallas_call(
        totals_kernel,
        grid=(heads, count // rows),
        in_specs=[
            in_vmem(),
            pl.BlockSpec((1, rows, width), lambda h, c: (h, c, 0)),
            in_vmem(),
        ],
        out_specs=pl.BlockSpec((1, 1, tokens), lambda h, c: (h, 0, 0)),
        out_shape=jax.ShapeDtypeStruct((heads, 1, tokens), F32),
        scratch_shapes=[
            pltpu.VMEM((tokens, 2 * width), BF16),
            pltpu.VMEM((8, tokens), F32),
        ],
        compiler_params=params(),
        name="own_totals",
    )(keep_vmem(keys), keep_hbm(cents), after)


def scale_rows(unit, inverse, scaled_ref):
    for t in range(0, unit.shape[0], LANES):
        scaled_ref[t : t + LANES] = (
            unit[t : t + LANES, :].astype(F32) * row_to_lanes(inverse[:, t : t + LANES])
        ).astype(BF16)


def first_kernel(fresh, _, keys_ref, tot_ref, cent_in, *refs):
    head = pl.program_id(0)
    if fresh:
        sums_ref, unit_ref, cent_ref, scaled_ref = refs
        cent = unit_rows(cent_in[0]).astype(BF16)
        cent_ref[head] = cent
    else:
        _, sums_ref, unit_ref, scaled_ref = refs
        cent = cent_in[head]
    unit = unit_rows(keys_ref[head].astype(F32)).astype(BF16)
    unit_ref[head] = unit
    scale_rows(unit, 1.0 / tot_ref[0], scaled_ref)
    part = 256
    for t in range(0, unit.shape[0], part):
        raw = jnp.exp2(dot_nt(cent, unit[t : t + part, :]) * EXP2_SCALE)
        more = dot_nn(raw.astype(BF16), scaled_ref[t : t + part])
        if fresh and t == 0:
            sums_ref[head] = more
        else:
            sums_ref[head] += more


def first_block(me, keys, totals, cents, n, before):
    heads, tokens, width = keys.shape
    fresh = before is None
    rows = cents.shape[1] // n if fresh else cents.shape[1]
    in_specs = [
        in_vmem(),
        pl.BlockSpec((1, 1, tokens), lambda h, me: (h, 0, 0)),
    ]
    args = [me, keep_vmem(keys), totals]
    out_shape = [
        pltpu.VMEM((heads, rows, width), F32),
        pltpu.VMEM((heads, tokens, width), BF16),
    ]
    aliases = {}
    if fresh:
        in_specs.append(pl.BlockSpec((1, rows, width), lambda h, me: (h, me[0], 0)))
        args.append(keep_hbm(cents))
        out_shape.append(pltpu.VMEM((heads, rows, width), BF16))
    else:
        in_specs += [in_vmem(), in_vmem()]
        args += [keep_vmem(cents), keep_vmem(before)]
        aliases = {4: 0}
    return pl.pallas_call(
        functools.partial(first_kernel, fresh),
        grid_spec=pltpu.PrefetchScalarGridSpec(
            num_scalar_prefetch=1,
            grid=(heads,),
            in_specs=in_specs,
            out_specs=(in_vmem(),) * len(out_shape),
            scratch_shapes=[pltpu.VMEM((tokens, width), BF16)],
        ),
        out_shape=tuple(out_shape),
        input_output_aliases=aliases,
        compiler_params=params(),
        name="first_block",
    )(*args)


def raw_kernel(blocks, sums_ref, *refs):
    units = refs[:blocks]
    raw_ref, total_ref, cent_ref = refs[blocks:]
    head = pl.program_id(0)
    cent_ref[...] = unit_rows(sums_ref[head]).astype(BF16)
    part = 256
    start = 0
    for unit_ref in units:
        for t in range(0, unit_ref.shape[1], part):
            here = slice(start + t, start + t + part)
            raw = jnp.exp2(dot_nt(cent_ref[...], unit_ref[head, t : t + part, :]) * EXP2_SCALE)
            raw_ref[head, :, here] = raw.astype(BF16)
            total = jnp.sum(raw.reshape(-1, 8, part), axis=0)
            total_ref[0, :, here] = jnp.sum(total, axis=0, keepdims=True)
        start += unit_ref.shape[1]


def raw_weights(sums, units):
    heads, rows, width = sums.shape
    tokens = units[0].shape[1]
    count = tokens * len(units)
    return pl.pallas_call(
        functools.partial(raw_kernel, len(units)),
        grid=(heads,),
        in_specs=[in_vmem()] * (1 + len(units)),
        out_specs=(in_vmem(), pl.BlockSpec((1, 1, count), lambda h: (h, 0, 0))),
        out_shape=(
            pltpu.VMEM((heads, rows, count), BF16),
            jax.ShapeDtypeStruct((heads, 1, count), F32),
        ),
        scratch_shapes=[pltpu.VMEM((rows, width), BF16)],
        compiler_params=params(),
        name="raw_weights",
    )(keep_vmem(sums), *map(keep_vmem, units))


def sums_kernel(blocks, raw_ref, *refs):
    totals, units = refs[:blocks], refs[blocks : 2 * blocks]
    out_hbm, scaled_ref, result_ref, sems = refs[2 * blocks :]
    heads, tokens, _ = units[0].shape
    copies = []
    for h in range(heads):
        for m, unit_ref in enumerate(units):
            row_total = totals[0][h, :, m * tokens : (m + 1) * tokens]
            for d in range(1, blocks):
                peer = m ^ d
                row_total += totals[d][h, :, peer * tokens : (peer + 1) * tokens]
            here = slice(m * tokens, (m + 1) * tokens)
            scale_rows(unit_ref[h], 1.0 / row_total, scaled_ref.at[h, here])
        result_ref[h] = unit_rows(dot_nn(raw_ref[h], scaled_ref[h]))
        copies.append(pltpu.make_async_copy(result_ref.at[h], out_hbm.at[h], sems.at[h]))
        copies[-1].start()
    for copy in copies:
        copy.wait()


def weighted_sums(raw, units, totals):
    heads, rows, count = raw.shape
    width = units[0].shape[2]
    return pl.pallas_call(
        functools.partial(sums_kernel, len(units)),
        in_specs=[in_vmem()] * (1 + 2 * len(units)),
        out_specs=anywhere(),
        out_shape=jax.ShapeDtypeStruct((heads, rows, width), F32),
        scratch_shapes=[
            pltpu.VMEM((heads, count, width), BF16),
            pltpu.VMEM((heads, rows, width), F32),
            pltpu.SemaphoreType.DMA((heads,)),
        ],
        compiler_params=params(),
        name="weighted_sums",
    )(keep_vmem(raw), *map(keep_vmem, totals), *map(keep_vmem, units))


def fill_windows(ids, size, scalar_ref, label_ref, keys, values, rows_ref, near_ref):
    heads, tokens, width = keys[0].shape
    digit_rows = tokens // LANES
    sent = values[0].shape[1] - 2 * digit_rows
    rows_ref[:, :, width:] = jnp.zeros((heads, len(ids) * size, width), BF16)
    for h in range(heads):
        low, high, first = (scalar_ref[i, h, 0].astype(F32) for i in range(2, 5))
        for i, m in enumerate(ids):
            start = pl.multiple_of(scalar_ref[0, h, m], 16)
            gap = pl.multiple_of(scalar_ref[1, h, m], 16)
            here = i * size
            rows_ref[h, here : here + size, :width] = keys[i][h, pl.ds(start, size), :]
            rows_ref[h, pl.ds(here + gap, sent), width:] = values[i][h, :sent, :]
            digits = values[i][h, sent:, :].astype(F32)
            rank = digits[:digit_rows] * 128.0 + digits[digit_rows:]
            rank = jnp.concatenate([rank[r : r + 1] for r in range(digit_rows)], axis=1)
            label = label_ref[h, m : m + 1, :]
            mine = (label >= low) & (label < high)
            spot = jnp.where(mine, rank - first, -1.0).astype(jnp.int32)
            spot = pltpu.roll(spot, lax.rem(tokens - start, tokens), 1)
            near_ref[h, :, here : here + size] = spot[:, :size]


def place_kernel(ids, size, fresh, scalar_ref, label_ref, *refs):
    count = len(ids)
    keys, values, refs = refs[:count], refs[count : 2 * count], refs[2 * count :]
    if fresh:
        so_far_ref, rows_ref, near_ref = refs
    else:
        so_far_ref, *out_hbm, rows_ref, near_ref, mixed_ref, done_ref, sems = refs
    fill_windows(ids, size, scalar_ref, label_ref, keys, values, rows_ref, near_ref)
    heads, cap, both = so_far_ref.shape
    width = both // 2
    rows = 512
    copies = []
    for r in range(0, cap, rows):
        for h in range(heads):
            total = dot_nn(one_hot_rows(rows, near_ref[h] - r), rows_ref[h])
            if fresh:
                so_far_ref[h, r : r + rows] = total.astype(BF16)
                continue
            total += so_far_ref[h, r : r + rows].astype(F32)
            for side in range(2):
                mixed_ref[side, pl.Slice(h, rows, heads), :] = total[
                    :, side * width : (side + 1) * width
                ]
        if fresh:
            continue
        here = slice(r * heads, (r + rows) * heads)
        for side in range(2):
            done_ref[side, here] = mixed_ref[side].astype(BF16)
            copies.append(
                pltpu.make_async_copy(
                    done_ref.at[side, here], out_hbm[side].at[here], sems.at[len(copies)]
                )
            )
            copies[-1].start()
    for copy in copies:
        copy.wait()


def place(scalars, labels, keys, values, ids, size, cap, so_far):
    heads, _, width = keys[0].shape
    fresh = so_far is None
    moved = [x[m] for x in (keys, values) for m in ids]
    scratch = [
        pltpu.VMEM((heads, len(ids) * size, 2 * width), BF16),
        pltpu.VMEM((heads, 1, len(ids) * size), jnp.int32),
    ]
    if fresh:
        out_shape = pltpu.VMEM((heads, cap, 2 * width), BF16)
        out_specs = in_vmem()
    else:
        moved.append(so_far)
        out_shape = (jax.ShapeDtypeStruct((heads * cap, width), BF16),) * 2
        out_specs = (anywhere(), anywhere())
        scratch += [
            pltpu.VMEM((2, heads * 512, width), F32),
            pltpu.VMEM((2, heads * cap, width), BF16),
            pltpu.SemaphoreType.DMA((2 * cap // 512,)),
        ]
    return pl.pallas_call(
        functools.partial(place_kernel, ids, size, fresh),
        in_specs=[pl.BlockSpec(memory_space=pltpu.SMEM)] + [in_vmem()] * (1 + len(moved)),
        out_specs=out_specs,
        out_shape=out_shape,
        scratch_shapes=scratch,
        compiler_params=params(),
        name="place",
    )(scalars, labels, *map(keep_vmem, moved))


def body(key_rows, value_rows, cluster_labels, owner_bounds, init_centroids):
    n = lax.axis_size("ctx")
    me = lax.axis_index("ctx").astype(jnp.int32)
    tokens, heads, width = key_rows.shape
    cap = 2 * tokens
    slot = cap // n
    send_size = slot + 16
    key_size = min(tokens, -(-send_size // LANES) * LANES)

    def swap(x, d):
        return lax.ppermute(x, "ctx", [(i, i ^ d) for i in range(n)])

    def spread(x):
        return [x] + [swap(x, d) for d in range(1, n)]

    def aligned(start, size):
        return jnp.minimum(start // 16 * 16, tokens - size)

    me_array = me.reshape(1)
    own_keys, own_labels, own_spots = sort_keys(
        cluster_labels, key_rows.reshape(heads * tokens, width)
    )
    keys = {0: own_keys}
    d = 1
    while d < n:
        keys[d] = swap(own_keys, d)
        d *= 2
    pairs = [(i, i ^ 1) for i in range(lax.axis_size("head"))]
    word = lax.ppermute(own_labels[:, :, :LANES], "head", pairs)
    own_total = own_totals(own_keys, init_centroids, word)
    shared = spread(jnp.concatenate([own_total, own_labels], axis=1))
    totals = [own_total] + [x[:, 0:1] for x in shared[1:]]

    sums, unit, cents = first_block(me_array, own_keys, own_total, init_centroids, n, None)
    units = [unit]
    *came, sums = lax.optimization_barrier((*keys.values(), sums))
    keys = dict(zip(keys, came))
    for m in range(1, n):
        if m not in keys:
            keys[m] = swap(keys[m & (m - 1)], m & -m)
    keys = [keys[m] for m in range(n)]
    peer_low = jnp.take(owner_bounds, me ^ jnp.arange(n, dtype=jnp.int32), axis=1)
    own_below = jnp.sum((own_labels < peer_low[:, :, None]).astype(jnp.int32), axis=2)
    own_values = sort_values(own_spots, value_rows.reshape(heads * tokens, width))

    labels = jnp.concatenate([x[:, -1:] for x in shared], axis=1)
    ranks = own_ranks(me_array, labels)
    low = lax.dynamic_slice_in_dim(owner_bounds, me, 1, 1)
    high = lax.dynamic_slice_in_dim(owner_bounds, me + 1, 1, 1)
    below = jnp.sum((labels < low[:, :, None]).astype(jnp.int32), axis=2)
    first = jnp.sum(below, axis=1, keepdims=True)
    key_starts = aligned(below, key_size)
    gaps = aligned(below, send_size) - key_starts
    one = jnp.ones((1, n), jnp.int32)
    scalars = jnp.stack([key_starts, gaps, low * one, high * one, first * one])

    starts = aligned(own_below, send_size)
    late = [2]
    early = [d for d in range(1, n) if d not in late]
    values = {}
    for m in range(1, n):
        sums, unit = first_block(me_array, keys[m], totals[m], cents, n, sums)
        units.append(unit)
        group = {1: early, 2: [0, *late]}.get(m)
        if group:
            some = jnp.stack([starts[:, d] for d in group], axis=1)
            for d, window in zip(group, windows(some, ranks, own_values, send_size, unit)):
                values[d] = swap(window, d) if d else window

    raw, part = raw_weights(sums, units)
    parts = spread(part)
    so_far = place(scalars, labels, keys, values, [0, *early], key_size, cap, None)
    out = weighted_sums(raw, units, parts)
    placed = place(scalars, labels, keys, values, late, key_size, cap, so_far)
    shape = (cap, heads, width)
    return out, placed[0].reshape(shape), placed[1].reshape(shape)


def solution(mesh):
    placed = (
        P(("grp", "ctx"), "head", None),
        P(("grp", "ctx"), "head", None),
        P("head", ("grp", "ctx")),
        P(("grp", "head"), None),
        P(("grp", "head"), None, None),
    )
    return jax.shard_map(
        body,
        mesh=mesh,
        in_specs=placed,
        out_specs=(
            P(("grp", "head"), "ctx", None),
            P(("grp", "ctx"), "head", None),
            P(("grp", "ctx"), "head", None),
        ),
        check_vma=False,
    )
```

```python
import functools
import math

import jax
import jax.numpy as jnp
from jax import lax
from jax.experimental import pallas as pl
from jax.experimental.pallas import tpu as pltpu
from jax.sharding import PartitionSpec as P

LANES = 128
EXP2_SCALE = 20.0 * math.log2(math.e)
VMEM_LIMIT = 16 * 1024 * 1024
F32 = jnp.float32
BF16 = jnp.bfloat16
NT = (((1,), (1,)), ((), ()))
NN = (((1,), (0,)), ((), ()))


def dot_nt(a, b):
    return lax.dot_general(a, b, NT, preferred_element_type=F32)


def dot_nn(a, b):
    return lax.dot_general(a, b, NN, preferred_element_type=F32)


def unit_rows(x):
    return x * lax.rsqrt(jnp.sum(x * x, axis=-1, keepdims=True) + 1e-06)


def params(**kwargs):
    return pltpu.CompilerParams(vmem_limit_bytes=VMEM_LIMIT, **kwargs)


def whole(shape):
    return pl.BlockSpec(shape, lambda *_: (0,) * len(shape))


def in_vmem():
    return pl.BlockSpec(memory_space=pltpu.VMEM)


def anywhere():
    return pl.BlockSpec(memory_space=pl.ANY)


def keep_hbm(x):
    return pltpu.with_memory_space_constraint(x, pltpu.HBM)


def keep_vmem(x):
    return pltpu.with_memory_space_constraint(x, pltpu.VMEM)


def row_to_lanes(row):
    return jnp.transpose(jnp.broadcast_to(row, (LANES, LANES)))


def split_heads(flat_ref, wide_ref):
    wide_ref[...] = flat_ref[...].astype(F32)


def head_rows(wide_ref, head, heads):
    if heads == 1:
        return wide_ref[...]
    return wide_ref[pl.Slice(head, wide_ref.shape[0] // heads, heads), :]


def count_below(all_ref, own_row, count):
    tokens = own_row.shape[1]
    mine = jnp.broadcast_to(own_row, (8, tokens))
    wide = 4 * LANES

    def step(i, total):
        row = all_ref[0, :, pl.ds(pl.multiple_of(i * wide, wide), wide)]
        for s in range(0, wide, LANES):
            column = row_to_lanes(row[:, s : s + LANES])
            for r in range(0, LANES, 8):
                other = jnp.tile(column[r : r + 8], (1, tokens // LANES))
                total += (other < mine).astype(jnp.int32)
        return total

    total = lax.fori_loop(
        0, count // wide, step, jnp.zeros((8, tokens), jnp.int32), unroll=True
    )
    return jnp.sum(total, axis=0, keepdims=True)


def one_hot_rows(size, spot):
    slots = lax.broadcasted_iota(jnp.int16, (size, spot.shape[1]), 0)
    return jnp.where(
        slots == spot.astype(jnp.int16), jnp.ones((), BF16), jnp.zeros((), BF16)
    )


def sort_kernel(label_hbm, keys_hbm, *refs):
    out_keys, out_labels, out_spots, flat_ref, wide_ref, order_ref, label_ref, sems = refs
    heads, tokens, _ = out_keys.shape
    label_copy = pltpu.make_async_copy(label_hbm, label_ref, sems.at[1])
    label_copy.start()
    copy = pltpu.make_async_copy(keys_hbm, flat_ref, sems.at[0])
    copy.start()
    label_copy.wait()
    labels = [label_ref[h : h + 1, :] for h in range(heads)]
    spots = []
    for h, label in enumerate(labels):
        order = label * tokens + lax.broadcasted_iota(jnp.int32, label.shape, 1)
        order_ref[0] = order
        spots.append(count_below(order_ref, order, tokens))
        out_spots[h] = spots[h]
    copy.wait()
    split_heads(flat_ref, wide_ref)
    rows = 512
    for h, label in enumerate(labels):
        keys = head_rows(wide_ref, h, heads).astype(BF16)
        digits = jnp.concatenate(
            [
                jnp.broadcast_to(label >> 6, (8, tokens)),
                jnp.broadcast_to(label & 63, (8, tokens)),
            ],
            axis=0,
        )
        digits = digits.astype(F32).astype(BF16)
        for r in range(0, tokens, rows):
            pick = one_hot_rows(rows, spots[h] - r)
            out_keys[h, r : r + rows] = dot_nn(pick, keys).astype(BF16)
            digit = dot_nt(digits, pick)
            out_labels[h, :, r : r + rows] = digit[0:1] * 64.0 + digit[8:9]


def sort_keys(labels, keys):
    heads, tokens = labels.shape
    flat, width = keys.shape
    return pl.pallas_call(
        sort_kernel,
        in_specs=[anywhere()] * 2,
        out_specs=(in_vmem(),) * 3,
        out_shape=(
            pltpu.VMEM((heads, tokens, width), BF16),
            pltpu.VMEM((heads, 1, tokens), F32),
            pltpu.VMEM((heads, 1, tokens), jnp.int32),
        ),
        scratch_shapes=[
            pltpu.VMEM((flat, width), BF16),
            pltpu.VMEM((flat, width), F32),
            pltpu.VMEM((1, 1, tokens), jnp.int32),
            pltpu.VMEM(labels.shape, jnp.int32),
            pltpu.SemaphoreType.DMA((2,)),
        ],
        compiler_params=params(),
        name="sort_keys",
    )(keep_hbm(labels), keep_hbm(keys))


def values_kernel(spot_ref, values_hbm, out_ref, flat_ref, wide_ref, sem):
    heads, _, tokens = spot_ref.shape
    copy = pltpu.make_async_copy(values_hbm, flat_ref, sem)
    copy.start()
    copy.wait()
    split_heads(flat_ref, wide_ref)
    rows = 512
    for h in range(heads):
        values = head_rows(wide_ref, h, heads).astype(BF16)
        for r in range(0, tokens, rows):
            pick = one_hot_rows(rows, spot_ref[h] - r)
            out_ref[h, r : r + rows] = dot_nn(pick, values).astype(BF16)


def sort_values(spots, values):
    heads, _, tokens = spots.shape
    flat, width = values.shape
    return pl.pallas_call(
        values_kernel,
        in_specs=[in_vmem(), anywhere()],
        out_specs=in_vmem(),
        out_shape=pltpu.VMEM((heads, tokens, width), BF16),
        scratch_shapes=[
            pltpu.VMEM((flat, width), BF16),
            pltpu.VMEM((flat, width), F32),
            pltpu.SemaphoreType.DMA,
        ],
        compiler_params=params(),
        name="sort_values",
    )(keep_vmem(spots), keep_hbm(values))


def windows_kernel(size, start_ref, rank_ref, values_ref, _, *out_refs):
    heads, tokens, _ = values_ref.shape
    for h in range(heads):
        rank = rank_ref[h].astype(jnp.int32)
        digits = [
            digit[:, t : t + LANES]
            for digit in (rank >> 7, rank & 127)
            for t in range(0, tokens, LANES)
        ]
        digits = jnp.concatenate(digits, axis=0).astype(F32).astype(BF16)
        for m, out_ref in enumerate(out_refs):
            start = pl.multiple_of(start_ref[h, m], 16)
            out_ref[h, :size] = values_ref[h, pl.ds(start, size), :]
            out_ref[h, size:] = digits


def windows(starts, ranks, values, size, after):
    heads, tokens, width = values.shape
    n = starts.shape[1]
    out = pltpu.VMEM((heads, size + 2 * tokens // LANES, width), BF16)
    return pl.pallas_call(
        functools.partial(windows_kernel, size),
        in_specs=[pl.BlockSpec(memory_space=pltpu.SMEM), in_vmem(), in_vmem(), in_vmem()],
        out_specs=(in_vmem(),) * n,
        out_shape=(out,) * n,
        compiler_params=params(),
        name="windows",
    )(starts, ranks, keep_vmem(values), keep_vmem(after))


def rank_kernel(me_ref, label_ref, rank_ref):
    heads, n, tokens = label_ref.shape
    me = me_ref[0]
    for h in range(heads):
        own = label_ref[h, 0:1, :].astype(jnp.int32)
        rank = lax.broadcasted_iota(jnp.int32, own.shape, 1)
        for m in range(1, n):
            bar = own + ((me ^ m) < me).astype(jnp.int32)
            bar = jnp.broadcast_to(bar, (16, tokens)).astype(jnp.int16)
            count = jnp.zeros((16, tokens), BF16)
            for s in range(0, tokens, LANES):
                column = row_to_lanes(label_ref[h, m : m + 1, s : s + LANES])
                column = column.astype(jnp.int32).astype(jnp.int16)
                for r in range(0, LANES, 16):
                    other = jnp.tile(column[r : r + 16], (1, tokens // LANES))
                    count += jnp.where(other < bar, jnp.ones((), BF16), jnp.zeros((), BF16))
            rank += jnp.sum(count.astype(F32), axis=0, keepdims=True).astype(jnp.int32)
        rank_ref[h] = rank.astype(F32)


def own_ranks(me, labels):
    heads, _, tokens = labels.shape
    return pl.pallas_call(
        rank_kernel,
        in_specs=[pl.BlockSpec(memory_space=pltpu.SMEM), in_vmem()],
        out_specs=in_vmem(),
        out_shape=jax.ShapeDtypeStruct((heads, 1, tokens), F32),
        compiler_params=params(),
        name="own_ranks",
    )(me, labels)


def totals_kernel(keys_ref, cent_ref, _, tot_ref, unit_ref, sum_ref):
    step = pl.program_id(1)
    tokens = unit_ref.shape[0]

    @pl.when(step == 0)
    def _():
        unit_ref[...] = unit_rows(keys_ref[pl.program_id(0)].astype(F32)).astype(BF16)
        sum_ref[...] = jnp.zeros_like(sum_ref)

    part = 512
    rows = min(1024, cent_ref.shape[1])
    for c in range(0, cent_ref.shape[1], rows):
        cent = unit_rows(cent_ref[0, c : c + rows]).astype(BF16)
        for t in range(0, tokens, part):
            raw = jnp.exp2(dot_nt(cent, unit_ref[t : t + part, :]) * EXP2_SCALE)
            sum_ref[:, t : t + part] += jnp.sum(raw.reshape(-1, 8, part), axis=0)

    @pl.when(step == pl.num_programs(1) - 1)
    def _():
        tot_ref[0] = jnp.sum(sum_ref[...], axis=0, keepdims=True)


def own_totals(keys, cents, after):
    heads, count, width = cents.shape
    tokens = keys.shape[1]
    rows = min(2048, count)
    return pl.pallas_call(
        totals_kernel,
        grid=(heads, count // rows),
        in_specs=[
            in_vmem(),
            pl.BlockSpec((1, rows, width), lambda h, c: (h, c, 0)),
            in_vmem(),
        ],
        out_specs=pl.BlockSpec((1, 1, tokens), lambda h, c: (h, 0, 0)),
        out_shape=jax.ShapeDtypeStruct((heads, 1, tokens), F32),
        scratch_shapes=[
            pltpu.VMEM((tokens, width), BF16),
            pltpu.VMEM((8, tokens), F32),
        ],
        compiler_params=params(),
        name="own_totals",
    )(keep_vmem(keys), keep_hbm(cents), after)


def scale_rows(unit, inverse, scaled_ref):
    for t in range(0, unit.shape[0], LANES):
        scaled_ref[t : t + LANES] = (
            unit[t : t + LANES, :].astype(F32) * row_to_lanes(inverse[:, t : t + LANES])
        ).astype(BF16)


def first_kernel(fresh, _, keys_ref, tot_ref, cent_in, *refs):
    head = pl.program_id(0)
    if fresh:
        sums_ref, unit_ref, cent_ref, scaled_ref = refs
        cent = unit_rows(cent_in[0]).astype(BF16)
        cent_ref[head] = cent
    else:
        _, sums_ref, unit_ref, scaled_ref = refs
        cent = cent_in[head]
    unit = unit_rows(keys_ref[head].astype(F32)).astype(BF16)
    unit_ref[head] = unit
    scale_rows(unit, 1.0 / tot_ref[0], scaled_ref)
    part = 512
    for t in range(0, unit.shape[0], part):
        raw = jnp.exp2(dot_nt(cent, unit[t : t + part, :]) * EXP2_SCALE)
        more = dot_nn(raw.astype(BF16), scaled_ref[t : t + part])
        if fresh and t == 0:
            sums_ref[head] = more
        else:
            sums_ref[head] += more


def first_block(me, keys, totals, cents, n, before):
    heads, tokens, width = keys.shape
    fresh = before is None
    rows = cents.shape[1] // n if fresh else cents.shape[1]
    in_specs = [
        in_vmem(),
        pl.BlockSpec((1, 1, tokens), lambda h, me: (h, 0, 0)),
    ]
    args = [me, keep_vmem(keys), totals]
    out_shape = [
        pltpu.VMEM((heads, rows, width), F32),
        pltpu.VMEM((heads, tokens, width), BF16),
    ]
    aliases = {}
    if fresh:
        in_specs.append(pl.BlockSpec((1, rows, width), lambda h, me: (h, me[0], 0)))
        args.append(keep_hbm(cents))
        out_shape.append(pltpu.VMEM((heads, rows, width), BF16))
    else:
        in_specs += [in_vmem(), in_vmem()]
        args += [keep_vmem(cents), keep_vmem(before)]
        aliases = {4: 0}
    return pl.pallas_call(
        functools.partial(first_kernel, fresh),
        grid_spec=pltpu.PrefetchScalarGridSpec(
            num_scalar_prefetch=1,
            grid=(heads,),
            in_specs=in_specs,
            out_specs=(in_vmem(),) * len(out_shape),
            scratch_shapes=[pltpu.VMEM((tokens, width), BF16)],
        ),
        out_shape=tuple(out_shape),
        input_output_aliases=aliases,
        compiler_params=params(),
        name="first_block",
    )(*args)


def raw_kernel(blocks, sums_ref, *refs):
    units = refs[:blocks]
    raw_ref, total_ref, cent_ref = refs[blocks:]
    head = pl.program_id(0)
    cent_ref[...] = unit_rows(sums_ref[head]).astype(BF16)
    part = 512
    start = 0
    for unit_ref in units:
        for t in range(0, unit_ref.shape[1], part):
            here = slice(start + t, start + t + part)
            raw = jnp.exp2(dot_nt(cent_ref[...], unit_ref[head, t : t + part, :]) * EXP2_SCALE)
            raw_ref[head, :, here] = raw.astype(BF16)
            total = jnp.sum(raw.reshape(-1, 8, part), axis=0)
            total_ref[0, :, here] = jnp.sum(total, axis=0, keepdims=True)
        start += unit_ref.shape[1]


def raw_weights(sums, units):
    heads, rows, width = sums.shape
    tokens = units[0].shape[1]
    count = tokens * len(units)
    return pl.pallas_call(
        functools.partial(raw_kernel, len(units)),
        grid=(heads,),
        in_specs=[in_vmem()] * (1 + len(units)),
        out_specs=(in_vmem(), pl.BlockSpec((1, 1, count), lambda h: (h, 0, 0))),
        out_shape=(
            pltpu.VMEM((heads, rows, count), BF16),
            jax.ShapeDtypeStruct((heads, 1, count), F32),
        ),
        scratch_shapes=[pltpu.VMEM((rows, width), BF16)],
        compiler_params=params(),
        name="raw_weights",
    )(keep_vmem(sums), *map(keep_vmem, units))


def sums_kernel(blocks, raw_ref, *refs):
    totals, units = refs[:blocks], refs[blocks : 2 * blocks]
    out_hbm, scaled_ref, result_ref, sems = refs[2 * blocks :]
    heads, tokens, _ = units[0].shape
    copies = []
    for h in range(heads):
        for m, unit_ref in enumerate(units):
            row_total = totals[0][h, :, m * tokens : (m + 1) * tokens]
            for d in range(1, blocks):
                peer = m ^ d
                row_total += totals[d][h, :, peer * tokens : (peer + 1) * tokens]
            here = slice(m * tokens, (m + 1) * tokens)
            scale_rows(unit_ref[h], 1.0 / row_total, scaled_ref.at[h, here])
        result_ref[h] = unit_rows(dot_nn(raw_ref[h], scaled_ref[h]))
        copies.append(pltpu.make_async_copy(result_ref.at[h], out_hbm.at[h], sems.at[h]))
        copies[-1].start()
    for copy in copies:
        copy.wait()


def weighted_sums(raw, units, totals):
    heads, rows, count = raw.shape
    width = units[0].shape[2]
    return pl.pallas_call(
        functools.partial(sums_kernel, len(units)),
        in_specs=[in_vmem()] * (1 + 2 * len(units)),
        out_specs=anywhere(),
        out_shape=jax.ShapeDtypeStruct((heads, rows, width), F32),
        scratch_shapes=[
            pltpu.VMEM((heads, count, width), BF16),
            pltpu.VMEM((heads, rows, width), F32),
            pltpu.SemaphoreType.DMA((heads,)),
        ],
        compiler_params=params(),
        name="weighted_sums",
    )(keep_vmem(raw), *map(keep_vmem, totals), *map(keep_vmem, units))


def fill_windows(ids, size, scalar_ref, label_ref, keys, values, rows_ref, near_ref):
    heads, tokens, width = keys[0].shape
    digit_rows = tokens // LANES
    sent = values[0].shape[1] - 2 * digit_rows
    rows_ref[:, :, width:] = jnp.zeros((heads, len(ids) * size, width), BF16)
    for h in range(heads):
        low, high, first = (scalar_ref[i, h, 0].astype(F32) for i in range(2, 5))
        for i, m in enumerate(ids):
            start = pl.multiple_of(scalar_ref[0, h, m], 16)
            gap = pl.multiple_of(scalar_ref[1, h, m], 16)
            here = i * size
            rows_ref[h, here : here + size, :width] = keys[i][h, pl.ds(start, size), :]
            rows_ref[h, pl.ds(here + gap, sent), width:] = values[i][h, :sent, :]
            digits = values[i][h, sent:, :].astype(F32)
            rank = digits[:digit_rows] * 128.0 + digits[digit_rows:]
            rank = jnp.concatenate([rank[r : r + 1] for r in range(digit_rows)], axis=1)
            label = label_ref[h, m : m + 1, :]
            mine = (label >= low) & (label < high)
            spot = jnp.where(mine, rank - first, -1.0).astype(jnp.int32)
            spot = pltpu.roll(spot, lax.rem(tokens - start, tokens), 1)
            near_ref[h, :, here : here + size] = spot[:, :size]


def place_kernel(ids, size, fresh, scalar_ref, label_ref, *refs):
    count = len(ids)
    keys, values, refs = refs[:count], refs[count : 2 * count], refs[2 * count :]
    if fresh:
        so_far_ref, rows_ref, near_ref = refs
    else:
        so_far_ref, *out_hbm, rows_ref, near_ref, mixed_ref, done_ref, sems = refs
    fill_windows(ids, size, scalar_ref, label_ref, keys, values, rows_ref, near_ref)
    heads, cap, both = so_far_ref.shape
    width = both // 2
    rows = 512
    copies = []
    for r in range(0, cap, rows):
        for h in range(heads):
            total = dot_nn(one_hot_rows(rows, near_ref[h] - r), rows_ref[h])
            if fresh:
                so_far_ref[h, r : r + rows] = total.astype(BF16)
                continue
            total += so_far_ref[h, r : r + rows].astype(F32)
            for side in range(2):
                mixed_ref[side, pl.Slice(h, rows, heads), :] = total[
                    :, side * width : (side + 1) * width
                ]
        if fresh:
            continue
        here = slice(r * heads, (r + rows) * heads)
        for side in range(2):
            done_ref[side, here] = mixed_ref[side].astype(BF16)
            copies.append(
                pltpu.make_async_copy(
                    done_ref.at[side, here], out_hbm[side].at[here], sems.at[len(copies)]
                )
            )
            copies[-1].start()
    for copy in copies:
        copy.wait()


def place(scalars, labels, keys, values, ids, size, cap, so_far):
    heads, _, width = keys[0].shape
    fresh = so_far is None
    moved = [x[m] for x in (keys, values) for m in ids]
    scratch = [
        pltpu.VMEM((heads, len(ids) * size, 2 * width), BF16),
        pltpu.VMEM((heads, 1, len(ids) * size), jnp.int32),
    ]
    if fresh:
        out_shape = pltpu.VMEM((heads, cap, 2 * width), BF16)
        out_specs = in_vmem()
    else:
        moved.append(so_far)
        out_shape = (jax.ShapeDtypeStruct((heads * cap, width), BF16),) * 2
        out_specs = (anywhere(), anywhere())
        scratch += [
            pltpu.VMEM((2, heads * 512, width), F32),
            pltpu.VMEM((2, heads * cap, width), BF16),
            pltpu.SemaphoreType.DMA((2 * cap // 512,)),
        ]
    return pl.pallas_call(
        functools.partial(place_kernel, ids, size, fresh),
        in_specs=[pl.BlockSpec(memory_space=pltpu.SMEM)] + [in_vmem()] * (1 + len(moved)),
        out_specs=out_specs,
        out_shape=out_shape,
        scratch_shapes=scratch,
        compiler_params=params(),
        name="place",
    )(scalars, labels, *map(keep_vmem, moved))


def body(key_rows, value_rows, cluster_labels, owner_bounds, init_centroids):
    n = lax.axis_size("ctx")
    me = lax.axis_index("ctx").astype(jnp.int32)
    tokens, heads, width = key_rows.shape
    cap = 2 * tokens
    slot = cap // n
    send_size = slot + 16
    key_size = min(tokens, -(-send_size // LANES) * LANES)

    def swap(x, d):
        return lax.ppermute(x, "ctx", [(i, i ^ d) for i in range(n)])

    def spread(x):
        return [x] + [swap(x, d) for d in range(1, n)]

    def aligned(start, size):
        return jnp.minimum(start // 16 * 16, tokens - size)

    me_array = me.reshape(1)
    own_keys, own_labels, own_spots = sort_keys(
        cluster_labels, key_rows.reshape(heads * tokens, width)
    )
    keys = {0: own_keys}
    d = 1
    while d < n:
        keys[d] = swap(own_keys, d)
        d *= 2
    pairs = [(i, i ^ 1) for i in range(lax.axis_size("head"))]
    word = lax.ppermute(own_labels[:, :, :LANES], "head", pairs)
    own_total = own_totals(own_keys, init_centroids, word)
    shared = spread(jnp.concatenate([own_total, own_labels], axis=1))
    totals = [own_total] + [x[:, 0:1] for x in shared[1:]]

    sums, unit, cents = first_block(me_array, own_keys, own_total, init_centroids, n, None)
    units = [unit]
    *came, sums = lax.optimization_barrier((*keys.values(), sums))
    keys = dict(zip(keys, came))
    for m in range(1, n):
        if m not in keys:
            keys[m] = swap(keys[m & (m - 1)], m & -m)
    keys = [keys[m] for m in range(n)]
    peer_low = jnp.take(owner_bounds, me ^ jnp.arange(n, dtype=jnp.int32), axis=1)
    own_below = jnp.sum((own_labels < peer_low[:, :, None]).astype(jnp.int32), axis=2)
    own_values = sort_values(own_spots, value_rows.reshape(heads * tokens, width))

    labels = jnp.concatenate([x[:, -1:] for x in shared], axis=1)
    ranks = own_ranks(me_array, labels)
    low = lax.dynamic_slice_in_dim(owner_bounds, me, 1, 1)
    high = lax.dynamic_slice_in_dim(owner_bounds, me + 1, 1, 1)
    below = jnp.sum((labels < low[:, :, None]).astype(jnp.int32), axis=2)
    first = jnp.sum(below, axis=1, keepdims=True)
    key_starts = aligned(below, key_size)
    gaps = aligned(below, send_size) - key_starts
    one = jnp.ones((1, n), jnp.int32)
    scalars = jnp.stack([key_starts, gaps, low * one, high * one, first * one])

    starts = aligned(own_below, send_size)
    late = [2]
    early = [d for d in range(1, n) if d not in late]
    values = {}
    for m in range(1, n):
        sums, unit = first_block(me_array, keys[m], totals[m], cents, n, sums)
        units.append(unit)
        group = {1: early, 2: [0, *late]}.get(m)
        if group:
            some = jnp.stack([starts[:, d] for d in group], axis=1)
            for d, window in zip(group, windows(some, ranks, own_values, send_size, unit)):
                values[d] = swap(window, d) if d else window

    raw, part = raw_weights(sums, units)
    parts = spread(part)
    so_far = place(scalars, labels, keys, values, [0, *early], key_size, cap, None)
    out = weighted_sums(raw, units, parts)
    placed = place(scalars, labels, keys, values, late, key_size, cap, so_far)
    shape = (cap, heads, width)
    return out, placed[0].reshape(shape), placed[1].reshape(shape)


def solution(mesh):
    placed = (
        P(("grp", "ctx"), "head", None),
        P(("grp", "ctx"), "head", None),
        P("head", ("grp", "ctx")),
        P(("grp", "head"), None),
        P(("grp", "head"), None, None),
    )
    return jax.shard_map(
        body,
        mesh=mesh,
        in_specs=placed,
        out_specs=(
            P(("grp", "head"), "ctx", None),
            P(("grp", "ctx"), "head", None),
            P(("grp", "ctx"), "head", None),
        ),
        check_vma=False,
    )
```

```python
import functools
import math

import jax
import jax.numpy as jnp
from jax import lax
from jax.experimental import pallas as pl
from jax.experimental.pallas import tpu as pltpu
from jax.sharding import PartitionSpec as P

LANES = 128
EXP2_SCALE = 20.0 * math.log2(math.e)
VMEM_LIMIT = 16 * 1024 * 1024
F32 = jnp.float32
BF16 = jnp.bfloat16
NT = (((1,), (1,)), ((), ()))
NN = (((1,), (0,)), ((), ()))


def dot_nt(a, b):
    return lax.dot_general(a, b, NT, preferred_element_type=F32)


def dot_nn(a, b):
    return lax.dot_general(a, b, NN, preferred_element_type=F32)


def unit_rows(x):
    return x * lax.rsqrt(jnp.sum(x * x, axis=-1, keepdims=True) + 1e-06)


def params(**kwargs):
    return pltpu.CompilerParams(vmem_limit_bytes=VMEM_LIMIT, **kwargs)


def whole(shape):
    return pl.BlockSpec(shape, lambda *_: (0,) * len(shape))


def in_vmem():
    return pl.BlockSpec(memory_space=pltpu.VMEM)


def anywhere():
    return pl.BlockSpec(memory_space=pl.ANY)


def keep_hbm(x):
    return pltpu.with_memory_space_constraint(x, pltpu.HBM)


def keep_vmem(x):
    return pltpu.with_memory_space_constraint(x, pltpu.VMEM)


def row_to_lanes(row):
    return jnp.transpose(jnp.broadcast_to(row, (LANES, LANES)))


def split_heads(flat_ref, wide_ref):
    wide_ref[...] = flat_ref[...].astype(F32)


def head_rows(wide_ref, head, heads):
    if heads == 1:
        return wide_ref[...]
    return wide_ref[pl.Slice(head, wide_ref.shape[0] // heads, heads), :]


def count_below(all_ref, own_row, count):
    tokens = own_row.shape[1]
    mine = jnp.broadcast_to(own_row, (8, tokens))
    wide = 4 * LANES

    def step(i, total):
        row = all_ref[0, :, pl.ds(pl.multiple_of(i * wide, wide), wide)]
        for s in range(0, wide, LANES):
            column = row_to_lanes(row[:, s : s + LANES])
            for r in range(0, LANES, 8):
                other = jnp.tile(column[r : r + 8], (1, tokens // LANES))
                total += (other < mine).astype(jnp.int32)
        return total

    total = lax.fori_loop(
        0, count // wide, step, jnp.zeros((8, tokens), jnp.int32), unroll=True
    )
    return jnp.sum(total, axis=0, keepdims=True)


def one_hot_rows(size, spot):
    slots = lax.broadcasted_iota(jnp.int16, (size, spot.shape[1]), 0)
    return jnp.where(
        slots == spot.astype(jnp.int16), jnp.ones((), BF16), jnp.zeros((), BF16)
    )


def sort_kernel(label_hbm, keys_hbm, *refs):
    out_keys, out_labels, out_spots, flat_ref, wide_ref, order_ref, label_ref, sems = refs
    heads, tokens, _ = out_keys.shape
    label_copy = pltpu.make_async_copy(label_hbm, label_ref, sems.at[1])
    label_copy.start()
    copy = pltpu.make_async_copy(keys_hbm, flat_ref, sems.at[0])
    copy.start()
    label_copy.wait()
    labels = [label_ref[h : h + 1, :] for h in range(heads)]
    spots = []
    for h, label in enumerate(labels):
        order = label * tokens + lax.broadcasted_iota(jnp.int32, label.shape, 1)
        order_ref[0] = order
        spots.append(count_below(order_ref, order, tokens))
        out_spots[h] = spots[h]
    copy.wait()
    split_heads(flat_ref, wide_ref)
    rows = 512
    for h, label in enumerate(labels):
        keys = head_rows(wide_ref, h, heads).astype(BF16)
        digits = jnp.concatenate(
            [
                jnp.broadcast_to(label >> 6, (8, tokens)),
                jnp.broadcast_to(label & 63, (8, tokens)),
            ],
            axis=0,
        )
        digits = digits.astype(F32).astype(BF16)
        for r in range(0, tokens, rows):
            pick = one_hot_rows(rows, spots[h] - r)
            out_keys[h, r : r + rows] = dot_nn(pick, keys).astype(BF16)
            digit = dot_nt(digits, pick)
            out_labels[h, :, r : r + rows] = digit[0:1] * 64.0 + digit[8:9]


def sort_keys(labels, keys):
    heads, tokens = labels.shape
    flat, width = keys.shape
    return pl.pallas_call(
        sort_kernel,
        in_specs=[anywhere()] * 2,
        out_specs=(in_vmem(),) * 3,
        out_shape=(
            pltpu.VMEM((heads, tokens, width), BF16),
            pltpu.VMEM((heads, 1, tokens), F32),
            pltpu.VMEM((heads, 1, tokens), jnp.int32),
        ),
        scratch_shapes=[
            pltpu.VMEM((flat, width), BF16),
            pltpu.VMEM((flat, width), F32),
            pltpu.VMEM((1, 1, tokens), jnp.int32),
            pltpu.VMEM(labels.shape, jnp.int32),
            pltpu.SemaphoreType.DMA((2,)),
        ],
        compiler_params=params(),
        name="sort_keys",
    )(keep_hbm(labels), keep_hbm(keys))


def values_kernel(spot_ref, values_hbm, out_ref, flat_ref, wide_ref, sem):
    heads, _, tokens = spot_ref.shape
    copy = pltpu.make_async_copy(values_hbm, flat_ref, sem)
    copy.start()
    copy.wait()
    split_heads(flat_ref, wide_ref)
    rows = 512
    for h in range(heads):
        values = head_rows(wide_ref, h, heads).astype(BF16)
        for r in range(0, tokens, rows):
            pick = one_hot_rows(rows, spot_ref[h] - r)
            out_ref[h, r : r + rows] = dot_nn(pick, values).astype(BF16)


def sort_values(spots, values):
    heads, _, tokens = spots.shape
    flat, width = values.shape
    return pl.pallas_call(
        values_kernel,
        in_specs=[in_vmem(), anywhere()],
        out_specs=in_vmem(),
        out_shape=pltpu.VMEM((heads, tokens, width), BF16),
        scratch_shapes=[
            pltpu.VMEM((flat, width), BF16),
            pltpu.VMEM((flat, width), F32),
            pltpu.SemaphoreType.DMA,
        ],
        compiler_params=params(),
        name="sort_values",
    )(keep_vmem(spots), keep_hbm(values))


def windows_kernel(size, start_ref, rank_ref, values_ref, _, *out_refs):
    heads, tokens, _ = values_ref.shape
    for h in range(heads):
        rank = rank_ref[h].astype(jnp.int32)
        digits = [
            digit[:, t : t + LANES]
            for digit in (rank >> 7, rank & 127)
            for t in range(0, tokens, LANES)
        ]
        digits = jnp.concatenate(digits, axis=0).astype(F32).astype(BF16)
        for m, out_ref in enumerate(out_refs):
            start = pl.multiple_of(start_ref[h, m], 16)
            out_ref[h, :size] = values_ref[h, pl.ds(start, size), :]
            out_ref[h, size:] = digits


def windows(starts, ranks, values, size, after):
    heads, tokens, width = values.shape
    n = starts.shape[1]
    out = pltpu.VMEM((heads, size + 2 * tokens // LANES, width), BF16)
    return pl.pallas_call(
        functools.partial(windows_kernel, size),
        in_specs=[pl.BlockSpec(memory_space=pltpu.SMEM), in_vmem(), in_vmem(), in_vmem()],
        out_specs=(in_vmem(),) * n,
        out_shape=(out,) * n,
        compiler_params=params(),
        name="windows",
    )(starts, ranks, keep_vmem(values), keep_vmem(after))


def rank_kernel(me_ref, label_ref, rank_ref):
    n, tokens = label_ref.shape[1:]
    me = me_ref[0]
    own = label_ref[0, 0:1, :].astype(jnp.int32)
    rank = lax.broadcasted_iota(jnp.int32, own.shape, 1)
    for m in range(1, n):
        bar = own + ((me ^ m) < me).astype(jnp.int32)
        bar = jnp.broadcast_to(bar, (16, tokens)).astype(jnp.int16)
        count = jnp.zeros((16, tokens), BF16)
        for s in range(0, tokens, LANES):
            column = row_to_lanes(label_ref[0, m : m + 1, s : s + LANES])
            column = column.astype(jnp.int32).astype(jnp.int16)
            for r in range(0, LANES, 16):
                other = jnp.tile(column[r : r + 16], (1, tokens // LANES))
                count += jnp.where(other < bar, jnp.ones((), BF16), jnp.zeros((), BF16))
        rank += jnp.sum(count.astype(F32), axis=0, keepdims=True).astype(jnp.int32)
    rank_ref[0] = rank.astype(F32)


def own_ranks(me, labels):
    heads, n, tokens = labels.shape
    return pl.pallas_call(
        rank_kernel,
        grid=(heads,),
        in_specs=[
            pl.BlockSpec(memory_space=pltpu.SMEM),
            pl.BlockSpec((1, n, tokens), lambda h: (h, 0, 0)),
        ],
        out_specs=pl.BlockSpec((1, 1, tokens), lambda h: (h, 0, 0)),
        out_shape=jax.ShapeDtypeStruct((heads, 1, tokens), F32),
        compiler_params=params(),
        name="own_ranks",
    )(me, labels)


def totals_kernel(keys_ref, cent_ref, _, tot_ref, unit_ref, sum_ref):
    step = pl.program_id(1)
    tokens = unit_ref.shape[0]

    @pl.when(step == 0)
    def _():
        unit_ref[...] = unit_rows(keys_ref[pl.program_id(0)].astype(F32)).astype(BF16)
        sum_ref[...] = jnp.zeros_like(sum_ref)

    part = 256
    rows = min(1024, cent_ref.shape[1])
    for c in range(0, cent_ref.shape[1], rows):
        cent = unit_rows(cent_ref[0, c : c + rows]).astype(BF16)
        for t in range(0, tokens, part):
            raw = jnp.exp2(dot_nt(cent, unit_ref[t : t + part, :]) * EXP2_SCALE)
            sum_ref[:, t : t + part] += jnp.sum(raw.reshape(-1, 8, part), axis=0)

    @pl.when(step == pl.num_programs(1) - 1)
    def _():
        tot_ref[0] = jnp.sum(sum_ref[...], axis=0, keepdims=True)


def own_totals(keys, cents, after):
    heads, count, width = cents.shape
    tokens = keys.shape[1]
    rows = min(2048, count)
    return pl.pallas_call(
        totals_kernel,
        grid=(heads, count // rows),
        in_specs=[
            in_vmem(),
            pl.BlockSpec((1, rows, width), lambda h, c: (h, c, 0)),
            in_vmem(),
        ],
        out_specs=pl.BlockSpec((1, 1, tokens), lambda h, c: (h, 0, 0)),
        out_shape=jax.ShapeDtypeStruct((heads, 1, tokens), F32),
        scratch_shapes=[
            pltpu.VMEM((tokens, width), BF16),
            pltpu.VMEM((8, tokens), F32),
        ],
        compiler_params=params(),
        name="own_totals",
    )(keep_vmem(keys), keep_hbm(cents), after)


def scale_rows(unit, inverse, scaled_ref):
    for t in range(0, unit.shape[0], LANES):
        scaled_ref[t : t + LANES] = (
            unit[t : t + LANES, :].astype(F32) * row_to_lanes(inverse[:, t : t + LANES])
        ).astype(BF16)


def first_kernel(fresh, _, keys_ref, tot_ref, cent_in, *refs):
    head = pl.program_id(0)
    if fresh:
        sums_ref, unit_ref, cent_ref, scaled_ref = refs
        cent = unit_rows(cent_in[0]).astype(BF16)
        cent_ref[head] = cent
    else:
        _, sums_ref, unit_ref, scaled_ref = refs
        cent = cent_in[head]
    unit = unit_rows(keys_ref[head].astype(F32)).astype(BF16)
    unit_ref[head] = unit
    scale_rows(unit, 1.0 / tot_ref[0], scaled_ref)
    part = 256
    for t in range(0, unit.shape[0], part):
        raw = jnp.exp2(dot_nt(cent, unit[t : t + part, :]) * EXP2_SCALE)
        more = dot_nn(raw.astype(BF16), scaled_ref[t : t + part])
        if fresh and t == 0:
            sums_ref[head] = more
        else:
            sums_ref[head] += more


def first_block(me, keys, totals, cents, n, before):
    heads, tokens, width = keys.shape
    fresh = before is None
    rows = cents.shape[1] // n if fresh else cents.shape[1]
    in_specs = [
        in_vmem(),
        pl.BlockSpec((1, 1, tokens), lambda h, me: (h, 0, 0)),
    ]
    args = [me, keep_vmem(keys), totals]
    out_shape = [
        pltpu.VMEM((heads, rows, width), F32),
        pltpu.VMEM((heads, tokens, width), BF16),
    ]
    aliases = {}
    if fresh:
        in_specs.append(pl.BlockSpec((1, rows, width), lambda h, me: (h, me[0], 0)))
        args.append(keep_hbm(cents))
        out_shape.append(pltpu.VMEM((heads, rows, width), BF16))
    else:
        in_specs += [in_vmem(), in_vmem()]
        args += [keep_vmem(cents), keep_vmem(before)]
        aliases = {4: 0}
    return pl.pallas_call(
        functools.partial(first_kernel, fresh),
        grid_spec=pltpu.PrefetchScalarGridSpec(
            num_scalar_prefetch=1,
            grid=(heads,),
            in_specs=in_specs,
            out_specs=(in_vmem(),) * len(out_shape),
            scratch_shapes=[pltpu.VMEM((tokens, width), BF16)],
        ),
        out_shape=tuple(out_shape),
        input_output_aliases=aliases,
        compiler_params=params(),
        name="first_block",
    )(*args)


def raw_kernel(blocks, size, sums_ref, *refs):
    units, refs = refs[:blocks], refs[blocks:]
    scalar_ref, label_ref, key_ref, value_ref, *refs = refs
    raw_ref, total_ref, so_far_ref, cent_ref, rows_ref, near_ref = refs
    head = pl.program_id(0)

    @pl.when(head == 0)
    def _():
        fill_windows(
            [0], size, scalar_ref, label_ref, [key_ref], [value_ref], rows_ref, near_ref
        )

    cent_ref[...] = unit_rows(sums_ref[head]).astype(BF16)
    part = 256
    start = 0
    for unit_ref in units:
        for t in range(0, unit_ref.shape[1], part):
            here = slice(start + t, start + t + part)
            raw = jnp.exp2(dot_nt(cent_ref[...], unit_ref[head, t : t + part, :]) * EXP2_SCALE)
            raw_ref[head, :, here] = raw.astype(BF16)
            total = jnp.sum(raw.reshape(-1, 8, part), axis=0)
            total_ref[0, :, here] = jnp.sum(total, axis=0, keepdims=True)
        start += unit_ref.shape[1]
    rows = 512
    for r in range(0, so_far_ref.shape[1], rows):
        pick = one_hot_rows(rows, near_ref[head] - r)
        so_far_ref[head, r : r + rows] = dot_nn(pick, rows_ref[head]).astype(BF16)


def raw_weights(sums, units, scalars, labels, keys, values, size, cap):
    heads, rows, width = sums.shape
    tokens = units[0].shape[1]
    count = tokens * len(units)
    return pl.pallas_call(
        functools.partial(raw_kernel, len(units), size),
        grid=(heads,),
        in_specs=[in_vmem()] * (1 + len(units))
        + [pl.BlockSpec(memory_space=pltpu.SMEM)]
        + [in_vmem()] * 3,
        out_specs=(
            in_vmem(),
            pl.BlockSpec((1, 1, count), lambda h: (h, 0, 0)),
            in_vmem(),
        ),
        out_shape=(
            pltpu.VMEM((heads, rows, count), BF16),
            jax.ShapeDtypeStruct((heads, 1, count), F32),
            pltpu.VMEM((heads, cap, 2 * width), BF16),
        ),
        scratch_shapes=[
            pltpu.VMEM((rows, width), BF16),
            pltpu.VMEM((heads, size, 2 * width), BF16),
            pltpu.VMEM((heads, 1, size), jnp.int32),
        ],
        compiler_params=params(),
        name="raw_weights",
    )(keep_vmem(sums), *map(keep_vmem, units), scalars, labels, *map(keep_vmem, (keys, values)))


def sums_kernel(blocks, raw_ref, *refs):
    totals, units = refs[:blocks], refs[blocks : 2 * blocks]
    out_hbm, scaled_ref, result_ref, sems = refs[2 * blocks :]
    heads, tokens, _ = units[0].shape
    copies = []
    for h in range(heads):
        for m, unit_ref in enumerate(units):
            row_total = totals[0][h, :, m * tokens : (m + 1) * tokens]
            for d in range(1, blocks):
                peer = m ^ d
                row_total += totals[d][h, :, peer * tokens : (peer + 1) * tokens]
            here = slice(m * tokens, (m + 1) * tokens)
            scale_rows(unit_ref[h], 1.0 / row_total, scaled_ref.at[h, here])
        result_ref[h] = unit_rows(dot_nn(raw_ref[h], scaled_ref[h]))
        copies.append(pltpu.make_async_copy(result_ref.at[h], out_hbm.at[h], sems.at[h]))
        copies[-1].start()
    for copy in copies:
        copy.wait()


def weighted_sums(raw, units, totals):
    heads, rows, count = raw.shape
    width = units[0].shape[2]
    return pl.pallas_call(
        functools.partial(sums_kernel, len(units)),
        in_specs=[in_vmem()] * (1 + 2 * len(units)),
        out_specs=anywhere(),
        out_shape=jax.ShapeDtypeStruct((heads, rows, width), F32),
        scratch_shapes=[
            pltpu.VMEM((heads, count, width), BF16),
            pltpu.VMEM((heads, rows, width), F32),
            pltpu.SemaphoreType.DMA((heads,)),
        ],
        compiler_params=params(),
        name="weighted_sums",
    )(keep_vmem(raw), *map(keep_vmem, totals), *map(keep_vmem, units))


def fill_windows(ids, size, scalar_ref, label_ref, keys, values, rows_ref, near_ref):
    heads, tokens, width = keys[0].shape
    digit_rows = tokens // LANES
    sent = values[0].shape[1] - 2 * digit_rows
    rows_ref[:, :, width:] = jnp.zeros((heads, len(ids) * size, width), BF16)
    for h in range(heads):
        low, high, first = (scalar_ref[i, h, 0].astype(F32) for i in range(2, 5))
        for i, m in enumerate(ids):
            start = pl.multiple_of(scalar_ref[0, h, m], 16)
            gap = pl.multiple_of(scalar_ref[1, h, m], 16)
            here = i * size
            rows_ref[h, here : here + size, :width] = keys[i][h, pl.ds(start, size), :]
            rows_ref[h, pl.ds(here + gap, sent), width:] = values[i][h, :sent, :]
            digits = values[i][h, sent:, :].astype(F32)
            rank = digits[:digit_rows] * 128.0 + digits[digit_rows:]
            rank = jnp.concatenate([rank[r : r + 1] for r in range(digit_rows)], axis=1)
            label = label_ref[h, m : m + 1, :]
            mine = (label >= low) & (label < high)
            spot = jnp.where(mine, rank - first, -1.0).astype(jnp.int32)
            spot = pltpu.roll(spot, lax.rem(tokens - start, tokens), 1)
            near_ref[h, :, here : here + size] = spot[:, :size]


def place_kernel(ids, size, last, scalar_ref, label_ref, *refs):
    count = len(ids)
    keys, values, refs = refs[:count], refs[count : 2 * count], refs[2 * count :]
    so_far_ref, *refs = refs
    if last:
        *out_hbm, rows_ref, near_ref, mixed_ref, done_ref, sems = refs
        width = done_ref.shape[2]
        cap = done_ref.shape[1] // rows_ref.shape[0]
    else:
        out_ref, rows_ref, near_ref = refs
        cap = out_ref.shape[1]
    heads = rows_ref.shape[0]
    fill_windows(ids, size, scalar_ref, label_ref, keys, values, rows_ref, near_ref)
    rows = 512
    copies = []
    for r in range(0, cap, rows):
        for h in range(heads):
            total = dot_nn(one_hot_rows(rows, near_ref[h] - r), rows_ref[h])
            total += so_far_ref[h, r : r + rows].astype(F32)
            if not last:
                out_ref[h, r : r + rows] = total.astype(BF16)
                continue
            for side in range(2):
                mixed_ref[side, pl.Slice(h, rows, heads), :] = total[
                    :, side * width : (side + 1) * width
                ]
        if not last:
            continue
        here = slice(r * heads, (r + rows) * heads)
        for side in range(2):
            done_ref[side, here] = mixed_ref[side].astype(BF16)
            copies.append(
                pltpu.make_async_copy(
                    done_ref.at[side, here], out_hbm[side].at[here], sems.at[len(copies)]
                )
            )
            copies[-1].start()
    for copy in copies:
        copy.wait()


def place(scalars, labels, keys, values, ids, size, cap, so_far, last=False):
    heads, _, width = keys[0].shape
    moved = [x[m] for x in (keys, values) for m in ids] + [so_far]
    scratch = [
        pltpu.VMEM((heads, len(ids) * size, 2 * width), BF16),
        pltpu.VMEM((heads, 1, len(ids) * size), jnp.int32),
    ]
    if last:
        out_shape = (jax.ShapeDtypeStruct((heads * cap, width), BF16),) * 2
        out_specs = (anywhere(), anywhere())
        scratch += [
            pltpu.VMEM((2, heads * 512, width), F32),
            pltpu.VMEM((2, heads * cap, width), BF16),
            pltpu.SemaphoreType.DMA((2 * cap // 512,)),
        ]
    else:
        out_shape = pltpu.VMEM((heads, cap, 2 * width), BF16)
        out_specs = in_vmem()
    return pl.pallas_call(
        functools.partial(place_kernel, ids, size, last),
        in_specs=[pl.BlockSpec(memory_space=pltpu.SMEM)] + [in_vmem()] * (1 + len(moved)),
        out_specs=out_specs,
        out_shape=out_shape,
        scratch_shapes=scratch,
        compiler_params=params(),
        name="place",
    )(scalars, labels, *map(keep_vmem, moved))


def body(key_rows, value_rows, cluster_labels, owner_bounds, init_centroids):
    n = lax.axis_size("ctx")
    me = lax.axis_index("ctx").astype(jnp.int32)
    tokens, heads, width = key_rows.shape
    cap = 2 * tokens
    slot = cap // n
    send_size = slot + 16
    key_size = min(tokens, -(-send_size // LANES) * LANES)

    def swap(x, d):
        return lax.ppermute(x, "ctx", [(i, i ^ d) for i in range(n)])

    def spread(x):
        return [x] + [swap(x, d) for d in range(1, n)]

    def aligned(start, size):
        return jnp.minimum(start // 16 * 16, tokens - size)

    me_array = me.reshape(1)
    own_keys, own_labels, own_spots = sort_keys(
        cluster_labels, key_rows.reshape(heads * tokens, width)
    )
    keys = {0: own_keys}
    d = 1
    while d < n:
        keys[d] = swap(own_keys, d)
        d *= 2
    pairs = [(i, i ^ 1) for i in range(lax.axis_size("head"))]
    word = lax.ppermute(own_labels[:, :, :LANES], "head", pairs)
    own_total = own_totals(own_keys, init_centroids, word)
    shared = spread(jnp.concatenate([own_total, own_labels], axis=1))
    totals = [own_total] + [x[:, 0:1] for x in shared[1:]]

    sums, unit, cents = first_block(me_array, own_keys, own_total, init_centroids, n, None)
    units = [unit]
    *came, sums = lax.optimization_barrier((*keys.values(), sums))
    keys = dict(zip(keys, came))
    for m in range(1, n):
        if m not in keys:
            keys[m] = swap(keys[m & (m - 1)], m & -m)
    keys = [keys[m] for m in range(n)]
    peer_low = jnp.take(owner_bounds, me ^ jnp.arange(n, dtype=jnp.int32), axis=1)
    own_below = jnp.sum((own_labels < peer_low[:, :, None]).astype(jnp.int32), axis=2)
    own_values = sort_values(own_spots, value_rows.reshape(heads * tokens, width))

    labels = jnp.concatenate([x[:, -1:] for x in shared], axis=1)
    ranks = own_ranks(me_array, labels)
    low = lax.dynamic_slice_in_dim(owner_bounds, me, 1, 1)
    high = lax.dynamic_slice_in_dim(owner_bounds, me + 1, 1, 1)
    below = jnp.sum((labels < low[:, :, None]).astype(jnp.int32), axis=2)
    first = jnp.sum(below, axis=1, keepdims=True)
    key_starts = aligned(below, key_size)
    gaps = aligned(below, send_size) - key_starts
    one = jnp.ones((1, n), jnp.int32)
    scalars = jnp.stack([key_starts, gaps, low * one, high * one, first * one])

    starts = aligned(own_below, send_size)
    late = [2]
    early = [d for d in range(1, n) if d not in late]
    values = {}
    for m in range(1, n):
        sums, unit = first_block(me_array, keys[m], totals[m], cents, n, sums)
        units.append(unit)
        group = {1: early, 2: [0, *late]}.get(m)
        if group:
            some = jnp.stack([starts[:, d] for d in group], axis=1)
            for d, window in zip(group, windows(some, ranks, own_values, send_size, unit)):
                values[d] = swap(window, d) if d else window

    raw, part, so_far = raw_weights(
        sums, units, scalars, labels, own_keys, values[0], key_size, cap
    )
    parts = spread(part)
    so_far = place(scalars, labels, keys, values, early, key_size, cap, so_far)
    so_far, units[0] = lax.optimization_barrier((so_far, units[0]))
    out = weighted_sums(raw, units, parts)
    placed = place(scalars, labels, keys, values, late, key_size, cap, so_far, last=True)
    shape = (cap, heads, width)
    return out, placed[0].reshape(shape), placed[1].reshape(shape)


def solution(mesh):
    placed = (
        P(("grp", "ctx"), "head", None),
        P(("grp", "ctx"), "head", None),
        P("head", ("grp", "ctx")),
        P(("grp", "head"), None),
        P(("grp", "head"), None, None),
    )
    return jax.shard_map(
        body,
        mesh=mesh,
        in_specs=placed,
        out_specs=(
            P(("grp", "head"), "ctx", None),
            P(("grp", "ctx"), "head", None),
            P(("grp", "ctx"), "head", None),
        ),
        check_vma=False,
    )
```

```python
import functools
import math

import jax
import jax.numpy as jnp
from jax import lax
from jax.experimental import pallas as pl
from jax.experimental.pallas import tpu as pltpu
from jax.sharding import PartitionSpec as P

LANES = 128
EXP2_SCALE = 20.0 * math.log2(math.e)
VMEM_LIMIT = 16 * 1024 * 1024
F32 = jnp.float32
BF16 = jnp.bfloat16
NT = (((1,), (1,)), ((), ()))
NN = (((1,), (0,)), ((), ()))


def dot_nt(a, b):
    return lax.dot_general(a, b, NT, preferred_element_type=F32)


def dot_nn(a, b):
    return lax.dot_general(a, b, NN, preferred_element_type=F32)


def unit_rows(x):
    return x * lax.rsqrt(jnp.sum(x * x, axis=-1, keepdims=True) + 1e-06)


def params(**kwargs):
    return pltpu.CompilerParams(vmem_limit_bytes=VMEM_LIMIT, **kwargs)


def whole(shape):
    return pl.BlockSpec(shape, lambda *_: (0,) * len(shape))


def in_vmem():
    return pl.BlockSpec(memory_space=pltpu.VMEM)


def anywhere():
    return pl.BlockSpec(memory_space=pl.ANY)


def keep_hbm(x):
    return pltpu.with_memory_space_constraint(x, pltpu.HBM)


def keep_vmem(x):
    return pltpu.with_memory_space_constraint(x, pltpu.VMEM)


def row_to_lanes(row):
    return jnp.transpose(jnp.broadcast_to(row, (LANES, LANES)))


def split_heads(flat_ref, wide_ref):
    wide_ref[...] = flat_ref[...].astype(F32)


def head_rows(wide_ref, head, heads):
    if heads == 1:
        return wide_ref[...]
    return wide_ref[pl.Slice(head, wide_ref.shape[0] // heads, heads), :]


def count_below(all_ref, own_row, count):
    tokens = own_row.shape[1]
    mine = jnp.broadcast_to(own_row, (8, tokens))
    wide = 4 * LANES

    def step(i, total):
        row = all_ref[0, :, pl.ds(pl.multiple_of(i * wide, wide), wide)]
        for s in range(0, wide, LANES):
            column = row_to_lanes(row[:, s : s + LANES])
            for r in range(0, LANES, 8):
                other = jnp.tile(column[r : r + 8], (1, tokens // LANES))
                total += (other < mine).astype(jnp.int32)
        return total

    total = lax.fori_loop(
        0, count // wide, step, jnp.zeros((8, tokens), jnp.int32), unroll=True
    )
    return jnp.sum(total, axis=0, keepdims=True)


def one_hot_rows(size, spot):
    slots = lax.broadcasted_iota(jnp.int16, (size, spot.shape[1]), 0)
    return jnp.where(
        slots == spot.astype(jnp.int16), jnp.ones((), BF16), jnp.zeros((), BF16)
    )


def sort_kernel(label_hbm, keys_hbm, *refs):
    out_keys, out_labels, out_spots, flat_ref, wide_ref, order_ref, label_ref, sems = refs
    heads, tokens, _ = out_keys.shape
    label_copy = pltpu.make_async_copy(label_hbm, label_ref, sems.at[1])
    label_copy.start()
    copy = pltpu.make_async_copy(keys_hbm, flat_ref, sems.at[0])
    copy.start()
    label_copy.wait()
    labels = [label_ref[h : h + 1, :] for h in range(heads)]
    spots = []
    for h, label in enumerate(labels):
        order = label * tokens + lax.broadcasted_iota(jnp.int32, label.shape, 1)
        order_ref[0] = order
        spots.append(count_below(order_ref, order, tokens))
        out_spots[h] = spots[h]
    copy.wait()
    split_heads(flat_ref, wide_ref)
    rows = 512
    for h, label in enumerate(labels):
        keys = head_rows(wide_ref, h, heads).astype(BF16)
        digits = jnp.concatenate(
            [
                jnp.broadcast_to(label >> 6, (8, tokens)),
                jnp.broadcast_to(label & 63, (8, tokens)),
            ],
            axis=0,
        )
        digits = digits.astype(F32).astype(BF16)
        for r in range(0, tokens, rows):
            pick = one_hot_rows(rows, spots[h] - r)
            out_keys[h, r : r + rows] = dot_nn(pick, keys).astype(BF16)
            digit = dot_nt(digits, pick)
            out_labels[h, :, r : r + rows] = digit[0:1] * 64.0 + digit[8:9]


def sort_keys(labels, keys):
    heads, tokens = labels.shape
    flat, width = keys.shape
    return pl.pallas_call(
        sort_kernel,
        in_specs=[anywhere()] * 2,
        out_specs=(in_vmem(),) * 3,
        out_shape=(
            pltpu.VMEM((heads, tokens, width), BF16),
            pltpu.VMEM((heads, 1, tokens), F32),
            pltpu.VMEM((heads, 1, tokens), jnp.int32),
        ),
        scratch_shapes=[
            pltpu.VMEM((flat, width), BF16),
            pltpu.VMEM((flat, width), F32),
            pltpu.VMEM((1, 1, tokens), jnp.int32),
            pltpu.VMEM(labels.shape, jnp.int32),
            pltpu.SemaphoreType.DMA((2,)),
        ],
        compiler_params=params(),
        name="sort_keys",
    )(keep_hbm(labels), keep_hbm(keys))


def values_kernel(spot_ref, values_hbm, out_ref, flat_ref, wide_ref, sem):
    heads, _, tokens = spot_ref.shape
    copy = pltpu.make_async_copy(values_hbm, flat_ref, sem)
    copy.start()
    copy.wait()
    split_heads(flat_ref, wide_ref)
    rows = 512
    for h in range(heads):
        values = head_rows(wide_ref, h, heads).astype(BF16)
        for r in range(0, tokens, rows):
            pick = one_hot_rows(rows, spot_ref[h] - r)
            out_ref[h, r : r + rows] = dot_nn(pick, values).astype(BF16)


def sort_values(spots, values):
    heads, _, tokens = spots.shape
    flat, width = values.shape
    return pl.pallas_call(
        values_kernel,
        in_specs=[in_vmem(), anywhere()],
        out_specs=in_vmem(),
        out_shape=pltpu.VMEM((heads, tokens, width), BF16),
        scratch_shapes=[
            pltpu.VMEM((flat, width), BF16),
            pltpu.VMEM((flat, width), F32),
            pltpu.SemaphoreType.DMA,
        ],
        compiler_params=params(),
        name="sort_values",
    )(keep_vmem(spots), keep_hbm(values))


def windows_kernel(size, start_ref, rank_ref, values_ref, _, *out_refs):
    heads, tokens, _ = values_ref.shape
    for h in range(heads):
        rank = rank_ref[h].astype(jnp.int32)
        digits = [
            digit[:, t : t + LANES]
            for digit in (rank >> 7, rank & 127)
            for t in range(0, tokens, LANES)
        ]
        digits = jnp.concatenate(digits, axis=0).astype(F32).astype(BF16)
        for m, out_ref in enumerate(out_refs):
            start = pl.multiple_of(start_ref[h, m], 16)
            out_ref[h, :size] = values_ref[h, pl.ds(start, size), :]
            out_ref[h, size:] = digits


def windows(starts, ranks, values, size, after):
    heads, tokens, width = values.shape
    n = starts.shape[1]
    out = pltpu.VMEM((heads, size + 2 * tokens // LANES, width), BF16)
    return pl.pallas_call(
        functools.partial(windows_kernel, size),
        in_specs=[pl.BlockSpec(memory_space=pltpu.SMEM), in_vmem(), in_vmem(), in_vmem()],
        out_specs=(in_vmem(),) * n,
        out_shape=(out,) * n,
        compiler_params=params(),
        name="windows",
    )(starts, ranks, keep_vmem(values), keep_vmem(after))


def rank_kernel(me_ref, label_ref, rank_ref):
    heads, n, tokens = label_ref.shape
    me = me_ref[0]
    for h in range(heads):
        own = label_ref[h, 0:1, :].astype(jnp.int32)
        rank = lax.broadcasted_iota(jnp.int32, own.shape, 1)
        for m in range(1, n):
            bar = own + ((me ^ m) < me).astype(jnp.int32)
            bar = jnp.broadcast_to(bar, (16, tokens)).astype(jnp.int16)
            count = jnp.zeros((16, tokens), BF16)
            for s in range(0, tokens, LANES):
                column = row_to_lanes(label_ref[h, m : m + 1, s : s + LANES])
                column = column.astype(jnp.int32).astype(jnp.int16)
                for r in range(0, LANES, 16):
                    other = jnp.tile(column[r : r + 16], (1, tokens // LANES))
                    count += jnp.where(other < bar, jnp.ones((), BF16), jnp.zeros((), BF16))
            rank += jnp.sum(count.astype(F32), axis=0, keepdims=True).astype(jnp.int32)
        rank_ref[h] = rank.astype(F32)


def own_ranks(me, labels):
    heads, _, tokens = labels.shape
    return pl.pallas_call(
        rank_kernel,
        in_specs=[pl.BlockSpec(memory_space=pltpu.SMEM), in_vmem()],
        out_specs=in_vmem(),
        out_shape=jax.ShapeDtypeStruct((heads, 1, tokens), F32),
        compiler_params=params(),
        name="own_ranks",
    )(me, labels)


def totals_kernel(keys_ref, cent_ref, _, tot_ref, unit_ref, sum_ref):
    step = pl.program_id(1)
    tokens = unit_ref.shape[0]

    @pl.when(step == 0)
    def _():
        unit_ref[...] = unit_rows(keys_ref[pl.program_id(0)].astype(F32)).astype(BF16)
        sum_ref[...] = jnp.zeros_like(sum_ref)

    part = 512
    rows = min(1024, cent_ref.shape[1])
    for c in range(0, cent_ref.shape[1], rows):
        cent = unit_rows(cent_ref[0, c : c + rows]).astype(BF16)
        for t in range(0, tokens, part):
            raw = jnp.exp2(dot_nt(cent, unit_ref[t : t + part, :]) * EXP2_SCALE)
            sum_ref[:, t : t + part] += jnp.sum(raw.reshape(-1, 8, part), axis=0)

    @pl.when(step == pl.num_programs(1) - 1)
    def _():
        tot_ref[0] = jnp.sum(sum_ref[...], axis=0, keepdims=True)


def own_totals(keys, cents, after):
    heads, count, width = cents.shape
    tokens = keys.shape[1]
    rows = min(2048, count)
    return pl.pallas_call(
        totals_kernel,
        grid=(heads, count // rows),
        in_specs=[
            in_vmem(),
            pl.BlockSpec((1, rows, width), lambda h, c: (h, c, 0)),
            in_vmem(),
        ],
        out_specs=pl.BlockSpec((1, 1, tokens), lambda h, c: (h, 0, 0)),
        out_shape=jax.ShapeDtypeStruct((heads, 1, tokens), F32),
        scratch_shapes=[
            pltpu.VMEM((tokens, width), BF16),
            pltpu.VMEM((8, tokens), F32),
        ],
        compiler_params=params(),
        name="own_totals",
    )(keep_vmem(keys), keep_hbm(cents), after)


def scale_rows(unit, inverse, scaled_ref):
    for t in range(0, unit.shape[0], LANES):
        scaled_ref[t : t + LANES] = (
            unit[t : t + LANES, :].astype(F32) * row_to_lanes(inverse[:, t : t + LANES])
        ).astype(BF16)


def first_kernel(fresh, _, keys_ref, tot_ref, cent_in, *refs):
    head = pl.program_id(0)
    if fresh:
        sums_ref, unit_ref, cent_ref, scaled_ref = refs
        cent = unit_rows(cent_in[0]).astype(BF16)
        cent_ref[head] = cent
    else:
        _, sums_ref, unit_ref, scaled_ref = refs
        cent = cent_in[head]
    unit = unit_rows(keys_ref[head].astype(F32)).astype(BF16)
    unit_ref[head] = unit
    scale_rows(unit, 1.0 / tot_ref[0], scaled_ref)
    part = 512
    for t in range(0, unit.shape[0], part):
        raw = jnp.exp2(dot_nt(cent, unit[t : t + part, :]) * EXP2_SCALE)
        more = dot_nn(raw.astype(BF16), scaled_ref[t : t + part])
        if fresh and t == 0:
            sums_ref[head] = more
        else:
            sums_ref[head] += more


def first_block(me, keys, totals, cents, n, before):
    heads, tokens, width = keys.shape
    fresh = before is None
    rows = cents.shape[1] // n if fresh else cents.shape[1]
    in_specs = [
        in_vmem(),
        pl.BlockSpec((1, 1, tokens), lambda h, me: (h, 0, 0)),
    ]
    args = [me, keep_vmem(keys), totals]
    out_shape = [
        pltpu.VMEM((heads, rows, width), F32),
        pltpu.VMEM((heads, tokens, width), BF16),
    ]
    aliases = {}
    if fresh:
        in_specs.append(pl.BlockSpec((1, rows, width), lambda h, me: (h, me[0], 0)))
        args.append(keep_hbm(cents))
        out_shape.append(pltpu.VMEM((heads, rows, width), BF16))
    else:
        in_specs += [in_vmem(), in_vmem()]
        args += [keep_vmem(cents), keep_vmem(before)]
        aliases = {4: 0}
    return pl.pallas_call(
        functools.partial(first_kernel, fresh),
        grid_spec=pltpu.PrefetchScalarGridSpec(
            num_scalar_prefetch=1,
            grid=(heads,),
            in_specs=in_specs,
            out_specs=(in_vmem(),) * len(out_shape),
            scratch_shapes=[pltpu.VMEM((tokens, width), BF16)],
        ),
        out_shape=tuple(out_shape),
        input_output_aliases=aliases,
        compiler_params=params(),
        name="first_block",
    )(*args)


def raw_kernel(blocks, sums_ref, *refs):
    units = refs[:blocks]
    raw_ref, total_ref, cent_ref = refs[blocks:]
    head = pl.program_id(0)
    cent_ref[...] = unit_rows(sums_ref[head]).astype(BF16)
    part = 512
    start = 0
    for unit_ref in units:
        for t in range(0, unit_ref.shape[1], part):
            here = slice(start + t, start + t + part)
            raw = jnp.exp2(dot_nt(cent_ref[...], unit_ref[head, t : t + part, :]) * EXP2_SCALE)
            raw_ref[head, :, here] = raw.astype(BF16)
            total = jnp.sum(raw.reshape(-1, 8, part), axis=0)
            total_ref[0, :, here] = jnp.sum(total, axis=0, keepdims=True)
        start += unit_ref.shape[1]


def raw_weights(sums, units):
    heads, rows, width = sums.shape
    tokens = units[0].shape[1]
    count = tokens * len(units)
    return pl.pallas_call(
        functools.partial(raw_kernel, len(units)),
        grid=(heads,),
        in_specs=[in_vmem()] * (1 + len(units)),
        out_specs=(in_vmem(), pl.BlockSpec((1, 1, count), lambda h: (h, 0, 0))),
        out_shape=(
            pltpu.VMEM((heads, rows, count), BF16),
            jax.ShapeDtypeStruct((heads, 1, count), F32),
        ),
        scratch_shapes=[pltpu.VMEM((rows, width), BF16)],
        compiler_params=params(),
        name="raw_weights",
    )(keep_vmem(sums), *map(keep_vmem, units))


def sums_kernel(blocks, raw_ref, *refs):
    totals, units = refs[:blocks], refs[blocks : 2 * blocks]
    out_hbm, scaled_ref, result_ref, sems = refs[2 * blocks :]
    heads, tokens, _ = units[0].shape
    copies = []
    for h in range(heads):
        for m, unit_ref in enumerate(units):
            row_total = totals[0][h, :, m * tokens : (m + 1) * tokens]
            for d in range(1, blocks):
                peer = m ^ d
                row_total += totals[d][h, :, peer * tokens : (peer + 1) * tokens]
            here = slice(m * tokens, (m + 1) * tokens)
            scale_rows(unit_ref[h], 1.0 / row_total, scaled_ref.at[h, here])
        turned = lax.dot_general(
            scaled_ref[h], raw_ref[h], (((0,), (1,)), ((), ())), preferred_element_type=F32
        )
        result_ref[h] = unit_rows(jnp.transpose(turned))
        copies.append(pltpu.make_async_copy(result_ref.at[h], out_hbm.at[h], sems.at[h]))
        copies[-1].start()
    for copy in copies:
        copy.wait()


def weighted_sums(raw, units, totals):
    heads, rows, count = raw.shape
    width = units[0].shape[2]
    return pl.pallas_call(
        functools.partial(sums_kernel, len(units)),
        in_specs=[in_vmem()] * (1 + 2 * len(units)),
        out_specs=anywhere(),
        out_shape=jax.ShapeDtypeStruct((heads, rows, width), F32),
        scratch_shapes=[
            pltpu.VMEM((heads, count, width), BF16),
            pltpu.VMEM((heads, rows, width), F32),
            pltpu.SemaphoreType.DMA((heads,)),
        ],
        compiler_params=params(),
        name="weighted_sums",
    )(keep_vmem(raw), *map(keep_vmem, totals), *map(keep_vmem, units))


def fill_windows(ids, size, scalar_ref, label_ref, keys, values, rows_ref, near_ref):
    heads, tokens, width = keys[0].shape
    digit_rows = tokens // LANES
    sent = values[0].shape[1] - 2 * digit_rows
    rows_ref[:, :, width:] = jnp.zeros((heads, len(ids) * size, width), BF16)
    for h in range(heads):
        low, high, first = (scalar_ref[i, h, 0].astype(F32) for i in range(2, 5))
        for i, m in enumerate(ids):
            start = pl.multiple_of(scalar_ref[0, h, m], 16)
            gap = pl.multiple_of(scalar_ref[1, h, m], 16)
            here = i * size
            rows_ref[h, here : here + size, :width] = keys[i][h, pl.ds(start, size), :]
            rows_ref[h, pl.ds(here + gap, sent), width:] = values[i][h, :sent, :]
            digits = values[i][h, sent:, :].astype(F32)
            rank = digits[:digit_rows] * 128.0 + digits[digit_rows:]
            rank = jnp.concatenate([rank[r : r + 1] for r in range(digit_rows)], axis=1)
            label = label_ref[h, m : m + 1, :]
            mine = (label >= low) & (label < high)
            spot = jnp.where(mine, rank - first, -1.0).astype(jnp.int32)
            spot = pltpu.roll(spot, lax.rem(tokens - start, tokens), 1)
            near_ref[h, :, here : here + size] = spot[:, :size]


def place_kernel(ids, size, fresh, scalar_ref, label_ref, *refs):
    count = len(ids)
    keys, values, refs = refs[:count], refs[count : 2 * count], refs[2 * count :]
    if fresh:
        so_far_ref, rows_ref, near_ref = refs
    else:
        so_far_ref, *out_hbm, rows_ref, near_ref, mixed_ref, done_ref, sems = refs
    fill_windows(ids, size, scalar_ref, label_ref, keys, values, rows_ref, near_ref)
    heads, cap, both = so_far_ref.shape
    width = both // 2
    rows = 512
    copies = []
    for r in range(0, cap, rows):
        for h in range(heads):
            total = dot_nn(one_hot_rows(rows, near_ref[h] - r), rows_ref[h])
            if fresh:
                so_far_ref[h, r : r + rows] = total.astype(BF16)
                continue
            total += so_far_ref[h, r : r + rows].astype(F32)
            for side in range(2):
                mixed_ref[side, pl.Slice(h, rows, heads), :] = total[
                    :, side * width : (side + 1) * width
                ]
        if fresh:
            continue
        here = slice(r * heads, (r + rows) * heads)
        for side in range(2):
            done_ref[side, here] = mixed_ref[side].astype(BF16)
            copies.append(
                pltpu.make_async_copy(
                    done_ref.at[side, here], out_hbm[side].at[here], sems.at[len(copies)]
                )
            )
            copies[-1].start()
    for copy in copies:
        copy.wait()


def place(scalars, labels, keys, values, ids, size, cap, so_far):
    heads, _, width = keys[0].shape
    fresh = so_far is None
    moved = [x[m] for x in (keys, values) for m in ids]
    scratch = [
        pltpu.VMEM((heads, len(ids) * size, 2 * width), BF16),
        pltpu.VMEM((heads, 1, len(ids) * size), jnp.int32),
    ]
    if fresh:
        out_shape = pltpu.VMEM((heads, cap, 2 * width), BF16)
        out_specs = in_vmem()
    else:
        moved.append(so_far)
        out_shape = (jax.ShapeDtypeStruct((heads * cap, width), BF16),) * 2
        out_specs = (anywhere(), anywhere())
        scratch += [
            pltpu.VMEM((2, heads * 512, width), F32),
            pltpu.VMEM((2, heads * cap, width), BF16),
            pltpu.SemaphoreType.DMA((2 * cap // 512,)),
        ]
    return pl.pallas_call(
        functools.partial(place_kernel, ids, size, fresh),
        in_specs=[pl.BlockSpec(memory_space=pltpu.SMEM)] + [in_vmem()] * (1 + len(moved)),
        out_specs=out_specs,
        out_shape=out_shape,
        scratch_shapes=scratch,
        compiler_params=params(),
        name="place",
    )(scalars, labels, *map(keep_vmem, moved))


def body(key_rows, value_rows, cluster_labels, owner_bounds, init_centroids):
    n = lax.axis_size("ctx")
    me = lax.axis_index("ctx").astype(jnp.int32)
    tokens, heads, width = key_rows.shape
    cap = 2 * tokens
    slot = cap // n
    send_size = slot + 16
    key_size = min(tokens, -(-send_size // LANES) * LANES)

    def swap(x, d):
        return lax.ppermute(x, "ctx", [(i, i ^ d) for i in range(n)])

    def spread(x):
        return [x] + [swap(x, d) for d in range(1, n)]

    def aligned(start, size):
        return jnp.minimum(start // 16 * 16, tokens - size)

    me_array = me.reshape(1)
    own_keys, own_labels, own_spots = sort_keys(
        cluster_labels, key_rows.reshape(heads * tokens, width)
    )
    keys = {0: own_keys}
    d = 1
    while d < n:
        keys[d] = swap(own_keys, d)
        d *= 2
    pairs = [(i, i ^ 1) for i in range(lax.axis_size("head"))]
    word = lax.ppermute(own_labels[:, :, :LANES], "head", pairs)
    own_total = own_totals(own_keys, init_centroids, word)
    shared = spread(jnp.concatenate([own_total, own_labels], axis=1))
    totals = [own_total] + [x[:, 0:1] for x in shared[1:]]

    sums, unit, cents = first_block(me_array, own_keys, own_total, init_centroids, n, None)
    units = [unit]
    *came, sums = lax.optimization_barrier((*keys.values(), sums))
    keys = dict(zip(keys, came))
    for m in range(1, n):
        if m not in keys:
            keys[m] = swap(keys[m & (m - 1)], m & -m)
    keys = [keys[m] for m in range(n)]
    peer_low = jnp.take(owner_bounds, me ^ jnp.arange(n, dtype=jnp.int32), axis=1)
    own_below = jnp.sum((own_labels < peer_low[:, :, None]).astype(jnp.int32), axis=2)
    own_values = sort_values(own_spots, value_rows.reshape(heads * tokens, width))

    labels = jnp.concatenate([x[:, -1:] for x in shared], axis=1)
    ranks = own_ranks(me_array, labels)
    low = lax.dynamic_slice_in_dim(owner_bounds, me, 1, 1)
    high = lax.dynamic_slice_in_dim(owner_bounds, me + 1, 1, 1)
    below = jnp.sum((labels < low[:, :, None]).astype(jnp.int32), axis=2)
    first = jnp.sum(below, axis=1, keepdims=True)
    key_starts = aligned(below, key_size)
    gaps = aligned(below, send_size) - key_starts
    one = jnp.ones((1, n), jnp.int32)
    scalars = jnp.stack([key_starts, gaps, low * one, high * one, first * one])

    starts = aligned(own_below, send_size)
    late = [2]
    early = [d for d in range(1, n) if d not in late]
    values = {}
    for m in range(1, n):
        sums, unit = first_block(me_array, keys[m], totals[m], cents, n, sums)
        units.append(unit)
        group = {1: early, 2: [0, *late]}.get(m)
        if group:
            some = jnp.stack([starts[:, d] for d in group], axis=1)
            for d, window in zip(group, windows(some, ranks, own_values, send_size, unit)):
                values[d] = swap(window, d) if d else window

    raw, part = raw_weights(sums, units)
    parts = spread(part)
    so_far = place(scalars, labels, keys, values, [0, *early], key_size, cap, None)
    out = weighted_sums(raw, units, parts)
    placed = place(scalars, labels, keys, values, late, key_size, cap, so_far)
    shape = (cap, heads, width)
    return out, placed[0].reshape(shape), placed[1].reshape(shape)


def solution(mesh):
    placed = (
        P(("grp", "ctx"), "head", None),
        P(("grp", "ctx"), "head", None),
        P("head", ("grp", "ctx")),
        P(("grp", "head"), None),
        P(("grp", "head"), None, None),
    )
    return jax.shard_map(
        body,
        mesh=mesh,
        in_specs=placed,
        out_specs=(
            P(("grp", "head"), "ctx", None),
            P(("grp", "ctx"), "head", None),
            P(("grp", "ctx"), "head", None),
        ),
        check_vma=False,
    )
```
